32 devices in a mesh: win: 4 (over x, core), chan: 8 (over z, y).
Axes of the slice: x: 2, y: 2, z: 4, core: 2. Of those that a mesh axis runs over, the one named last changes fastest.
Arguments:
- traces: bfloat16 [32, 256, 7680], P('win', 'chan'), may hold values from -6 to 6
- filter_taps: bfloat16 [32], replicated, may hold values from 0.019897461 to 0.14941406
- good_channels: int32 [256], P('chan'), may hold values 0 or 1
- source_index: int32 [256], replicated, may hold values from 0 to 255, as said below
Outputs:
- correlations: float32 [256, 256, 2048], P('win', 'chan')
The draws below stay inside these ranges and needn't reach their ends.
Inputs may be any that keep to these rules, and one draw needn't show every extreme that they name: `source_index`: 256 distinct channel numbers; channels 0 and 255 are among them; how many fall in one device's block varies.
All inputs are finite; a program needn't handle non-finite values. No bound on the sum of `good_channels` on one device may be relied on, other than what follows from the above.
Results may differ from the reference program's by a relative error of at most 0.0071.
Values may be sent and summed in bfloat16 or wider, within the bound.
No kernel may reach another device: no remote copies, remote signals or barrier semaphores. Data moves between devices by JAX's collectives and lax.ppermute only.
A program may use at most 192 MiB of HBM per device.

```python
import math
import jax
import jax.numpy as jnp
from jax import lax

L = 7680
F = 512
LAGS = 2048
S = 256
HALO = 16
SMOOTH = 64
K0 = 31
CH = 256
WINDOWS = 32


def draw_source_index(key, part):
    key_first, key_second = jax.random.split(jax.random.fold_in(key, 7))
    middle = jax.random.permutation(key_first, CH - 2)[:S - 2].astype(jnp.int32) + 1
    chosen = jnp.concatenate([jnp.array([0, CH - 1], jnp.int32), middle])
    shuffle = jax.random.permutation(key_second, S)
    return chosen[shuffle].astype(jnp.int32)


def touch_ends(result, own_key, least, largest):
    place = [jax.random.randint(jax.random.fold_in(own_key, axis), (), 0, length) for axis, length in enumerate(result.shape)]
    main_axis = result.shape.index(max(result.shape))
    beside = place[:main_axis] + [(place[main_axis] + 1) % result.shape[main_axis]] + place[main_axis + 1:]
    return result.at[tuple(place)].set(least).at[tuple(beside)].set(largest)


def shard_levels(rng, extent, cuts, low, largest):
    loudness, own = 1.0, jax.random.fold_in(rng, 6)
    for axis_at, shards_of in cuts:
        heights = jnp.exp(jax.random.uniform(jax.random.fold_in(own, axis_at), (shards_of,), jnp.float32, low / len(cuts), largest / len(cuts)))
        loudness = loudness * jnp.repeat(heights, extent[axis_at] // shards_of).reshape([-1 if axis == axis_at else 1 for axis in range(len(extent))])
    return loudness


def noise(rng, dims, scale, most, pieces=(), kind=jnp.bfloat16):
    factor_of = shard_levels(rng, dims, pieces, -0.22, 0.18) if pieces else 1.0
    values = jax.random.normal(rng, dims, jnp.float32) * scale * factor_of
    return jnp.minimum(jnp.maximum(values, -most), most).astype(kind)


def setup_inputs(seed: int = 0) -> dict:
    keys = jax.random.split(jax.random.key(seed), 5)
    return {
        "traces": noise(keys[0], (WINDOWS, CH, L), 1.0, 6.0, ((0, 4), (1, 8))),
        "filter_taps": jnp.clip(jnp.exp(jax.random.uniform(keys[1], (2 * HALO,), jnp.float32, math.log(0.019897461), math.log(0.14941406))), 0.019897461, 0.14941406).astype(jnp.bfloat16),
        "good_channels": touch_ends((jax.random.randint(keys[2], (CH,), 0, 16) < 15).astype(jnp.int32), jax.random.fold_in(keys[2], 1), 0, 1),
        "source_index": draw_source_index(jax.random.fold_in(keys[4], 71), 0),
    }


def forward_table():
    times_idx = jnp.arange(L, dtype=jnp.int32)
    band_bins = K0 + jnp.arange(F, dtype=jnp.int32)
    phase_index = times_idx[:, None] * band_bins[None, :] % L
    angles = phase_index.astype(jnp.float32) * (2.0 * math.pi / L)
    return jnp.concatenate([jnp.cos(angles), -jnp.sin(angles)], axis=1).astype(jnp.bfloat16)

def inverse_table():
    lag_values = jnp.arange(LAGS, dtype=jnp.int32) - LAGS // 2
    band_bins = K0 + jnp.arange(F, dtype=jnp.int32)
    phase_index = jnp.mod(band_bins[:, None] * lag_values[None, :], L)
    angles = phase_index.astype(jnp.float32) * (2.0 * math.pi / L)
    return jnp.concatenate([jnp.cos(angles), -jnp.sin(angles)], axis=0).astype(jnp.bfloat16)

def smoothing():
    positions = jnp.arange(F, dtype=jnp.int32)
    near = (jnp.abs(positions[:, None] - positions[None, :]) <= SMOOTH).astype(jnp.float32)
    return near / lax.optimization_barrier(jnp.sum(near, axis=0, keepdims=True))

def whiten(spectrum):
    real_part = spectrum[..., :F]
    imag_part = spectrum[..., F:]
    magnitude = jnp.sqrt(real_part * real_part + imag_part * imag_part)
    flat = magnitude.reshape(-1, F)
    amplitude = jnp.dot(flat, smoothing(), precision=lax.Precision.HIGHEST).reshape(magnitude.shape)
    divisor = jnp.concatenate([amplitude, amplitude], axis=-1) + 1e-06
    return (spectrum / divisor).astype(jnp.bfloat16)

def reference(traces, filter_taps, good_channels, source_index):
    kernel = jnp.concatenate([-filter_taps[:HALO].astype(jnp.float32), jnp.ones((1,), jnp.float32), -filter_taps[HALO:].astype(jnp.float32)])
    masked = traces * good_channels.astype(jnp.bfloat16)[None, :, None]
    keep = good_channels.astype(jnp.float32)[:, None]
    table = forward_table()

    def one_window(window):
        padded = jnp.pad(window, ((HALO, HALO), (0, 0))).astype(jnp.float32)
        total = jnp.zeros((CH, L), jnp.float32)
        for position in range(2 * HALO + 1):
            total = total + kernel[position] * padded[position:position + CH]
        filtered = (total * keep).astype(jnp.bfloat16)
        spectrum = jnp.dot(filtered, table, preferred_element_type=jnp.float32)
        return whiten(spectrum)
    whitened = lax.map(one_window, masked)
    wide = whitened.astype(jnp.float32)
    wide_real = wide[..., :F]
    wide_imag = wide[..., F:]
    picked = jnp.transpose(jnp.take(whitened, source_index.astype(jnp.int32), axis=1), (1, 0, 2))
    inverse = inverse_table()
    scaling = 1.0 / math.sqrt(F * WINDOWS)
    high = lax.Precision.HIGHEST

    def one_source(spectra):
        source = spectra.astype(jnp.float32)
        src_real = source[:, :F]
        src_imag = source[:, F:]
        real_sum = jnp.einsum('wf,wcf->cf', src_real, wide_real, precision=high) + jnp.einsum('wf,wcf->cf', src_imag, wide_imag, precision=high)
        imag_sum = jnp.einsum('wf,wcf->cf', src_real, wide_imag, precision=high) - jnp.einsum('wf,wcf->cf', src_imag, wide_real, precision=high)
        stacked = jnp.concatenate([real_sum, imag_sum], axis=-1).astype(jnp.bfloat16)
        return jnp.dot(stacked, inverse, preferred_element_type=jnp.float32) * scaling
    return lax.map(one_source, picked)
```

```python
import functools
import math

import jax
import jax.numpy as jnp
import numpy as np
from jax import lax
from jax.experimental import pallas as pl
from jax.experimental.pallas import tpu as pltpu
from jax.sharding import PartitionSpec as P

L = 7680
F = 512
LAGS = 2048
HALO = 16
SMOOTH = 64
K0 = 31
QUARTER = L // 4
STEP = 384
FINE = 32
CHUNKS = 2
LAG_FINE = 128
NT = (((1,), (1,)), ((), ()))
MIB = 1024 * 1024


def unit_angles(positions, axis):
    bins = K0 + np.arange(F, dtype=np.int64)
    phase = np.mod(np.expand_dims(positions, 1 - axis) * np.expand_dims(bins, axis), L)
    angles = phase * (2.0 * math.pi / L)
    return np.cos(angles).astype(np.float32), np.sin(angles).astype(np.float32)


def transform_kernel(x0, x1, x2, x3, coarse_cos, coarse_sin, fine_cos, fine_sin, good, spec, head, tail, table, total):
    step = pl.program_id(0)
    rows = x0.shape[0]
    for part in range(STEP // FINE):
        big_cos = coarse_cos[0, part : part + 1, :]
        big_sin = coarse_sin[0, part : part + 1, :]
        at = pl.ds(part * FINE, FINE)
        table[at, :F] = (big_cos * fine_cos[...] - big_sin * fine_sin[...]).astype(jnp.bfloat16)
        table[at, F:] = (-(big_sin * fine_cos[...] + big_cos * fine_sin[...])).astype(jnp.bfloat16)

    @pl.when(step == 0)
    def _():
        total[...] = jnp.zeros_like(total)

    for quarter, x in enumerate((x0, x1, x2, x3)):
        at = pl.ds(quarter * rows, rows)
        total[at, :] += jnp.dot(x[...], table[...], preferred_element_type=jnp.float32)

    @pl.when(step == pl.num_programs(0) - 1)
    def _():
        turn = (K0 + lax.broadcasted_iota(jnp.int32, (1, F), 1)) % 4
        even = turn % 2 == 0
        sign = jnp.where(turn < 2, 1.0, -1.0)
        channels = good.shape[0]
        for window in range(rows // channels):
            re = [total[pl.ds(q * rows + window * channels, channels), :F] for q in range(4)]
            im = [total[pl.ds(q * rows + window * channels, channels), F:] for q in range(4)]
            keep = good[...]
            real = jnp.where(even, re[0] + re[2] + sign * (re[1] + re[3]), re[0] - re[2] + sign * (im[1] - im[3])) * keep
            imag = jnp.where(even, im[0] + im[2] + sign * (im[1] + im[3]), im[0] - im[2] - sign * (re[1] - re[3])) * keep
            spec[window, :, :F] = real
            spec[window, :, F:] = imag
            head[window, :, :F] = real[:HALO]
            head[window, :, F:] = imag[:HALO]
            tail[window, :, :F] = real[channels - HALO :]
            tail[window, :, F:] = imag[channels - HALO :]


def transform(traces, keep):
    windows, channels, length = traces.shape
    rows = windows * channels
    steps = QUARTER // STEP
    flat = traces.reshape(rows, length)
    coarse = [t.reshape(steps, STEP // FINE, F) for t in unit_angles(np.arange(QUARTER // FINE) * FINE, 0)]
    fine = unit_angles(np.arange(FINE), 0)
    whole = lambda *shape: pl.BlockSpec(shape, lambda k: (0,) * len(shape))
    return pl.pallas_call(
        transform_kernel,
        grid=(steps,),
        in_specs=[pl.BlockSpec((rows, STEP), functools.partial(lambda q, k: (0, q * steps + k), q)) for q in range(4)]
        + [pl.BlockSpec((1, STEP // FINE, F), lambda k: (k, 0, 0))] * 2
        + [whole(FINE, F)] * 2
        + [whole(channels, 1)],
        out_specs=[whole(windows, channels, 2 * F), whole(windows, HALO, 2 * F), whole(windows, HALO, 2 * F)],
        out_shape=[
            jax.ShapeDtypeStruct((windows, channels, 2 * F), jnp.float32),
            jax.ShapeDtypeStruct((windows, HALO, 2 * F), jnp.float32),
            jax.ShapeDtypeStruct((windows, HALO, 2 * F), jnp.float32),
        ],
        scratch_shapes=[pltpu.VMEM((STEP, 2 * F), jnp.bfloat16), pltpu.VMEM((4 * rows, 2 * F), jnp.float32)],
        compiler_params=pltpu.CompilerParams(vmem_limit_bytes=40 * MIB),
        cost_estimate=pl.CostEstimate(flops=2 * rows * length * 2 * F, bytes_accessed=rows * length * 2, transcendentals=0),
    )(flat, flat, flat, flat, *coarse, *fine, keep)


def pieces(value):
    high = value.astype(jnp.bfloat16)
    rest = value - high.astype(jnp.float32)
    middle = rest.astype(jnp.bfloat16)
    return high, middle, (rest - middle.astype(jnp.float32)).astype(jnp.bfloat16)


def whiten_kernel(spec, left, right, band, good, *outs):
    windows, channels = spec.shape[:2]
    filtered = []
    for window in range(windows):
        padded = jnp.concatenate([left[window], spec[window], right[window]], axis=0)
        stack = jnp.concatenate(pieces(padded), axis=0)
        taps = jnp.concatenate([band[...]] * 3, axis=1)
        filtered.append(jnp.dot(taps, stack, preferred_element_type=jnp.float32) * good[...])
    spectrum = jnp.concatenate(filtered, axis=0)
    real, imag = spectrum[:, :F], spectrum[:, F:]
    magnitude = jnp.sqrt(real * real + imag * imag)
    bins = lax.broadcasted_iota(jnp.int32, (F, F), 0)
    others = lax.broadcasted_iota(jnp.int32, (F, F), 1)
    near = jnp.where(jnp.abs(bins - others) <= SMOOTH, 1.0, 0.0).astype(jnp.bfloat16)
    amplitude = sum(jnp.dot(piece, near, preferred_element_type=jnp.float32) for piece in pieces(magnitude))
    bin_row = lax.broadcasted_iota(jnp.int32, (1, F), 1)
    count = jnp.minimum(bin_row + SMOOTH, F - 1) - jnp.maximum(bin_row - SMOOTH, 0) + 1
    amplitude = amplitude * (1.0 / count.astype(jnp.float32))
    inverse = 1.0 / (amplitude + 1e-06)
    real = (real * inverse).astype(jnp.bfloat16)
    imag = (imag * inverse).astype(jnp.bfloat16)
    width = F // len(outs)
    for at, out in enumerate(outs):
        for window in range(windows):
            rows = slice(window * channels, (window + 1) * channels)
            cols = slice(at * width, (at + 1) * width)
            out[window, :, :width] = real[rows, cols]
            out[window, :, width:] = imag[rows, cols]


def whiten(spec, left, right, band, keep):
    windows, channels, _ = spec.shape
    width = 2 * F // CHUNKS
    return pl.pallas_call(
        whiten_kernel,
        out_shape=[jax.ShapeDtypeStruct((windows, channels, width), jnp.bfloat16)] * CHUNKS,
        compiler_params=pltpu.CompilerParams(vmem_limit_bytes=40 * MIB),
        cost_estimate=pl.CostEstimate(flops=2 * windows * channels * F * F * 3, bytes_accessed=5 * MIB // 2, transcendentals=windows * channels * F),
    )(spec, left, right, band, keep)


def eye(size):
    rows = lax.broadcasted_iota(jnp.int32, (size, size), 0)
    cols = lax.broadcasted_iota(jnp.int32, (size, size), 1)
    return jnp.where(rows == cols, 1.0, 0.0).astype(jnp.bfloat16)


def turned(left_unit, rows):
    return lax.dot_general(left_unit, rows, NT, preferred_element_type=jnp.float32)


def cross_kernel(sources, own, out, by_source, by_own, sums):
    windows, count, both = sources.shape
    channels = own.shape[0]
    width = both // 2
    unit = eye(width)
    for window in range(windows):
        rows = jnp.concatenate([sources[window, :, :width], sources[window, :, width:]], axis=0)
        by_source[pl.ds(window, width, stride=windows), :] = turned(unit, rows)
    for channel in range(channels):
        rows = jnp.concatenate([own[channel, :, :width], own[channel, :, width:]], axis=0)
        by_own[pl.ds(channel, width, stride=channels), :] = turned(unit, rows)
    sign = jnp.where(lax.broadcasted_iota(jnp.int32, (1, 2 * count), 1) < count, 1.0, -1.0)

    def one_bin(at, carry):
        src = by_source[pl.ds(pl.multiple_of(at * windows, windows), windows), :]
        right = jnp.concatenate([src * sign, pltpu.roll(src, count, axis=1)], axis=0).astype(jnp.bfloat16)
        here = pl.ds(pl.multiple_of(at * channels, channels), channels)
        left = by_own[here, :].astype(jnp.bfloat16)
        sums[here, :] = jnp.dot(left, right, preferred_element_type=jnp.float32)
        return carry

    lax.fori_loop(0, width, one_bin, 0, unroll=16)
    unit = eye(2 * count)
    for channel in range(channels):
        rows = sums[pl.ds(channel, width, stride=channels), :].astype(jnp.bfloat16)
        out[channel] = turned(unit, rows).astype(jnp.bfloat16)


def cross(sources, own):
    windows, count, both = sources.shape
    channels = own.shape[0]
    width = both // 2
    return pl.pallas_call(
        cross_kernel,
        out_shape=jax.ShapeDtypeStruct((channels, 2 * count, width), jnp.bfloat16),
        scratch_shapes=[
            pltpu.VMEM((width * windows, 2 * count), jnp.float32),
            pltpu.VMEM((width * channels, 2 * windows), jnp.float32),
            pltpu.VMEM((width * channels, 2 * count), jnp.float32),
        ],
        compiler_params=pltpu.CompilerParams(vmem_limit_bytes=48 * MIB),
        cost_estimate=pl.CostEstimate(flops=8 * windows * count * channels * width, bytes_accessed=8 * MIB, transcendentals=0),
    )(sources, own)


def lag_kernel(scaling, *refs):
    *stacked, table, out = refs
    channels, both, width = stacked[0].shape
    count = both // 2
    rows = []
    for channel in range(channels):
        rows.append(jnp.concatenate([s[channel, :count] for s in stacked] + [s[channel, count:] for s in stacked], axis=1))
    result = jnp.dot(jnp.concatenate(rows, axis=0), table[...], preferred_element_type=jnp.float32) * scaling
    for channel in range(channels):
        out[:, channel, :] = result[channel * count : (channel + 1) * count]


def lagged(stacked, table, scaling):
    channels, both, width = stacked[0].shape
    count = both // 2
    block, cols = 8, LAGS // 2
    return pl.pallas_call(
        functools.partial(lag_kernel, scaling),
        grid=(channels // block, LAGS // cols),
        in_specs=[pl.BlockSpec((block, both, width), lambda i, j: (i, 0, 0))] * len(stacked)
        + [pl.BlockSpec((2 * F, cols), lambda i, j: (0, j))],
        out_specs=pl.BlockSpec((count, block, cols), lambda i, j: (0, i, j)),
        out_shape=jax.ShapeDtypeStruct((count, channels, LAGS), jnp.float32),
        compiler_params=pltpu.CompilerParams(vmem_limit_bytes=48 * MIB),
        cost_estimate=pl.CostEstimate(flops=2 * count * channels * 2 * F * LAGS, bytes_accessed=count * channels * LAGS * 4, transcendentals=0),
    )(*stacked, table)


def inverse_table():
    coarse = unit_angles(np.arange(LAGS // LAG_FINE) * LAG_FINE - LAGS // 2, 1)
    fine = unit_angles(np.arange(LAG_FINE), 1)
    big_cos, big_sin = (jnp.asarray(t)[:, :, None] for t in coarse)
    small_cos, small_sin = (jnp.asarray(t)[:, None, :] for t in fine)
    cos = big_cos * small_cos - big_sin * small_sin
    sin = big_sin * small_cos + big_cos * small_sin
    return jnp.concatenate([cos, -sin], axis=0).astype(jnp.bfloat16).reshape(2 * F, LAGS)


def make_band(filter_taps, channel_count):
    kernel = jnp.concatenate(
        [
            -filter_taps[:HALO].astype(jnp.float32),
            jnp.ones((1,), jnp.float32),
            -filter_taps[HALO:].astype(jnp.float32),
        ]
    )
    row_ids = jnp.arange(channel_count, dtype=jnp.int32)[:, None]
    columns = jnp.arange(channel_count + 2 * HALO, dtype=jnp.int32)[None, :]
    offset = columns - row_ids
    choose = offset[:, :, None] == jnp.arange(2 * HALO + 1, dtype=jnp.int32)[None, None, :]
    return jnp.sum(jnp.where(choose, kernel[None, None, :], 0.0), axis=2).astype(jnp.bfloat16)


def per_device(traces, filter_taps, good_channels, source_index):
    window_count, channel_count, _ = traces.shape
    keep = good_channels.astype(jnp.float32)[:, None]
    spec, head, tail = transform(traces, keep)
    blocks = lax.axis_size("chan")
    left = lax.ppermute(tail, "chan", [(i, i + 1) for i in range(blocks - 1)])
    right = lax.ppermute(head, "chan", [(i + 1, i) for i in range(blocks - 1)])
    whitened = whiten(spec, left, right, make_band(filter_taps, channel_count), keep)
    groups = lax.axis_size("win")
    channel_ids = jnp.arange(blocks * channel_count, dtype=jnp.int32)
    selector = (source_index[:, None] == channel_ids[None, :]).astype(jnp.bfloat16)
    stacked = []
    for part in whitened:
        everything = lax.all_gather(part, "chan", axis=1, tiled=True)
        own = jnp.swapaxes(lax.all_gather(part, "win", axis=0, tiled=True), 0, 1)
        picked = jnp.einsum("sc,wcf->wsf", selector, everything, preferred_element_type=jnp.float32).astype(jnp.bfloat16)
        sources = lax.all_to_all(picked, "win", split_axis=1, concat_axis=0, tiled=True)
        stacked.append(cross(sources, own))
    return lagged(stacked, inverse_table(), 1.0 / math.sqrt(F * window_count * groups))


def solution(mesh):
    placed = (P("win", "chan", None), P(), P("chan"), P())
    return jax.shard_map(
        per_device, mesh=mesh, in_specs=placed, out_specs=P("win", "chan", None), check_vma=False
    )
```

```python
import functools
import math

import jax
import jax.numpy as jnp
import numpy as np
from jax import lax
from jax.experimental import pallas as pl
from jax.experimental.pallas import tpu as pltpu
from jax.sharding import PartitionSpec as P

L = 7680
F = 512
LAGS = 2048
HALO = 16
SMOOTH = 64
K0 = 31
QUARTER = L // 4
STEP = 384
FINE = 32
CHUNKS = 2
GROUP = 16
LAG_FINE = 128
NT = (((1,), (1,)), ((), ()))
MIB = 1024 * 1024


def unit_angles(positions, axis):
    bins = K0 + np.arange(F, dtype=np.int64)
    phase = np.mod(np.expand_dims(positions, 1 - axis) * np.expand_dims(bins, axis), L)
    angles = phase * (2.0 * math.pi / L)
    return np.cos(angles).astype(np.float32), np.sin(angles).astype(np.float32)


def transform_kernel(x0, x1, x2, x3, coarse_cos, coarse_sin, fine_cos, fine_sin, good, spec, head, tail, table, total):
    step = pl.program_id(0)
    rows = x0.shape[0]
    for part in range(STEP // FINE):
        big_cos = coarse_cos[0, part : part + 1, :]
        big_sin = coarse_sin[0, part : part + 1, :]
        at = pl.ds(part * FINE, FINE)
        table[at, :F] = (big_cos * fine_cos[...] - big_sin * fine_sin[...]).astype(jnp.bfloat16)
        table[at, F:] = (-(big_sin * fine_cos[...] + big_cos * fine_sin[...])).astype(jnp.bfloat16)

    @pl.when(step == 0)
    def _():
        total[...] = jnp.zeros_like(total)

    for quarter, x in enumerate((x0, x1, x2, x3)):
        at = pl.ds(quarter * rows, rows)
        total[at, :] += jnp.dot(x[...], table[...], preferred_element_type=jnp.float32)

    @pl.when(step == pl.num_programs(0) - 1)
    def _():
        turn = (K0 + lax.broadcasted_iota(jnp.int32, (1, F), 1)) % 4
        even = turn % 2 == 0
        sign = jnp.where(turn < 2, 1.0, -1.0)
        channels = good.shape[0]
        for window in range(rows // channels):
            re = [total[pl.ds(q * rows + window * channels, channels), :F] for q in range(4)]
            im = [total[pl.ds(q * rows + window * channels, channels), F:] for q in range(4)]
            keep = good[...]
            real = jnp.where(even, re[0] + re[2] + sign * (re[1] + re[3]), re[0] - re[2] + sign * (im[1] - im[3])) * keep
            imag = jnp.where(even, im[0] + im[2] + sign * (im[1] + im[3]), im[0] - im[2] - sign * (re[1] - re[3])) * keep
            spec[window, :, :F] = real
            spec[window, :, F:] = imag
            head[window, :, :F] = real[:HALO]
            head[window, :, F:] = imag[:HALO]
            tail[window, :, :F] = real[channels - HALO :]
            tail[window, :, F:] = imag[channels - HALO :]


def transform(traces, keep):
    windows, channels, length = traces.shape
    rows = windows * channels
    steps = QUARTER // STEP
    flat = traces.reshape(rows, length)
    coarse = [t.reshape(steps, STEP // FINE, F) for t in unit_angles(np.arange(QUARTER // FINE) * FINE, 0)]
    fine = unit_angles(np.arange(FINE), 0)
    whole = lambda *shape: pl.BlockSpec(shape, lambda k: (0,) * len(shape))
    return pl.pallas_call(
        transform_kernel,
        grid=(steps,),
        in_specs=[pl.BlockSpec((rows, STEP), functools.partial(lambda q, k: (0, q * steps + k), q)) for q in range(4)]
        + [pl.BlockSpec((1, STEP // FINE, F), lambda k: (k, 0, 0))] * 2
        + [whole(FINE, F)] * 2
        + [whole(channels, 1)],
        out_specs=[whole(windows, channels, 2 * F), whole(windows, HALO, 2 * F), whole(windows, HALO, 2 * F)],
        out_shape=[
            jax.ShapeDtypeStruct((windows, channels, 2 * F), jnp.float32),
            jax.ShapeDtypeStruct((windows, HALO, 2 * F), jnp.float32),
            jax.ShapeDtypeStruct((windows, HALO, 2 * F), jnp.float32),
        ],
        scratch_shapes=[pltpu.VMEM((STEP, 2 * F), jnp.bfloat16), pltpu.VMEM((4 * rows, 2 * F), jnp.float32)],
        compiler_params=pltpu.CompilerParams(vmem_limit_bytes=40 * MIB),
        cost_estimate=pl.CostEstimate(flops=2 * rows * length * 2 * F, bytes_accessed=rows * length * 2, transcendentals=0),
    )(flat, flat, flat, flat, *coarse, *fine, keep)


def pieces(value):
    high = value.astype(jnp.bfloat16)
    rest = value - high.astype(jnp.float32)
    middle = rest.astype(jnp.bfloat16)
    return high, middle, (rest - middle.astype(jnp.float32)).astype(jnp.bfloat16)


def whiten_kernel(spec, left, right, band, good, *outs):
    windows, channels = spec.shape[:2]
    filtered = []
    for window in range(windows):
        padded = jnp.concatenate([left[window], spec[window], right[window]], axis=0)
        stack = jnp.concatenate(pieces(padded), axis=0)
        taps = jnp.concatenate([band[...]] * 3, axis=1)
        filtered.append(jnp.dot(taps, stack, preferred_element_type=jnp.float32) * good[...])
    spectrum = jnp.concatenate(filtered, axis=0)
    real, imag = spectrum[:, :F], spectrum[:, F:]
    magnitude = jnp.sqrt(real * real + imag * imag)
    bins = lax.broadcasted_iota(jnp.int32, (F, F), 0)
    others = lax.broadcasted_iota(jnp.int32, (F, F), 1)
    near = jnp.where(jnp.abs(bins - others) <= SMOOTH, 1.0, 0.0).astype(jnp.bfloat16)
    amplitude = sum(jnp.dot(piece, near, preferred_element_type=jnp.float32) for piece in pieces(magnitude))
    bin_row = lax.broadcasted_iota(jnp.int32, (1, F), 1)
    count = jnp.minimum(bin_row + SMOOTH, F - 1) - jnp.maximum(bin_row - SMOOTH, 0) + 1
    amplitude = amplitude * (1.0 / count.astype(jnp.float32))
    inverse = 1.0 / (amplitude + 1e-06)
    real = (real * inverse).astype(jnp.bfloat16)
    imag = (imag * inverse).astype(jnp.bfloat16)
    width = F // len(outs)
    for at, out in enumerate(outs):
        for window in range(windows):
            rows = slice(window * channels, (window + 1) * channels)
            cols = slice(at * width, (at + 1) * width)
            out[window, :, :width] = real[rows, cols]
            out[window, :, width:] = imag[rows, cols]


def whiten(spec, left, right, band, keep):
    windows, channels, _ = spec.shape
    width = 2 * F // CHUNKS
    return pl.pallas_call(
        whiten_kernel,
        out_shape=[jax.ShapeDtypeStruct((windows, channels, width), jnp.bfloat16)] * CHUNKS,
        compiler_params=pltpu.CompilerParams(vmem_limit_bytes=40 * MIB),
        cost_estimate=pl.CostEstimate(flops=2 * windows * channels * F * F * 3, bytes_accessed=5 * MIB // 2, transcendentals=windows * channels * F),
    )(spec, left, right, band, keep)


def eye(size):
    rows = lax.broadcasted_iota(jnp.int32, (size, size), 0)
    cols = lax.broadcasted_iota(jnp.int32, (size, size), 1)
    return jnp.where(rows == cols, 1.0, 0.0).astype(jnp.bfloat16)


def turned(left_unit, rows):
    return lax.dot_general(left_unit, rows, NT, preferred_element_type=jnp.float32)


def swapper(outer, inner):
    size = outer * inner
    rows = lax.broadcasted_iota(jnp.int32, (size, size), 0)
    cols = lax.broadcasted_iota(jnp.int32, (size, size), 1)
    return jnp.where(cols == rows % outer * inner + rows // outer, 1.0, 0.0).astype(jnp.bfloat16)


def moved(swap, rows):
    return jnp.dot(swap, rows, preferred_element_type=jnp.float32).astype(jnp.bfloat16)


def cross_kernel(sources, own, out, by_window, by_channel, sums):
    windows, count, both = sources.shape
    channels = own.shape[0]
    width = both // 2
    quads = channels // 4
    unit = eye(width)
    for window in range(windows):
        re, im = sources[window, :, :width], sources[window, :, width:]
        by_window[window] = turned(unit, jnp.concatenate([re, -im, im, re], axis=0)).astype(jnp.bfloat16)
    for quad in range(quads):
        rows = []
        for channel in range(quad, channels, quads):
            rows += [own[channel, :, :width], own[channel, :, width:]]
        by_channel[quad] = turned(unit, jnp.concatenate(rows, axis=0)).astype(jnp.bfloat16)
    swap = swapper(GROUP, GROUP)
    swap_quads = swapper(quads, GROUP)

    def one_group(group, carry):
        bins = pl.ds(pl.multiple_of(group * GROUP, GROUP), GROUP)
        rights = []
        for start in range(0, windows, GROUP):
            rows = by_window[start : start + GROUP, bins, :].reshape(GROUP * GROUP, 4 * count)
            rights.append(moved(swap, rows))
        lefts = jnp.dot(
            swap_quads, by_channel[:, bins, :].reshape(quads * GROUP, 8 * windows), preferred_element_type=jnp.float32
        )
        results = []
        for at in range(GROUP):
            here = slice(at * GROUP, (at + 1) * GROUP)
            right = jnp.concatenate(
                [r[here, : 2 * count] for r in rights] + [r[here, 2 * count :] for r in rights], axis=0
            )
            left = lefts[at * quads : (at + 1) * quads]
            left = jnp.concatenate([left[:, 2 * windows * i : 2 * windows * (i + 1)] for i in range(4)], axis=0)
            results.append(jnp.dot(left.astype(jnp.bfloat16), right, preferred_element_type=jnp.float32).astype(jnp.bfloat16))
        halves = [
            jnp.concatenate([r[start : start + GROUP] for r in results], axis=0) for start in range(0, channels, GROUP)
        ]
        done = moved(swap, jnp.concatenate(halves, axis=1))
        for channel in range(channels):
            row, side = channel % GROUP, channel // GROUP
            sums[channel, bins, :] = done[
                row * GROUP : (row + 1) * GROUP, side * 2 * count : (side + 1) * 2 * count
            ]
        return carry

    lax.fori_loop(0, width // GROUP, one_group, 0)
    unit = eye(2 * count)
    for channel in range(channels):
        out[channel] = turned(unit, sums[channel]).astype(jnp.bfloat16)


def cross(sources, own):
    windows, count, both = sources.shape
    channels = own.shape[0]
    width = both // 2
    return pl.pallas_call(
        cross_kernel,
        out_shape=jax.ShapeDtypeStruct((channels, 2 * count, width), jnp.bfloat16),
        scratch_shapes=[
            pltpu.VMEM((windows, width, 4 * count), jnp.bfloat16),
            pltpu.VMEM((channels // 4, width, 8 * windows), jnp.bfloat16),
            pltpu.VMEM((channels, width, 2 * count), jnp.bfloat16),
        ],
        compiler_params=pltpu.CompilerParams(vmem_limit_bytes=48 * MIB),
        cost_estimate=pl.CostEstimate(flops=8 * windows * count * channels * width, bytes_accessed=8 * MIB, transcendentals=0),
    )(sources, own)


def lag_kernel(scaling, *refs):
    *stacked, table, out, rows = refs
    channels, both, width = stacked[0].shape
    count = both // 2
    part = 256 // channels

    @pl.when(pl.program_id(1) == 0)
    def _():
        swap = swapper(channels, part)
        for at, chunk in enumerate(stacked):
            for side in range(2):
                cols = slice(side * F + at * width, side * F + (at + 1) * width)
                for start in range(0, count, part):
                    from_rows = slice(side * count + start, side * count + start + part)
                    block = chunk[:, from_rows, :].reshape(channels * part, width)
                    rows[start * channels : (start + part) * channels, cols] = moved(swap, block)

    result = jnp.dot(rows[...], table[...], preferred_element_type=jnp.float32) * scaling
    out[...] = result.reshape(out.shape)


def lagged(stacked, table, scaling):
    channels, both, width = stacked[0].shape
    count = both // 2
    block, cols = 8, LAGS // 2
    return pl.pallas_call(
        functools.partial(lag_kernel, scaling),
        grid=(channels // block, LAGS // cols),
        in_specs=[pl.BlockSpec((block, both, width), lambda i, j: (i, 0, 0))] * len(stacked)
        + [pl.BlockSpec((2 * F, cols), lambda i, j: (0, j))],
        out_specs=pl.BlockSpec((count, block, cols), lambda i, j: (0, i, j)),
        out_shape=jax.ShapeDtypeStruct((count, channels, LAGS), jnp.float32),
        scratch_shapes=[pltpu.VMEM((count * block, 2 * F), jnp.bfloat16)],
        compiler_params=pltpu.CompilerParams(vmem_limit_bytes=48 * MIB),
        cost_estimate=pl.CostEstimate(flops=2 * count * channels * 2 * F * LAGS, bytes_accessed=count * channels * LAGS * 4, transcendentals=0),
    )(*stacked, table)


def inverse_table():
    coarse = unit_angles(np.arange(LAGS // LAG_FINE) * LAG_FINE - LAGS // 2, 1)
    fine = unit_angles(np.arange(LAG_FINE), 1)
    big_cos, big_sin = (jnp.asarray(t)[:, :, None] for t in coarse)
    small_cos, small_sin = (jnp.asarray(t)[:, None, :] for t in fine)
    cos = big_cos * small_cos - big_sin * small_sin
    sin = big_sin * small_cos + big_cos * small_sin
    return jnp.concatenate([cos, -sin], axis=0).astype(jnp.bfloat16).reshape(2 * F, LAGS)


def make_band(filter_taps, channel_count):
    kernel = jnp.concatenate(
        [
            -filter_taps[:HALO].astype(jnp.float32),
            jnp.ones((1,), jnp.float32),
            -filter_taps[HALO:].astype(jnp.float32),
        ]
    )
    row_ids = jnp.arange(channel_count, dtype=jnp.int32)[:, None]
    columns = jnp.arange(channel_count + 2 * HALO, dtype=jnp.int32)[None, :]
    offset = columns - row_ids
    choose = offset[:, :, None] == jnp.arange(2 * HALO + 1, dtype=jnp.int32)[None, None, :]
    return jnp.sum(jnp.where(choose, kernel[None, None, :], 0.0), axis=2).astype(jnp.bfloat16)


def per_device(traces, filter_taps, good_channels, source_index):
    window_count, channel_count, _ = traces.shape
    keep = good_channels.astype(jnp.float32)[:, None]
    spec, head, tail = transform(traces, keep)
    blocks = lax.axis_size("chan")
    left = lax.ppermute(tail, "chan", [(i, i + 1) for i in range(blocks - 1)])
    right = lax.ppermute(head, "chan", [(i + 1, i) for i in range(blocks - 1)])
    whitened = whiten(spec, left, right, make_band(filter_taps, channel_count), keep)
    groups = lax.axis_size("win")
    channel_ids = jnp.arange(blocks * channel_count, dtype=jnp.int32)
    selector = (source_index[:, None] == channel_ids[None, :]).astype(jnp.bfloat16)
    stacked = []
    for part in whitened:
        everything = lax.all_gather(part, "chan", axis=1, tiled=True)
        own = jnp.swapaxes(lax.all_gather(part, "win", axis=0, tiled=True), 0, 1)
        picked = jnp.einsum("sc,wcf->wsf", selector, everything, preferred_element_type=jnp.float32).astype(jnp.bfloat16)
        sources = lax.all_to_all(picked, "win", split_axis=1, concat_axis=0, tiled=True)
        stacked.append(cross(sources, own))
    return lagged(stacked, inverse_table(), 1.0 / math.sqrt(F * window_count * groups))


def solution(mesh):
    placed = (P("win", "chan", None), P(), P("chan"), P())
    return jax.shard_map(
        per_device, mesh=mesh, in_specs=placed, out_specs=P("win", "chan", None), check_vma=False
    )
```

```python
import functools
import math

import jax
import jax.numpy as jnp
import numpy as np
from jax import lax
from jax.experimental import pallas as pl
from jax.experimental.pallas import tpu as pltpu
from jax.sharding import PartitionSpec as P

L = 7680
F = 512
LAGS = 2048
HALO = 16
SMOOTH = 64
K0 = 31
QUARTER = L // 4
STEP = 384
FINE = 32
CHUNKS = 2
GROUP = 16
LAG_FINE = 128
NT = (((1,), (1,)), ((), ()))
MIB = 1024 * 1024


def unit_angles(positions, axis):
    bins = K0 + np.arange(F, dtype=np.int64)
    phase = np.mod(np.expand_dims(positions, 1 - axis) * np.expand_dims(bins, axis), L)
    angles = phase * (2.0 * math.pi / L)
    return np.cos(angles).astype(np.float32), np.sin(angles).astype(np.float32)


def keep_column(good):
    count = good.shape[1]
    rows = lax.broadcasted_iota(jnp.int32, (count, count), 0)
    cols = lax.broadcasted_iota(jnp.int32, (count, count), 1)
    return jnp.sum(jnp.where(rows == cols, good[...].astype(jnp.float32), 0.0), axis=1, keepdims=True)


def transform_kernel(x0, x1, x2, x3, angles, good, spec, head, tail, table, total):
    step = pl.program_id(0)
    rows = x0.shape[0]
    coarse = QUARTER // FINE
    fine_cos = angles[2 * coarse : 2 * coarse + FINE, :]
    fine_sin = angles[2 * coarse + FINE :, :]
    for part in range(STEP // FINE):
        big_cos = angles[pl.ds(step * (STEP // FINE) + part, 1), :]
        big_sin = angles[pl.ds(coarse + step * (STEP // FINE) + part, 1), :]
        at = pl.ds(part * FINE, FINE)
        table[at, :F] = (big_cos * fine_cos - big_sin * fine_sin).astype(jnp.bfloat16)
        table[at, F:] = (-(big_sin * fine_cos + big_cos * fine_sin)).astype(jnp.bfloat16)

    @pl.when(step == 0)
    def _():
        total[...] = jnp.zeros_like(total)

    for quarter, x in enumerate((x0, x1, x2, x3)):
        at = pl.ds(quarter * rows, rows)
        total[at, :] += jnp.dot(x[...], table[...], preferred_element_type=jnp.float32)

    @pl.when(step == pl.num_programs(0) - 1)
    def _():
        turn = (K0 + lax.broadcasted_iota(jnp.int32, (1, F), 1)) % 4
        even = turn % 2 == 0
        sign = jnp.where(turn < 2, 1.0, -1.0)
        channels = good.shape[1]
        keep = keep_column(good)
        for window in range(rows // channels):
            re = [total[pl.ds(q * rows + window * channels, channels), :F] for q in range(4)]
            im = [total[pl.ds(q * rows + window * channels, channels), F:] for q in range(4)]
            real = jnp.where(even, re[0] + re[2] + sign * (re[1] + re[3]), re[0] - re[2] + sign * (im[1] - im[3])) * keep
            imag = jnp.where(even, im[0] + im[2] + sign * (im[1] + im[3]), im[0] - im[2] - sign * (re[1] - re[3])) * keep
            spec[window, :, :F] = real
            spec[window, :, F:] = imag
            head[window, :, :F] = real[:HALO]
            head[window, :, F:] = imag[:HALO]
            tail[window, :, :F] = real[channels - HALO :]
            tail[window, :, F:] = imag[channels - HALO :]


def transform(traces, good):
    windows, channels, length = traces.shape
    rows = windows * channels
    steps = QUARTER // STEP
    flat = traces.reshape(rows, length)
    coarse = unit_angles(np.arange(QUARTER // FINE) * FINE, 0)
    angles = np.concatenate(coarse + unit_angles(np.arange(FINE), 0), axis=0)
    whole = lambda *shape: pl.BlockSpec(shape, lambda k: (0,) * len(shape))
    return pl.pallas_call(
        transform_kernel,
        grid=(steps,),
        in_specs=[pl.BlockSpec((rows, STEP), functools.partial(lambda q, k: (0, q * steps + k), q)) for q in range(4)]
        + [whole(*angles.shape), whole(1, channels)],
        out_specs=[whole(windows, channels, 2 * F), whole(windows, HALO, 2 * F), whole(windows, HALO, 2 * F)],
        out_shape=[
            jax.ShapeDtypeStruct((windows, channels, 2 * F), jnp.float32),
            jax.ShapeDtypeStruct((windows, HALO, 2 * F), jnp.float32),
            jax.ShapeDtypeStruct((windows, HALO, 2 * F), jnp.float32),
        ],
        scratch_shapes=[pltpu.VMEM((STEP, 2 * F), jnp.bfloat16), pltpu.VMEM((4 * rows, 2 * F), jnp.float32)],
        compiler_params=pltpu.CompilerParams(vmem_limit_bytes=40 * MIB),
        cost_estimate=pl.CostEstimate(flops=2 * rows * length * 2 * F, bytes_accessed=rows * length * 2, transcendentals=0),
    )(flat, flat, flat, flat, angles, good)


def pieces(value):
    high = value.astype(jnp.bfloat16)
    rest = value - high.astype(jnp.float32)
    middle = rest.astype(jnp.bfloat16)
    return high, middle, (rest - middle.astype(jnp.float32)).astype(jnp.bfloat16)


def whiten_kernel(spec, left, right, band, good, *outs):
    windows, channels = spec.shape[:2]
    filtered = []
    keep = keep_column(good)
    for window in range(windows):
        padded = jnp.concatenate([left[window], spec[window], right[window]], axis=0)
        stack = jnp.concatenate(pieces(padded), axis=0)
        taps = jnp.concatenate([band[...]] * 3, axis=1)
        filtered.append(jnp.dot(taps, stack, preferred_element_type=jnp.float32) * keep)
    spectrum = jnp.concatenate(filtered, axis=0)
    real, imag = spectrum[:, :F], spectrum[:, F:]
    magnitude = jnp.sqrt(real * real + imag * imag)
    bins = lax.broadcasted_iota(jnp.int32, (F, F), 0)
    others = lax.broadcasted_iota(jnp.int32, (F, F), 1)
    near = jnp.where(jnp.abs(bins - others) <= SMOOTH, 1.0, 0.0).astype(jnp.bfloat16)
    amplitude = sum(jnp.dot(piece, near, preferred_element_type=jnp.float32) for piece in pieces(magnitude))
    bin_row = lax.broadcasted_iota(jnp.int32, (1, F), 1)
    count = jnp.minimum(bin_row + SMOOTH, F - 1) - jnp.maximum(bin_row - SMOOTH, 0) + 1
    amplitude = amplitude * (1.0 / count.astype(jnp.float32))
    inverse = 1.0 / (amplitude + 1e-06)
    real = (real * inverse).astype(jnp.bfloat16)
    imag = (imag * inverse).astype(jnp.bfloat16)
    width = F // len(outs)
    for at, out in enumerate(outs):
        for window in range(windows):
            rows = slice(window * channels, (window + 1) * channels)
            cols = slice(at * width, (at + 1) * width)
            out[window, :, :width] = real[rows, cols]
            out[window, :, width:] = imag[rows, cols]


def whiten(spec, left, right, band, good):
    windows, channels, _ = spec.shape
    width = 2 * F // CHUNKS
    return pl.pallas_call(
        whiten_kernel,
        out_shape=[jax.ShapeDtypeStruct((windows, channels, width), jnp.bfloat16)] * CHUNKS,
        compiler_params=pltpu.CompilerParams(vmem_limit_bytes=40 * MIB),
        cost_estimate=pl.CostEstimate(flops=2 * windows * channels * F * F * 3, bytes_accessed=5 * MIB // 2, transcendentals=windows * channels * F),
    )(spec, left, right, band, good)


def eye(size):
    rows = lax.broadcasted_iota(jnp.int32, (size, size), 0)
    cols = lax.broadcasted_iota(jnp.int32, (size, size), 1)
    return jnp.where(rows == cols, 1.0, 0.0).astype(jnp.bfloat16)


def turned(left_unit, rows):
    return lax.dot_general(left_unit, rows, NT, preferred_element_type=jnp.float32)


def swapper(outer, inner):
    size = outer * inner
    rows = lax.broadcasted_iota(jnp.int32, (size, size), 0)
    cols = lax.broadcasted_iota(jnp.int32, (size, size), 1)
    return jnp.where(cols == rows % outer * inner + rows // outer, 1.0, 0.0).astype(jnp.bfloat16)


def moved(swap, rows):
    return jnp.dot(swap, rows, preferred_element_type=jnp.float32).astype(jnp.bfloat16)


def cross_kernel(*refs):
    *sources, own, out, by_window, by_channel, sums = refs
    each, count, both = sources[0].shape
    channels, windows, _ = own.shape
    width = both // 2
    quads = channels // 4
    unit = eye(width)
    for window in range(windows):
        source, at = sources[window // each], window % each
        re, im = source[at, :, :width], source[at, :, width:]
        by_window[window] = turned(unit, jnp.concatenate([re, -im, im, re], axis=0)).astype(jnp.bfloat16)
    for quad in range(quads):
        rows = []
        for channel in range(quad, channels, quads):
            rows += [own[channel, :, :width], own[channel, :, width:]]
        by_channel[quad] = turned(unit, jnp.concatenate(rows, axis=0)).astype(jnp.bfloat16)
    swap = swapper(GROUP, GROUP)
    swap_quads = swapper(quads, GROUP)

    def one_group(group, carry):
        bins = pl.ds(pl.multiple_of(group * GROUP, GROUP), GROUP)
        rights = []
        for start in range(0, windows, GROUP):
            rows = by_window[start : start + GROUP, bins, :].reshape(GROUP * GROUP, 4 * count)
            rights.append(moved(swap, rows))
        lefts = jnp.dot(
            swap_quads, by_channel[:, bins, :].reshape(quads * GROUP, 8 * windows), preferred_element_type=jnp.float32
        )
        results = []
        for at in range(GROUP):
            here = slice(at * GROUP, (at + 1) * GROUP)
            right = jnp.concatenate(
                [r[here, : 2 * count] for r in rights] + [r[here, 2 * count :] for r in rights], axis=0
            )
            left = lefts[at * quads : (at + 1) * quads]
            left = jnp.concatenate([left[:, 2 * windows * i : 2 * windows * (i + 1)] for i in range(4)], axis=0)
            results.append(jnp.dot(left.astype(jnp.bfloat16), right, preferred_element_type=jnp.float32).astype(jnp.bfloat16))
        halves = [
            jnp.concatenate([r[start : start + GROUP] for r in results], axis=0) for start in range(0, channels, GROUP)
        ]
        done = moved(swap, jnp.concatenate(halves, axis=1))
        for channel in range(channels):
            row, side = channel % GROUP, channel // GROUP
            sums[channel, bins, :] = done[
                row * GROUP : (row + 1) * GROUP, side * 2 * count : (side + 1) * 2 * count
            ]
        return carry

    lax.fori_loop(0, width // GROUP, one_group, 0)
    unit = eye(2 * count)
    for channel in range(channels):
        out[channel] = turned(unit, sums[channel]).astype(jnp.bfloat16)


def cross(sources, own):
    _, count, both = sources[0].shape
    channels, windows, _ = own.shape
    width = both // 2
    return pl.pallas_call(
        cross_kernel,
        out_shape=jax.ShapeDtypeStruct((channels, 2 * count, width), jnp.bfloat16),
        scratch_shapes=[
            pltpu.VMEM((windows, width, 4 * count), jnp.bfloat16),
            pltpu.VMEM((channels // 4, width, 8 * windows), jnp.bfloat16),
            pltpu.VMEM((channels, width, 2 * count), jnp.bfloat16),
        ],
        compiler_params=pltpu.CompilerParams(vmem_limit_bytes=48 * MIB),
        cost_estimate=pl.CostEstimate(flops=8 * windows * count * channels * width, bytes_accessed=8 * MIB, transcendentals=0),
    )(*sources, own)


def lag_kernel(scaling, *refs):
    *stacked, table, out, rows = refs
    channels, both, width = stacked[0].shape
    count = both // 2
    part = 256 // channels

    @pl.when(pl.program_id(1) == 0)
    def _():
        swap = swapper(channels, part)
        for at, chunk in enumerate(stacked):
            for side in range(2):
                cols = slice(side * F + at * width, side * F + (at + 1) * width)
                for start in range(0, count, part):
                    from_rows = slice(side * count + start, side * count + start + part)
                    block = chunk[:, from_rows, :].reshape(channels * part, width)
                    rows[start * channels : (start + part) * channels, cols] = moved(swap, block)

    result = jnp.dot(rows[...], table[...], preferred_element_type=jnp.float32) * scaling
    out[...] = result.reshape(out.shape)


def lagged(stacked, table, scaling):
    channels, both, width = stacked[0].shape
    count = both // 2
    block, cols = 8, LAGS // 2
    return pl.pallas_call(
        functools.partial(lag_kernel, scaling),
        grid=(channels // block, LAGS // cols),
        in_specs=[pl.BlockSpec((block, both, width), lambda i, j: (i, 0, 0))] * len(stacked)
        + [pl.BlockSpec((2 * F, cols), lambda i, j: (0, j))],
        out_specs=pl.BlockSpec((count, block, cols), lambda i, j: (0, i, j)),
        out_shape=jax.ShapeDtypeStruct((count, channels, LAGS), jnp.float32),
        scratch_shapes=[pltpu.VMEM((count * block, 2 * F), jnp.bfloat16)],
        compiler_params=pltpu.CompilerParams(vmem_limit_bytes=48 * MIB),
        cost_estimate=pl.CostEstimate(flops=2 * count * channels * 2 * F * LAGS, bytes_accessed=count * channels * LAGS * 4, transcendentals=0),
    )(*stacked, table)


def inverse_table():
    coarse = unit_angles(np.arange(LAGS // LAG_FINE) * LAG_FINE - LAGS // 2, 1)
    fine = unit_angles(np.arange(LAG_FINE), 1)
    big_cos, big_sin = (jnp.asarray(t)[:, :, None] for t in coarse)
    small_cos, small_sin = (jnp.asarray(t)[:, None, :] for t in fine)
    cos = big_cos * small_cos - big_sin * small_sin
    sin = big_sin * small_cos + big_cos * small_sin
    return jnp.concatenate([cos, -sin], axis=0).astype(jnp.bfloat16).reshape(2 * F, LAGS)


def make_band(filter_taps, channel_count):
    kernel = jnp.concatenate(
        [
            -filter_taps[:HALO].astype(jnp.float32),
            jnp.ones((1,), jnp.float32),
            -filter_taps[HALO:].astype(jnp.float32),
        ]
    )
    row_ids = jnp.arange(channel_count, dtype=jnp.int32)[:, None]
    columns = jnp.arange(channel_count + 2 * HALO, dtype=jnp.int32)[None, :]
    offset = columns - row_ids
    choose = offset[:, :, None] == jnp.arange(2 * HALO + 1, dtype=jnp.int32)[None, None, :]
    return jnp.sum(jnp.where(choose, kernel[None, None, :], 0.0), axis=2).astype(jnp.bfloat16)


def pick_kernel(block_count, *refs):
    blocks, selector, outs = refs[:block_count], refs[block_count], refs[block_count + 1 :]
    windows = blocks[0].shape[0]
    count = outs[0].shape[1]
    for window in range(windows):
        rows = jnp.concatenate([block[window] for block in blocks], axis=0)
        picked = jnp.dot(selector[...], rows, preferred_element_type=jnp.float32).astype(jnp.bfloat16)
        for at, out in enumerate(outs):
            out[window] = picked[at * count : (at + 1) * count]


def pick(blocks, selector, groups):
    windows, channels, both = blocks[0].shape
    count = selector.shape[0] // groups
    return pl.pallas_call(
        functools.partial(pick_kernel, len(blocks)),
        out_shape=[jax.ShapeDtypeStruct((windows, count, both), jnp.bfloat16)] * groups,
        compiler_params=pltpu.CompilerParams(vmem_limit_bytes=48 * MIB),
        cost_estimate=pl.CostEstimate(
            flops=2 * windows * selector.size * both, bytes_accessed=2 * windows * both * sum(selector.shape), transcendentals=0
        ),
    )(*blocks, selector)


def around(value, axis, step):
    count = lax.axis_size(axis)
    return lax.ppermute(value, axis, [(i, (i + step) % count) for i in range(count)])


def from_all_blocks(part, pair):
    count = lax.axis_size("chan")
    across = [(i, i - i % pair + (i + 1) % pair) for i in range(count)]
    held = [part] + [around(part, "chan", pair * step) for step in range(1, count // pair)]
    return held + [lax.ppermute(block, "chan", across) for block in held] if pair > 1 else held


def block_order(pair):
    count = lax.axis_size("chan")
    here = lax.axis_index("chan")
    held = [(here + count - pair * step) % count for step in range(count // pair)]
    other = [block - block % pair + (block + 1) % pair for block in held]
    return jnp.stack(held + other if pair > 1 else held)


def per_device(traces, filter_taps, good_channels, source_index):
    window_count, channel_count, _ = traces.shape
    good = good_channels[None, :]
    spec, head, tail = transform(traces, good)
    blocks = lax.axis_size("chan")
    groups = lax.axis_size("win")
    left = lax.ppermute(tail, "chan", [(i, i + 1) for i in range(blocks - 1)])
    right = lax.ppermute(head, "chan", [(i + 1, i) for i in range(blocks - 1)])
    whitened = whiten(spec, left, right, make_band(filter_taps, channel_count), good)
    pair = 2 if blocks % 2 == 0 else 1
    own_ids = jnp.arange(channel_count, dtype=jnp.int32)
    channel_ids = (block_order(pair)[:, None] * channel_count + own_ids[None, :]).reshape(-1)
    wanted = jnp.roll(source_index.reshape(groups, -1), -lax.axis_index("win"), axis=0).reshape(-1)
    selector = (wanted[:, None] == channel_ids[None, :]).astype(jnp.bfloat16)
    stacked = []
    for part in whitened:
        picked = pick(from_all_blocks(part, pair), selector, groups)
        sources = [picked[0]] + [around(picked[step], "win", step) for step in range(1, groups)]
        own = jnp.concatenate([part] + [around(part, "win", step) for step in range(1, groups)], axis=0)
        stacked.append(cross(sources, jnp.swapaxes(own, 0, 1)))
    return lagged(stacked, inverse_table(), 1.0 / math.sqrt(F * window_count * groups))


def solution(mesh):
    placed = (P("win", "chan", None), P(), P("chan"), P())
    return jax.shard_map(
        per_device, mesh=mesh, in_specs=placed, out_specs=P("win", "chan", None), check_vma=False
    )
```

```python
import functools
import math

import jax
import jax.numpy as jnp
import numpy as np
from jax import lax
from jax.experimental import pallas as pl
from jax.experimental.pallas import tpu as pltpu
from jax.sharding import PartitionSpec as P

L = 7680
F = 512
LAGS = 2048
HALO = 16
SMOOTH = 64
K0 = 31
QUARTER = L // 4
STEP = 384
FINE = 32
CHUNKS = 2
GROUP = 16
LAG_FINE = 128
NT = (((1,), (1,)), ((), ()))
MIB = 1024 * 1024


def unit_angles(positions, axis):
    bins = K0 + np.arange(F, dtype=np.int64)
    phase = np.mod(np.expand_dims(positions, 1 - axis) * np.expand_dims(bins, axis), L)
    angles = phase * (2.0 * math.pi / L)
    return np.cos(angles).astype(np.float32), np.sin(angles).astype(np.float32)


def keep_column(good):
    count = good.shape[1]
    rows = lax.broadcasted_iota(jnp.int32, (count, count), 0)
    cols = lax.broadcasted_iota(jnp.int32, (count, count), 1)
    return jnp.sum(jnp.where(rows == cols, good[...].astype(jnp.float32), 0.0), axis=1, keepdims=True)


def transform_kernel(x0, x1, x2, x3, angles, good, spec, head, tail, table, total):
    step = pl.program_id(0)
    rows = x0.shape[0]
    coarse = QUARTER // FINE
    fine_cos = angles[2 * coarse : 2 * coarse + FINE, :]
    fine_sin = angles[2 * coarse + FINE :, :]
    for part in range(STEP // FINE):
        big_cos = angles[pl.ds(step * (STEP // FINE) + part, 1), :]
        big_sin = angles[pl.ds(coarse + step * (STEP // FINE) + part, 1), :]
        at = pl.ds(part * FINE, FINE)
        table[at, :F] = (big_cos * fine_cos - big_sin * fine_sin).astype(jnp.bfloat16)
        table[at, F:] = (-(big_sin * fine_cos + big_cos * fine_sin)).astype(jnp.bfloat16)

    @pl.when(step == 0)
    def _():
        total[...] = jnp.zeros_like(total)

    for quarter, x in enumerate((x0, x1, x2, x3)):
        at = pl.ds(quarter * rows, rows)
        total[at, :] += jnp.dot(x[...], table[...], preferred_element_type=jnp.float32)

    @pl.when(step == pl.num_programs(0) - 1)
    def _():
        turn = (K0 + lax.broadcasted_iota(jnp.int32, (1, F), 1)) % 4
        even = turn % 2 == 0
        sign = jnp.where(turn < 2, 1.0, -1.0)
        channels = good.shape[1]
        keep = keep_column(good)
        for window in range(rows // channels):
            re = [total[pl.ds(q * rows + window * channels, channels), :F] for q in range(4)]
            im = [total[pl.ds(q * rows + window * channels, channels), F:] for q in range(4)]
            real = jnp.where(even, re[0] + re[2] + sign * (re[1] + re[3]), re[0] - re[2] + sign * (im[1] - im[3])) * keep
            imag = jnp.where(even, im[0] + im[2] + sign * (im[1] + im[3]), im[0] - im[2] - sign * (re[1] - re[3])) * keep
            spec[window, :, :F] = real
            spec[window, :, F:] = imag
            head[window, :, :F] = real[:HALO].astype(jnp.bfloat16)
            head[window, :, F:] = imag[:HALO].astype(jnp.bfloat16)
            tail[window, :, :F] = real[channels - HALO :].astype(jnp.bfloat16)
            tail[window, :, F:] = imag[channels - HALO :].astype(jnp.bfloat16)


def transform(traces, good):
    windows, channels, length = traces.shape
    rows = windows * channels
    steps = QUARTER // STEP
    flat = traces.reshape(rows, length)
    coarse = unit_angles(np.arange(QUARTER // FINE) * FINE, 0)
    angles = np.concatenate(coarse + unit_angles(np.arange(FINE), 0), axis=0)
    whole = lambda *shape: pl.BlockSpec(shape, lambda k: (0,) * len(shape))
    return pl.pallas_call(
        transform_kernel,
        grid=(steps,),
        in_specs=[pl.BlockSpec((rows, STEP), functools.partial(lambda q, k: (0, q * steps + k), q)) for q in range(4)]
        + [whole(*angles.shape), whole(1, channels)],
        out_specs=[whole(windows, channels, 2 * F), whole(windows, HALO, 2 * F), whole(windows, HALO, 2 * F)],
        out_shape=[
            jax.ShapeDtypeStruct((windows, channels, 2 * F), jnp.float32),
            jax.ShapeDtypeStruct((windows, HALO, 2 * F), jnp.bfloat16),
            jax.ShapeDtypeStruct((windows, HALO, 2 * F), jnp.bfloat16),
        ],
        scratch_shapes=[pltpu.VMEM((STEP, 2 * F), jnp.bfloat16), pltpu.VMEM((4 * rows, 2 * F), jnp.float32)],
        compiler_params=pltpu.CompilerParams(vmem_limit_bytes=60 * MIB),
        cost_estimate=pl.CostEstimate(flops=2 * rows * length * 2 * F, bytes_accessed=rows * length * 2, transcendentals=0),
    )(flat, flat, flat, flat, angles, good)


def pieces(value):
    high = value.astype(jnp.bfloat16)
    rest = value - high.astype(jnp.float32)
    middle = rest.astype(jnp.bfloat16)
    return high, middle, (rest - middle.astype(jnp.float32)).astype(jnp.bfloat16)


def whiten_kernel(spec, left, right, band, good, *outs):
    windows, channels = spec.shape[:2]
    filtered = []
    keep = keep_column(good)
    for window in range(windows):
        stack = jnp.concatenate([left[window], *pieces(spec[window]), right[window]], axis=0)
        own = band[:, HALO : HALO + channels]
        taps = jnp.concatenate([band[:, :HALO], own, own, own, band[:, HALO + channels :]], axis=1)
        filtered.append(jnp.dot(taps, stack, preferred_element_type=jnp.float32) * keep)
    spectrum = jnp.concatenate(filtered, axis=0)
    real, imag = spectrum[:, :F], spectrum[:, F:]
    magnitude = jnp.sqrt(real * real + imag * imag)
    bins = lax.broadcasted_iota(jnp.int32, (F, F), 0)
    others = lax.broadcasted_iota(jnp.int32, (F, F), 1)
    near = jnp.where(jnp.abs(bins - others) <= SMOOTH, 1.0, 0.0).astype(jnp.bfloat16)
    amplitude = sum(jnp.dot(piece, near, preferred_element_type=jnp.float32) for piece in pieces(magnitude))
    bin_row = lax.broadcasted_iota(jnp.int32, (1, F), 1)
    count = jnp.minimum(bin_row + SMOOTH, F - 1) - jnp.maximum(bin_row - SMOOTH, 0) + 1
    amplitude = amplitude * (1.0 / count.astype(jnp.float32))
    inverse = 1.0 / (amplitude + 1e-06)
    real = (real * inverse).astype(jnp.bfloat16)
    imag = (imag * inverse).astype(jnp.bfloat16)
    width = F // len(outs)
    for at, out in enumerate(outs):
        for window in range(windows):
            rows = slice(window * channels, (window + 1) * channels)
            cols = slice(at * width, (at + 1) * width)
            out[window, :, :width] = real[rows, cols]
            out[window, :, width:] = imag[rows, cols]


def whiten(spec, left, right, band, good):
    windows, channels, _ = spec.shape
    width = 2 * F // CHUNKS
    return pl.pallas_call(
        whiten_kernel,
        out_shape=[jax.ShapeDtypeStruct((windows, channels, width), jnp.bfloat16)] * CHUNKS,
        compiler_params=pltpu.CompilerParams(vmem_limit_bytes=40 * MIB),
        cost_estimate=pl.CostEstimate(flops=2 * windows * channels * F * F * 3, bytes_accessed=5 * MIB // 2, transcendentals=windows * channels * F),
    )(spec, left, right, band, good)


def eye(size):
    rows = lax.broadcasted_iota(jnp.int32, (size, size), 0)
    cols = lax.broadcasted_iota(jnp.int32, (size, size), 1)
    return jnp.where(rows == cols, 1.0, 0.0).astype(jnp.bfloat16)


def turned(left_unit, rows):
    return lax.dot_general(left_unit, rows, NT, preferred_element_type=jnp.float32)


def swapper(outer, inner):
    size = outer * inner
    rows = lax.broadcasted_iota(jnp.int32, (size, size), 0)
    cols = lax.broadcasted_iota(jnp.int32, (size, size), 1)
    return jnp.where(cols == rows % outer * inner + rows // outer, 1.0, 0.0).astype(jnp.bfloat16)


def moved(swap, rows):
    return jnp.dot(swap, rows, preferred_element_type=jnp.float32).astype(jnp.bfloat16)


def cross_kernel(sides, *refs):
    sources, own = refs[:sides], refs[sides : 2 * sides]
    out, by_window, by_channel, turned_own, sums = refs[2 * sides :]
    each, count, both = sources[0].shape
    channels = own[0].shape[1]
    windows, width, quads = each * sides, both // 2, channels // 4
    half = 2 * windows
    unit = eye(width)
    swap = swapper(GROUP, GROUP)
    swap_quads = swapper(quads, GROUP)
    for window in range(0, windows, 2):
        rows = []
        for one in range(window, window + 2):
            source = sources[one // each]
            rows += [source[one % each, :, :width], source[one % each, :, width:]]
        both_turned = turned(unit, jnp.concatenate(rows, axis=0)).astype(jnp.bfloat16)
        by_window[window] = both_turned[:, : 2 * count]
        by_window[window + 1] = both_turned[:, 2 * count :]
    joined = GROUP // each
    for start in range(0, windows, GROUP):
        for channel in range(0, channels, GROUP):
            block = [o[:, channel : channel + GROUP, :] for o in own[start // each : start // each + joined]]
            rows = moved(swap, jnp.concatenate(block, axis=0).reshape(GROUP * GROUP, both))
            turned_own[channel : channel + GROUP, start : start + GROUP, :] = rows.reshape(GROUP, GROUP, both)
    for quad in range(quads):
        rows = []
        for channel in range(quad, channels, quads):
            rows += [turned_own[channel, :, :width], turned_own[channel, :, width:]]
        by_channel[quad] = turned(unit, jnp.concatenate(rows, axis=0)).astype(jnp.bfloat16)
    first = lax.broadcasted_iota(jnp.int32, (1, 128), 1) < 64
    sign = jnp.where(first, 1.0, -1.0)
    empty = jnp.zeros((2 * windows, 2 * count), jnp.bfloat16)

    def one_group(group, carry):
        bins = pl.ds(pl.multiple_of(group * GROUP, GROUP), GROUP)
        rows = [
            by_window[start : start + GROUP, bins, :].reshape(GROUP * GROUP, 2 * count)
            for start in range(0, windows, GROUP)
        ]
        rights = jnp.dot(swap, jnp.concatenate(rows, axis=1), preferred_element_type=jnp.float32)
        lefts = jnp.dot(
            swap_quads, by_channel[:, bins, :].reshape(quads * GROUP, 4 * half), preferred_element_type=jnp.float32
        )
        results = []
        for at in range(0, GROUP, 2):
            two = []
            for one in range(at, at + 2):
                here = rights[one * GROUP : (one + 1) * GROUP]
                src = jnp.concatenate(
                    [here[:, i * 2 * count : (i + 1) * 2 * count] for i in range(windows // GROUP)], axis=0
                )
                two.append(jnp.concatenate([src * sign, pltpu.roll(src, count, axis=1)], axis=0).astype(jnp.bfloat16))
            right = jnp.concatenate(
                [jnp.concatenate([two[0], empty], axis=1), jnp.concatenate([empty, two[1]], axis=1)], axis=0
            )
            left = []
            for tile in range(0, 4 * half, 128):
                one, other = (lefts[i * quads : (i + 1) * quads, tile : tile + 128] for i in (at, at + 1))
                left.append(jnp.where(first, one, pltpu.roll(other, 64, axis=1)))
                left.append(jnp.where(first, pltpu.roll(one, 64, axis=1), other))
            left = jnp.concatenate(left, axis=0).astype(jnp.bfloat16)
            result = jnp.dot(left, right, preferred_element_type=jnp.float32).astype(jnp.bfloat16)
            results += [result[:, : 2 * count], result[:, 2 * count :]]
        halves = [
            jnp.concatenate([r[start : start + GROUP] for r in results], axis=0) for start in range(0, channels, GROUP)
        ]
        done = moved(swap, jnp.concatenate(halves, axis=1))
        for channel in range(channels):
            row, side = channel % GROUP, channel // GROUP
            sums[channel, bins, :] = done[
                row * GROUP : (row + 1) * GROUP, side * 2 * count : (side + 1) * 2 * count
            ]
        return carry

    lax.fori_loop(0, width // GROUP, one_group, 0, unroll=4)
    unit = eye(2 * count)
    for channel in range(channels):
        out[channel] = turned(unit, sums[channel]).astype(jnp.bfloat16)


def cross(sources, own):
    each, count, both = sources[0].shape
    channels, windows, width = own[0].shape[1], each * len(sources), both // 2
    return pl.pallas_call(
        functools.partial(cross_kernel, len(sources)),
        out_shape=jax.ShapeDtypeStruct((channels, 2 * count, width), jnp.bfloat16),
        scratch_shapes=[
            pltpu.VMEM((windows, width, 2 * count), jnp.bfloat16),
            pltpu.VMEM((channels // 4, width, 8 * windows), jnp.bfloat16),
            pltpu.VMEM((channels, windows, both), jnp.bfloat16),
            pltpu.VMEM((channels, width, 2 * count), jnp.bfloat16),
        ],
        compiler_params=pltpu.CompilerParams(vmem_limit_bytes=40 * MIB),
        cost_estimate=pl.CostEstimate(flops=2 * width * 36 * 65536, bytes_accessed=4 * MIB, transcendentals=0),
    )(*sources, *own)


def lag_kernel(scaling, *refs):
    *stacked, table, out, rows = refs
    channels, both, width = stacked[0].shape
    count = both // 2
    part = 256 // channels

    @pl.when(pl.program_id(1) == 0)
    def _():
        swap = swapper(channels, part)
        for at, chunk in enumerate(stacked):
            for side in range(2):
                cols = slice(side * F + at * width, side * F + (at + 1) * width)
                for start in range(0, count, part):
                    from_rows = slice(side * count + start, side * count + start + part)
                    block = chunk[:, from_rows, :].reshape(channels * part, width)
                    rows[start * channels : (start + part) * channels, cols] = moved(swap, block)

    lags = out.shape[2]
    for start in range(0, lags, 256):
        cols = pl.ds(pl.multiple_of(pl.program_id(1) * lags + start, 256), 256)
        result = jnp.dot(rows[...], table[:, cols], preferred_element_type=jnp.float32) * scaling
        out[:, :, start : start + 256] = result.reshape(count, channels, 256)


def lagged(stacked, table, scaling):
    channels, both, width = stacked[0].shape
    count = both // 2
    block, cols = 8, LAGS // 2
    return pl.pallas_call(
        functools.partial(lag_kernel, scaling),
        grid=(channels // block, LAGS // cols),
        in_specs=[pl.BlockSpec((block, both, width), lambda i, j: (i, 0, 0))] * len(stacked)
        + [pl.BlockSpec((2 * F, LAGS), lambda i, j: (0, 0))],
        out_specs=pl.BlockSpec((count, block, cols), lambda i, j: (0, i, j)),
        out_shape=jax.ShapeDtypeStruct((count, channels, LAGS), jnp.float32),
        scratch_shapes=[pltpu.VMEM((count * block, 2 * F), jnp.bfloat16)],
        compiler_params=pltpu.CompilerParams(vmem_limit_bytes=48 * MIB),
        cost_estimate=pl.CostEstimate(flops=2 * count * channels * 2 * F * LAGS, bytes_accessed=count * channels * LAGS * 4, transcendentals=0),
    )(*stacked, table)


def inverse_table():
    coarse = unit_angles(np.arange(LAGS // LAG_FINE) * LAG_FINE - LAGS // 2, 1)
    fine = unit_angles(np.arange(LAG_FINE), 1)
    big_cos, big_sin = (jnp.asarray(t)[:, :, None] for t in coarse)
    small_cos, small_sin = (jnp.asarray(t)[:, None, :] for t in fine)
    cos = big_cos * small_cos - big_sin * small_sin
    sin = big_sin * small_cos + big_cos * small_sin
    return jnp.concatenate([cos, -sin], axis=0).astype(jnp.bfloat16).reshape(2 * F, LAGS)


def make_band(filter_taps, channel_count):
    kernel = jnp.concatenate(
        [
            -filter_taps[:HALO].astype(jnp.float32),
            jnp.ones((1,), jnp.float32),
            -filter_taps[HALO:].astype(jnp.float32),
        ]
    )
    row_ids = jnp.arange(channel_count, dtype=jnp.int32)[:, None]
    columns = jnp.arange(channel_count + 2 * HALO, dtype=jnp.int32)[None, :]
    offset = columns - row_ids
    choose = offset[:, :, None] == jnp.arange(2 * HALO + 1, dtype=jnp.int32)[None, None, :]
    return jnp.sum(jnp.where(choose, kernel[None, None, :], 0.0), axis=2).astype(jnp.bfloat16)


def pick_kernel(block_count, *refs):
    blocks, selector, outs = refs[:block_count], refs[block_count], refs[block_count + 1 :]
    windows = blocks[0].shape[0]
    count = outs[0].shape[1]
    for window in range(windows):
        rows = jnp.concatenate([block[window] for block in blocks], axis=0)
        picked = jnp.dot(selector[...], rows, preferred_element_type=jnp.float32).astype(jnp.bfloat16)
        for at, out in enumerate(outs):
            out[window] = picked[at * count : (at + 1) * count]


def pick(blocks, selector, groups):
    windows, channels, both = blocks[0].shape
    count = selector.shape[0] // groups
    return pl.pallas_call(
        functools.partial(pick_kernel, len(blocks)),
        out_shape=[jax.ShapeDtypeStruct((windows, count, both), jnp.bfloat16)] * groups,
        compiler_params=pltpu.CompilerParams(vmem_limit_bytes=48 * MIB),
        cost_estimate=pl.CostEstimate(
            flops=2 * windows * selector.size * both, bytes_accessed=2 * windows * both * sum(selector.shape), transcendentals=0
        ),
    )(*blocks, selector)


def around(value, axis, step):
    count = lax.axis_size(axis)
    return lax.ppermute(value, axis, [(i, (i + step) % count) for i in range(count)])


def from_all_blocks(part, pair):
    count = lax.axis_size("chan")
    across = [(i, i - i % pair + (i + 1) % pair) for i in range(count)]
    held = [part] + [around(part, "chan", pair * step) for step in range(1, count // pair)]
    return held + [lax.ppermute(block, "chan", across) for block in held] if pair > 1 else held


def block_order(pair):
    count = lax.axis_size("chan")
    here = lax.axis_index("chan")
    held = [(here + count - pair * step) % count for step in range(count // pair)]
    other = [block - block % pair + (block + 1) % pair for block in held]
    return jnp.stack(held + other if pair > 1 else held)


def per_device(traces, filter_taps, good_channels, source_index):
    window_count, channel_count, _ = traces.shape
    good = good_channels[None, :]
    spec, head, tail = transform(traces, good)
    blocks = lax.axis_size("chan")
    groups = lax.axis_size("win")
    left = lax.ppermute(tail, "chan", [(i, i + 1) for i in range(blocks - 1)])
    right = lax.ppermute(head, "chan", [(i + 1, i) for i in range(blocks - 1)])
    whitened = whiten(spec, left, right, make_band(filter_taps, channel_count), good)
    pair = 2 if blocks % 2 == 0 else 1
    own_ids = jnp.arange(channel_count, dtype=jnp.int32)
    channel_ids = (block_order(pair)[:, None] * channel_count + own_ids[None, :]).reshape(-1)
    wanted = jnp.roll(source_index.reshape(groups, -1), -lax.axis_index("win"), axis=0).reshape(-1)
    selector = (wanted[:, None] == channel_ids[None, :]).astype(jnp.bfloat16)
    stacked = []
    for part in whitened:
        picked = pick(from_all_blocks(part, pair), selector, groups)
        sources = [picked[0]] + [around(picked[step], "win", step) for step in range(1, groups)]
        own = [part] + [around(part, "win", step) for step in range(1, groups)]
        stacked.append(cross(sources, own))
    return lagged(stacked, inverse_table(), 1.0 / math.sqrt(F * window_count * groups))


def solution(mesh):
    placed = (P("win", "chan", None), P(), P("chan"), P())
    return jax.shard_map(
        per_device, mesh=mesh, in_specs=placed, out_specs=P("win", "chan", None), check_vma=False
    )
```

```python
import functools
import math

import jax
import jax.numpy as jnp
import numpy as np
from jax import lax
from jax.experimental import pallas as pl
from jax.experimental.pallas import tpu as pltpu
from jax.sharding import PartitionSpec as P

L = 7680
F = 512
LAGS = 2048
HALO = 16
SMOOTH = 64
K0 = 31
QUARTER = L // 4
STEP = 384
FINE = 32
CHUNKS = ((0, 256), (256, 256))
GROUP = 16
LAG_FINE = 128
NT = (((1,), (1,)), ((), ()))
MIB = 1024 * 1024


def unit_angles(positions, axis):
    bins = K0 + np.arange(F, dtype=np.int64)
    phase = np.mod(np.expand_dims(positions, 1 - axis) * np.expand_dims(bins, axis), L)
    angles = phase * (2.0 * math.pi / L)
    return np.cos(angles).astype(np.float32), np.sin(angles).astype(np.float32)


def keep_column(good):
    count = good.shape[1]
    rows = lax.broadcasted_iota(jnp.int32, (count, count), 0)
    cols = lax.broadcasted_iota(jnp.int32, (count, count), 1)
    return jnp.sum(jnp.where(rows == cols, good[...].astype(jnp.float32), 0.0), axis=1, keepdims=True)


def transform_kernel(x0, x1, x2, x3, angles, good, spec, head, tail, table, total):
    step = pl.program_id(0)
    rows = x0.shape[0]
    coarse = QUARTER // FINE
    fine_cos = angles[2 * coarse : 2 * coarse + FINE, :]
    fine_sin = angles[2 * coarse + FINE :, :]
    for part in range(STEP // FINE):
        big_cos = angles[pl.ds(step * (STEP // FINE) + part, 1), :]
        big_sin = angles[pl.ds(coarse + step * (STEP // FINE) + part, 1), :]
        at = pl.ds(part * FINE, FINE)
        table[at, :F] = (big_cos * fine_cos - big_sin * fine_sin).astype(jnp.bfloat16)
        table[at, F:] = (-(big_sin * fine_cos + big_cos * fine_sin)).astype(jnp.bfloat16)

    @pl.when(step == 0)
    def _():
        total[...] = jnp.zeros_like(total)

    for quarter, x in enumerate((x0, x1, x2, x3)):
        at = pl.ds(quarter * rows, rows)
        total[at, :] += jnp.dot(x[...], table[...], preferred_element_type=jnp.float32)

    @pl.when(step == pl.num_programs(0) - 1)
    def _():
        turn = (K0 + lax.broadcasted_iota(jnp.int32, (1, F), 1)) % 4
        even = turn % 2 == 0
        sign = jnp.where(turn < 2, 1.0, -1.0)
        channels = good.shape[1]
        keep = keep_column(good)
        for window in range(rows // channels):
            re = [total[pl.ds(q * rows + window * channels, channels), :F] for q in range(4)]
            im = [total[pl.ds(q * rows + window * channels, channels), F:] for q in range(4)]
            real = jnp.where(even, re[0] + re[2] + sign * (re[1] + re[3]), re[0] - re[2] + sign * (im[1] - im[3])) * keep
            imag = jnp.where(even, im[0] + im[2] + sign * (im[1] + im[3]), im[0] - im[2] - sign * (re[1] - re[3])) * keep
            spec[window, :, :F] = real
            spec[window, :, F:] = imag
            head[window, :, :F] = real[:HALO].astype(jnp.bfloat16)
            head[window, :, F:] = imag[:HALO].astype(jnp.bfloat16)
            tail[window, :, :F] = real[channels - HALO :].astype(jnp.bfloat16)
            tail[window, :, F:] = imag[channels - HALO :].astype(jnp.bfloat16)


def transform(traces, good):
    windows, channels, length = traces.shape
    rows = windows * channels
    steps = QUARTER // STEP
    flat = traces.reshape(rows, length)
    coarse = unit_angles(np.arange(QUARTER // FINE) * FINE, 0)
    angles = np.concatenate(coarse + unit_angles(np.arange(FINE), 0), axis=0)
    whole = lambda *shape: pl.BlockSpec(shape, lambda k: (0,) * len(shape))
    return pl.pallas_call(
        transform_kernel,
        grid=(steps,),
        in_specs=[pl.BlockSpec((rows, STEP), functools.partial(lambda q, k: (0, q * steps + k), q)) for q in range(4)]
        + [whole(*angles.shape), whole(1, channels)],
        out_specs=[whole(windows, channels, 2 * F), whole(windows, HALO, 2 * F), whole(windows, HALO, 2 * F)],
        out_shape=[
            jax.ShapeDtypeStruct((windows, channels, 2 * F), jnp.float32),
            jax.ShapeDtypeStruct((windows, HALO, 2 * F), jnp.bfloat16),
            jax.ShapeDtypeStruct((windows, HALO, 2 * F), jnp.bfloat16),
        ],
        scratch_shapes=[pltpu.VMEM((STEP, 2 * F), jnp.bfloat16), pltpu.VMEM((4 * rows, 2 * F), jnp.float32)],
        compiler_params=pltpu.CompilerParams(vmem_limit_bytes=60 * MIB),
        cost_estimate=pl.CostEstimate(flops=2 * rows * length * 2 * F, bytes_accessed=rows * length * 2, transcendentals=0),
    )(flat, flat, flat, flat, angles, good)


def pieces(value):
    high = value.astype(jnp.bfloat16)
    rest = value - high.astype(jnp.float32)
    middle = rest.astype(jnp.bfloat16)
    return high, middle, (rest - middle.astype(jnp.float32)).astype(jnp.bfloat16)


def whiten_kernel(spec, left, right, band, good, *outs):
    windows, channels = spec.shape[:2]
    filtered = []
    keep = keep_column(good)
    for window in range(windows):
        stack = jnp.concatenate([left[window], *pieces(spec[window]), right[window]], axis=0)
        own = band[:, HALO : HALO + channels]
        taps = jnp.concatenate([band[:, :HALO], own, own, own, band[:, HALO + channels :]], axis=1)
        filtered.append(jnp.dot(taps, stack, preferred_element_type=jnp.float32) * keep)
    spectrum = jnp.concatenate(filtered, axis=0)
    real, imag = spectrum[:, :F], spectrum[:, F:]
    magnitude = jnp.sqrt(real * real + imag * imag)
    bins = lax.broadcasted_iota(jnp.int32, (F, F), 0)
    others = lax.broadcasted_iota(jnp.int32, (F, F), 1)
    near = jnp.where(jnp.abs(bins - others) <= SMOOTH, 1.0, 0.0).astype(jnp.bfloat16)
    amplitude = sum(jnp.dot(piece, near, preferred_element_type=jnp.float32) for piece in pieces(magnitude))
    bin_row = lax.broadcasted_iota(jnp.int32, (1, F), 1)
    count = jnp.minimum(bin_row + SMOOTH, F - 1) - jnp.maximum(bin_row - SMOOTH, 0) + 1
    amplitude = amplitude * (1.0 / count.astype(jnp.float32))
    inverse = 1.0 / (amplitude + 1e-06)
    real = (real * inverse).astype(jnp.bfloat16)
    imag = (imag * inverse).astype(jnp.bfloat16)
    for out, (start, width) in zip(outs, ((0, F),) + CHUNKS):
        for window in range(windows):
            rows = slice(window * channels, (window + 1) * channels)
            out[window, :, :width] = real[rows, start : start + width]
            out[window, :, width:] = imag[rows, start : start + width]


def whiten(spec, left, right, band, good):
    windows, channels, _ = spec.shape
    return pl.pallas_call(
        whiten_kernel,
        out_shape=[
            jax.ShapeDtypeStruct((windows, channels, 2 * width), jnp.bfloat16) for width in (F, *(w for _, w in CHUNKS))
        ],
        compiler_params=pltpu.CompilerParams(vmem_limit_bytes=40 * MIB),
        cost_estimate=pl.CostEstimate(flops=2 * windows * channels * F * F * 3, bytes_accessed=5 * MIB // 2, transcendentals=windows * channels * F),
    )(spec, left, right, band, good)


def eye(size):
    rows = lax.broadcasted_iota(jnp.int32, (size, size), 0)
    cols = lax.broadcasted_iota(jnp.int32, (size, size), 1)
    return jnp.where(rows == cols, 1.0, 0.0).astype(jnp.bfloat16)


def turned(left_unit, rows):
    return lax.dot_general(left_unit, rows, NT, preferred_element_type=jnp.float32)


def swapper(outer, inner):
    size = outer * inner
    rows = lax.broadcasted_iota(jnp.int32, (size, size), 0)
    cols = lax.broadcasted_iota(jnp.int32, (size, size), 1)
    return jnp.where(cols == rows % outer * inner + rows // outer, 1.0, 0.0).astype(jnp.bfloat16)


def moved(swap, rows):
    return jnp.dot(swap, rows, preferred_element_type=jnp.float32).astype(jnp.bfloat16)


def cross_kernel(sides, first_bin, *refs):
    sources, own = refs[:sides], refs[sides : 2 * sides]
    out, by_window, by_channel, turned_own, sums = refs[2 * sides :]
    each, count, both = sources[0].shape
    channels = own[0].shape[1]
    windows, width, quads = each * sides, both // 2, channels // 4
    half = 2 * windows
    unit = eye(width)
    swap = swapper(GROUP, GROUP)
    swap_quads = swapper(quads, GROUP)
    for window in range(0, windows, 2):
        rows = []
        for one in range(window, window + 2):
            source = sources[one // each]
            rows += [source[one % each, :, :width], source[one % each, :, width:]]
        both_turned = turned(unit, jnp.concatenate(rows, axis=0)).astype(jnp.bfloat16)
        by_window[window] = both_turned[:, : 2 * count]
        by_window[window + 1] = both_turned[:, 2 * count :]
    joined = GROUP // each
    for start in range(0, windows, GROUP):
        for channel in range(0, channels, GROUP):
            for side in range(2):
                bins = slice(side * F + first_bin, side * F + first_bin + width)
                block = [o[:, channel : channel + GROUP, bins] for o in own[start // each : start // each + joined]]
                rows = moved(swap, jnp.concatenate(block, axis=0).reshape(GROUP * GROUP, width))
                turned_own[
                    channel : channel + GROUP, start : start + GROUP, side * width : (side + 1) * width
                ] = rows.reshape(GROUP, GROUP, width)
    for quad in range(quads):
        rows = []
        for channel in range(quad, channels, quads):
            rows += [turned_own[channel, :, :width], turned_own[channel, :, width:]]
        by_channel[quad] = turned(unit, jnp.concatenate(rows, axis=0)).astype(jnp.bfloat16)
    first = lax.broadcasted_iota(jnp.int32, (1, 2 * half), 1) < half
    sign = jnp.where(lax.broadcasted_iota(jnp.int32, (1, 2 * count), 1) < count, 1.0, -1.0)
    empty = jnp.zeros((2 * windows, 2 * count), jnp.bfloat16)

    def one_group(group, carry):
        bins = pl.ds(pl.multiple_of(group * GROUP, GROUP), GROUP)
        rows = [
            by_window[start : start + GROUP, bins, :].reshape(GROUP * GROUP, 2 * count)
            for start in range(0, windows, GROUP)
        ]
        rights = jnp.dot(swap, jnp.concatenate(rows, axis=1), preferred_element_type=jnp.float32)
        lefts = jnp.dot(
            swap_quads, by_channel[:, bins, :].reshape(quads * GROUP, 4 * half), preferred_element_type=jnp.float32
        )
        results = []
        for at in range(0, GROUP, 2):
            two = []
            for one in range(at, at + 2):
                here = rights[one * GROUP : (one + 1) * GROUP]
                src = jnp.concatenate(
                    [here[:, i * 2 * count : (i + 1) * 2 * count] for i in range(windows // GROUP)], axis=0
                )
                two.append(jnp.concatenate([src * sign, pltpu.roll(src, count, axis=1)], axis=0).astype(jnp.bfloat16))
            right = jnp.concatenate(
                [jnp.concatenate([two[0], empty], axis=1), jnp.concatenate([empty, two[1]], axis=1)], axis=0
            )
            left = []
            for tile in range(0, 4 * half, 2 * half):
                one, other = (lefts[i * quads : (i + 1) * quads, tile : tile + 2 * half] for i in (at, at + 1))
                left.append(jnp.where(first, one, pltpu.roll(other, half, axis=1)))
                left.append(jnp.where(first, pltpu.roll(one, half, axis=1), other))
            left = jnp.concatenate(left, axis=0).astype(jnp.bfloat16)
            result = jnp.dot(left, right, preferred_element_type=jnp.float32).astype(jnp.bfloat16)
            results += [result[:, : 2 * count], result[:, 2 * count :]]
        halves = [
            jnp.concatenate([r[start : start + GROUP] for r in results], axis=0) for start in range(0, channels, GROUP)
        ]
        done = moved(swap, jnp.concatenate(halves, axis=1))
        for channel in range(channels):
            row, side = channel % GROUP, channel // GROUP
            sums[channel, bins, :] = done[
                row * GROUP : (row + 1) * GROUP, side * 2 * count : (side + 1) * 2 * count
            ]
        return carry

    lax.fori_loop(0, width // GROUP, one_group, 0, unroll=4)
    unit = eye(2 * count)
    for channel in range(channels):
        out[channel] = turned(unit, sums[channel]).astype(jnp.bfloat16)


def cross(sources, own, first_bin):
    each, count, both = sources[0].shape
    channels, windows, width = own[0].shape[1], each * len(sources), both // 2
    return pl.pallas_call(
        functools.partial(cross_kernel, len(sources), first_bin),
        out_shape=jax.ShapeDtypeStruct((channels, 2 * count, width), jnp.bfloat16),
        scratch_shapes=[
            pltpu.VMEM((windows, width, 2 * count), jnp.bfloat16),
            pltpu.VMEM((channels // 4, width, 8 * windows), jnp.bfloat16),
            pltpu.VMEM((channels, windows, both), jnp.bfloat16),
            pltpu.VMEM((channels, width, 2 * count), jnp.bfloat16),
        ],
        compiler_params=pltpu.CompilerParams(vmem_limit_bytes=40 * MIB),
        cost_estimate=pl.CostEstimate(flops=2 * width * 36 * 65536, bytes_accessed=4 * MIB, transcendentals=0),
    )(*sources, *own)


def lag_kernel(scaling, *refs):
    *stacked, table, out, rows = refs
    channels, both, _ = stacked[0].shape
    count = both // 2
    part = 256 // channels

    @pl.when(pl.program_id(1) == 0)
    def _():
        swap = swapper(channels, part)
        for chunk, (first_bin, width) in zip(stacked, CHUNKS):
            for side in range(2):
                cols = slice(side * F + first_bin, side * F + first_bin + width)
                for start in range(0, count, part):
                    from_rows = slice(side * count + start, side * count + start + part)
                    block = chunk[:, from_rows, :].reshape(channels * part, width)
                    rows[start * channels : (start + part) * channels, cols] = moved(swap, block)

    lags = out.shape[2]
    for start in range(0, lags, 256):
        cols = pl.ds(pl.multiple_of(pl.program_id(1) * lags + start, 256), 256)
        result = jnp.dot(rows[...], table[:, cols], preferred_element_type=jnp.float32) * scaling
        out[:, :, start : start + 256] = result.reshape(count, channels, 256)


def lagged(stacked, table, scaling):
    channels, both, _ = stacked[0].shape
    count = both // 2
    block, cols = 8, LAGS // 2
    return pl.pallas_call(
        functools.partial(lag_kernel, scaling),
        grid=(channels // block, LAGS // cols),
        in_specs=[pl.BlockSpec((block, both, s.shape[2]), lambda i, j: (i, 0, 0)) for s in stacked]
        + [pl.BlockSpec((2 * F, LAGS), lambda i, j: (0, 0))],
        out_specs=pl.BlockSpec((count, block, cols), lambda i, j: (0, i, j)),
        out_shape=jax.ShapeDtypeStruct((count, channels, LAGS), jnp.float32),
        scratch_shapes=[pltpu.VMEM((count * block, 2 * F), jnp.bfloat16)],
        compiler_params=pltpu.CompilerParams(vmem_limit_bytes=48 * MIB),
        cost_estimate=pl.CostEstimate(flops=2 * count * channels * 2 * F * LAGS, bytes_accessed=count * channels * LAGS * 4, transcendentals=0),
    )(*stacked, table)


def inverse_table():
    coarse = unit_angles(np.arange(LAGS // LAG_FINE) * LAG_FINE - LAGS // 2, 1)
    fine = unit_angles(np.arange(LAG_FINE), 1)
    big_cos, big_sin = (jnp.asarray(t)[:, :, None] for t in coarse)
    small_cos, small_sin = (jnp.asarray(t)[:, None, :] for t in fine)
    cos = big_cos * small_cos - big_sin * small_sin
    sin = big_sin * small_cos + big_cos * small_sin
    return jnp.concatenate([cos, -sin], axis=0).astype(jnp.bfloat16).reshape(2 * F, LAGS)


def make_band(filter_taps, channel_count):
    kernel = jnp.concatenate(
        [
            -filter_taps[:HALO].astype(jnp.float32),
            jnp.ones((1,), jnp.float32),
            -filter_taps[HALO:].astype(jnp.float32),
        ]
    )
    row_ids = jnp.arange(channel_count, dtype=jnp.int32)[:, None]
    columns = jnp.arange(channel_count + 2 * HALO, dtype=jnp.int32)[None, :]
    offset = columns - row_ids
    choose = offset[:, :, None] == jnp.arange(2 * HALO + 1, dtype=jnp.int32)[None, None, :]
    return jnp.sum(jnp.where(choose, kernel[None, None, :], 0.0), axis=2).astype(jnp.bfloat16)


def pick_kernel(held, width, first_bin, *refs):
    blocks, own_across, across, selector, *outs = refs[:held], *refs[held:]
    windows, channels, _ = blocks[0].shape
    count = outs[0].shape[1]
    for window in range(windows):
        rows = [block[window] for block in blocks]
        rows.append(
            jnp.concatenate(
                [own_across[window, :, first_bin : first_bin + width], own_across[window, :, F + first_bin : F + first_bin + width]],
                axis=1,
            )
        )
        rows += [across[block, window] for block in range(held - 1)]
        picked = jnp.dot(selector[...], jnp.concatenate(rows, axis=0), preferred_element_type=jnp.float32)
        for at, out in enumerate(outs):
            out[window] = picked[at * count : (at + 1) * count].astype(jnp.bfloat16)


def pick(blocks, own_across, across, selector, groups, first_bin):
    windows, _, both = blocks[0].shape
    count = selector.shape[0] // groups
    return pl.pallas_call(
        functools.partial(pick_kernel, len(blocks), both // 2, first_bin),
        out_shape=[jax.ShapeDtypeStruct((windows, count, both), jnp.bfloat16)] * groups,
        compiler_params=pltpu.CompilerParams(vmem_limit_bytes=40 * MIB),
        cost_estimate=pl.CostEstimate(
            flops=2 * windows * selector.size * both, bytes_accessed=2 * windows * both * sum(selector.shape), transcendentals=0
        ),
    )(*blocks, own_across, across, selector)


def swapped(value, axis, step):
    return lax.ppermute(value, axis, [(i, i ^ step) for i in range(lax.axis_size(axis))])


def after(value, earlier):
    return lax.optimization_barrier((value, earlier))[0]


def per_device(traces, filter_taps, good_channels, source_index):
    window_count, channel_count, _ = traces.shape
    good = good_channels[None, :]
    spec, head, tail = transform(traces, good)
    blocks = lax.axis_size("chan")
    groups = lax.axis_size("win")
    left = lax.ppermute(tail, "chan", [(i, i + 1) for i in range(blocks - 1)])
    right = lax.ppermute(head, "chan", [(i + 1, i) for i in range(blocks - 1)])
    full, *parts = whiten(spec, left, right, make_band(filter_taps, channel_count), good)

    order = jnp.asarray([*range(0, blocks, 2), *range(1, blocks, 2)], jnp.int32) ^ lax.axis_index("chan")
    own_ids = jnp.arange(channel_count, dtype=jnp.int32)
    channel_ids = (order[:, None] * channel_count + own_ids[None, :]).reshape(-1)
    by_group = source_index.reshape(groups, -1)
    here = lax.axis_index("win")
    wanted = jnp.concatenate([lax.dynamic_slice_in_dim(by_group, here ^ step, 1) for step in range(groups)], axis=0)
    selector = (wanted.reshape(-1)[:, None] == channel_ids[None, :]).astype(jnp.bfloat16)

    own = [full] + [None] * (groups - 1)
    for step in range(2, groups, 2):
        own[step] = swapped(full, "win", step)
    for step in range(1, groups, 2):
        own[step] = swapped(own[step - 1], "win", 1)
    own_across = swapped(full, "chan", 1)
    stacked = []
    earlier = picked = None
    for part, (first_bin, _) in zip(parts, CHUNKS):
        if earlier is not None:
            part = after(part, earlier)
        held = [swapped(part, "chan", step) for step in range(2, blocks, 2)]
        earlier = [held, own_across, own[2::2]]
        if picked is not None:
            held = after(held, picked)
        across = swapped(jnp.stack(held), "chan", 1)
        picked = pick([part] + held, own_across, across, selector, groups, first_bin)
        sources = [picked[0]] + [swapped(picked[step], "win", step) for step in range(1, groups)]
        stacked.append(cross(sources, own, first_bin))
    return lagged(stacked, inverse_table(), 1.0 / math.sqrt(F * window_count * groups))


def solution(mesh):
    placed = (P("win", "chan", None), P(), P("chan"), P())
    return jax.shard_map(
        per_device, mesh=mesh, in_specs=placed, out_specs=P("win", "chan", None), check_vma=False
    )
```

```python
import functools
import math

import jax
import jax.numpy as jnp
import numpy as np
from jax import lax
from jax.experimental import pallas as pl
from jax.experimental.pallas import tpu as pltpu
from jax.sharding import PartitionSpec as P

L = 7680
F = 512
LAGS = 2048
HALO = 16
SMOOTH = 64
K0 = 31
QUARTER = L // 4
STEP = 384
FINE = 32
CHUNKS = ((0, 128), (128, 128), (256, 128), (384, 128))
GROUP = 16
LAG_FINE = 128
NT = (((1,), (1,)), ((), ()))
MIB = 1024 * 1024


def unit_angles(positions, axis):
    bins = K0 + np.arange(F, dtype=np.int64)
    phase = np.mod(np.expand_dims(positions, 1 - axis) * np.expand_dims(bins, axis), L)
    angles = phase * (2.0 * math.pi / L)
    return np.cos(angles).astype(np.float32), np.sin(angles).astype(np.float32)


def keep_column(good):
    count = good.shape[1]
    rows = lax.broadcasted_iota(jnp.int32, (count, count), 0)
    cols = lax.broadcasted_iota(jnp.int32, (count, count), 1)
    return jnp.sum(jnp.where(rows == cols, good[...].astype(jnp.float32), 0.0), axis=1, keepdims=True)


def transform_kernel(x0, x1, x2, x3, angles, good, spec, head, tail, table, total):
    step = pl.program_id(0)
    rows = x0.shape[0]
    coarse = QUARTER // FINE
    fine_cos = angles[2 * coarse : 2 * coarse + FINE, :]
    fine_sin = angles[2 * coarse + FINE :, :]
    for part in range(STEP // FINE):
        big_cos = angles[pl.ds(step * (STEP // FINE) + part, 1), :]
        big_sin = angles[pl.ds(coarse + step * (STEP // FINE) + part, 1), :]
        at = pl.ds(part * FINE, FINE)
        table[at, :F] = (big_cos * fine_cos - big_sin * fine_sin).astype(jnp.bfloat16)
        table[at, F:] = (-(big_sin * fine_cos + big_cos * fine_sin)).astype(jnp.bfloat16)

    @pl.when(step == 0)
    def _():
        total[...] = jnp.zeros_like(total)

    for quarter, x in enumerate((x0, x1, x2, x3)):
        at = pl.ds(quarter * rows, rows)
        total[at, :] += jnp.dot(x[...], table[...], preferred_element_type=jnp.float32)

    @pl.when(step == pl.num_programs(0) - 1)
    def _():
        turn = (K0 + lax.broadcasted_iota(jnp.int32, (1, F), 1)) % 4
        even = turn % 2 == 0
        sign = jnp.where(turn < 2, 1.0, -1.0)
        channels = good.shape[1]
        keep = keep_column(good)
        for window in range(rows // channels):
            re = [total[pl.ds(q * rows + window * channels, channels), :F] for q in range(4)]
            im = [total[pl.ds(q * rows + window * channels, channels), F:] for q in range(4)]
            real = jnp.where(even, re[0] + re[2] + sign * (re[1] + re[3]), re[0] - re[2] + sign * (im[1] - im[3])) * keep
            imag = jnp.where(even, im[0] + im[2] + sign * (im[1] + im[3]), im[0] - im[2] - sign * (re[1] - re[3])) * keep
            spec[window, :, :F] = real
            spec[window, :, F:] = imag
            head[window, :, :F] = real[:HALO].astype(jnp.bfloat16)
            head[window, :, F:] = imag[:HALO].astype(jnp.bfloat16)
            tail[window, :, :F] = real[channels - HALO :].astype(jnp.bfloat16)
            tail[window, :, F:] = imag[channels - HALO :].astype(jnp.bfloat16)


def transform(traces, good):
    windows, channels, length = traces.shape
    rows = windows * channels
    steps = QUARTER // STEP
    flat = traces.reshape(rows, length)
    coarse = unit_angles(np.arange(QUARTER // FINE) * FINE, 0)
    angles = np.concatenate(coarse + unit_angles(np.arange(FINE), 0), axis=0)
    whole = lambda *shape: pl.BlockSpec(shape, lambda k: (0,) * len(shape))
    return pl.pallas_call(
        transform_kernel,
        grid=(steps,),
        in_specs=[pl.BlockSpec((rows, STEP), functools.partial(lambda q, k: (0, q * steps + k), q)) for q in range(4)]
        + [whole(*angles.shape), whole(1, channels)],
        out_specs=[whole(windows, channels, 2 * F), whole(windows, HALO, 2 * F), whole(windows, HALO, 2 * F)],
        out_shape=[
            jax.ShapeDtypeStruct((windows, channels, 2 * F), jnp.float32),
            jax.ShapeDtypeStruct((windows, HALO, 2 * F), jnp.bfloat16),
            jax.ShapeDtypeStruct((windows, HALO, 2 * F), jnp.bfloat16),
        ],
        scratch_shapes=[pltpu.VMEM((STEP, 2 * F), jnp.bfloat16), pltpu.VMEM((4 * rows, 2 * F), jnp.float32)],
        compiler_params=pltpu.CompilerParams(vmem_limit_bytes=60 * MIB),
        cost_estimate=pl.CostEstimate(flops=2 * rows * length * 2 * F, bytes_accessed=rows * length * 2, transcendentals=0),
    )(flat, flat, flat, flat, angles, good)


def pieces(value):
    high = value.astype(jnp.bfloat16)
    rest = value - high.astype(jnp.float32)
    middle = rest.astype(jnp.bfloat16)
    return high, middle, (rest - middle.astype(jnp.float32)).astype(jnp.bfloat16)


def whiten_kernel(spec, left, right, band, good, *outs):
    windows, channels = spec.shape[:2]
    filtered = []
    keep = keep_column(good)
    for window in range(windows):
        stack = jnp.concatenate([left[window], *pieces(spec[window]), right[window]], axis=0)
        own = band[:, HALO : HALO + channels]
        taps = jnp.concatenate([band[:, :HALO], own, own, own, band[:, HALO + channels :]], axis=1)
        filtered.append(jnp.dot(taps, stack, preferred_element_type=jnp.float32) * keep)
    spectrum = jnp.concatenate(filtered, axis=0)
    real, imag = spectrum[:, :F], spectrum[:, F:]
    magnitude = jnp.sqrt(real * real + imag * imag)
    bins = lax.broadcasted_iota(jnp.int32, (F, F), 0)
    others = lax.broadcasted_iota(jnp.int32, (F, F), 1)
    near = jnp.where(jnp.abs(bins - others) <= SMOOTH, 1.0, 0.0).astype(jnp.bfloat16)
    amplitude = sum(jnp.dot(piece, near, preferred_element_type=jnp.float32) for piece in pieces(magnitude))
    bin_row = lax.broadcasted_iota(jnp.int32, (1, F), 1)
    count = jnp.minimum(bin_row + SMOOTH, F - 1) - jnp.maximum(bin_row - SMOOTH, 0) + 1
    amplitude = amplitude * (1.0 / count.astype(jnp.float32))
    inverse = 1.0 / (amplitude + 1e-06)
    real = (real * inverse).astype(jnp.bfloat16)
    imag = (imag * inverse).astype(jnp.bfloat16)
    for out, (start, width) in zip(outs, ((0, F),) + CHUNKS):
        for window in range(windows):
            rows = slice(window * channels, (window + 1) * channels)
            out[window, :, :width] = real[rows, start : start + width]
            out[window, :, width:] = imag[rows, start : start + width]


def whiten(spec, left, right, band, good):
    windows, channels, _ = spec.shape
    return pl.pallas_call(
        whiten_kernel,
        out_shape=[
            jax.ShapeDtypeStruct((windows, channels, 2 * width), jnp.bfloat16) for width in (F, *(w for _, w in CHUNKS))
        ],
        compiler_params=pltpu.CompilerParams(vmem_limit_bytes=40 * MIB),
        cost_estimate=pl.CostEstimate(flops=2 * windows * channels * F * F * 3, bytes_accessed=5 * MIB // 2, transcendentals=windows * channels * F),
    )(spec, left, right, band, good)


def eye(size):
    rows = lax.broadcasted_iota(jnp.int32, (size, size), 0)
    cols = lax.broadcasted_iota(jnp.int32, (size, size), 1)
    return jnp.where(rows == cols, 1.0, 0.0).astype(jnp.bfloat16)


def turned(left_unit, rows):
    return lax.dot_general(left_unit, rows, NT, preferred_element_type=jnp.float32)


def swapper(outer, inner):
    size = outer * inner
    rows = lax.broadcasted_iota(jnp.int32, (size, size), 0)
    cols = lax.broadcasted_iota(jnp.int32, (size, size), 1)
    return jnp.where(cols == rows % outer * inner + rows // outer, 1.0, 0.0).astype(jnp.bfloat16)


def moved(swap, rows):
    return jnp.dot(swap, rows, preferred_element_type=jnp.float32).astype(jnp.bfloat16)


def cross_kernel(
    first_bin, here, near, far, own_here, own_near, own_far, out, by_window, by_channel, turned_own, sums
):
    sources = [here, near.at[0], far.at[0], near.at[1]]
    own = [own_here, own_near.at[0], own_far, own_near.at[1]]
    each, count, both = here.shape
    sides, channels = len(sources), own_here.shape[1]
    windows, width, quads = each * sides, both // 2, channels // 4
    half = 2 * windows
    unit = eye(width)
    swap = swapper(GROUP, GROUP)
    swap_quads = swapper(quads, GROUP)
    for window in range(0, windows, 2):
        rows = []
        for one in range(window, window + 2):
            source = sources[one // each]
            rows += [source[one % each, :, :width], source[one % each, :, width:]]
        both_turned = turned(unit, jnp.concatenate(rows, axis=0)).astype(jnp.bfloat16)
        by_window[window] = both_turned[:, : 2 * count]
        by_window[window + 1] = both_turned[:, 2 * count :]
    joined = GROUP // each
    for start in range(0, windows, GROUP):
        for channel in range(0, channels, GROUP):
            for side in range(2):
                bins = slice(side * F + first_bin, side * F + first_bin + width)
                block = [o[:, channel : channel + GROUP, bins] for o in own[start // each : start // each + joined]]
                rows = moved(swap, jnp.concatenate(block, axis=0).reshape(GROUP * GROUP, width))
                turned_own[
                    channel : channel + GROUP, start : start + GROUP, side * width : (side + 1) * width
                ] = rows.reshape(GROUP, GROUP, width)
    for quad in range(quads):
        rows = []
        for channel in range(quad, channels, quads):
            rows += [turned_own[channel, :, :width], turned_own[channel, :, width:]]
        by_channel[quad] = turned(unit, jnp.concatenate(rows, axis=0)).astype(jnp.bfloat16)
    first = lax.broadcasted_iota(jnp.int32, (1, 2 * half), 1) < half
    sign = jnp.where(lax.broadcasted_iota(jnp.int32, (1, 2 * count), 1) < count, 1.0, -1.0)
    empty = jnp.zeros((2 * windows, 2 * count), jnp.bfloat16)

    def one_group(group, carry):
        bins = pl.ds(pl.multiple_of(group * GROUP, GROUP), GROUP)
        rows = [
            by_window[start : start + GROUP, bins, :].reshape(GROUP * GROUP, 2 * count)
            for start in range(0, windows, GROUP)
        ]
        rights = jnp.dot(swap, jnp.concatenate(rows, axis=1), preferred_element_type=jnp.float32)
        lefts = jnp.dot(
            swap_quads, by_channel[:, bins, :].reshape(quads * GROUP, 4 * half), preferred_element_type=jnp.float32
        )
        results = []
        for at in range(0, GROUP, 2):
            two = []
            for one in range(at, at + 2):
                here = rights[one * GROUP : (one + 1) * GROUP]
                src = jnp.concatenate(
                    [here[:, i * 2 * count : (i + 1) * 2 * count] for i in range(windows // GROUP)], axis=0
                )
                two.append(jnp.concatenate([src * sign, pltpu.roll(src, count, axis=1)], axis=0).astype(jnp.bfloat16))
            right = jnp.concatenate(
                [jnp.concatenate([two[0], empty], axis=1), jnp.concatenate([empty, two[1]], axis=1)], axis=0
            )
            left = []
            for tile in range(0, 4 * half, 2 * half):
                one, other = (lefts[i * quads : (i + 1) * quads, tile : tile + 2 * half] for i in (at, at + 1))
                left.append(jnp.where(first, one, pltpu.roll(other, half, axis=1)))
                left.append(jnp.where(first, pltpu.roll(one, half, axis=1), other))
            left = jnp.concatenate(left, axis=0).astype(jnp.bfloat16)
            result = jnp.dot(left, right, preferred_element_type=jnp.float32).astype(jnp.bfloat16)
            results += [result[:, : 2 * count], result[:, 2 * count :]]
        halves = [
            jnp.concatenate([r[start : start + GROUP] for r in results], axis=0) for start in range(0, channels, GROUP)
        ]
        done = moved(swap, jnp.concatenate(halves, axis=1))
        for channel in range(channels):
            row, side = channel % GROUP, channel // GROUP
            sums[channel, bins, :] = done[
                row * GROUP : (row + 1) * GROUP, side * 2 * count : (side + 1) * 2 * count
            ]
        return carry

    lax.fori_loop(0, width // GROUP, one_group, 0, unroll=4)
    unit = eye(2 * count)
    for channel in range(channels):
        out[channel] = turned(unit, sums[channel]).astype(jnp.bfloat16)


def cross(sources, own, first_bin):
    each, count, both = sources[0].shape
    channels, windows, width = own[0].shape[1], each * 4, both // 2
    return pl.pallas_call(
        functools.partial(cross_kernel, first_bin),
        out_shape=jax.ShapeDtypeStruct((channels, 2 * count, width), jnp.bfloat16),
        scratch_shapes=[
            pltpu.VMEM((windows, width, 2 * count), jnp.bfloat16),
            pltpu.VMEM((channels // 4, width, 8 * windows), jnp.bfloat16),
            pltpu.VMEM((channels, windows, both), jnp.bfloat16),
            pltpu.VMEM((channels, width, 2 * count), jnp.bfloat16),
        ],
        compiler_params=pltpu.CompilerParams(vmem_limit_bytes=40 * MIB),
        cost_estimate=pl.CostEstimate(flops=2 * width * 36 * 65536, bytes_accessed=4 * MIB, transcendentals=0),
    )(*sources, *own)


def lag_kernel(scaling, *refs):
    *stacked, table, out, rows = refs
    channels, both, _ = stacked[0].shape
    count = both // 2
    part = 256 // channels

    @pl.when(pl.program_id(1) == 0)
    def _():
        swap = swapper(channels, part)
        for chunk, (first_bin, width) in zip(stacked, CHUNKS):
            for side in range(2):
                cols = slice(side * F + first_bin, side * F + first_bin + width)
                for start in range(0, count, part):
                    from_rows = slice(side * count + start, side * count + start + part)
                    block = chunk[:, from_rows, :].reshape(channels * part, width)
                    rows[start * channels : (start + part) * channels, cols] = moved(swap, block)

    lags = out.shape[2]
    for start in range(0, lags, 256):
        cols = pl.ds(pl.multiple_of(pl.program_id(1) * lags + start, 256), 256)
        result = jnp.dot(rows[...], table[:, cols], preferred_element_type=jnp.float32) * scaling
        out[:, :, start : start + 256] = result.reshape(count, channels, 256)


def lagged(stacked, table, scaling):
    channels, both, _ = stacked[0].shape
    count = both // 2
    block, cols = 8, LAGS // 2
    return pl.pallas_call(
        functools.partial(lag_kernel, scaling),
        grid=(channels // block, LAGS // cols),
        in_specs=[pl.BlockSpec((block, both, s.shape[2]), lambda i, j: (i, 0, 0)) for s in stacked]
        + [pl.BlockSpec((2 * F, LAGS), lambda i, j: (0, 0))],
        out_specs=pl.BlockSpec((count, block, cols), lambda i, j: (0, i, j)),
        out_shape=jax.ShapeDtypeStruct((count, channels, LAGS), jnp.float32),
        scratch_shapes=[pltpu.VMEM((count * block, 2 * F), jnp.bfloat16)],
        compiler_params=pltpu.CompilerParams(vmem_limit_bytes=48 * MIB),
        cost_estimate=pl.CostEstimate(flops=2 * count * channels * 2 * F * LAGS, bytes_accessed=count * channels * LAGS * 4, transcendentals=0),
    )(*stacked, table)


def inverse_table():
    coarse = unit_angles(np.arange(LAGS // LAG_FINE) * LAG_FINE - LAGS // 2, 1)
    fine = unit_angles(np.arange(LAG_FINE), 1)
    big_cos, big_sin = (jnp.asarray(t)[:, :, None] for t in coarse)
    small_cos, small_sin = (jnp.asarray(t)[:, None, :] for t in fine)
    cos = big_cos * small_cos - big_sin * small_sin
    sin = big_sin * small_cos + big_cos * small_sin
    return jnp.concatenate([cos, -sin], axis=0).astype(jnp.bfloat16).reshape(2 * F, LAGS)


def make_band(filter_taps, channel_count):
    kernel = jnp.concatenate(
        [
            -filter_taps[:HALO].astype(jnp.float32),
            jnp.ones((1,), jnp.float32),
            -filter_taps[HALO:].astype(jnp.float32),
        ]
    )
    row_ids = jnp.arange(channel_count, dtype=jnp.int32)[:, None]
    columns = jnp.arange(channel_count + 2 * HALO, dtype=jnp.int32)[None, :]
    offset = columns - row_ids
    choose = offset[:, :, None] == jnp.arange(2 * HALO + 1, dtype=jnp.int32)[None, None, :]
    return jnp.sum(jnp.where(choose, kernel[None, None, :], 0.0), axis=2).astype(jnp.bfloat16)


def pick_kernel(held, across, selector, here, near, far):
    count = here.shape[1]
    for window in range(held.shape[1]):
        rows = [blocks[i, window] for blocks in (held, across) for i in range(blocks.shape[0])]
        picked = jnp.dot(selector[...], jnp.concatenate(rows, axis=0), preferred_element_type=jnp.float32)
        picked = picked.astype(jnp.bfloat16)
        here[window] = picked[:count]
        near[window] = picked[count : 2 * count]
        for at in range(far.shape[0]):
            far[at, window] = picked[(2 + at) * count : (3 + at) * count]


def pick(held, across, selector, groups):
    _, windows, _, both = held.shape
    count = selector.shape[0] // groups
    one = (windows, count, both)
    return pl.pallas_call(
        pick_kernel,
        out_shape=[jax.ShapeDtypeStruct(shape, jnp.bfloat16) for shape in (one, one, (groups - 2, *one))],
        compiler_params=pltpu.CompilerParams(vmem_limit_bytes=40 * MIB),
        cost_estimate=pl.CostEstimate(
            flops=2 * windows * selector.size * both, bytes_accessed=2 * windows * both * sum(selector.shape), transcendentals=0
        ),
    )(held, across, selector)


def swapped(value, axis, step):
    return lax.ppermute(value, axis, [(i, i ^ step) for i in range(lax.axis_size(axis))])


def after(value, earlier):
    return lax.optimization_barrier((value, earlier))[0]


def per_device(traces, filter_taps, good_channels, source_index):
    window_count, channel_count, _ = traces.shape
    good = good_channels[None, :]
    spec, head, tail = transform(traces, good)
    blocks = lax.axis_size("chan")
    groups = lax.axis_size("win")
    left = lax.ppermute(tail, "chan", [(i, i + 1) for i in range(blocks - 1)])
    right = lax.ppermute(head, "chan", [(i + 1, i) for i in range(blocks - 1)])
    full, *parts = whiten(spec, left, right, make_band(filter_taps, channel_count), good)

    order = [0]
    step = blocks // 2
    while step:
        order += [place ^ step for place in order]
        step //= 2
    order = jnp.asarray(order, jnp.int32) ^ lax.axis_index("chan")
    own_ids = jnp.arange(channel_count, dtype=jnp.int32)
    channel_ids = (order[:, None] * channel_count + own_ids[None, :]).reshape(-1)
    by_group = source_index.reshape(groups, -1)
    here = lax.axis_index("win")
    wanted = jnp.concatenate([lax.dynamic_slice_in_dim(by_group, here ^ step, 1) for step in range(groups)], axis=0)
    selector = (wanted.reshape(-1)[:, None] == channel_ids[None, :]).astype(jnp.bfloat16)

    own_far = swapped(full, "win", 2)
    own_near = swapped(jnp.stack([full, own_far]), "win", 1)
    stacked = []
    first_held = across = None
    for at, (part, (first_bin, _)) in enumerate(zip(parts, CHUNKS)):
        if at:
            part = after(part, first_held if at != 2 else [first_held, own_far])
        held = part[None]
        step = blocks // 2
        while step > 1:
            held = jnp.concatenate([held, swapped(held, "chan", step)], axis=0)
            first_held = held if step == blocks // 2 else first_held
            step //= 2
        if at:
            held = after(held, across)
        across = swapped(held, "chan", 1)
        here, near, far = pick(held, across, selector, groups)
        far = swapped(far, "win", 2)
        near = swapped(jnp.stack([near, far[1]]), "win", 1)
        stacked.append(cross([here, near, far], [full, own_near, own_far], first_bin))
    return lagged(stacked, inverse_table(), 1.0 / math.sqrt(F * window_count * groups))


def solution(mesh):
    placed = (P("win", "chan", None), P(), P("chan"), P())
    return jax.shard_map(
        per_device, mesh=mesh, in_specs=placed, out_specs=P("win", "chan", None), check_vma=False
    )
```

```python
import functools
import math

import jax
import jax.numpy as jnp
import numpy as np
from jax import lax
from jax.experimental import pallas as pl
from jax.experimental.pallas import tpu as pltpu
from jax.sharding import PartitionSpec as P

L = 7680
F = 512
LAGS = 2048
HALO = 16
SMOOTH = 64
K0 = 31
QUARTER = L // 4
STEP = 384
FINE = 32
CHUNKS = ((0, 128), (128, 128), (256, 128), (384, 128))
GROUP = 16
LAG_FINE = 128
NT = (((1,), (1,)), ((), ()))
MIB = 1024 * 1024


def unit_angles(positions, axis):
    bins = K0 + np.arange(F, dtype=np.int64)
    phase = np.mod(np.expand_dims(positions, 1 - axis) * np.expand_dims(bins, axis), L)
    angles = phase * (2.0 * math.pi / L)
    return np.cos(angles).astype(np.float32), np.sin(angles).astype(np.float32)


def keep_column(good):
    count = good.shape[1]
    rows = lax.broadcasted_iota(jnp.int32, (count, count), 0)
    cols = lax.broadcasted_iota(jnp.int32, (count, count), 1)
    return jnp.sum(jnp.where(rows == cols, good[...].astype(jnp.float32), 0.0), axis=1, keepdims=True)


def transform_kernel(x0, x1, x2, x3, angles, good, spec, head, tail, table, total):
    step = pl.program_id(0)
    rows = x0.shape[0]
    coarse = QUARTER // FINE
    fine_cos = angles[2 * coarse : 2 * coarse + FINE, :]
    fine_sin = angles[2 * coarse + FINE :, :]
    for part in range(STEP // FINE):
        big_cos = angles[pl.ds(step * (STEP // FINE) + part, 1), :]
        big_sin = angles[pl.ds(coarse + step * (STEP // FINE) + part, 1), :]
        at = pl.ds(part * FINE, FINE)
        table[at, :F] = (big_cos * fine_cos - big_sin * fine_sin).astype(jnp.bfloat16)
        table[at, F:] = (-(big_sin * fine_cos + big_cos * fine_sin)).astype(jnp.bfloat16)

    @pl.when(step == 0)
    def _():
        total[...] = jnp.zeros_like(total)

    for quarter, x in enumerate((x0, x1, x2, x3)):
        at = pl.ds(quarter * rows, rows)
        total[at, :] += jnp.dot(x[...], table[...], preferred_element_type=jnp.float32)

    @pl.when(step == pl.num_programs(0) - 1)
    def _():
        turn = (K0 + lax.broadcasted_iota(jnp.int32, (1, F), 1)) % 4
        even = turn % 2 == 0
        sign = jnp.where(turn < 2, 1.0, -1.0)
        channels = good.shape[1]
        keep = keep_column(good)
        for window in range(rows // channels):
            re = [total[pl.ds(q * rows + window * channels, channels), :F] for q in range(4)]
            im = [total[pl.ds(q * rows + window * channels, channels), F:] for q in range(4)]
            real = jnp.where(even, re[0] + re[2] + sign * (re[1] + re[3]), re[0] - re[2] + sign * (im[1] - im[3])) * keep
            imag = jnp.where(even, im[0] + im[2] + sign * (im[1] + im[3]), im[0] - im[2] - sign * (re[1] - re[3])) * keep
            spec[window, :, :F] = real
            spec[window, :, F:] = imag
            head[window, :, :F] = real[:HALO].astype(jnp.bfloat16)
            head[window, :, F:] = imag[:HALO].astype(jnp.bfloat16)
            tail[window, :, :F] = real[channels - HALO :].astype(jnp.bfloat16)
            tail[window, :, F:] = imag[channels - HALO :].astype(jnp.bfloat16)


def transform(traces, good):
    windows, channels, length = traces.shape
    rows = windows * channels
    steps = QUARTER // STEP
    flat = traces.reshape(rows, length)
    coarse = unit_angles(np.arange(QUARTER // FINE) * FINE, 0)
    angles = np.concatenate(coarse + unit_angles(np.arange(FINE), 0), axis=0)
    whole = lambda *shape: pl.BlockSpec(shape, lambda k: (0,) * len(shape))
    return pl.pallas_call(
        transform_kernel,
        grid=(steps,),
        in_specs=[pl.BlockSpec((rows, STEP), functools.partial(lambda q, k: (0, q * steps + k), q)) for q in range(4)]
        + [whole(*angles.shape), whole(1, channels)],
        out_specs=[whole(windows, channels, 2 * F), whole(windows, HALO, 2 * F), whole(windows, HALO, 2 * F)],
        out_shape=[
            jax.ShapeDtypeStruct((windows, channels, 2 * F), jnp.float32),
            jax.ShapeDtypeStruct((windows, HALO, 2 * F), jnp.bfloat16),
            jax.ShapeDtypeStruct((windows, HALO, 2 * F), jnp.bfloat16),
        ],
        scratch_shapes=[pltpu.VMEM((STEP, 2 * F), jnp.bfloat16), pltpu.VMEM((4 * rows, 2 * F), jnp.float32)],
        compiler_params=pltpu.CompilerParams(vmem_limit_bytes=60 * MIB),
        cost_estimate=pl.CostEstimate(flops=2 * rows * length * 2 * F, bytes_accessed=rows * length * 2, transcendentals=0),
    )(flat, flat, flat, flat, angles, good)


def pieces(value):
    high = value.astype(jnp.bfloat16)
    rest = value - high.astype(jnp.float32)
    middle = rest.astype(jnp.bfloat16)
    return high, middle, (rest - middle.astype(jnp.float32)).astype(jnp.bfloat16)


def whiten_kernel(spec, left, right, band, good, *outs):
    windows, channels = spec.shape[:2]
    filtered = []
    keep = keep_column(good)
    for window in range(windows):
        stack = jnp.concatenate([left[window], *pieces(spec[window]), right[window]], axis=0)
        own = band[:, HALO : HALO + channels]
        taps = jnp.concatenate([band[:, :HALO], own, own, own, band[:, HALO + channels :]], axis=1)
        filtered.append(jnp.dot(taps, stack, preferred_element_type=jnp.float32) * keep)
    spectrum = jnp.concatenate(filtered, axis=0)
    real, imag = spectrum[:, :F], spectrum[:, F:]
    magnitude = jnp.sqrt(real * real + imag * imag)
    bins = lax.broadcasted_iota(jnp.int32, (F, F), 0)
    others = lax.broadcasted_iota(jnp.int32, (F, F), 1)
    near = jnp.where(jnp.abs(bins - others) <= SMOOTH, 1.0, 0.0).astype(jnp.bfloat16)
    amplitude = sum(jnp.dot(piece, near, preferred_element_type=jnp.float32) for piece in pieces(magnitude))
    bin_row = lax.broadcasted_iota(jnp.int32, (1, F), 1)
    count = jnp.minimum(bin_row + SMOOTH, F - 1) - jnp.maximum(bin_row - SMOOTH, 0) + 1
    amplitude = amplitude * (1.0 / count.astype(jnp.float32))
    inverse = 1.0 / (amplitude + 1e-06)
    real = (real * inverse).astype(jnp.bfloat16)
    imag = (imag * inverse).astype(jnp.bfloat16)
    for out, (start, width) in zip(outs, ((0, F),) + CHUNKS):
        for window in range(windows):
            rows = slice(window * channels, (window + 1) * channels)
            out[window, :, :width] = real[rows, start : start + width]
            out[window, :, width:] = imag[rows, start : start + width]


def whiten(spec, left, right, band, good):
    windows, channels, _ = spec.shape
    return pl.pallas_call(
        whiten_kernel,
        out_shape=[
            jax.ShapeDtypeStruct((windows, channels, 2 * width), jnp.bfloat16) for width in (F, *(w for _, w in CHUNKS))
        ],
        compiler_params=pltpu.CompilerParams(vmem_limit_bytes=40 * MIB),
        cost_estimate=pl.CostEstimate(flops=2 * windows * channels * F * F * 3, bytes_accessed=5 * MIB // 2, transcendentals=windows * channels * F),
    )(spec, left, right, band, good)


def eye(size):
    rows = lax.broadcasted_iota(jnp.int32, (size, size), 0)
    cols = lax.broadcasted_iota(jnp.int32, (size, size), 1)
    return jnp.where(rows == cols, 1.0, 0.0).astype(jnp.bfloat16)


def turned(left_unit, rows):
    return lax.dot_general(left_unit, rows, NT, preferred_element_type=jnp.float32)


def swapper(outer, inner):
    size = outer * inner
    rows = lax.broadcasted_iota(jnp.int32, (size, size), 0)
    cols = lax.broadcasted_iota(jnp.int32, (size, size), 1)
    return jnp.where(cols == rows % outer * inner + rows // outer, 1.0, 0.0).astype(jnp.bfloat16)


def moved(swap, rows):
    return jnp.dot(swap, rows, preferred_element_type=jnp.float32).astype(jnp.bfloat16)


def cross_kernel(
    first_bin, here, near, far, own_here, own_near, own_far, out, by_window, by_channel, turned_own, sums
):
    sources = [here, near.at[0], far.at[0], near.at[1]]
    own = [own_here, own_near.at[0], own_far, own_near.at[1]]
    each, count, both = here.shape
    sides, channels = len(sources), own_here.shape[1]
    windows, width, quads = each * sides, both // 2, channels // 4
    half = 2 * windows
    unit = eye(width)
    swap = swapper(GROUP, GROUP)
    swap_quads = swapper(quads, GROUP)
    for window in range(0, windows, 2):
        rows = []
        for one in range(window, window + 2):
            source = sources[one // each]
            rows += [source[one % each, :, :width], source[one % each, :, width:]]
        both_turned = turned(unit, jnp.concatenate(rows, axis=0)).astype(jnp.bfloat16)
        by_window[window] = both_turned[:, : 2 * count]
        by_window[window + 1] = both_turned[:, 2 * count :]
    joined = GROUP // each
    for start in range(0, windows, GROUP):
        for channel in range(0, channels, GROUP):
            for side in range(2):
                bins = slice(side * F + first_bin, side * F + first_bin + width)
                block = [o[:, channel : channel + GROUP, bins] for o in own[start // each : start // each + joined]]
                rows = moved(swap, jnp.concatenate(block, axis=0).reshape(GROUP * GROUP, width))
                turned_own[
                    channel : channel + GROUP, start : start + GROUP, side * width : (side + 1) * width
                ] = rows.reshape(GROUP, GROUP, width)
    for quad in range(quads):
        rows = []
        for channel in range(quad, channels, quads):
            rows += [turned_own[channel, :, :width], turned_own[channel, :, width:]]
        by_channel[quad] = turned(unit, jnp.concatenate(rows, axis=0)).astype(jnp.bfloat16)
    first = lax.broadcasted_iota(jnp.int32, (1, 2 * half), 1) < half
    sign = jnp.where(lax.broadcasted_iota(jnp.int32, (1, 2 * count), 1) < count, 1.0, -1.0)
    empty = jnp.zeros((2 * windows, 2 * count), jnp.bfloat16)

    def one_group(group, carry):
        bins = pl.ds(pl.multiple_of(group * GROUP, GROUP), GROUP)
        rows = [
            by_window[start : start + GROUP, bins, :].reshape(GROUP * GROUP, 2 * count)
            for start in range(0, windows, GROUP)
        ]
        rights = jnp.dot(swap, jnp.concatenate(rows, axis=1), preferred_element_type=jnp.float32)
        lefts = jnp.dot(
            swap_quads, by_channel[:, bins, :].reshape(quads * GROUP, 4 * half), preferred_element_type=jnp.float32
        )
        results = []
        for at in range(0, GROUP, 2):
            two = []
            for one in range(at, at + 2):
                here = rights[one * GROUP : (one + 1) * GROUP]
                src = jnp.concatenate(
                    [here[:, i * 2 * count : (i + 1) * 2 * count] for i in range(windows // GROUP)], axis=0
                )
                two.append(jnp.concatenate([src * sign, pltpu.roll(src, count, axis=1)], axis=0).astype(jnp.bfloat16))
            right = jnp.concatenate(
                [jnp.concatenate([two[0], empty], axis=1), jnp.concatenate([empty, two[1]], axis=1)], axis=0
            )
            left = []
            for tile in range(0, 4 * half, 2 * half):
                one, other = (lefts[i * quads : (i + 1) * quads, tile : tile + 2 * half] for i in (at, at + 1))
                left.append(jnp.where(first, one, pltpu.roll(other, half, axis=1)))
                left.append(jnp.where(first, pltpu.roll(one, half, axis=1), other))
            left = jnp.concatenate(left, axis=0).astype(jnp.bfloat16)
            result = jnp.dot(left, right, preferred_element_type=jnp.float32).astype(jnp.bfloat16)
            results += [result[:, : 2 * count], result[:, 2 * count :]]
        halves = [
            jnp.concatenate([r[start : start + GROUP] for r in results], axis=0) for start in range(0, channels, GROUP)
        ]
        done = moved(swap, jnp.concatenate(halves, axis=1))
        for channel in range(channels):
            row, side = channel % GROUP, channel // GROUP
            sums[channel, bins, :] = done[
                row * GROUP : (row + 1) * GROUP, side * 2 * count : (side + 1) * 2 * count
            ]
        return carry

    lax.fori_loop(0, width // GROUP, one_group, 0, unroll=4)
    unit = eye(2 * count)
    for channel in range(channels):
        out[channel] = turned(unit, sums[channel]).astype(jnp.bfloat16)


def cross(sources, own, first_bin):
    each, count, both = sources[0].shape
    channels, windows, width = own[0].shape[1], each * 4, both // 2
    return pl.pallas_call(
        functools.partial(cross_kernel, first_bin),
        out_shape=jax.ShapeDtypeStruct((channels, 2 * count, width), jnp.bfloat16),
        scratch_shapes=[
            pltpu.VMEM((windows, width, 2 * count), jnp.bfloat16),
            pltpu.VMEM((channels // 4, width, 8 * windows), jnp.bfloat16),
            pltpu.VMEM((channels, windows, both), jnp.bfloat16),
            pltpu.VMEM((channels, width, 2 * count), jnp.bfloat16),
        ],
        compiler_params=pltpu.CompilerParams(vmem_limit_bytes=40 * MIB),
        cost_estimate=pl.CostEstimate(flops=2 * width * 36 * 65536 * 8, bytes_accessed=4 * MIB, transcendentals=0),
    )(*sources, *own)


def lag_kernel(scaling, *refs):
    *stacked, table, out, rows = refs
    channels, both, _ = stacked[0].shape
    count = both // 2
    part = 256 // channels

    @pl.when(pl.program_id(1) == 0)
    def _():
        swap = swapper(channels, part)
        for chunk, (first_bin, width) in zip(stacked, CHUNKS):
            for side in range(2):
                cols = slice(side * F + first_bin, side * F + first_bin + width)
                for start in range(0, count, part):
                    from_rows = slice(side * count + start, side * count + start + part)
                    block = chunk[:, from_rows, :].reshape(channels * part, width)
                    rows[start * channels : (start + part) * channels, cols] = moved(swap, block)

    lags = out.shape[2]
    for start in range(0, lags, 256):
        cols = pl.ds(pl.multiple_of(pl.program_id(1) * lags + start, 256), 256)
        result = jnp.dot(rows[...], table[:, cols], preferred_element_type=jnp.float32) * scaling
        out[:, :, start : start + 256] = result.reshape(count, channels, 256)


def lagged(stacked, table, scaling):
    channels, both, _ = stacked[0].shape
    count = both // 2
    block, cols = 8, LAGS // 2
    return pl.pallas_call(
        functools.partial(lag_kernel, scaling),
        grid=(channels // block, LAGS // cols),
        in_specs=[pl.BlockSpec((block, both, s.shape[2]), lambda i, j: (i, 0, 0)) for s in stacked]
        + [pl.BlockSpec((2 * F, LAGS), lambda i, j: (0, 0))],
        out_specs=pl.BlockSpec((count, block, cols), lambda i, j: (0, i, j)),
        out_shape=jax.ShapeDtypeStruct((count, channels, LAGS), jnp.float32),
        scratch_shapes=[pltpu.VMEM((count * block, 2 * F), jnp.bfloat16)],
        compiler_params=pltpu.CompilerParams(vmem_limit_bytes=48 * MIB),
        cost_estimate=pl.CostEstimate(flops=2 * count * channels * 2 * F * LAGS, bytes_accessed=count * channels * LAGS * 4, transcendentals=0),
    )(*stacked, table)


def inverse_table():
    coarse = unit_angles(np.arange(LAGS // LAG_FINE) * LAG_FINE - LAGS // 2, 1)
    fine = unit_angles(np.arange(LAG_FINE), 1)
    big_cos, big_sin = (jnp.asarray(t)[:, :, None] for t in coarse)
    small_cos, small_sin = (jnp.asarray(t)[:, None, :] for t in fine)
    cos = big_cos * small_cos - big_sin * small_sin
    sin = big_sin * small_cos + big_cos * small_sin
    return jnp.concatenate([cos, -sin], axis=0).astype(jnp.bfloat16).reshape(2 * F, LAGS)


def make_band(filter_taps, channel_count):
    kernel = jnp.concatenate(
        [
            -filter_taps[:HALO].astype(jnp.float32),
            jnp.ones((1,), jnp.float32),
            -filter_taps[HALO:].astype(jnp.float32),
        ]
    )
    row_ids = jnp.arange(channel_count, dtype=jnp.int32)[:, None]
    columns = jnp.arange(channel_count + 2 * HALO, dtype=jnp.int32)[None, :]
    offset = columns - row_ids
    choose = offset[:, :, None] == jnp.arange(2 * HALO + 1, dtype=jnp.int32)[None, None, :]
    return jnp.sum(jnp.where(choose, kernel[None, None, :], 0.0), axis=2).astype(jnp.bfloat16)


def pick_kernel(held, across, selector, here, near, far):
    count = here.shape[1]
    for window in range(held.shape[1]):
        rows = [blocks[i, window] for blocks in (held, across) for i in range(blocks.shape[0])]
        picked = jnp.dot(selector[...], jnp.concatenate(rows, axis=0), preferred_element_type=jnp.float32)
        picked = picked.astype(jnp.bfloat16)
        here[window] = picked[:count]
        near[window] = picked[count : 2 * count]
        for at in range(far.shape[0]):
            far[at, window] = picked[(2 + at) * count : (3 + at) * count]


def pick(held, across, selector, groups):
    _, windows, _, both = held.shape
    count = selector.shape[0] // groups
    one = (windows, count, both)
    return pl.pallas_call(
        pick_kernel,
        out_shape=[jax.ShapeDtypeStruct(shape, jnp.bfloat16) for shape in (one, one, (groups - 2, *one))],
        compiler_params=pltpu.CompilerParams(vmem_limit_bytes=40 * MIB),
        cost_estimate=pl.CostEstimate(
            flops=2 * windows * selector.size * both, bytes_accessed=2 * windows * both * sum(selector.shape), transcendentals=0
        ),
    )(held, across, selector)


def swapped(value, axis, step):
    return lax.ppermute(value, axis, [(i, i ^ step) for i in range(lax.axis_size(axis))])


def after(value, earlier):
    return lax.optimization_barrier((value, earlier))[0]


def per_device(traces, filter_taps, good_channels, source_index):
    window_count, channel_count, _ = traces.shape
    good = good_channels[None, :]
    spec, head, tail = transform(traces, good)
    blocks = lax.axis_size("chan")
    groups = lax.axis_size("win")
    left = lax.ppermute(tail, "chan", [(i, i + 1) for i in range(blocks - 1)])
    right = lax.ppermute(head, "chan", [(i + 1, i) for i in range(blocks - 1)])
    full, *parts = whiten(spec, left, right, make_band(filter_taps, channel_count), good)

    order = [0]
    step = blocks // 2
    while step:
        order += [place ^ step for place in order]
        step //= 2
    order = jnp.asarray(order, jnp.int32) ^ lax.axis_index("chan")
    own_ids = jnp.arange(channel_count, dtype=jnp.int32)
    channel_ids = (order[:, None] * channel_count + own_ids[None, :]).reshape(-1)
    by_group = source_index.reshape(groups, -1)
    here = lax.axis_index("win")
    wanted = jnp.concatenate([lax.dynamic_slice_in_dim(by_group, here ^ step, 1) for step in range(groups)], axis=0)
    selector = (wanted.reshape(-1)[:, None] == channel_ids[None, :]).astype(jnp.bfloat16)

    own_far = swapped(full, "win", 2)
    own_near = swapped(jnp.stack([full, own_far]), "win", 1)
    picked = []
    first_held = None
    for at, part in enumerate(parts):
        if at:
            part = after(part, first_held if at != 2 else [first_held, own_far])
        held = part[None]
        step = blocks // 2
        while step > 1:
            held = jnp.concatenate([held, swapped(held, "chan", step)], axis=0)
            first_held = held if step == blocks // 2 else first_held
            step //= 2
        if at:
            held = after(held, picked[-1][0])
        here, near, far = pick(held, swapped(held, "chan", 1), selector, groups)
        picked.append((here, near, swapped(far, "win", 2)))
    stacked = []
    for at, (here, near, far) in enumerate(picked):
        earlier = stacked[-1:] + [later[0] for later in picked[at + 1 : at + 2]]
        if earlier:
            far = after(far, earlier)
        near = swapped(jnp.stack([near, far[1]]), "win", 1)
        stacked.append(cross([here, near, far], [full, own_near, own_far], CHUNKS[at][0]))
    return lagged(stacked, inverse_table(), 1.0 / math.sqrt(F * window_count * groups))


def solution(mesh):
    placed = (P("win", "chan", None), P(), P("chan"), P())
    return jax.shard_map(
        per_device, mesh=mesh, in_specs=placed, out_specs=P("win", "chan", None), check_vma=False
    )
```

```python
import functools
import math

import jax
import jax.numpy as jnp
import numpy as np
from jax import lax
from jax.experimental import pallas as pl
from jax.experimental.pallas import tpu as pltpu
from jax.sharding import PartitionSpec as P

L = 7680
F = 512
LAGS = 2048
HALO = 16
SMOOTH = 64
K0 = 31
QUARTER = L // 4
STEP = 384
FINE = 32
CHUNKS = ((0, 128), (128, 128), (256, 128), (384, 128))
GROUP = 16
LAG_FINE = 128
NT = (((1,), (1,)), ((), ()))
MIB = 1024 * 1024


def unit_angles(positions, axis):
    bins = K0 + np.arange(F, dtype=np.int64)
    phase = np.mod(np.expand_dims(positions, 1 - axis) * np.expand_dims(bins, axis), L)
    angles = phase * (2.0 * math.pi / L)
    return np.cos(angles).astype(np.float32), np.sin(angles).astype(np.float32)


def keep_column(good):
    count = good.shape[1]
    rows = lax.broadcasted_iota(jnp.int32, (count, count), 0)
    cols = lax.broadcasted_iota(jnp.int32, (count, count), 1)
    return jnp.sum(jnp.where(rows == cols, good[...].astype(jnp.float32), 0.0), axis=1, keepdims=True)


def transform_kernel(x0, x1, x2, x3, angles, good, spec, head, tail, table, total):
    step = pl.program_id(0)
    rows = x0.shape[0]
    coarse = QUARTER // FINE
    fine_cos = angles[2 * coarse : 2 * coarse + FINE, :]
    fine_sin = angles[2 * coarse + FINE :, :]
    for part in range(STEP // FINE):
        big_cos = angles[pl.ds(step * (STEP // FINE) + part, 1), :]
        big_sin = angles[pl.ds(coarse + step * (STEP // FINE) + part, 1), :]
        at = pl.ds(part * FINE, FINE)
        table[at, :F] = (big_cos * fine_cos - big_sin * fine_sin).astype(jnp.bfloat16)
        table[at, F:] = (-(big_sin * fine_cos + big_cos * fine_sin)).astype(jnp.bfloat16)

    @pl.when(step == 0)
    def _():
        total[...] = jnp.zeros_like(total)

    for quarter, x in enumerate((x0, x1, x2, x3)):
        at = pl.ds(quarter * rows, rows)
        total[at, :] += jnp.dot(x[...], table[...], preferred_element_type=jnp.float32)

    @pl.when(step == pl.num_programs(0) - 1)
    def _():
        turn = (K0 + lax.broadcasted_iota(jnp.int32, (1, F), 1)) % 4
        even = turn % 2 == 0
        sign = jnp.where(turn < 2, 1.0, -1.0)
        channels = good.shape[1]
        keep = keep_column(good)
        for window in range(rows // channels):
            re = [total[pl.ds(q * rows + window * channels, channels), :F] for q in range(4)]
            im = [total[pl.ds(q * rows + window * channels, channels), F:] for q in range(4)]
            real = jnp.where(even, re[0] + re[2] + sign * (re[1] + re[3]), re[0] - re[2] + sign * (im[1] - im[3])) * keep
            imag = jnp.where(even, im[0] + im[2] + sign * (im[1] + im[3]), im[0] - im[2] - sign * (re[1] - re[3])) * keep
            spec[window, :, :F] = real
            spec[window, :, F:] = imag
            head[window, :, :F] = real[:HALO].astype(jnp.bfloat16)
            head[window, :, F:] = imag[:HALO].astype(jnp.bfloat16)
            tail[window, :, :F] = real[channels - HALO :].astype(jnp.bfloat16)
            tail[window, :, F:] = imag[channels - HALO :].astype(jnp.bfloat16)


def transform(traces, good):
    windows, channels, length = traces.shape
    rows = windows * channels
    steps = QUARTER // STEP
    flat = traces.reshape(rows, length)
    coarse = unit_angles(np.arange(QUARTER // FINE) * FINE, 0)
    angles = np.concatenate(coarse + unit_angles(np.arange(FINE), 0), axis=0)
    whole = lambda *shape: pl.BlockSpec(shape, lambda k: (0,) * len(shape))
    return pl.pallas_call(
        transform_kernel,
        grid=(steps,),
        in_specs=[pl.BlockSpec((rows, STEP), functools.partial(lambda q, k: (0, q * steps + k), q)) for q in range(4)]
        + [whole(*angles.shape), whole(1, channels)],
        out_specs=[whole(windows, channels, 2 * F), whole(windows, HALO, 2 * F), whole(windows, HALO, 2 * F)],
        out_shape=[
            jax.ShapeDtypeStruct((windows, channels, 2 * F), jnp.float32),
            jax.ShapeDtypeStruct((windows, HALO, 2 * F), jnp.bfloat16),
            jax.ShapeDtypeStruct((windows, HALO, 2 * F), jnp.bfloat16),
        ],
        scratch_shapes=[pltpu.VMEM((STEP, 2 * F), jnp.bfloat16), pltpu.VMEM((4 * rows, 2 * F), jnp.float32)],
        compiler_params=pltpu.CompilerParams(vmem_limit_bytes=60 * MIB),
        cost_estimate=pl.CostEstimate(flops=2 * rows * length * 2 * F, bytes_accessed=rows * length * 2, transcendentals=0),
    )(flat, flat, flat, flat, angles, good)


def pieces(value):
    high = value.astype(jnp.bfloat16)
    rest = value - high.astype(jnp.float32)
    middle = rest.astype(jnp.bfloat16)
    return high, middle, (rest - middle.astype(jnp.float32)).astype(jnp.bfloat16)


def whiten_kernel(spec, left, right, band, good, *outs):
    windows, channels = spec.shape[:2]
    filtered = []
    keep = keep_column(good)
    for window in range(windows):
        stack = jnp.concatenate([left[window], *pieces(spec[window]), right[window]], axis=0)
        own = band[:, HALO : HALO + channels]
        taps = jnp.concatenate([band[:, :HALO], own, own, own, band[:, HALO + channels :]], axis=1)
        filtered.append(jnp.dot(taps, stack, preferred_element_type=jnp.float32) * keep)
    spectrum = jnp.concatenate(filtered, axis=0)
    real, imag = spectrum[:, :F], spectrum[:, F:]
    magnitude = jnp.sqrt(real * real + imag * imag)
    bins = lax.broadcasted_iota(jnp.int32, (F, F), 0)
    others = lax.broadcasted_iota(jnp.int32, (F, F), 1)
    near = jnp.where(jnp.abs(bins - others) <= SMOOTH, 1.0, 0.0).astype(jnp.bfloat16)
    amplitude = sum(jnp.dot(piece, near, preferred_element_type=jnp.float32) for piece in pieces(magnitude))
    bin_row = lax.broadcasted_iota(jnp.int32, (1, F), 1)
    count = jnp.minimum(bin_row + SMOOTH, F - 1) - jnp.maximum(bin_row - SMOOTH, 0) + 1
    amplitude = amplitude * (1.0 / count.astype(jnp.float32))
    inverse = 1.0 / (amplitude + 1e-06)
    real = (real * inverse).astype(jnp.bfloat16)
    imag = (imag * inverse).astype(jnp.bfloat16)
    for out, (start, width) in zip(outs, ((0, F),) + CHUNKS):
        for window in range(windows):
            rows = slice(window * channels, (window + 1) * channels)
            out[window, :, :width] = real[rows, start : start + width]
            out[window, :, width:] = imag[rows, start : start + width]


def whiten(spec, left, right, band, good):
    windows, channels, _ = spec.shape
    return pl.pallas_call(
        whiten_kernel,
        out_shape=[
            jax.ShapeDtypeStruct((windows, channels, 2 * width), jnp.bfloat16) for width in (F, *(w for _, w in CHUNKS))
        ],
        compiler_params=pltpu.CompilerParams(vmem_limit_bytes=40 * MIB),
        cost_estimate=pl.CostEstimate(flops=2 * windows * channels * F * F * 3, bytes_accessed=5 * MIB // 2, transcendentals=windows * channels * F),
    )(spec, left, right, band, good)


def eye(size):
    rows = lax.broadcasted_iota(jnp.int32, (size, size), 0)
    cols = lax.broadcasted_iota(jnp.int32, (size, size), 1)
    return jnp.where(rows == cols, 1.0, 0.0).astype(jnp.bfloat16)


def turned(left_unit, rows):
    return lax.dot_general(left_unit, rows, NT, preferred_element_type=jnp.float32)


def swapper(outer, inner):
    size = outer * inner
    rows = lax.broadcasted_iota(jnp.int32, (size, size), 0)
    cols = lax.broadcasted_iota(jnp.int32, (size, size), 1)
    return jnp.where(cols == rows % outer * inner + rows // outer, 1.0, 0.0).astype(jnp.bfloat16)


def moved(swap, rows):
    return jnp.dot(swap, rows, preferred_element_type=jnp.float32).astype(jnp.bfloat16)


def cross_kernel(
    first_bin, here, near, far, own_here, own_near, own_far, out, by_window, by_channel, turned_own, sums
):
    sources = [here, near.at[0], far.at[0], near.at[1]]
    own = [own_here, own_near.at[0], own_far, own_near.at[1]]
    each, count, both = here.shape
    sides, channels = len(sources), own_here.shape[1]
    windows, width, quads = each * sides, both // 2, channels // 4
    half = 2 * windows
    unit = eye(width)
    swap = swapper(GROUP, GROUP)
    swap_quads = swapper(quads, GROUP)
    for window in range(0, windows, 2):
        rows = []
        for one in range(window, window + 2):
            source = sources[one // each]
            rows += [source[one % each, :, :width], source[one % each, :, width:]]
        both_turned = turned(unit, jnp.concatenate(rows, axis=0)).astype(jnp.bfloat16)
        by_window[window] = both_turned[:, : 2 * count]
        by_window[window + 1] = both_turned[:, 2 * count :]
    joined = GROUP // each
    for start in range(0, windows, GROUP):
        for channel in range(0, channels, GROUP):
            for side in range(2):
                bins = slice(side * F + first_bin, side * F + first_bin + width)
                block = [o[:, channel : channel + GROUP, bins] for o in own[start // each : start // each + joined]]
                rows = moved(swap, jnp.concatenate(block, axis=0).reshape(GROUP * GROUP, width))
                turned_own[
                    channel : channel + GROUP, start : start + GROUP, side * width : (side + 1) * width
                ] = rows.reshape(GROUP, GROUP, width)
    for quad in range(quads):
        rows = []
        for channel in range(quad, channels, quads):
            rows += [turned_own[channel, :, :width], turned_own[channel, :, width:]]
        by_channel[quad] = turned(unit, jnp.concatenate(rows, axis=0)).astype(jnp.bfloat16)
    first = lax.broadcasted_iota(jnp.int32, (1, 2 * half), 1) < half
    sign = jnp.where(lax.broadcasted_iota(jnp.int32, (1, 2 * count), 1) < count, 1.0, -1.0)
    empty = jnp.zeros((2 * windows, 2 * count), jnp.bfloat16)

    def one_group(group, carry):
        bins = pl.ds(pl.multiple_of(group * GROUP, GROUP), GROUP)
        rows = [
            by_window[start : start + GROUP, bins, :].reshape(GROUP * GROUP, 2 * count)
            for start in range(0, windows, GROUP)
        ]
        rights = jnp.dot(swap, jnp.concatenate(rows, axis=1), preferred_element_type=jnp.float32)
        lefts = jnp.dot(
            swap_quads, by_channel[:, bins, :].reshape(quads * GROUP, 4 * half), preferred_element_type=jnp.float32
        )
        results = []
        for at in range(0, GROUP, 2):
            two = []
            for one in range(at, at + 2):
                here = rights[one * GROUP : (one + 1) * GROUP]
                src = jnp.concatenate(
                    [here[:, i * 2 * count : (i + 1) * 2 * count] for i in range(windows // GROUP)], axis=0
                )
                two.append(jnp.concatenate([src * sign, pltpu.roll(src, count, axis=1)], axis=0).astype(jnp.bfloat16))
            right = jnp.concatenate(
                [jnp.concatenate([two[0], empty], axis=1), jnp.concatenate([empty, two[1]], axis=1)], axis=0
            )
            left = []
            for tile in range(0, 4 * half, 2 * half):
                one, other = (lefts[i * quads : (i + 1) * quads, tile : tile + 2 * half] for i in (at, at + 1))
                left.append(jnp.where(first, one, pltpu.roll(other, half, axis=1)))
                left.append(jnp.where(first, pltpu.roll(one, half, axis=1), other))
            left = jnp.concatenate(left, axis=0).astype(jnp.bfloat16)
            result = jnp.dot(left, right, preferred_element_type=jnp.float32).astype(jnp.bfloat16)
            results += [result[:, : 2 * count], result[:, 2 * count :]]
        halves = [
            jnp.concatenate([r[start : start + GROUP] for r in results], axis=0) for start in range(0, channels, GROUP)
        ]
        done = moved(swap, jnp.concatenate(halves, axis=1))
        for channel in range(channels):
            row, side = channel % GROUP, channel // GROUP
            sums[channel, bins, :] = done[
                row * GROUP : (row + 1) * GROUP, side * 2 * count : (side + 1) * 2 * count
            ]
        return carry

    lax.fori_loop(0, width // GROUP, one_group, 0, unroll=4)
    unit = eye(2 * count)
    for channel in range(channels):
        out[channel] = turned(unit, sums[channel]).astype(jnp.bfloat16)


def cross(sources, own, first_bin):
    each, count, both = sources[0].shape
    channels, windows, width = own[0].shape[1], each * 4, both // 2
    return pl.pallas_call(
        functools.partial(cross_kernel, first_bin),
        out_shape=jax.ShapeDtypeStruct((channels, 2 * count, width), jnp.bfloat16),
        scratch_shapes=[
            pltpu.VMEM((windows, width, 2 * count), jnp.bfloat16),
            pltpu.VMEM((channels // 4, width, 8 * windows), jnp.bfloat16),
            pltpu.VMEM((channels, windows, both), jnp.bfloat16),
            pltpu.VMEM((channels, width, 2 * count), jnp.bfloat16),
        ],
        compiler_params=pltpu.CompilerParams(vmem_limit_bytes=40 * MIB),
        cost_estimate=pl.CostEstimate(flops=2 * width * 36 * 65536, bytes_accessed=4 * MIB, transcendentals=0),
    )(*sources, *own)


def lag_kernel(scaling, *refs):
    *stacked, table, out, rows = refs
    channels, both, _ = stacked[0].shape
    count = both // 2
    part = 256 // channels
    swap = swapper(channels, part)
    for chunk, (first_bin, width) in zip(stacked, CHUNKS):
        for side in range(2):
            cols = slice(side * F + first_bin, side * F + first_bin + width)
            for start in range(0, count, part):
                from_rows = slice(side * count + start, side * count + start + part)
                block = chunk[:, from_rows, :].reshape(channels * part, width)
                rows[start * channels : (start + part) * channels, cols] = moved(swap, block)

    size = rows.shape[0]
    lane = lax.broadcasted_iota(jnp.int32, (size, LAG_FINE), 1)
    mirror = (LAG_FINE - lane) % LAG_FINE

    def parts(start, width):
        even = jnp.dot(rows[:, :F], table[:F, start : start + width], preferred_element_type=jnp.float32)
        odd = jnp.dot(rows[:, F:], table[F:, start : start + width], preferred_element_type=jnp.float32)
        return even, odd

    half = LAGS // 2
    even, odd = parts(half, LAG_FINE)
    above = (even + odd) * scaling
    for start in range(half - 2 * LAG_FINE, -1, -2 * LAG_FINE):
        even, odd = parts(start, 2 * LAG_FINE)
        after_zero = (even - odd) * scaling
        before_zero = (even + odd) * scaling
        out[:, :, half + start : half + start + 2 * LAG_FINE] = after_zero.reshape(count, channels, 2 * LAG_FINE)
        for tile in (1, 0):
            turned_round = jnp.take_along_axis(
                before_zero[:, tile * LAG_FINE : (tile + 1) * LAG_FINE], mirror, axis=1, mode="promise_in_bounds"
            )
            at = half - start - (tile + 1) * LAG_FINE
            out[:, :, at : at + LAG_FINE] = jnp.where(lane == 0, above, turned_round).reshape(count, channels, LAG_FINE)
            above = turned_round


def lagged(stacked, table, scaling):
    channels, both, _ = stacked[0].shape
    count = both // 2
    block = 8
    return pl.pallas_call(
        functools.partial(lag_kernel, scaling),
        grid=(channels // block,),
        in_specs=[pl.BlockSpec((block, both, s.shape[2]), lambda i: (i, 0, 0)) for s in stacked]
        + [pl.BlockSpec(table.shape, lambda i: (0, 0))],
        out_specs=pl.BlockSpec((count, block, LAGS), lambda i: (0, i, 0)),
        out_shape=jax.ShapeDtypeStruct((count, channels, LAGS), jnp.float32),
        scratch_shapes=[pltpu.VMEM((count * block, 2 * F), jnp.bfloat16)],
        compiler_params=pltpu.CompilerParams(vmem_limit_bytes=48 * MIB),
        cost_estimate=pl.CostEstimate(flops=2 * count * channels * F * LAGS, bytes_accessed=count * channels * LAGS * 4, transcendentals=0),
    )(*stacked, table)


def table_kernel(angles, out):
    fine_cos, fine_sin = angles[:, :LAG_FINE], angles[:, LAG_FINE : 2 * LAG_FINE]
    tiles = out.shape[1] // LAG_FINE
    for tile in range(tiles):
        big_cos = angles[:, 2 * LAG_FINE + tile : 2 * LAG_FINE + tile + 1]
        big_sin = angles[:, 2 * LAG_FINE + tiles + tile : 2 * LAG_FINE + tiles + tile + 1]
        cols = slice(tile * LAG_FINE, (tile + 1) * LAG_FINE)
        out[:F, cols] = (big_cos * fine_cos - big_sin * fine_sin).astype(jnp.bfloat16)
        out[F:, cols] = (big_sin * fine_cos + big_cos * fine_sin).astype(jnp.bfloat16)


def lag_table():
    tiles = LAGS // 2 // LAG_FINE + 1
    coarse = unit_angles(np.arange(tiles) * LAG_FINE, 1)
    angles = np.concatenate(unit_angles(np.arange(LAG_FINE), 1) + coarse, axis=1)
    return pl.pallas_call(
        table_kernel,
        out_shape=jax.ShapeDtypeStruct((2 * F, tiles * LAG_FINE), jnp.bfloat16),
        compiler_params=pltpu.CompilerParams(vmem_limit_bytes=40 * MIB),
        cost_estimate=pl.CostEstimate(flops=8 * F * tiles * LAG_FINE, bytes_accessed=4 * MIB, transcendentals=0),
    )(angles)


def make_band(filter_taps, channel_count):
    kernel = jnp.concatenate(
        [
            -filter_taps[:HALO].astype(jnp.float32),
            jnp.ones((1,), jnp.float32),
            -filter_taps[HALO:].astype(jnp.float32),
        ]
    )
    row_ids = jnp.arange(channel_count, dtype=jnp.int32)[:, None]
    columns = jnp.arange(channel_count + 2 * HALO, dtype=jnp.int32)[None, :]
    offset = columns - row_ids
    choose = offset[:, :, None] == jnp.arange(2 * HALO + 1, dtype=jnp.int32)[None, None, :]
    return jnp.sum(jnp.where(choose, kernel[None, None, :], 0.0), axis=2).astype(jnp.bfloat16)


def pick_kernel(held, across, selector, here, near, far):
    count = here.shape[1]
    for window in range(held.shape[1]):
        rows = [blocks[i, window] for blocks in (held, across) for i in range(blocks.shape[0])]
        picked = jnp.dot(selector[...], jnp.concatenate(rows, axis=0), preferred_element_type=jnp.float32)
        picked = picked.astype(jnp.bfloat16)
        here[window] = picked[:count]
        near[window] = picked[count : 2 * count]
        for at in range(far.shape[0]):
            far[at, window] = picked[(2 + at) * count : (3 + at) * count]


def pick(held, across, selector, groups):
    _, windows, _, both = held.shape
    count = selector.shape[0] // groups
    one = (windows, count, both)
    return pl.pallas_call(
        pick_kernel,
        out_shape=[jax.ShapeDtypeStruct(shape, jnp.bfloat16) for shape in (one, one, (groups - 2, *one))],
        compiler_params=pltpu.CompilerParams(vmem_limit_bytes=40 * MIB),
        cost_estimate=pl.CostEstimate(
            flops=2 * windows * selector.size * both, bytes_accessed=2 * windows * both * sum(selector.shape), transcendentals=0
        ),
    )(held, across, selector)


def swapped(value, axis, step):
    return lax.ppermute(value, axis, [(i, i ^ step) for i in range(lax.axis_size(axis))])


def after(value, earlier):
    return lax.optimization_barrier((value, earlier))[0]


def per_device(traces, filter_taps, good_channels, source_index):
    window_count, channel_count, _ = traces.shape
    good = good_channels[None, :]
    spec, head, tail = transform(traces, good)
    blocks = lax.axis_size("chan")
    groups = lax.axis_size("win")
    left = lax.ppermute(tail, "chan", [(i, i + 1) for i in range(blocks - 1)])
    right = lax.ppermute(head, "chan", [(i + 1, i) for i in range(blocks - 1)])
    table = lag_table()
    left = after(left, table)
    full, *parts = whiten(spec, left, right, make_band(filter_taps, channel_count), good)

    order = [0]
    step = blocks // 2
    while step:
        order += [place ^ step for place in order]
        step //= 2
    order = jnp.asarray(order, jnp.int32) ^ lax.axis_index("chan")
    own_ids = jnp.arange(channel_count, dtype=jnp.int32)
    channel_ids = (order[:, None] * channel_count + own_ids[None, :]).reshape(-1)
    by_group = source_index.reshape(groups, -1)
    here = lax.axis_index("win")
    wanted = jnp.concatenate([lax.dynamic_slice_in_dim(by_group, here ^ step, 1) for step in range(groups)], axis=0)
    selector = (wanted.reshape(-1)[:, None] == channel_ids[None, :]).astype(jnp.bfloat16)

    own_far = swapped(full, "win", 2)
    own_near = swapped(jnp.stack([full, own_far]), "win", 1)
    picked, stacked = [], []
    first_held = None

    def finish(at):
        here, near, far = picked[at]
        earlier = stacked[-1:] + [later[0] for later in picked[at + 1 : at + 2]]
        if earlier:
            far = after(far, earlier)
        near = swapped(jnp.stack([near, far[1]]), "win", 1)
        stacked.append(cross([here, near, far], [full, own_near, own_far], CHUNKS[at][0]))

    for at, part in enumerate(parts):
        if at:
            part = after(part, first_held if at != 2 else [first_held, own_far])
        held = part[None]
        step = blocks // 2
        while step > 1:
            held = jnp.concatenate([held, swapped(held, "chan", step)], axis=0)
            first_held = held if step == blocks // 2 else first_held
            step //= 2
        if at:
            held = after(held, picked[-1][0])
        across = swapped(held, "chan", 1)
        if at > 1:
            finish(at - 2)
            across = after(across, stacked[-1])
        here, near, far = pick(held, across, selector, groups)
        picked.append((here, near, swapped(far, "win", 2)))
    for at in range(len(stacked), len(parts)):
        finish(at)
    return lagged(stacked, table, 1.0 / math.sqrt(F * window_count * groups))


def solution(mesh):
    placed = (P("win", "chan", None), P(), P("chan"), P())
    return jax.shard_map(
        per_device, mesh=mesh, in_specs=placed, out_specs=P("win", "chan", None), check_vma=False
    )
```

```python
import functools
import math

import jax
import jax.numpy as jnp
import numpy as np
from jax import lax
from jax.experimental import pallas as pl
from jax.experimental.pallas import tpu as pltpu
from jax.sharding import PartitionSpec as P

L = 7680
F = 512
LAGS = 2048
HALO = 16
SMOOTH = 64
K0 = 31
QUARTER = L // 4
STEP = 640
FINE = 32
CHUNKS = ((0, 128), (128, 256), (384, 128))
GROUP = 16
LAG_FINE = 128
LAG_ROWS = 8
NT = (((1,), (1,)), ((), ()))
MIB = 1024 * 1024


def unit_angles(positions, axis):
    bins = K0 + np.arange(F, dtype=np.int64)
    phase = np.mod(np.expand_dims(positions, 1 - axis) * np.expand_dims(bins, axis), L)
    angles = phase * (2.0 * math.pi / L)
    return np.cos(angles).astype(np.float32), np.sin(angles).astype(np.float32)


def keep_column(good):
    count = good.shape[1]
    rows = lax.broadcasted_iota(jnp.int32, (count, count), 0)
    cols = lax.broadcasted_iota(jnp.int32, (count, count), 1)
    return jnp.sum(jnp.where(rows == cols, good[...].astype(jnp.float32), 0.0), axis=1, keepdims=True)


def transform_kernel(x0, x1, x2, x3, angles, good, spec, head, tail, table, total):
    step = pl.program_id(0)
    rows = x0.shape[0]
    coarse = QUARTER // FINE

    def fill(of_step):
        fine_cos = angles[2 * coarse : 2 * coarse + FINE, :]
        fine_sin = angles[2 * coarse + FINE :, :]
        for part in range(STEP // FINE):
            big_cos = angles[pl.ds(of_step * (STEP // FINE) + part, 1), :]
            big_sin = angles[pl.ds(coarse + of_step * (STEP // FINE) + part, 1), :]
            at = pl.ds(part * FINE, FINE)
            table[of_step % 2, at, :F] = (big_cos * fine_cos - big_sin * fine_sin).astype(jnp.bfloat16)
            table[of_step % 2, at, F:] = (-(big_sin * fine_cos + big_cos * fine_sin)).astype(jnp.bfloat16)

    @pl.when(step == 0)
    def _():
        total[...] = jnp.zeros_like(total)
        fill(step)

    for quarter, x in enumerate((x0, x1, x2, x3)):
        at = pl.ds(quarter * rows, rows)
        total[at, :] += jnp.dot(x[...], table[step % 2], preferred_element_type=jnp.float32)
    fill(jnp.minimum(step + 1, pl.num_programs(0) - 1))

    @pl.when(step == pl.num_programs(0) - 1)
    def _():
        turn = (K0 + lax.broadcasted_iota(jnp.int32, (1, F), 1)) % 4
        even = turn % 2 == 0
        sign = jnp.where(turn < 2, 1.0, -1.0)
        channels = good.shape[1]
        keep = keep_column(good)
        for window in range(rows // channels):
            re = [total[pl.ds(q * rows + window * channels, channels), :F] for q in range(4)]
            im = [total[pl.ds(q * rows + window * channels, channels), F:] for q in range(4)]
            real = jnp.where(even, re[0] + re[2] + sign * (re[1] + re[3]), re[0] - re[2] + sign * (im[1] - im[3])) * keep
            imag = jnp.where(even, im[0] + im[2] + sign * (im[1] + im[3]), im[0] - im[2] - sign * (re[1] - re[3])) * keep
            spec[window, :, :F] = real
            spec[window, :, F:] = imag
            head[window, :, :F] = real[:HALO].astype(jnp.bfloat16)
            head[window, :, F:] = imag[:HALO].astype(jnp.bfloat16)
            tail[window, :, :F] = real[channels - HALO :].astype(jnp.bfloat16)
            tail[window, :, F:] = imag[channels - HALO :].astype(jnp.bfloat16)


def transform(traces, good):
    windows, channels, length = traces.shape
    rows = windows * channels
    steps = QUARTER // STEP
    flat = traces.reshape(rows, length)
    coarse = unit_angles(np.arange(QUARTER // FINE) * FINE, 0)
    angles = np.concatenate(coarse + unit_angles(np.arange(FINE), 0), axis=0)
    whole = lambda *shape: pl.BlockSpec(shape, lambda k: (0,) * len(shape))
    return pl.pallas_call(
        transform_kernel,
        grid=(steps,),
        in_specs=[pl.BlockSpec((rows, STEP), functools.partial(lambda q, k: (0, q * steps + k), q)) for q in range(4)]
        + [whole(*angles.shape), whole(1, channels)],
        out_specs=[whole(windows, channels, 2 * F), whole(windows, HALO, 2 * F), whole(windows, HALO, 2 * F)],
        out_shape=[
            jax.ShapeDtypeStruct((windows, channels, 2 * F), jnp.float32),
            jax.ShapeDtypeStruct((windows, HALO, 2 * F), jnp.bfloat16),
            jax.ShapeDtypeStruct((windows, HALO, 2 * F), jnp.bfloat16),
        ],
        scratch_shapes=[pltpu.VMEM((2, STEP, 2 * F), jnp.bfloat16), pltpu.VMEM((4 * rows, 2 * F), jnp.float32)],
        compiler_params=pltpu.CompilerParams(vmem_limit_bytes=60 * MIB),
        cost_estimate=pl.CostEstimate(flops=2 * rows * length * 2 * F, bytes_accessed=rows * length * 2, transcendentals=0),
    )(flat, flat, flat, flat, angles, good)


def pieces(value):
    high = value.astype(jnp.bfloat16)
    rest = value - high.astype(jnp.float32)
    middle = rest.astype(jnp.bfloat16)
    return high, middle, (rest - middle.astype(jnp.float32)).astype(jnp.bfloat16)


def whiten_kernel(spec, left, right, band, good, *outs):
    windows, channels = spec.shape[:2]
    filtered = []
    keep = keep_column(good)
    for window in range(windows):
        stack = jnp.concatenate([left[window], *pieces(spec[window]), right[window]], axis=0)
        own = band[:, HALO : HALO + channels]
        taps = jnp.concatenate([band[:, :HALO], own, own, own, band[:, HALO + channels :]], axis=1)
        filtered.append(jnp.dot(taps, stack, preferred_element_type=jnp.float32) * keep)
    spectrum = jnp.concatenate(filtered, axis=0)
    real, imag = spectrum[:, :F], spectrum[:, F:]
    magnitude = jnp.sqrt(real * real + imag * imag)
    bins = lax.broadcasted_iota(jnp.int32, (F, F), 0)
    others = lax.broadcasted_iota(jnp.int32, (F, F), 1)
    near = jnp.where(jnp.abs(bins - others) <= SMOOTH, 1.0, 0.0).astype(jnp.bfloat16)
    amplitude = sum(jnp.dot(piece, near, preferred_element_type=jnp.float32) for piece in pieces(magnitude))
    bin_row = lax.broadcasted_iota(jnp.int32, (1, F), 1)
    count = jnp.minimum(bin_row + SMOOTH, F - 1) - jnp.maximum(bin_row - SMOOTH, 0) + 1
    amplitude = amplitude * (1.0 / count.astype(jnp.float32))
    inverse = 1.0 / (amplitude + 1e-06)
    real = (real * inverse).astype(jnp.bfloat16)
    imag = (imag * inverse).astype(jnp.bfloat16)
    for out, (start, width) in zip(outs, ((0, F),) + CHUNKS):
        for window in range(windows):
            rows = slice(window * channels, (window + 1) * channels)
            out[window, :, :width] = real[rows, start : start + width]
            out[window, :, width:] = imag[rows, start : start + width]


def whiten(spec, left, right, band, good):
    windows, channels, _ = spec.shape
    return pl.pallas_call(
        whiten_kernel,
        out_shape=[
            jax.ShapeDtypeStruct((windows, channels, 2 * width), jnp.bfloat16) for width in (F, *(w for _, w in CHUNKS))
        ],
        compiler_params=pltpu.CompilerParams(vmem_limit_bytes=40 * MIB),
        cost_estimate=pl.CostEstimate(flops=2 * windows * channels * F * F * 3, bytes_accessed=5 * MIB // 2, transcendentals=windows * channels * F),
    )(spec, left, right, band, good)


def eye(size):
    rows = lax.broadcasted_iota(jnp.int32, (size, size), 0)
    cols = lax.broadcasted_iota(jnp.int32, (size, size), 1)
    return jnp.where(rows == cols, 1.0, 0.0).astype(jnp.bfloat16)


def turned(left_unit, rows):
    return lax.dot_general(left_unit, rows, NT, preferred_element_type=jnp.float32)


def swapper(outer, inner):
    size = outer * inner
    rows = lax.broadcasted_iota(jnp.int32, (size, size), 0)
    cols = lax.broadcasted_iota(jnp.int32, (size, size), 1)
    return jnp.where(cols == rows % outer * inner + rows // outer, 1.0, 0.0).astype(jnp.bfloat16)


def moved(swap, rows):
    return jnp.dot(swap, rows, preferred_element_type=jnp.float32).astype(jnp.bfloat16)


def own_kernel(here, near, far, out, by_window):
    own = [here, near.at[0], far, near.at[1]]
    each, channels, _ = here.shape
    windows, quads = each * len(own), channels // 4
    joined = GROUP // each
    swap = swapper(GROUP, GROUP)
    for start in range(0, windows, GROUP):
        for channel in range(0, channels, GROUP):
            block = [o[:, channel : channel + GROUP, :] for o in own[start // each : start // each + joined]]
            rows = moved(swap, jnp.concatenate(block, axis=0).reshape(GROUP * GROUP, 2 * F))
            by_window[channel : channel + GROUP, start : start + GROUP, :] = rows.reshape(GROUP, GROUP, 2 * F)
    unit = eye(F // 2)
    for quad in range(quads):
        for start in range(0, F, F // 2):
            rows = []
            for channel in range(quad, channels, quads):
                rows += [by_window[channel, :, side + start : side + start + F // 2] for side in (0, F)]
            out[quad, start : start + F // 2, :] = turned(unit, jnp.concatenate(rows, axis=0)).astype(jnp.bfloat16)


def turn_own(here, near, far):
    each, channels, _ = here.shape
    windows = each * 4
    return pl.pallas_call(
        own_kernel,
        out_shape=jax.ShapeDtypeStruct((channels // 4, F, 8 * windows), jnp.bfloat16),
        scratch_shapes=[pltpu.VMEM((channels, windows, 2 * F), jnp.bfloat16)],
        compiler_params=pltpu.CompilerParams(vmem_limit_bytes=40 * MIB),
        cost_estimate=pl.CostEstimate(flops=2 * 8192 * 65536, bytes_accessed=4 * MIB, transcendentals=0),
    )(here, near, far)


def cross_kernel(first_bin, here, near, far, by_channel, out, by_window, sums):
    sources = [here, near.at[0], far.at[0], near.at[1]]
    each, count, both = here.shape
    quads, _, wide = by_channel.shape
    channels, half = 4 * quads, wide // 4
    windows, width = half // 2, both // 2
    unit = eye(width)
    swap = swapper(GROUP, GROUP)
    swap_quads = swapper(quads, GROUP)
    for window in range(0, windows, 2):
        rows = []
        for one in range(window, window + 2):
            source = sources[one // each]
            rows += [source[one % each, :, :width], source[one % each, :, width:]]
        both_turned = turned(unit, jnp.concatenate(rows, axis=0)).astype(jnp.bfloat16)
        by_window[window] = both_turned[:, : 2 * count]
        by_window[window + 1] = both_turned[:, 2 * count :]
    first = lax.broadcasted_iota(jnp.int32, (1, 2 * half), 1) < half
    sign = jnp.where(lax.broadcasted_iota(jnp.int32, (1, 2 * count), 1) < count, 1.0, -1.0)
    empty = jnp.zeros((2 * windows, 2 * count), jnp.bfloat16)

    def one_group(group, carry):
        bins = pl.ds(pl.multiple_of(group * GROUP, GROUP), GROUP)
        rows = [
            by_window[start : start + GROUP, bins, :].reshape(GROUP * GROUP, 2 * count)
            for start in range(0, windows, GROUP)
        ]
        rights = jnp.dot(swap, jnp.concatenate(rows, axis=1), preferred_element_type=jnp.float32)
        own_bins = pl.ds(pl.multiple_of(first_bin + group * GROUP, GROUP), GROUP)
        lefts = jnp.dot(
            swap_quads, by_channel[:, own_bins, :].reshape(quads * GROUP, 4 * half), preferred_element_type=jnp.float32
        )
        results = []
        for at in range(0, GROUP, 2):
            two = []
            for one in range(at, at + 2):
                here = rights[one * GROUP : (one + 1) * GROUP]
                src = jnp.concatenate(
                    [here[:, i * 2 * count : (i + 1) * 2 * count] for i in range(windows // GROUP)], axis=0
                )
                two.append(jnp.concatenate([src * sign, pltpu.roll(src, count, axis=1)], axis=0).astype(jnp.bfloat16))
            right = jnp.concatenate(
                [jnp.concatenate([two[0], empty], axis=1), jnp.concatenate([empty, two[1]], axis=1)], axis=0
            )
            left = []
            for tile in range(0, 4 * half, 2 * half):
                one, other = (lefts[i * quads : (i + 1) * quads, tile : tile + 2 * half] for i in (at, at + 1))
                left.append(jnp.where(first, one, pltpu.roll(other, half, axis=1)))
                left.append(jnp.where(first, pltpu.roll(one, half, axis=1), other))
            left = jnp.concatenate(left, axis=0).astype(jnp.bfloat16)
            result = jnp.dot(left, right, preferred_element_type=jnp.float32).astype(jnp.bfloat16)
            results += [result[:, : 2 * count], result[:, 2 * count :]]
        halves = [
            jnp.concatenate([r[start : start + GROUP] for r in results], axis=0) for start in range(0, channels, GROUP)
        ]
        done = moved(swap, jnp.concatenate(halves, axis=1))
        for channel in range(channels):
            row, side = channel % GROUP, channel // GROUP
            sums[channel, bins, :] = done[
                row * GROUP : (row + 1) * GROUP, side * 2 * count : (side + 1) * 2 * count
            ]
        return carry

    lax.fori_loop(0, width // GROUP, one_group, 0, unroll=4)
    unit = eye(2 * count)
    part = 256 // LAG_ROWS
    swap = swapper(LAG_ROWS, part)
    for group in range(channels // LAG_ROWS):
        by_bin = []
        for channel in range(group * LAG_ROWS, (group + 1) * LAG_ROWS, 2):
            rows = jnp.concatenate([sums[channel], sums[channel + 1]], axis=0)
            both_turned = turned(unit, rows).astype(jnp.bfloat16)
            by_bin += [both_turned[:, :width], both_turned[:, width:]]
        for start in range(0, count, part):
            rows = jnp.concatenate(
                [
                    jnp.concatenate([b[start : start + part], b[count + start : count + start + part]], axis=1)
                    for b in by_bin
                ],
                axis=0,
            )
            rows = moved(swap, rows)
            at = slice(start * LAG_ROWS, (start + part) * LAG_ROWS)
            out[group, 0, at, :] = rows[:, :width]
            out[group, 1, at, :] = rows[:, width:]


def cross(here, near, far, by_channel, first_bin):
    each, count, both = here.shape
    quads, _, wide = by_channel.shape
    channels, windows, width = 4 * quads, wide // 8, both // 2
    return pl.pallas_call(
        functools.partial(cross_kernel, first_bin),
        out_shape=jax.ShapeDtypeStruct((channels // LAG_ROWS, 2, count * LAG_ROWS, width), jnp.bfloat16),
        scratch_shapes=[
            pltpu.VMEM((windows, width, 2 * count), jnp.bfloat16),
            pltpu.VMEM((channels, width, 2 * count), jnp.bfloat16),
        ],
        compiler_params=pltpu.CompilerParams(vmem_limit_bytes=40 * MIB),
        cost_estimate=pl.CostEstimate(flops=2 * width * 36 * 65536, bytes_accessed=4 * MIB, transcendentals=0),
    )(here, near, far, by_channel)


def lag_kernel(scaling, *refs):
    *stacked, table, out = refs
    count, channels, _ = out.shape
    real, imag = (jnp.concatenate([chunk[0, side] for chunk in stacked], axis=1) for side in range(2))
    size = count * channels
    lane = lax.broadcasted_iota(jnp.int32, (size, LAG_FINE), 1)
    mirror = (LAG_FINE - lane) % LAG_FINE

    def parts(start, width):
        even = jnp.dot(real, table[:F, start : start + width], preferred_element_type=jnp.float32)
        odd = jnp.dot(imag, table[F:, start : start + width], preferred_element_type=jnp.float32)
        return even, odd

    half = LAGS // 2
    even, odd = parts(half, LAG_FINE)
    above = (even + odd) * scaling
    for start in range(half - 2 * LAG_FINE, -1, -2 * LAG_FINE):
        even, odd = parts(start, 2 * LAG_FINE)
        after_zero = (even - odd) * scaling
        before_zero = (even + odd) * scaling
        out[:, :, half + start : half + start + 2 * LAG_FINE] = after_zero.reshape(count, channels, 2 * LAG_FINE)
        for tile in (1, 0):
            turned_round = jnp.take_along_axis(
                before_zero[:, tile * LAG_FINE : (tile + 1) * LAG_FINE], mirror, axis=1, mode="promise_in_bounds"
            )
            at = half - start - (tile + 1) * LAG_FINE
            out[:, :, at : at + LAG_FINE] = jnp.where(lane == 0, above, turned_round).reshape(count, channels, LAG_FINE)
            above = turned_round


def lagged(stacked, table, scaling):
    groups, _, size, _ = stacked[0].shape
    count = size // LAG_ROWS
    return pl.pallas_call(
        functools.partial(lag_kernel, scaling),
        grid=(groups,),
        in_specs=[pl.BlockSpec((1, 2, size, s.shape[3]), lambda i: (i, 0, 0, 0)) for s in stacked]
        + [pl.BlockSpec(table.shape, lambda i: (0, 0))],
        out_specs=pl.BlockSpec((count, LAG_ROWS, LAGS), lambda i: (0, i, 0)),
        out_shape=jax.ShapeDtypeStruct((count, groups * LAG_ROWS, LAGS), jnp.float32),
        compiler_params=pltpu.CompilerParams(vmem_limit_bytes=48 * MIB),
        cost_estimate=pl.CostEstimate(
            flops=2 * groups * size * F * LAGS, bytes_accessed=groups * size * LAGS * 4, transcendentals=0
        ),
    )(*stacked, table)


def table_kernel(angles, out):
    fine_cos, fine_sin = angles[:, :LAG_FINE], angles[:, LAG_FINE : 2 * LAG_FINE]
    tiles = out.shape[1] // LAG_FINE
    for tile in range(tiles):
        big_cos = angles[:, 2 * LAG_FINE + tile : 2 * LAG_FINE + tile + 1]
        big_sin = angles[:, 2 * LAG_FINE + tiles + tile : 2 * LAG_FINE + tiles + tile + 1]
        cols = slice(tile * LAG_FINE, (tile + 1) * LAG_FINE)
        out[:F, cols] = (big_cos * fine_cos - big_sin * fine_sin).astype(jnp.bfloat16)
        out[F:, cols] = (big_sin * fine_cos + big_cos * fine_sin).astype(jnp.bfloat16)


def lag_table():
    tiles = LAGS // 2 // LAG_FINE + 1
    coarse = unit_angles(np.arange(tiles) * LAG_FINE, 1)
    angles = np.concatenate(unit_angles(np.arange(LAG_FINE), 1) + coarse, axis=1)
    return pl.pallas_call(
        table_kernel,
        out_shape=jax.ShapeDtypeStruct((2 * F, tiles * LAG_FINE), jnp.bfloat16),
        compiler_params=pltpu.CompilerParams(vmem_limit_bytes=40 * MIB),
        cost_estimate=pl.CostEstimate(flops=8 * F * tiles * LAG_FINE, bytes_accessed=4 * MIB, transcendentals=0),
    )(angles)


def make_band(filter_taps, channel_count):
    kernel = jnp.concatenate(
        [
            -filter_taps[:HALO].astype(jnp.float32),
            jnp.ones((1,), jnp.float32),
            -filter_taps[HALO:].astype(jnp.float32),
        ]
    )
    row_ids = jnp.arange(channel_count, dtype=jnp.int32)[:, None]
    columns = jnp.arange(channel_count + 2 * HALO, dtype=jnp.int32)[None, :]
    offset = columns - row_ids
    choose = offset[:, :, None] == jnp.arange(2 * HALO + 1, dtype=jnp.int32)[None, None, :]
    return jnp.sum(jnp.where(choose, kernel[None, None, :], 0.0), axis=2).astype(jnp.bfloat16)


def pick_kernel(held, across, selector, here, near, far):
    count = here.shape[1]
    for window in range(held.shape[1]):
        rows = [blocks[i, window] for blocks in (held, across) for i in range(blocks.shape[0])]
        picked = jnp.dot(selector[...], jnp.concatenate(rows, axis=0), preferred_element_type=jnp.float32)
        picked = picked.astype(jnp.bfloat16)
        here[window] = picked[:count]
        near[window] = picked[count : 2 * count]
        for at in range(far.shape[0]):
            far[at, window] = picked[(2 + at) * count : (3 + at) * count]


def pick(held, across, selector, groups):
    _, windows, _, both = held.shape
    count = selector.shape[0] // groups
    one = (windows, count, both)
    return pl.pallas_call(
        pick_kernel,
        out_shape=[jax.ShapeDtypeStruct(shape, jnp.bfloat16) for shape in (one, one, (groups - 2, *one))],
        compiler_params=pltpu.CompilerParams(vmem_limit_bytes=40 * MIB),
        cost_estimate=pl.CostEstimate(
            flops=2 * windows * selector.size * both, bytes_accessed=2 * windows * both * sum(selector.shape), transcendentals=0
        ),
    )(held, across, selector)


def swapped(value, axis, step):
    return lax.ppermute(value, axis, [(i, i ^ step) for i in range(lax.axis_size(axis))])


def after(value, earlier):
    return lax.optimization_barrier((value, earlier))[0]


def per_device(traces, filter_taps, good_channels, source_index):
    window_count, channel_count, _ = traces.shape
    good = good_channels[None, :]
    spec, head, tail = transform(traces, good)
    blocks = lax.axis_size("chan")
    groups = lax.axis_size("win")
    left = lax.ppermute(tail, "chan", [(i, i + 1) for i in range(blocks - 1)])
    right = lax.ppermute(head, "chan", [(i + 1, i) for i in range(blocks - 1)])
    table = lag_table()
    left = after(left, table)
    full, *parts = whiten(spec, left, right, make_band(filter_taps, channel_count), good)

    order = [0]
    step = blocks // 2
    while step:
        order += [place ^ step for place in order]
        step //= 2
    order = jnp.asarray(order, jnp.int32) ^ lax.axis_index("chan")
    own_ids = jnp.arange(channel_count, dtype=jnp.int32)
    channel_ids = (order[:, None] * channel_count + own_ids[None, :]).reshape(-1)
    by_group = source_index.reshape(groups, -1)
    here = lax.axis_index("win")
    wanted = jnp.concatenate([lax.dynamic_slice_in_dim(by_group, here ^ step, 1) for step in range(groups)], axis=0)
    selector = (wanted.reshape(-1)[:, None] == channel_ids[None, :]).astype(jnp.bfloat16)

    own_far = swapped(full, "win", 2)
    own_near = swapped(jnp.stack([full, own_far]), "win", 1)
    by_channel = turn_own(full, own_near, own_far)
    picked, stacked = [], []
    first_held = None

    def finish(at):
        here, near, far = picked[at]
        earlier = stacked[-1:] + [later[0] for later in picked[at + 1 : at + 2]]
        if earlier:
            far = after(far, earlier)
        near = swapped(jnp.stack([near, far[1]]), "win", 1)
        stacked.append(cross(here, near, far, by_channel, CHUNKS[at][0]))

    for at, part in enumerate(parts):
        if at:
            part = after(part, [first_held, own_far])
        held = part[None]
        step = blocks // 2
        while step > 1:
            held = jnp.concatenate([held, swapped(held, "chan", step)], axis=0)
            first_held = held if step == blocks // 2 else first_held
            step //= 2
        if at:
            held = after(held, picked[-1][0])
        across = swapped(held, "chan", 1)
        if at > 1:
            finish(at - 2)
            across = after(across, stacked[-1])
        here, near, far = pick(held, across, selector, groups)
        picked.append((here, near, swapped(far, "win", 2)))
    for at in range(len(stacked), len(parts)):
        finish(at)
    return lagged(stacked, table, 1.0 / math.sqrt(F * window_count * groups))


def solution(mesh):
    placed = (P("win", "chan", None), P(), P("chan"), P())
    return jax.shard_map(
        per_device, mesh=mesh, in_specs=placed, out_specs=P("win", "chan", None), check_vma=False
    )
```

```python
import functools
import math

import jax
import jax.numpy as jnp
import numpy as np
from jax import lax
from jax.experimental import pallas as pl
from jax.experimental.pallas import tpu as pltpu
from jax.sharding import PartitionSpec as P

L = 7680
F = 512
LAGS = 2048
HALO = 16
SMOOTH = 64
K0 = 31
QUARTER = L // 4
STEP = 640
FINE = 32
CHUNKS = tuple((start, 128) for start in range(0, F, 128))
TOGETHER = 2
GROUP = 16
LAG_FINE = 128
LAG_ROWS = 8
NT = (((1,), (1,)), ((), ()))
MIB = 1024 * 1024


def unit_angles(positions, axis):
    bins = K0 + np.arange(F, dtype=np.int64)
    phase = np.mod(np.expand_dims(positions, 1 - axis) * np.expand_dims(bins, axis), L)
    angles = phase * (2.0 * math.pi / L)
    return np.cos(angles).astype(np.float32), np.sin(angles).astype(np.float32)


def keep_column(good):
    count = good.shape[1]
    rows = lax.broadcasted_iota(jnp.int32, (count, count), 0)
    cols = lax.broadcasted_iota(jnp.int32, (count, count), 1)
    return jnp.sum(jnp.where(rows == cols, good[...].astype(jnp.float32), 0.0), axis=1, keepdims=True)


def transform_kernel(x0, x1, x2, x3, angles, good, spec, head, tail, table, total):
    step = pl.program_id(0)
    rows = x0.shape[0]
    coarse = QUARTER // FINE

    def fill(of_step):
        fine_cos = angles[2 * coarse : 2 * coarse + FINE, :]
        fine_sin = angles[2 * coarse + FINE :, :]
        for part in range(STEP // FINE):
            big_cos = angles[pl.ds(of_step * (STEP // FINE) + part, 1), :]
            big_sin = angles[pl.ds(coarse + of_step * (STEP // FINE) + part, 1), :]
            at = pl.ds(part * FINE, FINE)
            table[of_step % 2, at, :F] = (big_cos * fine_cos - big_sin * fine_sin).astype(jnp.bfloat16)
            table[of_step % 2, at, F:] = (-(big_sin * fine_cos + big_cos * fine_sin)).astype(jnp.bfloat16)

    @pl.when(step == 0)
    def _():
        total[...] = jnp.zeros_like(total)
        fill(step)

    for quarter, x in enumerate((x0, x1, x2, x3)):
        at = pl.ds(quarter * rows, rows)
        total[at, :] += jnp.dot(x[...], table[step % 2], preferred_element_type=jnp.float32)
    fill(jnp.minimum(step + 1, pl.num_programs(0) - 1))

    @pl.when(step == pl.num_programs(0) - 1)
    def _():
        turn = (K0 + lax.broadcasted_iota(jnp.int32, (1, F), 1)) % 4
        even = turn % 2 == 0
        sign = jnp.where(turn < 2, 1.0, -1.0)
        channels = good.shape[1]
        keep = keep_column(good)
        for window in range(rows // channels):
            re = [total[pl.ds(q * rows + window * channels, channels), :F] for q in range(4)]
            im = [total[pl.ds(q * rows + window * channels, channels), F:] for q in range(4)]
            real = jnp.where(even, re[0] + re[2] + sign * (re[1] + re[3]), re[0] - re[2] + sign * (im[1] - im[3])) * keep
            imag = jnp.where(even, im[0] + im[2] + sign * (im[1] + im[3]), im[0] - im[2] - sign * (re[1] - re[3])) * keep
            spec[window, :, :F] = real
            spec[window, :, F:] = imag
            head[window, :, :F] = real[:HALO].astype(jnp.bfloat16)
            head[window, :, F:] = imag[:HALO].astype(jnp.bfloat16)
            tail[window, :, :F] = real[channels - HALO :].astype(jnp.bfloat16)
            tail[window, :, F:] = imag[channels - HALO :].astype(jnp.bfloat16)


def transform(traces, good):
    windows, channels, length = traces.shape
    rows = windows * channels
    steps = QUARTER // STEP
    flat = traces.reshape(rows, length)
    coarse = unit_angles(np.arange(QUARTER // FINE) * FINE, 0)
    angles = np.concatenate(coarse + unit_angles(np.arange(FINE), 0), axis=0)
    whole = lambda *shape: pl.BlockSpec(shape, lambda k: (0,) * len(shape))
    return pl.pallas_call(
        transform_kernel,
        grid=(steps,),
        in_specs=[pl.BlockSpec((rows, STEP), functools.partial(lambda q, k: (0, q * steps + k), q)) for q in range(4)]
        + [whole(*angles.shape), whole(1, channels)],
        out_specs=[whole(windows, channels, 2 * F), whole(windows, HALO, 2 * F), whole(windows, HALO, 2 * F)],
        out_shape=[
            jax.ShapeDtypeStruct((windows, channels, 2 * F), jnp.float32),
            jax.ShapeDtypeStruct((windows, HALO, 2 * F), jnp.bfloat16),
            jax.ShapeDtypeStruct((windows, HALO, 2 * F), jnp.bfloat16),
        ],
        scratch_shapes=[pltpu.VMEM((2, STEP, 2 * F), jnp.bfloat16), pltpu.VMEM((4 * rows, 2 * F), jnp.float32)],
        compiler_params=pltpu.CompilerParams(vmem_limit_bytes=60 * MIB),
        cost_estimate=pl.CostEstimate(flops=2 * rows * length * 2 * F, bytes_accessed=rows * length * 2, transcendentals=0),
    )(flat, flat, flat, flat, angles, good)


def pieces(value):
    high = value.astype(jnp.bfloat16)
    rest = value - high.astype(jnp.float32)
    middle = rest.astype(jnp.bfloat16)
    return high, middle, (rest - middle.astype(jnp.float32)).astype(jnp.bfloat16)


def whiten_kernel(spec, left, right, band, good, *outs):
    windows, channels = spec.shape[:2]
    filtered = []
    keep = keep_column(good)
    for window in range(windows):
        stack = jnp.concatenate([left[window], *pieces(spec[window]), right[window]], axis=0)
        own = band[:, HALO : HALO + channels]
        taps = jnp.concatenate([band[:, :HALO], own, own, own, band[:, HALO + channels :]], axis=1)
        filtered.append(jnp.dot(taps, stack, preferred_element_type=jnp.float32) * keep)
    spectrum = jnp.concatenate(filtered, axis=0)
    real, imag = spectrum[:, :F], spectrum[:, F:]
    magnitude = jnp.sqrt(real * real + imag * imag)
    bins = lax.broadcasted_iota(jnp.int32, (F, F), 0)
    others = lax.broadcasted_iota(jnp.int32, (F, F), 1)
    near = jnp.where(jnp.abs(bins - others) <= SMOOTH, 1.0, 0.0).astype(jnp.bfloat16)
    amplitude = sum(jnp.dot(piece, near, preferred_element_type=jnp.float32) for piece in pieces(magnitude))
    bin_row = lax.broadcasted_iota(jnp.int32, (1, F), 1)
    count = jnp.minimum(bin_row + SMOOTH, F - 1) - jnp.maximum(bin_row - SMOOTH, 0) + 1
    amplitude = amplitude * (1.0 / count.astype(jnp.float32))
    inverse = 1.0 / (amplitude + 1e-06)
    real = (real * inverse).astype(jnp.bfloat16)
    imag = (imag * inverse).astype(jnp.bfloat16)
    full, *parts = outs
    for window in range(windows):
        rows = slice(window * channels, (window + 1) * channels)
        full[window, :, :F] = real[rows]
        full[window, :, F:] = imag[rows]
        for at, (start, width) in enumerate(CHUNKS):
            part = parts[at // TOGETHER]
            part[at % TOGETHER, 0, window, :, :width] = real[rows, start : start + width]
            part[at % TOGETHER, 0, window, :, width:] = imag[rows, start : start + width]


def whiten(spec, left, right, band, good):
    windows, channels, _ = spec.shape
    return pl.pallas_call(
        whiten_kernel,
        out_shape=[
            jax.ShapeDtypeStruct(shape, jnp.bfloat16)
            for shape in [(windows, channels, 2 * F)]
            + [(TOGETHER, 1, windows, channels, 2 * CHUNKS[0][1])] * (len(CHUNKS) // TOGETHER)
        ],
        compiler_params=pltpu.CompilerParams(vmem_limit_bytes=40 * MIB),
        cost_estimate=pl.CostEstimate(flops=2 * windows * channels * F * F * 3, bytes_accessed=5 * MIB // 2, transcendentals=windows * channels * F),
    )(spec, left, right, band, good)


def eye(size):
    rows = lax.broadcasted_iota(jnp.int32, (size, size), 0)
    cols = lax.broadcasted_iota(jnp.int32, (size, size), 1)
    return jnp.where(rows == cols, 1.0, 0.0).astype(jnp.bfloat16)


def turned(left_unit, rows):
    return lax.dot_general(left_unit, rows, NT, preferred_element_type=jnp.float32)


def swapper(outer, inner):
    size = outer * inner
    rows = lax.broadcasted_iota(jnp.int32, (size, size), 0)
    cols = lax.broadcasted_iota(jnp.int32, (size, size), 1)
    return jnp.where(cols == rows % outer * inner + rows // outer, 1.0, 0.0).astype(jnp.bfloat16)


def moved(swap, rows):
    return jnp.dot(swap, rows, preferred_element_type=jnp.float32).astype(jnp.bfloat16)


def own_kernel(here, near, far, out, by_window):
    own = [here, near.at[0], far, near.at[1]]
    each, channels, _ = here.shape
    windows, quads = each * len(own), channels // 4
    joined = GROUP // each
    swap = swapper(GROUP, GROUP)
    for start in range(0, windows, GROUP):
        for channel in range(0, channels, GROUP):
            block = [o[:, channel : channel + GROUP, :] for o in own[start // each : start // each + joined]]
            rows = moved(swap, jnp.concatenate(block, axis=0).reshape(GROUP * GROUP, 2 * F))
            by_window[channel : channel + GROUP, start : start + GROUP, :] = rows.reshape(GROUP, GROUP, 2 * F)
    unit = eye(F // 2)
    for quad in range(quads):
        for start in range(0, F, F // 2):
            rows = []
            for channel in range(quad, channels, quads):
                rows += [by_window[channel, :, side + start : side + start + F // 2] for side in (0, F)]
            out[quad, start : start + F // 2, :] = turned(unit, jnp.concatenate(rows, axis=0)).astype(jnp.bfloat16)


def turn_own(here, near, far):
    each, channels, _ = here.shape
    windows = each * 4
    return pl.pallas_call(
        own_kernel,
        out_shape=jax.ShapeDtypeStruct((channels // 4, F, 8 * windows), jnp.bfloat16),
        scratch_shapes=[pltpu.VMEM((channels, windows, 2 * F), jnp.bfloat16)],
        compiler_params=pltpu.CompilerParams(vmem_limit_bytes=40 * MIB),
        cost_estimate=pl.CostEstimate(flops=2 * 8192 * 65536, bytes_accessed=4 * MIB, transcendentals=0),
    )(here, near, far)


def cross_kernel(here, near, far, by_channel, out, by_window, sums):
    sources = [here, near.at[0], far.at[0], near.at[1]]
    each, count, both = here.shape
    quads, _, wide = by_channel.shape
    channels, half = 4 * quads, wide // 4
    windows, width = half // 2, both // 2
    unit = eye(width)
    swap = swapper(GROUP, GROUP)
    swap_quads = swapper(quads, GROUP)
    for window in range(0, windows, 2):
        rows = []
        for one in range(window, window + 2):
            source = sources[one // each]
            rows += [source[one % each, :, :width], source[one % each, :, width:]]
        both_turned = turned(unit, jnp.concatenate(rows, axis=0)).astype(jnp.bfloat16)
        by_window[window] = both_turned[:, : 2 * count]
        by_window[window + 1] = both_turned[:, 2 * count :]
    first = lax.broadcasted_iota(jnp.int32, (1, 2 * half), 1) < half
    sign = jnp.where(lax.broadcasted_iota(jnp.int32, (1, 2 * count), 1) < count, 1.0, -1.0)
    empty = jnp.zeros((2 * windows, 2 * count), jnp.bfloat16)

    def one_group(group, carry):
        bins = pl.ds(pl.multiple_of(group * GROUP, GROUP), GROUP)
        rows = [
            by_window[start : start + GROUP, bins, :].reshape(GROUP * GROUP, 2 * count)
            for start in range(0, windows, GROUP)
        ]
        rights = jnp.dot(swap, jnp.concatenate(rows, axis=1), preferred_element_type=jnp.float32)
        lefts = jnp.dot(
            swap_quads, by_channel[:, bins, :].reshape(quads * GROUP, 4 * half), preferred_element_type=jnp.float32
        )
        results = []
        for at in range(0, GROUP, 2):
            two = []
            for one in range(at, at + 2):
                here = rights[one * GROUP : (one + 1) * GROUP]
                src = jnp.concatenate(
                    [here[:, i * 2 * count : (i + 1) * 2 * count] for i in range(windows // GROUP)], axis=0
                )
                two.append(jnp.concatenate([src * sign, pltpu.roll(src, count, axis=1)], axis=0).astype(jnp.bfloat16))
            right = jnp.concatenate(
                [jnp.concatenate([two[0], empty], axis=1), jnp.concatenate([empty, two[1]], axis=1)], axis=0
            )
            left = []
            for tile in range(0, 4 * half, 2 * half):
                one, other = (lefts[i * quads : (i + 1) * quads, tile : tile + 2 * half] for i in (at, at + 1))
                left.append(jnp.where(first, one, pltpu.roll(other, half, axis=1)))
                left.append(jnp.where(first, pltpu.roll(one, half, axis=1), other))
            left = jnp.concatenate(left, axis=0).astype(jnp.bfloat16)
            result = jnp.dot(left, right, preferred_element_type=jnp.float32).astype(jnp.bfloat16)
            results += [result[:, : 2 * count], result[:, 2 * count :]]
        halves = [
            jnp.concatenate([r[start : start + GROUP] for r in results], axis=0) for start in range(0, channels, GROUP)
        ]
        done = moved(swap, jnp.concatenate(halves, axis=1))
        for channel in range(channels):
            row, side = channel % GROUP, channel // GROUP
            sums[channel, bins, :] = done[
                row * GROUP : (row + 1) * GROUP, side * 2 * count : (side + 1) * 2 * count
            ]
        return carry

    lax.fori_loop(0, width // GROUP, one_group, 0, unroll=4)
    unit = eye(2 * count)
    part = 256 // LAG_ROWS
    swap = swapper(LAG_ROWS, part)
    for group in range(channels // LAG_ROWS):
        by_bin = []
        for channel in range(group * LAG_ROWS, (group + 1) * LAG_ROWS, 2):
            rows = jnp.concatenate([sums[channel], sums[channel + 1]], axis=0)
            both_turned = turned(unit, rows).astype(jnp.bfloat16)
            by_bin += [both_turned[:, :width], both_turned[:, width:]]
        for start in range(0, count, part):
            rows = jnp.concatenate(
                [
                    jnp.concatenate([b[start : start + part], b[count + start : count + start + part]], axis=1)
                    for b in by_bin
                ],
                axis=0,
            )
            rows = moved(swap, rows)
            at = slice(start * LAG_ROWS, (start + part) * LAG_ROWS)
            out[group, 0, at, :] = rows[:, :width]
            out[group, 1, at, :] = rows[:, width:]


def cross(here, near, far, by_channel, first_bin):
    each, count, both = here.shape
    quads, _, wide = by_channel.shape
    channels, windows, width = 4 * quads, wide // 8, both // 2
    return pl.pallas_call(
        cross_kernel,
        grid=(1,),
        in_specs=[pl.BlockSpec(a.shape, functools.partial(lambda n, i: (0,) * n, a.ndim)) for a in (here, near, far)]
        + [pl.BlockSpec((quads, width, wide), lambda i: (0, first_bin // width, 0))],
        out_specs=pl.BlockSpec((channels // LAG_ROWS, 2, count * LAG_ROWS, width), lambda i: (0, 0, 0, 0)),
        out_shape=jax.ShapeDtypeStruct((channels // LAG_ROWS, 2, count * LAG_ROWS, width), jnp.bfloat16),
        scratch_shapes=[
            pltpu.VMEM((windows, width, 2 * count), jnp.bfloat16),
            pltpu.VMEM((channels, width, 2 * count), jnp.bfloat16),
        ],
        compiler_params=pltpu.CompilerParams(vmem_limit_bytes=40 * MIB),
        cost_estimate=pl.CostEstimate(flops=2 * width * 36 * 65536, bytes_accessed=4 * MIB, transcendentals=0),
    )(here, near, far, by_channel)


def lag_kernel(scaling, *refs):
    *stacked, table, out = refs
    count, channels, _ = out.shape
    real, imag = (jnp.concatenate([chunk[0, side] for chunk in stacked], axis=1) for side in range(2))
    size = count * channels
    lane = lax.broadcasted_iota(jnp.int32, (size, LAG_FINE), 1)
    mirror = (LAG_FINE - lane) % LAG_FINE

    def parts(start, width):
        even = jnp.dot(real, table[:F, start : start + width], preferred_element_type=jnp.float32)
        odd = jnp.dot(imag, table[F:, start : start + width], preferred_element_type=jnp.float32)
        return even, odd

    half = LAGS // 2
    even, odd = parts(half, LAG_FINE)
    above = (even + odd) * scaling
    for start in range(half - 2 * LAG_FINE, -1, -2 * LAG_FINE):
        even, odd = parts(start, 2 * LAG_FINE)
        after_zero = (even - odd) * scaling
        before_zero = (even + odd) * scaling
        out[:, :, half + start : half + start + 2 * LAG_FINE] = after_zero.reshape(count, channels, 2 * LAG_FINE)
        for tile in (1, 0):
            turned_round = jnp.take_along_axis(
                before_zero[:, tile * LAG_FINE : (tile + 1) * LAG_FINE], mirror, axis=1, mode="promise_in_bounds"
            )
            at = half - start - (tile + 1) * LAG_FINE
            out[:, :, at : at + LAG_FINE] = jnp.where(lane == 0, above, turned_round).reshape(count, channels, LAG_FINE)
            above = turned_round


def lagged(stacked, table, scaling):
    groups, _, size, _ = stacked[0].shape
    count = size // LAG_ROWS
    return pl.pallas_call(
        functools.partial(lag_kernel, scaling),
        grid=(groups,),
        in_specs=[pl.BlockSpec((1, 2, size, s.shape[3]), lambda i: (i, 0, 0, 0)) for s in stacked]
        + [pl.BlockSpec(table.shape, lambda i: (0, 0))],
        out_specs=pl.BlockSpec((count, LAG_ROWS, LAGS), lambda i: (0, i, 0)),
        out_shape=jax.ShapeDtypeStruct((count, groups * LAG_ROWS, LAGS), jnp.float32),
        compiler_params=pltpu.CompilerParams(vmem_limit_bytes=48 * MIB),
        cost_estimate=pl.CostEstimate(
            flops=2 * groups * size * F * LAGS, bytes_accessed=groups * size * LAGS * 4, transcendentals=0
        ),
    )(*stacked, table)


def table_kernel(angles, out):
    fine_cos, fine_sin = angles[:, :LAG_FINE], angles[:, LAG_FINE : 2 * LAG_FINE]
    tiles = out.shape[1] // LAG_FINE
    for tile in range(tiles):
        big_cos = angles[:, 2 * LAG_FINE + tile : 2 * LAG_FINE + tile + 1]
        big_sin = angles[:, 2 * LAG_FINE + tiles + tile : 2 * LAG_FINE + tiles + tile + 1]
        cols = slice(tile * LAG_FINE, (tile + 1) * LAG_FINE)
        out[:F, cols] = (big_cos * fine_cos - big_sin * fine_sin).astype(jnp.bfloat16)
        out[F:, cols] = (big_sin * fine_cos + big_cos * fine_sin).astype(jnp.bfloat16)


def lag_table():
    tiles = LAGS // 2 // LAG_FINE + 1
    coarse = unit_angles(np.arange(tiles) * LAG_FINE, 1)
    angles = np.concatenate(unit_angles(np.arange(LAG_FINE), 1) + coarse, axis=1)
    return pl.pallas_call(
        table_kernel,
        out_shape=jax.ShapeDtypeStruct((2 * F, tiles * LAG_FINE), jnp.bfloat16),
        compiler_params=pltpu.CompilerParams(vmem_limit_bytes=40 * MIB),
        cost_estimate=pl.CostEstimate(flops=8 * F * tiles * LAG_FINE, bytes_accessed=4 * MIB, transcendentals=0),
    )(angles)


def make_band(filter_taps, channel_count):
    kernel = jnp.concatenate(
        [
            -filter_taps[:HALO].astype(jnp.float32),
            jnp.ones((1,), jnp.float32),
            -filter_taps[HALO:].astype(jnp.float32),
        ]
    )
    row_ids = jnp.arange(channel_count, dtype=jnp.int32)[:, None]
    columns = jnp.arange(channel_count + 2 * HALO, dtype=jnp.int32)[None, :]
    offset = columns - row_ids
    choose = offset[:, :, None] == jnp.arange(2 * HALO + 1, dtype=jnp.int32)[None, None, :]
    return jnp.sum(jnp.where(choose, kernel[None, None, :], 0.0), axis=2).astype(jnp.bfloat16)


def pick_kernel(held, across, selector, here, near, far):
    count = here.shape[1]
    for window in range(held.shape[1]):
        rows = [blocks[i, window] for blocks in (held, across) for i in range(blocks.shape[0])]
        picked = jnp.dot(selector[...], jnp.concatenate(rows, axis=0), preferred_element_type=jnp.float32)
        picked = picked.astype(jnp.bfloat16)
        here[window] = picked[:count]
        near[window] = picked[count : 2 * count]
        for at in range(far.shape[0]):
            far[at, window] = picked[(2 + at) * count : (3 + at) * count]


def pick(held, across, selector, groups):
    _, windows, _, both = held.shape
    count = selector.shape[0] // groups
    one = (windows, count, both)
    return pl.pallas_call(
        pick_kernel,
        out_shape=[jax.ShapeDtypeStruct(shape, jnp.bfloat16) for shape in (one, one, (groups - 2, *one))],
        compiler_params=pltpu.CompilerParams(vmem_limit_bytes=40 * MIB),
        cost_estimate=pl.CostEstimate(
            flops=2 * windows * selector.size * both, bytes_accessed=2 * windows * both * sum(selector.shape), transcendentals=0
        ),
    )(held, across, selector)


def swapped(value, axis, step):
    return lax.ppermute(value, axis, [(i, i ^ step) for i in range(lax.axis_size(axis))])


def after(value, earlier):
    return lax.optimization_barrier((value, earlier))[0]


def per_device(traces, filter_taps, good_channels, source_index):
    window_count, channel_count, _ = traces.shape
    good = good_channels[None, :]
    spec, head, tail = transform(traces, good)
    blocks = lax.axis_size("chan")
    groups = lax.axis_size("win")
    left = lax.ppermute(tail, "chan", [(i, i + 1) for i in range(blocks - 1)])
    right = lax.ppermute(head, "chan", [(i + 1, i) for i in range(blocks - 1)])
    table = lag_table()
    left = after(left, table)
    full, *parts = whiten(spec, left, right, make_band(filter_taps, channel_count), good)

    order = [0]
    step = blocks // 2
    while step:
        order += [place ^ step for place in order]
        step //= 2
    order = jnp.asarray(order, jnp.int32) ^ lax.axis_index("chan")
    own_ids = jnp.arange(channel_count, dtype=jnp.int32)
    channel_ids = (order[:, None] * channel_count + own_ids[None, :]).reshape(-1)
    by_group = source_index.reshape(groups, -1)
    here = lax.axis_index("win")
    wanted = jnp.concatenate([lax.dynamic_slice_in_dim(by_group, here ^ step, 1) for step in range(groups)], axis=0)
    selector = (wanted.reshape(-1)[:, None] == channel_ids[None, :]).astype(jnp.bfloat16)

    own_far = swapped(full, "win", 2)
    own_near = swapped(jnp.stack([full, own_far]), "win", 1)
    by_channel = turn_own(full, own_near, own_far)
    picked, stacked = [], []

    def finish(at):
        here, near, far = picked[at]
        earlier = stacked[-1:] + [later[0] for later in picked[at + 1 : at + 2]]
        if earlier:
            far = after(far, earlier)
        near = swapped(jnp.stack([near, far[1]]), "win", 1)
        stacked.append(cross(here, near, far, by_channel, CHUNKS[at][0]))

    gathered = []
    first_held = None
    for part in parts:
        held = part if first_held is None else after(part, [first_held, own_far])
        step = blocks // 2
        while step > 1:
            received = swapped(held, "chan", step)
            if step > 2:
                held = jnp.concatenate([held, received], axis=1)
                first_held = held if step == blocks // 2 else first_held
            step //= 2
        gathered += [jnp.concatenate([held[i], received[i]], axis=0) for i in range(TOGETHER)]
    for at, held in enumerate(gathered):
        if at:
            held = after(held, picked[-1][0])
        across = swapped(held, "chan", 1)
        if at > 1:
            finish(at - 2)
            across = after(across, stacked[-1])
        here, near, far = pick(held, across, selector, groups)
        picked.append((here, near, swapped(far, "win", 2)))
    for at in range(len(stacked), len(gathered)):
        finish(at)
    return lagged(stacked, table, 1.0 / math.sqrt(F * window_count * groups))


def solution(mesh):
    placed = (P("win", "chan", None), P(), P("chan"), P())
    return jax.shard_map(
        per_device, mesh=mesh, in_specs=placed, out_specs=P("win", "chan", None), check_vma=False
    )
```

```python
import functools
import math

import jax
import jax.numpy as jnp
import numpy as np
from jax import lax
from jax.experimental import pallas as pl
from jax.experimental.pallas import tpu as pltpu
from jax.sharding import PartitionSpec as P

L = 7680
F = 512
LAGS = 2048
HALO = 16
SMOOTH = 64
K0 = 31
QUARTER = L // 4
STEP = 640
FINE = 32
CHUNKS = tuple((start, 128) for start in range(0, F, 128))
Z_GROUPS = ((0, 1), (1, 2), (2, 4))
GROUP = 16
LAG_FINE = 128
LAG_ROWS = 8
NT = (((1,), (1,)), ((), ()))
MIB = 1024 * 1024


def unit_angles(positions, axis):
    bins = K0 + np.arange(F, dtype=np.int64)
    phase = np.mod(np.expand_dims(positions, 1 - axis) * np.expand_dims(bins, axis), L)
    angles = phase * (2.0 * math.pi / L)
    return np.cos(angles).astype(np.float32), np.sin(angles).astype(np.float32)


def keep_column(good):
    count = good.shape[1]
    rows = lax.broadcasted_iota(jnp.int32, (count, count), 0)
    cols = lax.broadcasted_iota(jnp.int32, (count, count), 1)
    return jnp.sum(jnp.where(rows == cols, good[...].astype(jnp.float32), 0.0), axis=1, keepdims=True)


def transform_kernel(x0, x1, x2, x3, angles, good, spec, head, tail, table, total):
    step = pl.program_id(0)
    rows = x0.shape[0]
    coarse = QUARTER // FINE

    def fill(of_step):
        fine_cos = angles[2 * coarse : 2 * coarse + FINE, :]
        fine_sin = angles[2 * coarse + FINE :, :]
        for part in range(STEP // FINE):
            big_cos = angles[pl.ds(of_step * (STEP // FINE) + part, 1), :]
            big_sin = angles[pl.ds(coarse + of_step * (STEP // FINE) + part, 1), :]
            at = pl.ds(part * FINE, FINE)
            table[of_step % 2, at, :F] = (big_cos * fine_cos - big_sin * fine_sin).astype(jnp.bfloat16)
            table[of_step % 2, at, F:] = (-(big_sin * fine_cos + big_cos * fine_sin)).astype(jnp.bfloat16)

    @pl.when(step == 0)
    def _():
        total[...] = jnp.zeros_like(total)
        fill(step)

    for quarter, x in enumerate((x0, x1, x2, x3)):
        at = pl.ds(quarter * rows, rows)
        total[at, :] += jnp.dot(x[...], table[step % 2], preferred_element_type=jnp.float32)
    fill(jnp.minimum(step + 1, pl.num_programs(0) - 1))

    @pl.when(step == pl.num_programs(0) - 1)
    def _():
        turn = (K0 + lax.broadcasted_iota(jnp.int32, (1, F), 1)) % 4
        even = turn % 2 == 0
        sign = jnp.where(turn < 2, 1.0, -1.0)
        channels = good.shape[1]
        keep = keep_column(good)
        for window in range(rows // channels):
            re = [total[pl.ds(q * rows + window * channels, channels), :F] for q in range(4)]
            im = [total[pl.ds(q * rows + window * channels, channels), F:] for q in range(4)]
            real = jnp.where(even, re[0] + re[2] + sign * (re[1] + re[3]), re[0] - re[2] + sign * (im[1] - im[3])) * keep
            imag = jnp.where(even, im[0] + im[2] + sign * (im[1] + im[3]), im[0] - im[2] - sign * (re[1] - re[3])) * keep
            spec[window, :, :F] = real
            spec[window, :, F:] = imag
            head[window, :, :F] = real[:HALO].astype(jnp.bfloat16)
            head[window, :, F:] = imag[:HALO].astype(jnp.bfloat16)
            tail[window, :, :F] = real[channels - HALO :].astype(jnp.bfloat16)
            tail[window, :, F:] = imag[channels - HALO :].astype(jnp.bfloat16)


def transform(traces, good):
    windows, channels, length = traces.shape
    rows = windows * channels
    steps = QUARTER // STEP
    flat = traces.reshape(rows, length)
    coarse = unit_angles(np.arange(QUARTER // FINE) * FINE, 0)
    angles = np.concatenate(coarse + unit_angles(np.arange(FINE), 0), axis=0)
    whole = lambda *shape: pl.BlockSpec(shape, lambda k: (0,) * len(shape))
    return pl.pallas_call(
        transform_kernel,
        grid=(steps,),
        in_specs=[pl.BlockSpec((rows, STEP), functools.partial(lambda q, k: (0, q * steps + k), q)) for q in range(4)]
        + [whole(*angles.shape), whole(1, channels)],
        out_specs=[whole(windows, channels, 2 * F), whole(windows, HALO, 2 * F), whole(windows, HALO, 2 * F)],
        out_shape=[
            jax.ShapeDtypeStruct((windows, channels, 2 * F), jnp.float32),
            jax.ShapeDtypeStruct((windows, HALO, 2 * F), jnp.bfloat16),
            jax.ShapeDtypeStruct((windows, HALO, 2 * F), jnp.bfloat16),
        ],
        scratch_shapes=[pltpu.VMEM((2, STEP, 2 * F), jnp.bfloat16), pltpu.VMEM((4 * rows, 2 * F), jnp.float32)],
        compiler_params=pltpu.CompilerParams(vmem_limit_bytes=60 * MIB),
        cost_estimate=pl.CostEstimate(flops=2 * rows * length * 2 * F, bytes_accessed=rows * length * 2, transcendentals=0),
    )(flat, flat, flat, flat, angles, good)


def pieces(value):
    high = value.astype(jnp.bfloat16)
    rest = value - high.astype(jnp.float32)
    middle = rest.astype(jnp.bfloat16)
    return high, middle, (rest - middle.astype(jnp.float32)).astype(jnp.bfloat16)


def whiten_kernel(spec, left, right, band, good, *outs):
    windows, channels = spec.shape[:2]
    filtered = []
    keep = keep_column(good)
    for window in range(windows):
        stack = jnp.concatenate([left[window], *pieces(spec[window]), right[window]], axis=0)
        own = band[:, HALO : HALO + channels]
        taps = jnp.concatenate([band[:, :HALO], own, own, own, band[:, HALO + channels :]], axis=1)
        filtered.append(jnp.dot(taps, stack, preferred_element_type=jnp.float32) * keep)
    spectrum = jnp.concatenate(filtered, axis=0)
    real, imag = spectrum[:, :F], spectrum[:, F:]
    magnitude = jnp.sqrt(real * real + imag * imag)
    bins = lax.broadcasted_iota(jnp.int32, (F, F), 0)
    others = lax.broadcasted_iota(jnp.int32, (F, F), 1)
    near = jnp.where(jnp.abs(bins - others) <= SMOOTH, 1.0, 0.0).astype(jnp.bfloat16)
    amplitude = sum(jnp.dot(piece, near, preferred_element_type=jnp.float32) for piece in pieces(magnitude))
    bin_row = lax.broadcasted_iota(jnp.int32, (1, F), 1)
    count = jnp.minimum(bin_row + SMOOTH, F - 1) - jnp.maximum(bin_row - SMOOTH, 0) + 1
    amplitude = amplitude * (1.0 / count.astype(jnp.float32))
    inverse = 1.0 / (amplitude + 1e-06)
    real = (real * inverse).astype(jnp.bfloat16)
    imag = (imag * inverse).astype(jnp.bfloat16)
    full, *parts = outs
    for window in range(windows):
        rows = slice(window * channels, (window + 1) * channels)
        full[window, :, :F] = real[rows]
        full[window, :, F:] = imag[rows]
        for part, (begin, end) in zip(parts, Z_GROUPS):
            for at, (start, width) in enumerate(CHUNKS[begin:end]):
                part[at, 0, window, :, :width] = real[rows, start : start + width]
                part[at, 0, window, :, width:] = imag[rows, start : start + width]


def whiten(spec, left, right, band, good):
    windows, channels, _ = spec.shape
    return pl.pallas_call(
        whiten_kernel,
        out_shape=[
            jax.ShapeDtypeStruct(shape, jnp.bfloat16)
            for shape in [(windows, channels, 2 * F)]
            + [(end - begin, 1, windows, channels, 2 * CHUNKS[0][1]) for begin, end in Z_GROUPS]
        ],
        compiler_params=pltpu.CompilerParams(vmem_limit_bytes=40 * MIB),
        cost_estimate=pl.CostEstimate(flops=2 * windows * channels * F * F * 3, bytes_accessed=5 * MIB // 2, transcendentals=windows * channels * F),
    )(spec, left, right, band, good)


def eye(size):
    rows = lax.broadcasted_iota(jnp.int32, (size, size), 0)
    cols = lax.broadcasted_iota(jnp.int32, (size, size), 1)
    return jnp.where(rows == cols, 1.0, 0.0).astype(jnp.bfloat16)


def turned(left_unit, rows):
    return lax.dot_general(left_unit, rows, NT, preferred_element_type=jnp.float32)


def swapper(outer, inner):
    size = outer * inner
    rows = lax.broadcasted_iota(jnp.int32, (size, size), 0)
    cols = lax.broadcasted_iota(jnp.int32, (size, size), 1)
    return jnp.where(cols == rows % outer * inner + rows // outer, 1.0, 0.0).astype(jnp.bfloat16)


def moved(swap, rows):
    return jnp.dot(swap, rows, preferred_element_type=jnp.float32).astype(jnp.bfloat16)


def own_kernel(here, near, far, out, by_window):
    own = [here, near.at[0], far, near.at[1]]
    each, channels, _ = here.shape
    windows, quads = each * len(own), channels // 4
    joined = GROUP // each
    swap = swapper(GROUP, GROUP)
    for start in range(0, windows, GROUP):
        for channel in range(0, channels, GROUP):
            block = [o[:, channel : channel + GROUP, :] for o in own[start // each : start // each + joined]]
            rows = moved(swap, jnp.concatenate(block, axis=0).reshape(GROUP * GROUP, 2 * F))
            by_window[channel : channel + GROUP, start : start + GROUP, :] = rows.reshape(GROUP, GROUP, 2 * F)
    unit = eye(F // 2)
    for quad in range(quads):
        for start in range(0, F, F // 2):
            rows = []
            for channel in range(quad, channels, quads):
                rows += [by_window[channel, :, side + start : side + start + F // 2] for side in (0, F)]
            out[quad, start : start + F // 2, :] = turned(unit, jnp.concatenate(rows, axis=0)).astype(jnp.bfloat16)


def turn_own(here, near, far):
    each, channels, _ = here.shape
    windows = each * 4
    return pl.pallas_call(
        own_kernel,
        out_shape=jax.ShapeDtypeStruct((channels // 4, F, 8 * windows), jnp.bfloat16),
        scratch_shapes=[pltpu.VMEM((channels, windows, 2 * F), jnp.bfloat16)],
        compiler_params=pltpu.CompilerParams(vmem_limit_bytes=40 * MIB),
        cost_estimate=pl.CostEstimate(flops=2 * 8192 * 65536, bytes_accessed=4 * MIB, transcendentals=0),
    )(here, near, far)


def cross_kernel(here, near, far, by_channel, out, by_window, sums):
    sources = [here, near.at[0], far.at[0], near.at[1]]
    each, count, both = here.shape
    quads, _, wide = by_channel.shape
    channels, half = 4 * quads, wide // 4
    windows, width = half // 2, both // 2
    unit = eye(width)
    swap = swapper(GROUP, GROUP)
    swap_quads = swapper(quads, GROUP)
    for window in range(0, windows, 2):
        rows = []
        for one in range(window, window + 2):
            source = sources[one // each]
            rows += [source[one % each, :, :width], source[one % each, :, width:]]
        both_turned = turned(unit, jnp.concatenate(rows, axis=0)).astype(jnp.bfloat16)
        by_window[window] = both_turned[:, : 2 * count]
        by_window[window + 1] = both_turned[:, 2 * count :]
    first = lax.broadcasted_iota(jnp.int32, (1, 2 * half), 1) < half
    sign = jnp.where(lax.broadcasted_iota(jnp.int32, (1, 2 * count), 1) < count, 1.0, -1.0)
    empty = jnp.zeros((2 * windows, 2 * count), jnp.bfloat16)

    def one_group(group, carry):
        bins = pl.ds(pl.multiple_of(group * GROUP, GROUP), GROUP)
        rows = [
            by_window[start : start + GROUP, bins, :].reshape(GROUP * GROUP, 2 * count)
            for start in range(0, windows, GROUP)
        ]
        rights = jnp.dot(swap, jnp.concatenate(rows, axis=1), preferred_element_type=jnp.float32)
        lefts = jnp.dot(
            swap_quads, by_channel[:, bins, :].reshape(quads * GROUP, 4 * half), preferred_element_type=jnp.float32
        )
        results = []
        for at in range(0, GROUP, 2):
            two = []
            for one in range(at, at + 2):
                here = rights[one * GROUP : (one + 1) * GROUP]
                src = jnp.concatenate(
                    [here[:, i * 2 * count : (i + 1) * 2 * count] for i in range(windows // GROUP)], axis=0
                )
                two.append(jnp.concatenate([src * sign, pltpu.roll(src, count, axis=1)], axis=0).astype(jnp.bfloat16))
            right = jnp.concatenate(
                [jnp.concatenate([two[0], empty], axis=1), jnp.concatenate([empty, two[1]], axis=1)], axis=0
            )
            left = []
            for tile in range(0, 4 * half, 2 * half):
                one, other = (lefts[i * quads : (i + 1) * quads, tile : tile + 2 * half] for i in (at, at + 1))
                left.append(jnp.where(first, one, pltpu.roll(other, half, axis=1)))
                left.append(jnp.where(first, pltpu.roll(one, half, axis=1), other))
            left = jnp.concatenate(left, axis=0).astype(jnp.bfloat16)
            result = jnp.dot(left, right, preferred_element_type=jnp.float32).astype(jnp.bfloat16)
            results += [result[:, : 2 * count], result[:, 2 * count :]]
        halves = [
            jnp.concatenate([r[start : start + GROUP] for r in results], axis=0) for start in range(0, channels, GROUP)
        ]
        done = moved(swap, jnp.concatenate(halves, axis=1))
        for channel in range(channels):
            row, side = channel % GROUP, channel // GROUP
            sums[channel, bins, :] = done[
                row * GROUP : (row + 1) * GROUP, side * 2 * count : (side + 1) * 2 * count
            ]
        return carry

    lax.fori_loop(0, width // GROUP, one_group, 0, unroll=8)
    unit = eye(2 * count)
    part = 256 // LAG_ROWS
    swap = swapper(LAG_ROWS, part)
    for group in range(channels // LAG_ROWS):
        by_bin = []
        for channel in range(group * LAG_ROWS, (group + 1) * LAG_ROWS, 2):
            rows = jnp.concatenate([sums[channel], sums[channel + 1]], axis=0)
            both_turned = turned(unit, rows).astype(jnp.bfloat16)
            by_bin += [both_turned[:, :width], both_turned[:, width:]]
        for start in range(0, count, part):
            rows = jnp.concatenate(
                [
                    jnp.concatenate([b[start : start + part], b[count + start : count + start + part]], axis=1)
                    for b in by_bin
                ],
                axis=0,
            )
            rows = moved(swap, rows)
            at = slice(start * LAG_ROWS, (start + part) * LAG_ROWS)
            out[group, 0, at, :] = rows[:, :width]
            out[group, 1, at, :] = rows[:, width:]


def cross(here, near, far, by_channel, first_bin):
    each, count, both = here.shape
    quads, _, wide = by_channel.shape
    channels, windows, width = 4 * quads, wide // 8, both // 2
    return pl.pallas_call(
        cross_kernel,
        grid=(1,),
        in_specs=[pl.BlockSpec(a.shape, functools.partial(lambda n, i: (0,) * n, a.ndim)) for a in (here, near, far)]
        + [pl.BlockSpec((quads, width, wide), lambda i: (0, first_bin // width, 0))],
        out_specs=pl.BlockSpec((channels // LAG_ROWS, 2, count * LAG_ROWS, width), lambda i: (0, 0, 0, 0)),
        out_shape=jax.ShapeDtypeStruct((channels // LAG_ROWS, 2, count * LAG_ROWS, width), jnp.bfloat16),
        scratch_shapes=[
            pltpu.VMEM((windows, width, 2 * count), jnp.bfloat16),
            pltpu.VMEM((channels, width, 2 * count), jnp.bfloat16),
        ],
        compiler_params=pltpu.CompilerParams(vmem_limit_bytes=40 * MIB),
        cost_estimate=pl.CostEstimate(flops=2 * width * 36 * 65536, bytes_accessed=4 * MIB, transcendentals=0),
    )(here, near, far, by_channel)


def lag_kernel(scaling, *refs):
    *stacked, table, out = refs
    count, channels, _ = out.shape
    real, imag = (jnp.concatenate([chunk[0, side] for chunk in stacked], axis=1) for side in range(2))
    size = count * channels
    lane = lax.broadcasted_iota(jnp.int32, (size, LAG_FINE), 1)
    mirror = (LAG_FINE - lane) % LAG_FINE

    def parts(start, width):
        even = jnp.dot(real, table[:F, start : start + width], preferred_element_type=jnp.float32)
        odd = jnp.dot(imag, table[F:, start : start + width], preferred_element_type=jnp.float32)
        return even, odd

    half = LAGS // 2
    even, odd = parts(half, LAG_FINE)
    above = (even + odd) * scaling
    for start in range(half - 2 * LAG_FINE, -1, -2 * LAG_FINE):
        even, odd = parts(start, 2 * LAG_FINE)
        after_zero = (even - odd) * scaling
        before_zero = (even + odd) * scaling
        out[:, :, half + start : half + start + 2 * LAG_FINE] = after_zero.reshape(count, channels, 2 * LAG_FINE)
        for tile in (1, 0):
            turned_round = jnp.take_along_axis(
                before_zero[:, tile * LAG_FINE : (tile + 1) * LAG_FINE], mirror, axis=1, mode="promise_in_bounds"
            )
            at = half - start - (tile + 1) * LAG_FINE
            out[:, :, at : at + LAG_FINE] = jnp.where(lane == 0, above, turned_round).reshape(count, channels, LAG_FINE)
            above = turned_round


def lagged(stacked, table, scaling):
    groups, _, size, _ = stacked[0].shape
    count = size // LAG_ROWS
    return pl.pallas_call(
        functools.partial(lag_kernel, scaling),
        grid=(groups,),
        in_specs=[pl.BlockSpec((1, 2, size, s.shape[3]), lambda i: (i, 0, 0, 0)) for s in stacked]
        + [pl.BlockSpec(table.shape, lambda i: (0, 0))],
        out_specs=pl.BlockSpec((count, LAG_ROWS, LAGS), lambda i: (0, i, 0)),
        out_shape=jax.ShapeDtypeStruct((count, groups * LAG_ROWS, LAGS), jnp.float32),
        compiler_params=pltpu.CompilerParams(vmem_limit_bytes=48 * MIB),
        cost_estimate=pl.CostEstimate(
            flops=2 * groups * size * F * LAGS, bytes_accessed=groups * size * LAGS * 4, transcendentals=0
        ),
    )(*stacked, table)


def table_kernel(angles, out):
    fine_cos, fine_sin = angles[:, :LAG_FINE], angles[:, LAG_FINE : 2 * LAG_FINE]
    tiles = out.shape[1] // LAG_FINE
    for tile in range(tiles):
        big_cos = angles[:, 2 * LAG_FINE + tile : 2 * LAG_FINE + tile + 1]
        big_sin = angles[:, 2 * LAG_FINE + tiles + tile : 2 * LAG_FINE + tiles + tile + 1]
        cols = slice(tile * LAG_FINE, (tile + 1) * LAG_FINE)
        out[:F, cols] = (big_cos * fine_cos - big_sin * fine_sin).astype(jnp.bfloat16)
        out[F:, cols] = (big_sin * fine_cos + big_cos * fine_sin).astype(jnp.bfloat16)


def lag_table():
    tiles = LAGS // 2 // LAG_FINE + 1
    coarse = unit_angles(np.arange(tiles) * LAG_FINE, 1)
    angles = np.concatenate(unit_angles(np.arange(LAG_FINE), 1) + coarse, axis=1)
    return pl.pallas_call(
        table_kernel,
        out_shape=jax.ShapeDtypeStruct((2 * F, tiles * LAG_FINE), jnp.bfloat16),
        compiler_params=pltpu.CompilerParams(vmem_limit_bytes=40 * MIB),
        cost_estimate=pl.CostEstimate(flops=8 * F * tiles * LAG_FINE, bytes_accessed=4 * MIB, transcendentals=0),
    )(angles)


def make_band(filter_taps, channel_count):
    kernel = jnp.concatenate(
        [
            -filter_taps[:HALO].astype(jnp.float32),
            jnp.ones((1,), jnp.float32),
            -filter_taps[HALO:].astype(jnp.float32),
        ]
    )
    row_ids = jnp.arange(channel_count, dtype=jnp.int32)[:, None]
    columns = jnp.arange(channel_count + 2 * HALO, dtype=jnp.int32)[None, :]
    offset = columns - row_ids
    choose = offset[:, :, None] == jnp.arange(2 * HALO + 1, dtype=jnp.int32)[None, None, :]
    return jnp.sum(jnp.where(choose, kernel[None, None, :], 0.0), axis=2).astype(jnp.bfloat16)


def pick_kernel(held, across, selector, here, near, far):
    count = here.shape[1]
    for window in range(held.shape[1]):
        rows = [blocks[i, window] for blocks in (held, across) for i in range(blocks.shape[0])]
        picked = jnp.dot(selector[...], jnp.concatenate(rows, axis=0), preferred_element_type=jnp.float32)
        picked = picked.astype(jnp.bfloat16)
        here[window] = picked[:count]
        near[window] = picked[count : 2 * count]
        for at in range(far.shape[0]):
            far[at, window] = picked[(2 + at) * count : (3 + at) * count]


def pick(held, across, selector, groups):
    _, windows, _, both = held.shape
    count = selector.shape[0] // groups
    one = (windows, count, both)
    return pl.pallas_call(
        pick_kernel,
        out_shape=[jax.ShapeDtypeStruct(shape, jnp.bfloat16) for shape in (one, one, (groups - 2, *one))],
        compiler_params=pltpu.CompilerParams(vmem_limit_bytes=40 * MIB),
        cost_estimate=pl.CostEstimate(
            flops=2 * windows * selector.size * both, bytes_accessed=2 * windows * both * sum(selector.shape), transcendentals=0
        ),
    )(held, across, selector)


def swapped(value, axis, step):
    return lax.ppermute(value, axis, [(i, i ^ step) for i in range(lax.axis_size(axis))])


def after(value, earlier):
    return lax.optimization_barrier((value, earlier))[0]


def per_device(traces, filter_taps, good_channels, source_index):
    window_count, channel_count, _ = traces.shape
    good = good_channels[None, :]
    spec, head, tail = transform(traces, good)
    blocks = lax.axis_size("chan")
    groups = lax.axis_size("win")
    left = lax.ppermute(tail, "chan", [(i, i + 1) for i in range(blocks - 1)])
    right = lax.ppermute(head, "chan", [(i + 1, i) for i in range(blocks - 1)])
    table = lag_table()
    left = after(left, table)
    full, *parts = whiten(spec, left, right, make_band(filter_taps, channel_count), good)

    order = [0]
    step = blocks // 2
    while step:
        order += [place ^ step for place in order]
        step //= 2
    order = jnp.asarray(order, jnp.int32) ^ lax.axis_index("chan")
    own_ids = jnp.arange(channel_count, dtype=jnp.int32)
    channel_ids = (order[:, None] * channel_count + own_ids[None, :]).reshape(-1)
    by_group = source_index.reshape(groups, -1)
    here = lax.axis_index("win")
    wanted = jnp.concatenate([lax.dynamic_slice_in_dim(by_group, here ^ step, 1) for step in range(groups)], axis=0)
    selector = (wanted.reshape(-1)[:, None] == channel_ids[None, :]).astype(jnp.bfloat16)

    own_far = swapped(full, "win", 2)
    own_near = swapped(jnp.stack([full, own_far]), "win", 1)
    by_channel = turn_own(full, own_near, own_far)
    picked, stacked = [], []

    def finish(at):
        here, near, far = picked[at]
        earlier = stacked[-1:] + [later[0] for later in picked[at + 1 : at + 2]]
        if earlier:
            far = after(far, earlier)
        near = swapped(jnp.stack([near, far[1]]), "win", 1)
        stacked.append(cross(here, near, far, by_channel, CHUNKS[at][0]))

    gathered = []
    first_held = None
    for part in parts:
        held = part if first_held is None else after(part, [first_held] + [own_far] * (len(gathered) > 1))
        step = blocks // 2
        while step > 1:
            received = swapped(held, "chan", step)
            if step > 2:
                held = jnp.concatenate([held, received], axis=1)
                first_held = held if step == blocks // 2 else first_held
            step //= 2
        gathered += [jnp.concatenate([held[i], received[i]], axis=0) for i in range(part.shape[0])]
    for at, held in enumerate(gathered):
        if at:
            held = after(held, picked[-1][0])
        across = swapped(held, "chan", 1)
        if at > 1:
            finish(at - 2)
            across = after(across, stacked[-1])
        here, near, far = pick(held, across, selector, groups)
        picked.append((here, near, swapped(far, "win", 2)))
    for at in range(len(stacked), len(gathered)):
        finish(at)
    return lagged(stacked, table, 1.0 / math.sqrt(F * window_count * groups))


def solution(mesh):
    placed = (P("win", "chan", None), P(), P("chan"), P())
    return jax.shard_map(
        per_device, mesh=mesh, in_specs=placed, out_specs=P("win", "chan", None), check_vma=False
    )
```

```python
import functools
import math

import jax
import jax.numpy as jnp
import numpy as np
from jax import lax
from jax.experimental import pallas as pl
from jax.experimental.pallas import tpu as pltpu
from jax.sharding import PartitionSpec as P

L = 7680
F = 512
LAGS = 2048
HALO = 16
SMOOTH = 64
K0 = 31
QUARTER = L // 4
STEP = 640
FINE = 32
CHUNKS = tuple((start, 128) for start in range(0, F, 128))
Z_GROUPS = ((0, 1), (1, 2), (2, 4))
GROUP = 16
LAG_FINE = 128
LAG_ROWS = 8
NT = (((1,), (1,)), ((), ()))
MIB = 1024 * 1024


def unit_angles(positions, axis):
    bins = K0 + np.arange(F, dtype=np.int64)
    phase = np.mod(np.expand_dims(positions, 1 - axis) * np.expand_dims(bins, axis), L)
    angles = phase * (2.0 * math.pi / L)
    return np.cos(angles).astype(np.float32), np.sin(angles).astype(np.float32)


def keep_column(good):
    count = good.shape[1]
    rows = lax.broadcasted_iota(jnp.int32, (count, count), 0)
    cols = lax.broadcasted_iota(jnp.int32, (count, count), 1)
    return jnp.sum(jnp.where(rows == cols, good[...].astype(jnp.float32), 0.0), axis=1, keepdims=True)


def transform_kernel(x0, x1, x2, x3, angles, good, spec, head, tail, table, total):
    step = pl.program_id(0)
    rows = x0.shape[0]
    coarse = QUARTER // FINE

    def fill(of_step):
        fine_cos = angles[2 * coarse : 2 * coarse + FINE, :]
        fine_sin = angles[2 * coarse + FINE :, :]
        for part in range(STEP // FINE):
            big_cos = angles[pl.ds(of_step * (STEP // FINE) + part, 1), :]
            big_sin = angles[pl.ds(coarse + of_step * (STEP // FINE) + part, 1), :]
            at = pl.ds(part * FINE, FINE)
            table[of_step % 2, at, :F] = (big_cos * fine_cos - big_sin * fine_sin).astype(jnp.bfloat16)
            table[of_step % 2, at, F:] = (-(big_sin * fine_cos + big_cos * fine_sin)).astype(jnp.bfloat16)

    @pl.when(step == 0)
    def _():
        total[...] = jnp.zeros_like(total)
        fill(step)

    for quarter, x in enumerate((x0, x1, x2, x3)):
        at = pl.ds(quarter * rows, rows)
        total[at, :] += jnp.dot(x[...], table[step % 2], preferred_element_type=jnp.float32)
    fill(jnp.minimum(step + 1, pl.num_programs(0) - 1))

    @pl.when(step == pl.num_programs(0) - 1)
    def _():
        turn = (K0 + lax.broadcasted_iota(jnp.int32, (1, F), 1)) % 4
        even = turn % 2 == 0
        sign = jnp.where(turn < 2, 1.0, -1.0)
        channels = good.shape[1]
        keep = keep_column(good)
        for window in range(rows // channels):
            re = [total[pl.ds(q * rows + window * channels, channels), :F] for q in range(4)]
            im = [total[pl.ds(q * rows + window * channels, channels), F:] for q in range(4)]
            real = jnp.where(even, re[0] + re[2] + sign * (re[1] + re[3]), re[0] - re[2] + sign * (im[1] - im[3])) * keep
            imag = jnp.where(even, im[0] + im[2] + sign * (im[1] + im[3]), im[0] - im[2] - sign * (re[1] - re[3])) * keep
            spec[window, :, :F] = real
            spec[window, :, F:] = imag
            head[window, :, :F] = real[:HALO].astype(jnp.bfloat16)
            head[window, :, F:] = imag[:HALO].astype(jnp.bfloat16)
            tail[window, :, :F] = real[channels - HALO :].astype(jnp.bfloat16)
            tail[window, :, F:] = imag[channels - HALO :].astype(jnp.bfloat16)


def transform(traces, good):
    windows, channels, length = traces.shape
    rows = windows * channels
    steps = QUARTER // STEP
    flat = traces.reshape(rows, length)
    coarse = unit_angles(np.arange(QUARTER // FINE) * FINE, 0)
    angles = np.concatenate(coarse + unit_angles(np.arange(FINE), 0), axis=0)
    whole = lambda *shape: pl.BlockSpec(shape, lambda k: (0,) * len(shape))
    return pl.pallas_call(
        transform_kernel,
        grid=(steps,),
        in_specs=[pl.BlockSpec((rows, STEP), functools.partial(lambda q, k: (0, q * steps + k), q)) for q in range(4)]
        + [whole(*angles.shape), whole(1, channels)],
        out_specs=[whole(windows, channels, 2 * F), whole(windows, HALO, 2 * F), whole(windows, HALO, 2 * F)],
        out_shape=[
            jax.ShapeDtypeStruct((windows, channels, 2 * F), jnp.float32),
            jax.ShapeDtypeStruct((windows, HALO, 2 * F), jnp.bfloat16),
            jax.ShapeDtypeStruct((windows, HALO, 2 * F), jnp.bfloat16),
        ],
        scratch_shapes=[pltpu.VMEM((2, STEP, 2 * F), jnp.bfloat16), pltpu.VMEM((4 * rows, 2 * F), jnp.float32)],
        compiler_params=pltpu.CompilerParams(vmem_limit_bytes=60 * MIB),
        cost_estimate=pl.CostEstimate(flops=2 * rows * length * 2 * F, bytes_accessed=rows * length * 2, transcendentals=0),
    )(flat, flat, flat, flat, angles, good)


def pieces(value):
    high = value.astype(jnp.bfloat16)
    rest = value - high.astype(jnp.float32)
    middle = rest.astype(jnp.bfloat16)
    return high, middle, (rest - middle.astype(jnp.float32)).astype(jnp.bfloat16)


def whiten_kernel(spec, left, right, band, good, *outs):
    windows, channels = spec.shape[:2]
    filtered = []
    keep = keep_column(good)
    for window in range(windows):
        stack = jnp.concatenate([left[window], *pieces(spec[window]), right[window]], axis=0)
        own = band[:, HALO : HALO + channels]
        taps = jnp.concatenate([band[:, :HALO], own, own, own, band[:, HALO + channels :]], axis=1)
        filtered.append(jnp.dot(taps, stack, preferred_element_type=jnp.float32) * keep)
    spectrum = jnp.concatenate(filtered, axis=0)
    real, imag = spectrum[:, :F], spectrum[:, F:]
    magnitude = jnp.sqrt(real * real + imag * imag)
    bins = lax.broadcasted_iota(jnp.int32, (F, F), 0)
    others = lax.broadcasted_iota(jnp.int32, (F, F), 1)
    near = jnp.where(jnp.abs(bins - others) <= SMOOTH, 1.0, 0.0).astype(jnp.bfloat16)
    amplitude = sum(jnp.dot(piece, near, preferred_element_type=jnp.float32) for piece in pieces(magnitude))
    bin_row = lax.broadcasted_iota(jnp.int32, (1, F), 1)
    count = jnp.minimum(bin_row + SMOOTH, F - 1) - jnp.maximum(bin_row - SMOOTH, 0) + 1
    amplitude = amplitude * (1.0 / count.astype(jnp.float32))
    inverse = 1.0 / (amplitude + 1e-06)
    real = (real * inverse).astype(jnp.bfloat16)
    imag = (imag * inverse).astype(jnp.bfloat16)
    full, *parts = outs
    for window in range(windows):
        rows = slice(window * channels, (window + 1) * channels)
        full[window, :, :F] = real[rows]
        full[window, :, F:] = imag[rows]
        for part, (begin, end) in zip(parts, Z_GROUPS):
            for at, (start, width) in enumerate(CHUNKS[begin:end]):
                part[at, 0, window, :, :width] = real[rows, start : start + width]
                part[at, 0, window, :, width:] = imag[rows, start : start + width]


def whiten(spec, left, right, band, good):
    windows, channels, _ = spec.shape
    return pl.pallas_call(
        whiten_kernel,
        out_shape=[
            jax.ShapeDtypeStruct(shape, jnp.bfloat16)
            for shape in [(windows, channels, 2 * F)]
            + [(end - begin, 1, windows, channels, 2 * CHUNKS[0][1]) for begin, end in Z_GROUPS]
        ],
        compiler_params=pltpu.CompilerParams(vmem_limit_bytes=40 * MIB),
        cost_estimate=pl.CostEstimate(flops=2 * windows * channels * F * F * 3, bytes_accessed=5 * MIB // 2, transcendentals=windows * channels * F),
    )(spec, left, right, band, good)


def eye(size):
    rows = lax.broadcasted_iota(jnp.int32, (size, size), 0)
    cols = lax.broadcasted_iota(jnp.int32, (size, size), 1)
    return jnp.where(rows == cols, 1.0, 0.0).astype(jnp.bfloat16)


def turned(left_unit, rows):
    return lax.dot_general(left_unit, rows, NT, preferred_element_type=jnp.float32)


def swapper(outer, inner):
    size = outer * inner
    rows = lax.broadcasted_iota(jnp.int32, (size, size), 0)
    cols = lax.broadcasted_iota(jnp.int32, (size, size), 1)
    return jnp.where(cols == rows % outer * inner + rows // outer, 1.0, 0.0).astype(jnp.bfloat16)


def moved(swap, rows):
    return jnp.dot(swap, rows, preferred_element_type=jnp.float32).astype(jnp.bfloat16)


def own_kernel(here, near, far, out, by_window):
    own = [here, near.at[0], far, near.at[1]]
    each, channels, _ = here.shape
    windows, quads = each * len(own), channels // 4
    joined = GROUP // each
    swap = swapper(GROUP, GROUP)
    for start in range(0, windows, GROUP):
        for channel in range(0, channels, GROUP):
            block = [o[:, channel : channel + GROUP, :] for o in own[start // each : start // each + joined]]
            rows = moved(swap, jnp.concatenate(block, axis=0).reshape(GROUP * GROUP, 2 * F))
            by_window[channel : channel + GROUP, start : start + GROUP, :] = rows.reshape(GROUP, GROUP, 2 * F)
    unit = eye(F // 2)
    for quad in range(quads):
        for start in range(0, F, F // 2):
            rows = []
            for channel in range(quad, channels, quads):
                rows += [by_window[channel, :, side + start : side + start + F // 2] for side in (0, F)]
            out[quad, start : start + F // 2, :] = turned(unit, jnp.concatenate(rows, axis=0)).astype(jnp.bfloat16)


def turn_own(here, near, far):
    each, channels, _ = here.shape
    windows = each * 4
    return pl.pallas_call(
        own_kernel,
        out_shape=jax.ShapeDtypeStruct((channels // 4, F, 8 * windows), jnp.bfloat16),
        scratch_shapes=[pltpu.VMEM((channels, windows, 2 * F), jnp.bfloat16)],
        compiler_params=pltpu.CompilerParams(vmem_limit_bytes=40 * MIB),
        cost_estimate=pl.CostEstimate(flops=2 * 8192 * 65536, bytes_accessed=4 * MIB, transcendentals=0),
    )(here, near, far)


def cross_kernel(here, near, far, by_channel, out, by_window, sums):
    sources = [here, near.at[0], far.at[0], near.at[1]]
    each, count, both = here.shape
    quads, _, wide = by_channel.shape
    channels, half = 4 * quads, wide // 4
    windows, width = half // 2, both // 2
    unit = eye(width)
    swap = swapper(GROUP, GROUP)
    swap_quads = swapper(quads, GROUP)
    for window in range(0, windows, 2):
        rows = []
        for one in range(window, window + 2):
            source = sources[one // each]
            rows += [source[one % each, :, :width], source[one % each, :, width:]]
        both_turned = turned(unit, jnp.concatenate(rows, axis=0)).astype(jnp.bfloat16)
        by_window[window] = both_turned[:, : 2 * count]
        by_window[window + 1] = both_turned[:, 2 * count :]
    first = lax.broadcasted_iota(jnp.int32, (1, 2 * half), 1) < half
    sign = jnp.where(lax.broadcasted_iota(jnp.int32, (1, 2 * count), 1) < count, 1.0, -1.0)
    empty = jnp.zeros((2 * windows, 2 * count), jnp.bfloat16)

    def one_group(group, carry):
        bins = pl.ds(pl.multiple_of(group * GROUP, GROUP), GROUP)
        rows = [
            by_window[start : start + GROUP, bins, :].reshape(GROUP * GROUP, 2 * count)
            for start in range(0, windows, GROUP)
        ]
        rights = jnp.dot(swap, jnp.concatenate(rows, axis=1), preferred_element_type=jnp.float32)
        lefts = jnp.dot(
            swap_quads, by_channel[:, bins, :].reshape(quads * GROUP, 4 * half), preferred_element_type=jnp.float32
        )
        results = []
        for at in range(0, GROUP, 2):
            two = []
            for one in range(at, at + 2):
                here = rights[one * GROUP : (one + 1) * GROUP]
                src = jnp.concatenate(
                    [here[:, i * 2 * count : (i + 1) * 2 * count] for i in range(windows // GROUP)], axis=0
                )
                two.append(jnp.concatenate([src * sign, pltpu.roll(src, count, axis=1)], axis=0).astype(jnp.bfloat16))
            right = jnp.concatenate(
                [jnp.concatenate([two[0], empty], axis=1), jnp.concatenate([empty, two[1]], axis=1)], axis=0
            )
            left = []
            for tile in range(0, 4 * half, 2 * half):
                one, other = (lefts[i * quads : (i + 1) * quads, tile : tile + 2 * half] for i in (at, at + 1))
                left.append(jnp.where(first, one, pltpu.roll(other, half, axis=1)))
                left.append(jnp.where(first, pltpu.roll(one, half, axis=1), other))
            left = jnp.concatenate(left, axis=0).astype(jnp.bfloat16)
            result = jnp.dot(left, right, preferred_element_type=jnp.float32).astype(jnp.bfloat16)
            results += [result[:, : 2 * count], result[:, 2 * count :]]
        halves = [
            jnp.concatenate([r[start : start + GROUP] for r in results], axis=0) for start in range(0, channels, GROUP)
        ]
        done = moved(swap, jnp.concatenate(halves, axis=1))
        for channel in range(channels):
            row, side = channel % GROUP, channel // GROUP
            sums[channel, bins, :] = done[
                row * GROUP : (row + 1) * GROUP, side * 2 * count : (side + 1) * 2 * count
            ]
        return carry

    lax.fori_loop(0, width // GROUP, one_group, 0, unroll=8)
    unit = eye(2 * count)
    part = 256 // LAG_ROWS
    swap = swapper(LAG_ROWS, part)
    for group in range(channels // LAG_ROWS):
        by_bin = []
        for channel in range(group * LAG_ROWS, (group + 1) * LAG_ROWS, 2):
            rows = jnp.concatenate([sums[channel], sums[channel + 1]], axis=0)
            both_turned = turned(unit, rows).astype(jnp.bfloat16)
            by_bin += [both_turned[:, :width], both_turned[:, width:]]
        for start in range(0, count, part):
            rows = jnp.concatenate(
                [
                    jnp.concatenate([b[start : start + part], b[count + start : count + start + part]], axis=1)
                    for b in by_bin
                ],
                axis=0,
            )
            rows = moved(swap, rows)
            at = slice(start * LAG_ROWS, (start + part) * LAG_ROWS)
            out[group, 0, at, :] = rows[:, :width]
            out[group, 1, at, :] = rows[:, width:]


def cross(here, near, far, by_channel, first_bin):
    each, count, both = here.shape
    quads, _, wide = by_channel.shape
    channels, windows, width = 4 * quads, wide // 8, both // 2
    return pl.pallas_call(
        cross_kernel,
        grid=(1,),
        in_specs=[pl.BlockSpec(a.shape, functools.partial(lambda n, i: (0,) * n, a.ndim)) for a in (here, near, far)]
        + [pl.BlockSpec((quads, width, wide), lambda i: (0, first_bin // width, 0))],
        out_specs=pl.BlockSpec((channels // LAG_ROWS, 2, count * LAG_ROWS, width), lambda i: (0, 0, 0, 0)),
        out_shape=jax.ShapeDtypeStruct((channels // LAG_ROWS, 2, count * LAG_ROWS, width), jnp.bfloat16),
        scratch_shapes=[
            pltpu.VMEM((windows, width, 2 * count), jnp.bfloat16),
            pltpu.VMEM((channels, width, 2 * count), jnp.bfloat16),
        ],
        compiler_params=pltpu.CompilerParams(vmem_limit_bytes=40 * MIB),
        cost_estimate=pl.CostEstimate(flops=2 * width * 36 * 65536, bytes_accessed=4 * MIB, transcendentals=0),
    )(here, near, far, by_channel)


def lag_kernel(scaling, *refs):
    *stacked, table, out = refs
    count, channels, _ = out.shape
    real, imag = (jnp.concatenate([chunk[0, side] for chunk in stacked], axis=1) for side in range(2))
    size = count * channels
    lane = lax.broadcasted_iota(jnp.int32, (size, LAG_FINE), 1)
    mirror = (LAG_FINE - lane) % LAG_FINE

    def parts(start, width):
        even = jnp.dot(real, table[:F, start : start + width], preferred_element_type=jnp.float32)
        odd = jnp.dot(imag, table[F:, start : start + width], preferred_element_type=jnp.float32)
        return even, odd

    half = LAGS // 2
    even, odd = parts(half, LAG_FINE)
    above = (even + odd) * scaling
    for start in range(half - 2 * LAG_FINE, -1, -2 * LAG_FINE):
        even, odd = parts(start, 2 * LAG_FINE)
        after_zero = (even - odd) * scaling
        before_zero = (even + odd) * scaling
        out[:, :, half + start : half + start + 2 * LAG_FINE] = after_zero.reshape(count, channels, 2 * LAG_FINE)
        for tile in (1, 0):
            turned_round = jnp.take_along_axis(
                before_zero[:, tile * LAG_FINE : (tile + 1) * LAG_FINE], mirror, axis=1, mode="promise_in_bounds"
            )
            at = half - start - (tile + 1) * LAG_FINE
            out[:, :, at : at + LAG_FINE] = jnp.where(lane == 0, above, turned_round).reshape(count, channels, LAG_FINE)
            above = turned_round


def lagged(stacked, table, scaling):
    groups, _, size, _ = stacked[0].shape
    count = size // LAG_ROWS
    return pl.pallas_call(
        functools.partial(lag_kernel, scaling),
        grid=(groups,),
        in_specs=[pl.BlockSpec((1, 2, size, s.shape[3]), lambda i: (i, 0, 0, 0)) for s in stacked]
        + [pl.BlockSpec(table.shape, lambda i: (0, 0))],
        out_specs=pl.BlockSpec((count, LAG_ROWS, LAGS), lambda i: (0, i, 0)),
        out_shape=jax.ShapeDtypeStruct((count, groups * LAG_ROWS, LAGS), jnp.float32),
        compiler_params=pltpu.CompilerParams(vmem_limit_bytes=48 * MIB),
        cost_estimate=pl.CostEstimate(
            flops=2 * groups * size * F * LAGS, bytes_accessed=groups * size * LAGS * 4, transcendentals=0
        ),
    )(*stacked, table)


def table_kernel(angles, out):
    fine_cos, fine_sin = angles[:, :LAG_FINE], angles[:, LAG_FINE : 2 * LAG_FINE]
    tiles = out.shape[1] // LAG_FINE
    for tile in range(tiles):
        big_cos = angles[:, 2 * LAG_FINE + tile : 2 * LAG_FINE + tile + 1]
        big_sin = angles[:, 2 * LAG_FINE + tiles + tile : 2 * LAG_FINE + tiles + tile + 1]
        cols = slice(tile * LAG_FINE, (tile + 1) * LAG_FINE)
        out[:F, cols] = (big_cos * fine_cos - big_sin * fine_sin).astype(jnp.bfloat16)
        out[F:, cols] = (big_sin * fine_cos + big_cos * fine_sin).astype(jnp.bfloat16)


def lag_table():
    tiles = LAGS // 2 // LAG_FINE + 1
    coarse = unit_angles(np.arange(tiles) * LAG_FINE, 1)
    angles = np.concatenate(unit_angles(np.arange(LAG_FINE), 1) + coarse, axis=1)
    return pl.pallas_call(
        table_kernel,
        out_shape=jax.ShapeDtypeStruct((2 * F, tiles * LAG_FINE), jnp.bfloat16),
        compiler_params=pltpu.CompilerParams(vmem_limit_bytes=40 * MIB),
        cost_estimate=pl.CostEstimate(flops=8 * F * tiles * LAG_FINE, bytes_accessed=4 * MIB, transcendentals=0),
    )(angles)


def make_band(filter_taps, channel_count):
    kernel = jnp.concatenate(
        [
            -filter_taps[:HALO].astype(jnp.float32),
            jnp.ones((1,), jnp.float32),
            -filter_taps[HALO:].astype(jnp.float32),
        ]
    )
    row_ids = jnp.arange(channel_count, dtype=jnp.int32)[:, None]
    columns = jnp.arange(channel_count + 2 * HALO, dtype=jnp.int32)[None, :]
    offset = columns - row_ids
    choose = offset[:, :, None] == jnp.arange(2 * HALO + 1, dtype=jnp.int32)[None, None, :]
    return jnp.sum(jnp.where(choose, kernel[None, None, :], 0.0), axis=2).astype(jnp.bfloat16)


def pick_kernel(held, across, selector, here, near, far):
    count = here.shape[1]
    for window in range(held.shape[1]):
        rows = [blocks[i, window] for blocks in (held, across) for i in range(blocks.shape[0])]
        picked = jnp.dot(selector[...], jnp.concatenate(rows, axis=0), preferred_element_type=jnp.float32)
        picked = picked.astype(jnp.bfloat16)
        here[window] = picked[:count]
        near[window] = picked[count : 2 * count]
        for at in range(far.shape[0]):
            far[at, window] = picked[(2 + at) * count : (3 + at) * count]


def pick(held, across, selector, groups):
    _, windows, _, both = held.shape
    count = selector.shape[0] // groups
    one = (windows, count, both)
    return pl.pallas_call(
        pick_kernel,
        out_shape=[jax.ShapeDtypeStruct(shape, jnp.bfloat16) for shape in (one, one, (groups - 2, *one))],
        compiler_params=pltpu.CompilerParams(vmem_limit_bytes=40 * MIB),
        cost_estimate=pl.CostEstimate(
            flops=2 * windows * selector.size * both, bytes_accessed=2 * windows * both * sum(selector.shape), transcendentals=0
        ),
    )(held, across, selector)


def swapped(value, axis, step):
    return lax.ppermute(value, axis, [(i, i ^ step) for i in range(lax.axis_size(axis))])


def after(value, earlier):
    return lax.optimization_barrier((value, earlier))[0]


def per_device(traces, filter_taps, good_channels, source_index):
    window_count, channel_count, _ = traces.shape
    good = good_channels[None, :]
    spec, head, tail = transform(traces, good)
    blocks = lax.axis_size("chan")
    groups = lax.axis_size("win")
    left = lax.ppermute(tail, "chan", [(i, i + 1) for i in range(blocks - 1)])
    right = lax.ppermute(head, "chan", [(i + 1, i) for i in range(blocks - 1)])
    table = lag_table()
    left = after(left, table)
    full, *parts = whiten(spec, left, right, make_band(filter_taps, channel_count), good)

    order = [0]
    step = blocks // 2
    while step:
        order += [place ^ step for place in order]
        step //= 2
    order = jnp.asarray(order, jnp.int32) ^ lax.axis_index("chan")
    own_ids = jnp.arange(channel_count, dtype=jnp.int32)
    channel_ids = (order[:, None] * channel_count + own_ids[None, :]).reshape(-1)
    by_group = source_index.reshape(groups, -1)
    here = lax.axis_index("win")
    wanted = jnp.concatenate([lax.dynamic_slice_in_dim(by_group, here ^ step, 1) for step in range(groups)], axis=0)
    selector = (wanted.reshape(-1)[:, None] == channel_ids[None, :]).astype(jnp.bfloat16)

    own_far = swapped(full, "win", 2)
    own_near = swapped(jnp.stack([full, own_far]), "win", 1)
    by_channel = turn_own(full, own_near, own_far)
    gathered, picked, stacked = [], [], []
    chunks = len(CHUNKS)

    def gather(part):
        held, step = part, blocks // 2
        while step > 1:
            received = swapped(held, "chan", step)
            if step > 2:
                held = jnp.concatenate([held, received], axis=1)
                if step == blocks // 2:
                    first_held.append(held)
                    if len(gathered) > 1:
                        held = after(held, picked[0][0])
            step //= 2
        gathered.extend(jnp.concatenate([held[i], received[i]], axis=0) for i in range(part.shape[0]))

    def exchange(at):
        held = after(gathered[at], picked[-1][0]) if at else gathered[at]
        across = swapped(held, "chan", 1)
        if at > 1:
            finish(at - 2)
            across = after(across, stacked[-1])
        here, near, far = pick(held, across, selector, groups)
        picked.append((here, near, swapped(far, "win", 2)))

    def finish(at):
        here, near, far = picked[at]
        near = swapped(jnp.stack([near, far[1]]), "win", 1)
        stacked.append(cross(here, near, far, by_channel, CHUNKS[at][0]))

    first_held = []
    for part in parts:
        gather(after(part, [first_held[-1]] + [own_far] * (len(first_held) > 1)) if first_held else part)
        if len(gathered) == 2:
            exchange(0)
    for at in range(1, chunks):
        exchange(at)
    for at in range(len(stacked), chunks):
        finish(at)
    return lagged(stacked, table, 1.0 / math.sqrt(F * window_count * groups))


def solution(mesh):
    placed = (P("win", "chan", None), P(), P("chan"), P())
    return jax.shard_map(
        per_device, mesh=mesh, in_specs=placed, out_specs=P("win", "chan", None), check_vma=False
    )
```

```python
import functools
import math

import jax
import jax.numpy as jnp
import numpy as np
from jax import lax
from jax.experimental import pallas as pl
from jax.experimental.pallas import tpu as pltpu
from jax.sharding import PartitionSpec as P

L = 7680
F = 512
LAGS = 2048
HALO = 16
SMOOTH = 64
K0 = 31
QUARTER = L // 4
STEP = 640
FINE = 32
CHUNKS = tuple((start, 128) for start in range(0, F, 128))
Z_GROUPS = ((0, 1), (1, 2), (2, 4))
GROUP = 16
LAG_FINE = 128
LAG_ROWS = 8
NT = (((1,), (1,)), ((), ()))
MIB = 1024 * 1024


def unit_angles(positions, axis):
    bins = K0 + np.arange(F, dtype=np.int64)
    phase = np.mod(np.expand_dims(positions, 1 - axis) * np.expand_dims(bins, axis), L)
    angles = phase * (2.0 * math.pi / L)
    return np.cos(angles).astype(np.float32), np.sin(angles).astype(np.float32)


def keep_column(good):
    count = good.shape[1]
    rows = lax.broadcasted_iota(jnp.int32, (count, count), 0)
    cols = lax.broadcasted_iota(jnp.int32, (count, count), 1)
    return jnp.sum(jnp.where(rows == cols, good[...].astype(jnp.float32), 0.0), axis=1, keepdims=True)


def transform_kernel(x0, x1, x2, x3, angles, good, spec, head, tail, table, total):
    step = pl.program_id(0)
    rows = x0.shape[0]
    coarse = QUARTER // FINE

    def fill(of_step):
        fine_cos = angles[2 * coarse : 2 * coarse + FINE, :]
        fine_sin = angles[2 * coarse + FINE :, :]
        for part in range(STEP // FINE):
            big_cos = angles[pl.ds(of_step * (STEP // FINE) + part, 1), :]
            big_sin = angles[pl.ds(coarse + of_step * (STEP // FINE) + part, 1), :]
            at = pl.ds(part * FINE, FINE)
            table[of_step % 2, at, :F] = (big_cos * fine_cos - big_sin * fine_sin).astype(jnp.bfloat16)
            table[of_step % 2, at, F:] = (-(big_sin * fine_cos + big_cos * fine_sin)).astype(jnp.bfloat16)

    @pl.when(step == 0)
    def _():
        total[...] = jnp.zeros_like(total)
        fill(step)

    for quarter, x in enumerate((x0, x1, x2, x3)):
        at = pl.ds(quarter * rows, rows)
        total[at, :] += jnp.dot(x[...], table[step % 2], preferred_element_type=jnp.float32)
    fill(jnp.minimum(step + 1, pl.num_programs(0) - 1))

    @pl.when(step == pl.num_programs(0) - 1)
    def _():
        turn = (K0 + lax.broadcasted_iota(jnp.int32, (1, F), 1)) % 4
        even = turn % 2 == 0
        sign = jnp.where(turn < 2, 1.0, -1.0)
        channels = good.shape[1]
        keep = keep_column(good)
        for window in range(rows // channels):
            re = [total[pl.ds(q * rows + window * channels, channels), :F] for q in range(4)]
            im = [total[pl.ds(q * rows + window * channels, channels), F:] for q in range(4)]
            real = jnp.where(even, re[0] + re[2] + sign * (re[1] + re[3]), re[0] - re[2] + sign * (im[1] - im[3])) * keep
            imag = jnp.where(even, im[0] + im[2] + sign * (im[1] + im[3]), im[0] - im[2] - sign * (re[1] - re[3])) * keep
            spec[window, :, :F] = real
            spec[window, :, F:] = imag
            head[window, :, :F] = real[:HALO].astype(jnp.bfloat16)
            head[window, :, F:] = imag[:HALO].astype(jnp.bfloat16)
            tail[window, :, :F] = real[channels - HALO :].astype(jnp.bfloat16)
            tail[window, :, F:] = imag[channels - HALO :].astype(jnp.bfloat16)


def transform(traces, good):
    windows, channels, length = traces.shape
    rows = windows * channels
    steps = QUARTER // STEP
    flat = traces.reshape(rows, length)
    coarse = unit_angles(np.arange(QUARTER // FINE) * FINE, 0)
    angles = np.concatenate(coarse + unit_angles(np.arange(FINE), 0), axis=0)
    whole = lambda *shape: pl.BlockSpec(shape, lambda k: (0,) * len(shape))
    return pl.pallas_call(
        transform_kernel,
        grid=(steps,),
        in_specs=[pl.BlockSpec((rows, STEP), functools.partial(lambda q, k: (0, q * steps + k), q)) for q in range(4)]
        + [whole(*angles.shape), whole(1, channels)],
        out_specs=[whole(windows, channels, 2 * F), whole(windows, HALO, 2 * F), whole(windows, HALO, 2 * F)],
        out_shape=[
            jax.ShapeDtypeStruct((windows, channels, 2 * F), jnp.float32),
            jax.ShapeDtypeStruct((windows, HALO, 2 * F), jnp.bfloat16),
            jax.ShapeDtypeStruct((windows, HALO, 2 * F), jnp.bfloat16),
        ],
        scratch_shapes=[pltpu.VMEM((2, STEP, 2 * F), jnp.bfloat16), pltpu.VMEM((4 * rows, 2 * F), jnp.float32)],
        compiler_params=pltpu.CompilerParams(vmem_limit_bytes=60 * MIB),
        cost_estimate=pl.CostEstimate(flops=2 * rows * length * 2 * F, bytes_accessed=rows * length * 2, transcendentals=0),
    )(flat, flat, flat, flat, angles, good)


def pieces(value):
    high = value.astype(jnp.bfloat16)
    rest = value - high.astype(jnp.float32)
    middle = rest.astype(jnp.bfloat16)
    return high, middle, (rest - middle.astype(jnp.float32)).astype(jnp.bfloat16)


def whiten_kernel(spec, left, right, band, good, *outs):
    windows, channels = spec.shape[:2]
    filtered = []
    keep = keep_column(good)
    for window in range(windows):
        stack = jnp.concatenate([left[window], *pieces(spec[window]), right[window]], axis=0)
        own = band[:, HALO : HALO + channels]
        taps = jnp.concatenate([band[:, :HALO], own, own, own, band[:, HALO + channels :]], axis=1)
        filtered.append(jnp.dot(taps, stack, preferred_element_type=jnp.float32) * keep)
    spectrum = jnp.concatenate(filtered, axis=0)
    real, imag = spectrum[:, :F], spectrum[:, F:]
    magnitude = jnp.sqrt(real * real + imag * imag)
    bins = lax.broadcasted_iota(jnp.int32, (F, F), 0)
    others = lax.broadcasted_iota(jnp.int32, (F, F), 1)
    near = jnp.where(jnp.abs(bins - others) <= SMOOTH, 1.0, 0.0).astype(jnp.bfloat16)
    amplitude = sum(jnp.dot(piece, near, preferred_element_type=jnp.float32) for piece in pieces(magnitude))
    bin_row = lax.broadcasted_iota(jnp.int32, (1, F), 1)
    count = jnp.minimum(bin_row + SMOOTH, F - 1) - jnp.maximum(bin_row - SMOOTH, 0) + 1
    amplitude = amplitude * (1.0 / count.astype(jnp.float32))
    inverse = 1.0 / (amplitude + 1e-06)
    real = (real * inverse).astype(jnp.bfloat16)
    imag = (imag * inverse).astype(jnp.bfloat16)
    full, *parts = outs
    for window in range(windows):
        rows = slice(window * channels, (window + 1) * channels)
        full[window, :, :F] = real[rows]
        full[window, :, F:] = imag[rows]
        for part, (begin, end) in zip(parts, Z_GROUPS):
            for at, (start, width) in enumerate(CHUNKS[begin:end]):
                part[at, 0, window, :, :width] = real[rows, start : start + width]
                part[at, 0, window, :, width:] = imag[rows, start : start + width]


def whiten(spec, left, right, band, good):
    windows, channels, _ = spec.shape
    return pl.pallas_call(
        whiten_kernel,
        out_shape=[
            jax.ShapeDtypeStruct(shape, jnp.bfloat16)
            for shape in [(windows, channels, 2 * F)]
            + [(end - begin, 1, windows, channels, 2 * CHUNKS[0][1]) for begin, end in Z_GROUPS]
        ],
        compiler_params=pltpu.CompilerParams(vmem_limit_bytes=40 * MIB),
        cost_estimate=pl.CostEstimate(flops=2 * windows * channels * F * F * 3, bytes_accessed=5 * MIB // 2, transcendentals=windows * channels * F),
    )(spec, left, right, band, good)


def eye(size):
    rows = lax.broadcasted_iota(jnp.int32, (size, size), 0)
    cols = lax.broadcasted_iota(jnp.int32, (size, size), 1)
    return jnp.where(rows == cols, 1.0, 0.0).astype(jnp.bfloat16)


def turned(left_unit, rows):
    return lax.dot_general(left_unit, rows, NT, preferred_element_type=jnp.float32)


def swapper(outer, inner):
    size = outer * inner
    rows = lax.broadcasted_iota(jnp.int32, (size, size), 0)
    cols = lax.broadcasted_iota(jnp.int32, (size, size), 1)
    return jnp.where(cols == rows % outer * inner + rows // outer, 1.0, 0.0).astype(jnp.bfloat16)


def moved(swap, rows):
    return jnp.dot(swap, rows, preferred_element_type=jnp.float32).astype(jnp.bfloat16)


def own_kernel(here, near, far, out, by_window):
    own = [here, near.at[0], far, near.at[1]]
    each, channels, _ = here.shape
    windows, quads = each * len(own), channels // 4
    joined = GROUP // each
    swap = swapper(GROUP, GROUP)
    for start in range(0, windows, GROUP):
        for channel in range(0, channels, GROUP):
            block = [o[:, channel : channel + GROUP, :] for o in own[start // each : start // each + joined]]
            rows = moved(swap, jnp.concatenate(block, axis=0).reshape(GROUP * GROUP, 2 * F))
            by_window[channel : channel + GROUP, start : start + GROUP, :] = rows.reshape(GROUP, GROUP, 2 * F)
    unit = eye(F // 2)
    for quad in range(quads):
        for start in range(0, F, F // 2):
            rows = []
            for channel in range(quad, channels, quads):
                rows += [by_window[channel, :, side + start : side + start + F // 2] for side in (0, F)]
            out[quad, start : start + F // 2, :] = turned(unit, jnp.concatenate(rows, axis=0)).astype(jnp.bfloat16)


def turn_own(here, near, far):
    each, channels, _ = here.shape
    windows = each * 4
    return pl.pallas_call(
        own_kernel,
        out_shape=jax.ShapeDtypeStruct((channels // 4, F, 8 * windows), jnp.bfloat16),
        scratch_shapes=[pltpu.VMEM((channels, windows, 2 * F), jnp.bfloat16)],
        compiler_params=pltpu.CompilerParams(vmem_limit_bytes=40 * MIB),
        cost_estimate=pl.CostEstimate(flops=2 * 8192 * 65536, bytes_accessed=4 * MIB, transcendentals=0),
    )(here, near, far)


def cross_kernel(here, near, far, by_channel, out, by_window, sums):
    sources = [here, near.at[0], far.at[0], near.at[1]]
    each, count, both = here.shape
    quads, _, wide = by_channel.shape
    channels, half = 4 * quads, wide // 4
    windows, width = half // 2, both // 2
    unit = eye(width)
    swap = swapper(GROUP, GROUP)
    swap_quads = swapper(quads, GROUP)
    for window in range(0, windows, 2):
        rows = []
        for one in range(window, window + 2):
            source = sources[one // each]
            rows += [source[one % each, :, :width], source[one % each, :, width:]]
        both_turned = turned(unit, jnp.concatenate(rows, axis=0)).astype(jnp.bfloat16)
        by_window[window] = both_turned[:, : 2 * count]
        by_window[window + 1] = both_turned[:, 2 * count :]
    first = lax.broadcasted_iota(jnp.int32, (1, 2 * half), 1) < half
    sign = jnp.where(lax.broadcasted_iota(jnp.int32, (1, 2 * count), 1) < count, 1.0, -1.0)
    empty = jnp.zeros((2 * windows, 2 * count), jnp.bfloat16)

    def one_group(group, carry):
        bins = pl.ds(pl.multiple_of(group * GROUP, GROUP), GROUP)
        rows = [
            by_window[start : start + GROUP, bins, :].reshape(GROUP * GROUP, 2 * count)
            for start in range(0, windows, GROUP)
        ]
        rights = jnp.dot(swap, jnp.concatenate(rows, axis=1), preferred_element_type=jnp.float32)
        lefts = jnp.dot(
            swap_quads, by_channel[:, bins, :].reshape(quads * GROUP, 4 * half), preferred_element_type=jnp.float32
        )
        results = []
        for at in range(0, GROUP, 2):
            two = []
            for one in range(at, at + 2):
                here = rights[one * GROUP : (one + 1) * GROUP]
                src = jnp.concatenate(
                    [here[:, i * 2 * count : (i + 1) * 2 * count] for i in range(windows // GROUP)], axis=0
                )
                two.append(jnp.concatenate([src * sign, pltpu.roll(src, count, axis=1)], axis=0).astype(jnp.bfloat16))
            right = jnp.concatenate(
                [jnp.concatenate([two[0], empty], axis=1), jnp.concatenate([empty, two[1]], axis=1)], axis=0
            )
            left = []
            for tile in range(0, 4 * half, 2 * half):
                one, other = (lefts[i * quads : (i + 1) * quads, tile : tile + 2 * half] for i in (at, at + 1))
                left.append(jnp.where(first, one, pltpu.roll(other, half, axis=1)))
                left.append(jnp.where(first, pltpu.roll(one, half, axis=1), other))
            left = jnp.concatenate(left, axis=0).astype(jnp.bfloat16)
            result = jnp.dot(left, right, preferred_element_type=jnp.float32).astype(jnp.bfloat16)
            results += [result[:, : 2 * count], result[:, 2 * count :]]
        halves = [
            jnp.concatenate([r[start : start + GROUP] for r in results], axis=0) for start in range(0, channels, GROUP)
        ]
        done = moved(swap, jnp.concatenate(halves, axis=1))
        for channel in range(channels):
            row, side = channel % GROUP, channel // GROUP
            sums[channel, bins, :] = done[
                row * GROUP : (row + 1) * GROUP, side * 2 * count : (side + 1) * 2 * count
            ]
        return carry

    lax.fori_loop(0, width // GROUP, one_group, 0, unroll=8)
    unit = eye(2 * count)
    part = 256 // LAG_ROWS
    swap = swapper(LAG_ROWS, part)
    for group in range(channels // LAG_ROWS):
        by_bin = []
        for channel in range(group * LAG_ROWS, (group + 1) * LAG_ROWS, 2):
            rows = jnp.concatenate([sums[channel], sums[channel + 1]], axis=0)
            both_turned = turned(unit, rows).astype(jnp.bfloat16)
            by_bin += [both_turned[:, :width], both_turned[:, width:]]
        for start in range(0, count, part):
            rows = jnp.concatenate(
                [
                    jnp.concatenate([b[start : start + part], b[count + start : count + start + part]], axis=1)
                    for b in by_bin
                ],
                axis=0,
            )
            rows = moved(swap, rows)
            at = slice(start * LAG_ROWS, (start + part) * LAG_ROWS)
            out[group, 0, at, :] = rows[:, :width]
            out[group, 1, at, :] = rows[:, width:]


def cross(here, near, far, by_channel, first_bin):
    each, count, both = here.shape
    quads, _, wide = by_channel.shape
    channels, windows, width = 4 * quads, wide // 8, both // 2
    return pl.pallas_call(
        cross_kernel,
        grid=(1,),
        in_specs=[pl.BlockSpec(a.shape, functools.partial(lambda n, i: (0,) * n, a.ndim)) for a in (here, near, far)]
        + [pl.BlockSpec((quads, width, wide), lambda i: (0, first_bin // width, 0))],
        out_specs=pl.BlockSpec((channels // LAG_ROWS, 2, count * LAG_ROWS, width), lambda i: (0, 0, 0, 0)),
        out_shape=jax.ShapeDtypeStruct((channels // LAG_ROWS, 2, count * LAG_ROWS, width), jnp.bfloat16),
        scratch_shapes=[
            pltpu.VMEM((windows, width, 2 * count), jnp.bfloat16),
            pltpu.VMEM((channels, width, 2 * count), jnp.bfloat16),
        ],
        compiler_params=pltpu.CompilerParams(vmem_limit_bytes=40 * MIB),
        cost_estimate=pl.CostEstimate(flops=2 * width * 36 * 65536, bytes_accessed=4 * MIB, transcendentals=0),
    )(here, near, far, by_channel)


def lag_kernel(scaling, *refs):
    *stacked, table, edge, out = refs
    count, channels, _ = out.shape
    real, imag = (jnp.concatenate([chunk[0, side] for chunk in stacked], axis=1) for side in range(2))
    size = count * channels
    lane = lax.broadcasted_iota(jnp.int32, (size, LAG_FINE), 1)
    mirror = (LAG_FINE - lane) % LAG_FINE

    def parts(start, width):
        even = jnp.dot(real, table[:F, start : start + width], preferred_element_type=jnp.float32)
        odd = jnp.dot(imag, table[F:, start : start + width], preferred_element_type=jnp.float32)
        return even, odd

    half = LAGS // 2
    products = real.astype(jnp.float32) * edge[:1] + imag.astype(jnp.float32) * edge[1:]
    above = jnp.sum(products, axis=1, keepdims=True) * scaling
    for start in range(half - 2 * LAG_FINE, -1, -2 * LAG_FINE):
        even, odd = parts(start, 2 * LAG_FINE)
        after_zero = (even - odd) * scaling
        before_zero = (even + odd) * scaling
        out[:, :, half + start : half + start + 2 * LAG_FINE] = after_zero.reshape(count, channels, 2 * LAG_FINE)
        for tile in (1, 0):
            turned_round = jnp.take_along_axis(
                before_zero[:, tile * LAG_FINE : (tile + 1) * LAG_FINE], mirror, axis=1, mode="promise_in_bounds"
            )
            at = half - start - (tile + 1) * LAG_FINE
            out[:, :, at : at + LAG_FINE] = jnp.where(lane == 0, above, turned_round).reshape(count, channels, LAG_FINE)
            above = turned_round


def lagged(stacked, table, scaling):
    groups, _, size, _ = stacked[0].shape
    edge = np.concatenate(unit_angles(np.array([LAGS // 2]), 0), axis=0).astype(jnp.bfloat16).astype(np.float32)
    count = size // LAG_ROWS
    return pl.pallas_call(
        functools.partial(lag_kernel, scaling),
        grid=(groups,),
        in_specs=[pl.BlockSpec((1, 2, size, s.shape[3]), lambda i: (i, 0, 0, 0)) for s in stacked]
        + [pl.BlockSpec(a.shape, lambda i: (0, 0)) for a in (table, edge)],
        out_specs=pl.BlockSpec((count, LAG_ROWS, LAGS), lambda i: (0, i, 0)),
        out_shape=jax.ShapeDtypeStruct((count, groups * LAG_ROWS, LAGS), jnp.float32),
        compiler_params=pltpu.CompilerParams(vmem_limit_bytes=48 * MIB),
        cost_estimate=pl.CostEstimate(
            flops=2 * groups * size * F * LAGS, bytes_accessed=groups * size * LAGS * 4, transcendentals=0
        ),
    )(*stacked, table, edge)


def table_kernel(angles, out):
    fine_cos, fine_sin = angles[:, :LAG_FINE], angles[:, LAG_FINE : 2 * LAG_FINE]
    tiles = out.shape[1] // LAG_FINE
    for tile in range(tiles):
        big_cos = angles[:, 2 * LAG_FINE + tile : 2 * LAG_FINE + tile + 1]
        big_sin = angles[:, 2 * LAG_FINE + tiles + tile : 2 * LAG_FINE + tiles + tile + 1]
        cols = slice(tile * LAG_FINE, (tile + 1) * LAG_FINE)
        out[:F, cols] = (big_cos * fine_cos - big_sin * fine_sin).astype(jnp.bfloat16)
        out[F:, cols] = (big_sin * fine_cos + big_cos * fine_sin).astype(jnp.bfloat16)


def lag_table():
    tiles = LAGS // 2 // LAG_FINE
    coarse = unit_angles(np.arange(tiles) * LAG_FINE, 1)
    angles = np.concatenate(unit_angles(np.arange(LAG_FINE), 1) + coarse, axis=1)
    return pl.pallas_call(
        table_kernel,
        out_shape=jax.ShapeDtypeStruct((2 * F, tiles * LAG_FINE), jnp.bfloat16),
        compiler_params=pltpu.CompilerParams(vmem_limit_bytes=40 * MIB),
        cost_estimate=pl.CostEstimate(flops=8 * F * tiles * LAG_FINE, bytes_accessed=4 * MIB, transcendentals=0),
    )(angles)


def make_band(filter_taps, channel_count):
    kernel = jnp.concatenate(
        [
            -filter_taps[:HALO].astype(jnp.float32),
            jnp.ones((1,), jnp.float32),
            -filter_taps[HALO:].astype(jnp.float32),
        ]
    )
    row_ids = jnp.arange(channel_count, dtype=jnp.int32)[:, None]
    columns = jnp.arange(channel_count + 2 * HALO, dtype=jnp.int32)[None, :]
    offset = columns - row_ids
    choose = offset[:, :, None] == jnp.arange(2 * HALO + 1, dtype=jnp.int32)[None, None, :]
    return jnp.sum(jnp.where(choose, kernel[None, None, :], 0.0), axis=2).astype(jnp.bfloat16)


def pick_kernel(held, across, selector, here, near, far):
    count = here.shape[1]
    for window in range(held.shape[1]):
        rows = [blocks[i, window] for blocks in (held, across) for i in range(blocks.shape[0])]
        picked = jnp.dot(selector[...], jnp.concatenate(rows, axis=0), preferred_element_type=jnp.float32)
        picked = picked.astype(jnp.bfloat16)
        here[window] = picked[:count]
        near[window] = picked[count : 2 * count]
        for at in range(far.shape[0]):
            far[at, window] = picked[(2 + at) * count : (3 + at) * count]


def pick(held, across, selector, groups):
    _, windows, _, both = held.shape
    count = selector.shape[0] // groups
    one = (windows, count, both)
    return pl.pallas_call(
        pick_kernel,
        out_shape=[jax.ShapeDtypeStruct(shape, jnp.bfloat16) for shape in (one, one, (groups - 2, *one))],
        compiler_params=pltpu.CompilerParams(vmem_limit_bytes=40 * MIB),
        cost_estimate=pl.CostEstimate(
            flops=2 * windows * selector.size * both, bytes_accessed=2 * windows * both * sum(selector.shape), transcendentals=0
        ),
    )(held, across, selector)


def swapped(value, axis, step):
    return lax.ppermute(value, axis, [(i, i ^ step) for i in range(lax.axis_size(axis))])


def after(value, earlier):
    return lax.optimization_barrier((value, earlier))[0]


def per_device(traces, filter_taps, good_channels, source_index):
    window_count, channel_count, _ = traces.shape
    good = good_channels[None, :]
    spec, head, tail = transform(traces, good)
    blocks = lax.axis_size("chan")
    groups = lax.axis_size("win")
    left = lax.ppermute(tail, "chan", [(i, i + 1) for i in range(blocks - 1)])
    right = lax.ppermute(head, "chan", [(i + 1, i) for i in range(blocks - 1)])
    table = lag_table()
    left = after(left, table)
    full, *parts = whiten(spec, left, right, make_band(filter_taps, channel_count), good)

    order = [0]
    step = blocks // 2
    while step:
        order += [place ^ step for place in order]
        step //= 2
    order = jnp.asarray(order, jnp.int32) ^ lax.axis_index("chan")
    own_ids = jnp.arange(channel_count, dtype=jnp.int32)
    channel_ids = (order[:, None] * channel_count + own_ids[None, :]).reshape(-1)
    by_group = source_index.reshape(groups, -1)
    here = lax.axis_index("win")
    wanted = jnp.concatenate([lax.dynamic_slice_in_dim(by_group, here ^ step, 1) for step in range(groups)], axis=0)
    selector = (wanted.reshape(-1)[:, None] == channel_ids[None, :]).astype(jnp.bfloat16)

    own_far = swapped(full, "win", 2)
    own_near = swapped(jnp.stack([full, own_far]), "win", 1)
    by_channel = turn_own(full, own_near, own_far)
    gathered, picked, stacked = [], [], []
    chunks = len(CHUNKS)

    def gather(part):
        held, step = part, blocks // 2
        while step > 1:
            received = swapped(held, "chan", step)
            if step > 2:
                held = jnp.concatenate([held, received], axis=1)
                if step == blocks // 2:
                    first_held.append(held)
                    if len(gathered) > 1:
                        held = after(held, picked[0][0])
            step //= 2
        gathered.extend(jnp.concatenate([held[i], received[i]], axis=0) for i in range(part.shape[0]))

    def exchange(at):
        held = after(gathered[at], picked[min(at, 2) - 1][0]) if at else gathered[at]
        across = swapped(held, "chan", 1)
        if at > 1:
            finish(at - 2)
        across = after(across, stacked[-1] if stacked else by_channel)
        here, near, far = pick(held, across, selector, groups)
        picked.append((here, near, swapped(far, "win", 2)))

    def finish(at):
        here, near, far = picked[at]
        if stacked:
            far = after(far, stacked[-1])
        near = swapped(jnp.stack([near, far[1]]), "win", 1)
        stacked.append(cross(here, near, far, by_channel, CHUNKS[at][0]))

    first_held = []
    for part in parts:
        gather(after(part, first_held[0]) if first_held else part)
        if len(gathered) == 2:
            exchange(0)
    for at in range(1, chunks):
        exchange(at)
    for at in range(len(stacked), chunks):
        finish(at)
    return lagged(stacked, table, 1.0 / math.sqrt(F * window_count * groups))


def solution(mesh):
    placed = (P("win", "chan", None), P(), P("chan"), P())
    return jax.shard_map(
        per_device, mesh=mesh, in_specs=placed, out_specs=P("win", "chan", None), check_vma=False
    )
```

```python
import functools
import math

import jax
import jax.numpy as jnp
import numpy as np
from jax import lax
from jax.experimental import pallas as pl
from jax.experimental.pallas import tpu as pltpu
from jax.sharding import PartitionSpec as P

L = 7680
F = 512
LAGS = 2048
HALO = 16
SMOOTH = 64
K0 = 31
QUARTER = L // 4
STEP = 640
FINE = 32
CHUNKS = tuple((start, 128) for start in range(0, F, 128))
Z_GROUPS = ((0, 1), (1, 2), (2, 4))
GROUP = 16
LAG_FINE = 128
LAG_ROWS = 8
NT = (((1,), (1,)), ((), ()))
MIB = 1024 * 1024


def unit_angles(positions, axis):
    bins = K0 + np.arange(F, dtype=np.int64)
    phase = np.mod(np.expand_dims(positions, 1 - axis) * np.expand_dims(bins, axis), L)
    angles = phase * (2.0 * math.pi / L)
    return np.cos(angles).astype(np.float32), np.sin(angles).astype(np.float32)


def keep_column(good):
    count = good.shape[1]
    rows = lax.broadcasted_iota(jnp.int32, (count, count), 0)
    cols = lax.broadcasted_iota(jnp.int32, (count, count), 1)
    return jnp.sum(jnp.where(rows == cols, good[...].astype(jnp.float32), 0.0), axis=1, keepdims=True)


def transform_kernel(x0, x1, x2, x3, angles, good, spec, head, tail, table, total):
    step = pl.program_id(0)
    rows = x0.shape[0]
    coarse = QUARTER // FINE

    def fill(of_step):
        fine_cos = angles[2 * coarse : 2 * coarse + FINE, :]
        fine_sin = angles[2 * coarse + FINE :, :]
        for part in range(STEP // FINE):
            big_cos = angles[pl.ds(of_step * (STEP // FINE) + part, 1), :]
            big_sin = angles[pl.ds(coarse + of_step * (STEP // FINE) + part, 1), :]
            at = pl.ds(part * FINE, FINE)
            table[of_step % 2, at, :F] = (big_cos * fine_cos - big_sin * fine_sin).astype(jnp.bfloat16)
            table[of_step % 2, at, F:] = (-(big_sin * fine_cos + big_cos * fine_sin)).astype(jnp.bfloat16)

    @pl.when(step == 0)
    def _():
        total[...] = jnp.zeros_like(total)
        fill(step)

    for quarter, x in enumerate((x0, x1, x2, x3)):
        at = pl.ds(quarter * rows, rows)
        total[at, :] += jnp.dot(x[...], table[step % 2], preferred_element_type=jnp.float32)
    fill(jnp.minimum(step + 1, pl.num_programs(0) - 1))

    @pl.when(step == pl.num_programs(0) - 1)
    def _():
        turn = (K0 + lax.broadcasted_iota(jnp.int32, (1, F), 1)) % 4
        even = turn % 2 == 0
        sign = jnp.where(turn < 2, 1.0, -1.0)
        channels = good.shape[1]
        keep = keep_column(good)
        for window in range(rows // channels):
            re = [total[pl.ds(q * rows + window * channels, channels), :F] for q in range(4)]
            im = [total[pl.ds(q * rows + window * channels, channels), F:] for q in range(4)]
            real = jnp.where(even, re[0] + re[2] + sign * (re[1] + re[3]), re[0] - re[2] + sign * (im[1] - im[3])) * keep
            imag = jnp.where(even, im[0] + im[2] + sign * (im[1] + im[3]), im[0] - im[2] - sign * (re[1] - re[3])) * keep
            spec[window, :, :F] = real
            spec[window, :, F:] = imag
            head[window, :, :F] = real[:HALO].astype(jnp.bfloat16)
            head[window, :, F:] = imag[:HALO].astype(jnp.bfloat16)
            tail[window, :, :F] = real[channels - HALO :].astype(jnp.bfloat16)
            tail[window, :, F:] = imag[channels - HALO :].astype(jnp.bfloat16)


def transform(traces, good):
    windows, channels, length = traces.shape
    rows = windows * channels
    steps = QUARTER // STEP
    flat = traces.reshape(rows, length)
    coarse = unit_angles(np.arange(QUARTER // FINE) * FINE, 0)
    angles = np.concatenate(coarse + unit_angles(np.arange(FINE), 0), axis=0)
    whole = lambda *shape: pl.BlockSpec(shape, lambda k: (0,) * len(shape))
    return pl.pallas_call(
        transform_kernel,
        grid=(steps,),
        in_specs=[pl.BlockSpec((rows, STEP), functools.partial(lambda q, k: (0, q * steps + k), q)) for q in range(4)]
        + [whole(*angles.shape), whole(1, channels)],
        out_specs=[whole(windows, channels, 2 * F), whole(windows, HALO, 2 * F), whole(windows, HALO, 2 * F)],
        out_shape=[
            jax.ShapeDtypeStruct((windows, channels, 2 * F), jnp.float32),
            jax.ShapeDtypeStruct((windows, HALO, 2 * F), jnp.bfloat16),
            jax.ShapeDtypeStruct((windows, HALO, 2 * F), jnp.bfloat16),
        ],
        scratch_shapes=[pltpu.VMEM((2, STEP, 2 * F), jnp.bfloat16), pltpu.VMEM((4 * rows, 2 * F), jnp.float32)],
        compiler_params=pltpu.CompilerParams(vmem_limit_bytes=60 * MIB),
        cost_estimate=pl.CostEstimate(flops=2 * rows * length * 2 * F, bytes_accessed=rows * length * 2, transcendentals=0),
    )(flat, flat, flat, flat, angles, good)


def pieces(value):
    high = value.astype(jnp.bfloat16)
    rest = value - high.astype(jnp.float32)
    middle = rest.astype(jnp.bfloat16)
    return high, middle, (rest - middle.astype(jnp.float32)).astype(jnp.bfloat16)


def whiten_kernel(spec, left, right, band, good, *outs):
    windows, channels = spec.shape[:2]
    filtered = []
    keep = keep_column(good)
    for window in range(windows):
        stack = jnp.concatenate([left[window], *pieces(spec[window]), right[window]], axis=0)
        own = band[:, HALO : HALO + channels]
        taps = jnp.concatenate([band[:, :HALO], own, own, own, band[:, HALO + channels :]], axis=1)
        filtered.append(jnp.dot(taps, stack, preferred_element_type=jnp.float32) * keep)
    spectrum = jnp.concatenate(filtered, axis=0)
    real, imag = spectrum[:, :F], spectrum[:, F:]
    magnitude = jnp.sqrt(real * real + imag * imag)
    bins = lax.broadcasted_iota(jnp.int32, (F, F), 0)
    others = lax.broadcasted_iota(jnp.int32, (F, F), 1)
    near = jnp.where(jnp.abs(bins - others) <= SMOOTH, 1.0, 0.0).astype(jnp.bfloat16)
    amplitude = sum(jnp.dot(piece, near, preferred_element_type=jnp.float32) for piece in pieces(magnitude))
    bin_row = lax.broadcasted_iota(jnp.int32, (1, F), 1)
    count = jnp.minimum(bin_row + SMOOTH, F - 1) - jnp.maximum(bin_row - SMOOTH, 0) + 1
    amplitude = amplitude * (1.0 / count.astype(jnp.float32))
    inverse = 1.0 / (amplitude + 1e-06)
    real = (real * inverse).astype(jnp.bfloat16)
    imag = (imag * inverse).astype(jnp.bfloat16)
    full, *parts = outs
    for window in range(windows):
        rows = slice(window * channels, (window + 1) * channels)
        full[window, :, :F] = real[rows]
        full[window, :, F:] = imag[rows]
        for part, (begin, end) in zip(parts, Z_GROUPS):
            for at, (start, width) in enumerate(CHUNKS[begin:end]):
                part[at, 0, window, :, :width] = real[rows, start : start + width]
                part[at, 0, window, :, width:] = imag[rows, start : start + width]


def whiten(spec, left, right, band, good):
    windows, channels, _ = spec.shape
    return pl.pallas_call(
        whiten_kernel,
        out_shape=[
            jax.ShapeDtypeStruct(shape, jnp.bfloat16)
            for shape in [(windows, channels, 2 * F)]
            + [(end - begin, 1, windows, channels, 2 * CHUNKS[0][1]) for begin, end in Z_GROUPS]
        ],
        compiler_params=pltpu.CompilerParams(vmem_limit_bytes=40 * MIB),
        cost_estimate=pl.CostEstimate(flops=2 * windows * channels * F * F * 3, bytes_accessed=5 * MIB // 2, transcendentals=windows * channels * F),
    )(spec, left, right, band, good)


def eye(size):
    rows = lax.broadcasted_iota(jnp.int32, (size, size), 0)
    cols = lax.broadcasted_iota(jnp.int32, (size, size), 1)
    return jnp.where(rows == cols, 1.0, 0.0).astype(jnp.bfloat16)


def turned(left_unit, rows):
    return lax.dot_general(left_unit, rows, NT, preferred_element_type=jnp.float32)


def swapper(outer, inner):
    size = outer * inner
    rows = lax.broadcasted_iota(jnp.int32, (size, size), 0)
    cols = lax.broadcasted_iota(jnp.int32, (size, size), 1)
    return jnp.where(cols == rows % outer * inner + rows // outer, 1.0, 0.0).astype(jnp.bfloat16)


def moved(swap, rows):
    return jnp.dot(swap, rows, preferred_element_type=jnp.float32).astype(jnp.bfloat16)


def own_kernel(here, near, far, out, by_window):
    own = [here, near.at[0], far, near.at[1]]
    each, channels, _ = here.shape
    windows, quads = each * len(own), channels // 4
    joined = GROUP // each
    swap = swapper(GROUP, GROUP)
    for start in range(0, windows, GROUP):
        for channel in range(0, channels, GROUP):
            block = [o[:, channel : channel + GROUP, :] for o in own[start // each : start // each + joined]]
            rows = moved(swap, jnp.concatenate(block, axis=0).reshape(GROUP * GROUP, 2 * F))
            by_window[channel : channel + GROUP, start : start + GROUP, :] = rows.reshape(GROUP, GROUP, 2 * F)
    unit = eye(F // 2)
    for quad in range(quads):
        for start in range(0, F, F // 2):
            rows = []
            for channel in range(quad, channels, quads):
                rows += [by_window[channel, :, side + start : side + start + F // 2] for side in (0, F)]
            out[quad, start : start + F // 2, :] = turned(unit, jnp.concatenate(rows, axis=0)).astype(jnp.bfloat16)


def turn_own(here, near, far):
    each, channels, _ = here.shape
    windows = each * 4
    return pl.pallas_call(
        own_kernel,
        out_shape=jax.ShapeDtypeStruct((channels // 4, F, 8 * windows), jnp.bfloat16),
        scratch_shapes=[pltpu.VMEM((channels, windows, 2 * F), jnp.bfloat16)],
        compiler_params=pltpu.CompilerParams(vmem_limit_bytes=40 * MIB),
        cost_estimate=pl.CostEstimate(flops=2 * 8192 * 65536, bytes_accessed=4 * MIB, transcendentals=0),
    )(here, near, far)


def cross_kernel(here, near, far, by_channel, out, by_window, sums):
    sources = [here, near.at[0], far.at[0], near.at[1]]
    each, count, both = here.shape
    quads, _, wide = by_channel.shape
    channels, half = 4 * quads, wide // 4
    windows, width = half // 2, both // 2
    unit = eye(width)
    swap = swapper(GROUP, GROUP)
    swap_quads = swapper(quads, GROUP)
    for window in range(0, windows, 2):
        rows = []
        for one in range(window, window + 2):
            source = sources[one // each]
            rows += [source[one % each, :, :width], source[one % each, :, width:]]
        both_turned = turned(unit, jnp.concatenate(rows, axis=0)).astype(jnp.bfloat16)
        by_window[window] = both_turned[:, : 2 * count]
        by_window[window + 1] = both_turned[:, 2 * count :]
    first = lax.broadcasted_iota(jnp.int32, (1, 2 * half), 1) < half
    sign = jnp.where(lax.broadcasted_iota(jnp.int32, (1, 2 * count), 1) < count, 1.0, -1.0)
    empty = jnp.zeros((2 * windows, 2 * count), jnp.bfloat16)

    def one_group(group, carry):
        bins = pl.ds(pl.multiple_of(group * GROUP, GROUP), GROUP)
        rows = [
            by_window[start : start + GROUP, bins, :].reshape(GROUP * GROUP, 2 * count)
            for start in range(0, windows, GROUP)
        ]
        rights = jnp.dot(swap, jnp.concatenate(rows, axis=1), preferred_element_type=jnp.float32)
        lefts = jnp.dot(
            swap_quads, by_channel[:, bins, :].reshape(quads * GROUP, 4 * half), preferred_element_type=jnp.float32
        )
        results = []
        for at in range(0, GROUP, 2):
            two = []
            for one in range(at, at + 2):
                here = rights[one * GROUP : (one + 1) * GROUP]
                src = jnp.concatenate(
                    [here[:, i * 2 * count : (i + 1) * 2 * count] for i in range(windows // GROUP)], axis=0
                )
                two.append(jnp.concatenate([src * sign, pltpu.roll(src, count, axis=1)], axis=0).astype(jnp.bfloat16))
            right = jnp.concatenate(
                [jnp.concatenate([two[0], empty], axis=1), jnp.concatenate([empty, two[1]], axis=1)], axis=0
            )
            left = []
            for tile in range(0, 4 * half, 2 * half):
                one, other = (lefts[i * quads : (i + 1) * quads, tile : tile + 2 * half] for i in (at, at + 1))
                left.append(jnp.where(first, one, pltpu.roll(other, half, axis=1)))
                left.append(jnp.where(first, pltpu.roll(one, half, axis=1), other))
            left = jnp.concatenate(left, axis=0).astype(jnp.bfloat16)
            result = jnp.dot(left, right, preferred_element_type=jnp.float32).astype(jnp.bfloat16)
            results += [result[:, : 2 * count], result[:, 2 * count :]]
        halves = [
            jnp.concatenate([r[start : start + GROUP] for r in results], axis=0) for start in range(0, channels, GROUP)
        ]
        done = moved(swap, jnp.concatenate(halves, axis=1))
        for channel in range(channels):
            row, side = channel % GROUP, channel // GROUP
            sums[channel, bins, :] = done[
                row * GROUP : (row + 1) * GROUP, side * 2 * count : (side + 1) * 2 * count
            ]
        return carry

    lax.fori_loop(0, width // GROUP, one_group, 0, unroll=8)
    unit = eye(2 * count)
    part = 256 // LAG_ROWS
    swap = swapper(LAG_ROWS, part)
    for group in range(channels // LAG_ROWS):
        by_bin = []
        for channel in range(group * LAG_ROWS, (group + 1) * LAG_ROWS, 2):
            rows = jnp.concatenate([sums[channel], sums[channel + 1]], axis=0)
            both_turned = turned(unit, rows).astype(jnp.bfloat16)
            by_bin += [both_turned[:, :width], both_turned[:, width:]]
        for start in range(0, count, part):
            rows = jnp.concatenate(
                [
                    jnp.concatenate([b[start : start + part], b[count + start : count + start + part]], axis=1)
                    for b in by_bin
                ],
                axis=0,
            )
            rows = moved(swap, rows)
            at = slice(start * LAG_ROWS, (start + part) * LAG_ROWS)
            out[group, 0, at, :] = rows[:, :width]
            out[group, 1, at, :] = rows[:, width:]


def cross(here, near, far, by_channel, first_bin):
    each, count, both = here.shape
    quads, _, wide = by_channel.shape
    channels, windows, width = 4 * quads, wide // 8, both // 2
    return pl.pallas_call(
        cross_kernel,
        grid=(1,),
        in_specs=[pl.BlockSpec(a.shape, functools.partial(lambda n, i: (0,) * n, a.ndim)) for a in (here, near, far)]
        + [pl.BlockSpec((quads, width, wide), lambda i: (0, first_bin // width, 0))],
        out_specs=pl.BlockSpec((channels // LAG_ROWS, 2, count * LAG_ROWS, width), lambda i: (0, 0, 0, 0)),
        out_shape=jax.ShapeDtypeStruct((channels // LAG_ROWS, 2, count * LAG_ROWS, width), jnp.bfloat16),
        scratch_shapes=[
            pltpu.VMEM((windows, width, 2 * count), jnp.bfloat16),
            pltpu.VMEM((channels, width, 2 * count), jnp.bfloat16),
        ],
        compiler_params=pltpu.CompilerParams(vmem_limit_bytes=40 * MIB),
        cost_estimate=pl.CostEstimate(flops=2 * width * 36 * 65536, bytes_accessed=4 * MIB, transcendentals=0),
    )(here, near, far, by_channel)


def lag_kernel(scaling, *refs):
    *stacked, table, edge, out = refs
    count, channels, _ = out.shape
    real, imag = (jnp.concatenate([chunk[0, side] for chunk in stacked], axis=1) for side in range(2))
    size = count * channels
    lane = lax.broadcasted_iota(jnp.int32, (size, LAG_FINE), 1)
    mirror = (LAG_FINE - lane) % LAG_FINE

    def parts(start, width):
        even = jnp.dot(real, table[:F, start : start + width], preferred_element_type=jnp.float32)
        odd = jnp.dot(imag, table[F:, start : start + width], preferred_element_type=jnp.float32)
        return even, odd

    half = LAGS // 2
    products = real.astype(jnp.float32) * edge[:1] + imag.astype(jnp.float32) * edge[1:]
    above = jnp.sum(products, axis=1, keepdims=True) * scaling
    for start in range(half - 2 * LAG_FINE, -1, -2 * LAG_FINE):
        even, odd = parts(start, 2 * LAG_FINE)
        after_zero = (even - odd) * scaling
        before_zero = (even + odd) * scaling
        out[:, :, half + start : half + start + 2 * LAG_FINE] = after_zero.reshape(count, channels, 2 * LAG_FINE)
        for tile in (1, 0):
            turned_round = jnp.take_along_axis(
                before_zero[:, tile * LAG_FINE : (tile + 1) * LAG_FINE], mirror, axis=1, mode="promise_in_bounds"
            )
            at = half - start - (tile + 1) * LAG_FINE
            out[:, :, at : at + LAG_FINE] = jnp.where(lane == 0, above, turned_round).reshape(count, channels, LAG_FINE)
            above = turned_round


def lagged(stacked, table, scaling):
    groups, _, size, _ = stacked[0].shape
    edge = np.concatenate(unit_angles(np.array([LAGS // 2]), 0), axis=0).astype(jnp.bfloat16).astype(np.float32)
    count = size // LAG_ROWS
    return pl.pallas_call(
        functools.partial(lag_kernel, scaling),
        grid=(groups,),
        in_specs=[pl.BlockSpec((1, 2, size, s.shape[3]), lambda i: (i, 0, 0, 0)) for s in stacked]
        + [pl.BlockSpec(a.shape, lambda i: (0, 0)) for a in (table, edge)],
        out_specs=pl.BlockSpec((count, LAG_ROWS, LAGS), lambda i: (0, i, 0)),
        out_shape=jax.ShapeDtypeStruct((count, groups * LAG_ROWS, LAGS), jnp.float32),
        compiler_params=pltpu.CompilerParams(vmem_limit_bytes=48 * MIB),
        cost_estimate=pl.CostEstimate(
            flops=2 * groups * size * F * LAGS, bytes_accessed=groups * size * LAGS * 4, transcendentals=0
        ),
    )(*stacked, table, edge)


def table_kernel(angles, out):
    fine_cos, fine_sin = angles[:, :LAG_FINE], angles[:, LAG_FINE : 2 * LAG_FINE]
    tiles = out.shape[1] // LAG_FINE
    for tile in range(tiles):
        big_cos = angles[:, 2 * LAG_FINE + tile : 2 * LAG_FINE + tile + 1]
        big_sin = angles[:, 2 * LAG_FINE + tiles + tile : 2 * LAG_FINE + tiles + tile + 1]
        cols = slice(tile * LAG_FINE, (tile + 1) * LAG_FINE)
        out[:F, cols] = (big_cos * fine_cos - big_sin * fine_sin).astype(jnp.bfloat16)
        out[F:, cols] = (big_sin * fine_cos + big_cos * fine_sin).astype(jnp.bfloat16)


def lag_table():
    tiles = LAGS // 2 // LAG_FINE
    coarse = unit_angles(np.arange(tiles) * LAG_FINE, 1)
    angles = np.concatenate(unit_angles(np.arange(LAG_FINE), 1) + coarse, axis=1)
    return pl.pallas_call(
        table_kernel,
        out_shape=jax.ShapeDtypeStruct((2 * F, tiles * LAG_FINE), jnp.bfloat16),
        compiler_params=pltpu.CompilerParams(vmem_limit_bytes=40 * MIB),
        cost_estimate=pl.CostEstimate(flops=8 * F * tiles * LAG_FINE, bytes_accessed=4 * MIB, transcendentals=0),
    )(angles)


def make_band(filter_taps, channel_count):
    kernel = jnp.concatenate(
        [
            -filter_taps[:HALO].astype(jnp.float32),
            jnp.ones((1,), jnp.float32),
            -filter_taps[HALO:].astype(jnp.float32),
        ]
    )
    row_ids = jnp.arange(channel_count, dtype=jnp.int32)[:, None]
    columns = jnp.arange(channel_count + 2 * HALO, dtype=jnp.int32)[None, :]
    offset = columns - row_ids
    choose = offset[:, :, None] == jnp.arange(2 * HALO + 1, dtype=jnp.int32)[None, None, :]
    return jnp.sum(jnp.where(choose, kernel[None, None, :], 0.0), axis=2).astype(jnp.bfloat16)


def pick_kernel(held, across, selector, here, near, far):
    count = here.shape[1]
    for window in range(held.shape[1]):
        rows = [blocks[i, window] for blocks in (held, across) for i in range(blocks.shape[0])]
        picked = jnp.dot(selector[...], jnp.concatenate(rows, axis=0), preferred_element_type=jnp.float32)
        picked = picked.astype(jnp.bfloat16)
        here[window] = picked[:count]
        near[window] = picked[count : 2 * count]
        for at in range(far.shape[0]):
            far[at, window] = picked[(2 + at) * count : (3 + at) * count]


def pick(held, across, selector, groups):
    _, windows, _, both = held.shape
    count = selector.shape[0] // groups
    one = (windows, count, both)
    return pl.pallas_call(
        pick_kernel,
        out_shape=[jax.ShapeDtypeStruct(shape, jnp.bfloat16) for shape in (one, one, (groups - 2, *one))],
        compiler_params=pltpu.CompilerParams(vmem_limit_bytes=40 * MIB),
        cost_estimate=pl.CostEstimate(
            flops=2 * windows * selector.size * both, bytes_accessed=2 * windows * both * sum(selector.shape), transcendentals=0
        ),
    )(held, across, selector)


def swapped(value, axis, step):
    return lax.ppermute(value, axis, [(i, i ^ step) for i in range(lax.axis_size(axis))])


def after(value, earlier):
    return lax.optimization_barrier((value, earlier))[0]


def per_device(traces, filter_taps, good_channels, source_index):
    window_count, channel_count, _ = traces.shape
    good = good_channels[None, :]
    spec, head, tail = transform(traces, good)
    blocks = lax.axis_size("chan")
    groups = lax.axis_size("win")
    left = lax.ppermute(tail, "chan", [(i, i + 1) for i in range(blocks - 1)])
    right = lax.ppermute(head, "chan", [(i + 1, i) for i in range(blocks - 1)])
    table = lag_table()
    left = after(left, table)
    full, *parts = whiten(spec, left, right, make_band(filter_taps, channel_count), good)

    order = [0]
    step = blocks // 2
    while step:
        order += [place ^ step for place in order]
        step //= 2
    order = jnp.asarray(order, jnp.int32) ^ lax.axis_index("chan")
    own_ids = jnp.arange(channel_count, dtype=jnp.int32)
    channel_ids = (order[:, None] * channel_count + own_ids[None, :]).reshape(-1)
    by_group = source_index.reshape(groups, -1)
    here = lax.axis_index("win")
    wanted = jnp.concatenate([lax.dynamic_slice_in_dim(by_group, here ^ step, 1) for step in range(groups)], axis=0)
    selector = (wanted.reshape(-1)[:, None] == channel_ids[None, :]).astype(jnp.bfloat16)

    own_far = swapped(full, "win", 2)
    own_near = swapped(jnp.stack([full, own_far]), "win", 1)
    by_channel = turn_own(full, own_near, own_far)
    gathered, picked, stacked = [], [], []
    chunks = len(CHUNKS)

    def gather(part):
        held, step = part, blocks // 2
        while step > 1:
            received = swapped(held, "chan", step)
            if step > 2:
                held = jnp.concatenate([held, received], axis=1)
                if step == blocks // 2:
                    first_held.append(held)
                    if len(gathered) > 1:
                        held = after(held, picked[0][0])
            step //= 2
        gathered.extend(jnp.concatenate([held[i], received[i]], axis=0) for i in range(part.shape[0]))

    def exchange(at):
        held = after(gathered[at], picked[-1][0]) if at else gathered[at]
        across = swapped(held, "chan", 1)
        if at > 1:
            finish(at - 2)
        if at:
            across = after(across, stacked[-1] if stacked else by_channel)
        here, near, far = pick(held, across, selector, groups)
        picked.append((here, near, swapped(far, "win", 2)))

    def finish(at):
        here, near, far = picked[at]
        if stacked:
            far = after(far, stacked[-1])
        near = swapped(jnp.stack([near, far[1]]), "win", 1)
        stacked.append(cross(here, near, far, by_channel, CHUNKS[at][0]))

    first_held = []
    for part in parts:
        gather(after(part, [first_held[-1]] + [own_far] * (len(first_held) > 1)) if first_held else part)
        if len(gathered) == 2:
            exchange(0)
    for at in range(1, chunks):
        exchange(at)
    for at in range(len(stacked), chunks):
        finish(at)
    return lagged(stacked, table, 1.0 / math.sqrt(F * window_count * groups))


def solution(mesh):
    placed = (P("win", "chan", None), P(), P("chan"), P())
    return jax.shard_map(
        per_device, mesh=mesh, in_specs=placed, out_specs=P("win", "chan", None), check_vma=False
    )
```

```python
import functools
import math

import jax
import jax.numpy as jnp
import numpy as np
from jax import lax
from jax.experimental import pallas as pl
from jax.experimental.pallas import tpu as pltpu
from jax.sharding import PartitionSpec as P

L = 7680
F = 512
LAGS = 2048
HALO = 16
SMOOTH = 64
K0 = 31
QUARTER = L // 4
STEP = 640
FINE = 32
CHUNKS = tuple((start, 128) for start in range(0, F, 128))
Z_GROUPS = ((0, 1), (1, 2), (2, 4))
GROUP = 16
LAG_FINE = 128
LAG_ROWS = 8
NT = (((1,), (1,)), ((), ()))
MIB = 1024 * 1024


def unit_angles(positions, axis, first_bin=0, count=F):
    bins = K0 + first_bin + np.arange(count, dtype=np.int64)
    phase = np.mod(np.expand_dims(positions, 1 - axis) * np.expand_dims(bins, axis), L)
    angles = phase * (2.0 * math.pi / L)
    return np.cos(angles).astype(np.float32), np.sin(angles).astype(np.float32)


def keep_column(good):
    count = good.shape[1]
    rows = lax.broadcasted_iota(jnp.int32, (count, count), 0)
    cols = lax.broadcasted_iota(jnp.int32, (count, count), 1)
    return jnp.sum(jnp.where(rows == cols, good[...].astype(jnp.float32), 0.0), axis=1, keepdims=True)


def transform_kernel(first_bin, x0, x1, x2, x3, angles, good, spec, head, tail, table, total):
    step = pl.program_id(0)
    rows = x0.shape[0]
    coarse = QUARTER // FINE
    width = angles.shape[1]

    def fill(of_step):
        fine_cos = angles[2 * coarse : 2 * coarse + FINE, :]
        fine_sin = angles[2 * coarse + FINE :, :]
        for part in range(STEP // FINE):
            big_cos = angles[pl.ds(of_step * (STEP // FINE) + part, 1), :]
            big_sin = angles[pl.ds(coarse + of_step * (STEP // FINE) + part, 1), :]
            at = pl.ds(part * FINE, FINE)
            table[of_step % 2, at, :width] = (big_cos * fine_cos - big_sin * fine_sin).astype(jnp.bfloat16)
            table[of_step % 2, at, width:] = (-(big_sin * fine_cos + big_cos * fine_sin)).astype(jnp.bfloat16)

    @pl.when(step == 0)
    def _():
        total[...] = jnp.zeros_like(total)
        fill(step)

    for quarter, x in enumerate((x0, x1, x2, x3)):
        at = pl.ds(quarter * rows, rows)
        total[at, :] += jnp.dot(x[...], table[step % 2], preferred_element_type=jnp.float32)
    fill(jnp.minimum(step + 1, pl.num_programs(0) - 1))

    @pl.when(step == pl.num_programs(0) - 1)
    def _():
        turn = (K0 + first_bin + lax.broadcasted_iota(jnp.int32, (1, width), 1)) % 4
        even = turn % 2 == 0
        sign = jnp.where(turn < 2, 1.0, -1.0)
        channels = good.shape[1]
        keep = keep_column(good)
        for window in range(rows // channels):
            re = [total[pl.ds(q * rows + window * channels, channels), :width] for q in range(4)]
            im = [total[pl.ds(q * rows + window * channels, channels), width:] for q in range(4)]
            real = jnp.where(even, re[0] + re[2] + sign * (re[1] + re[3]), re[0] - re[2] + sign * (im[1] - im[3])) * keep
            imag = jnp.where(even, im[0] + im[2] + sign * (im[1] + im[3]), im[0] - im[2] - sign * (re[1] - re[3])) * keep
            spec[window, :, :width] = real
            spec[window, :, width:] = imag
            head[window, :, :width] = real[:HALO].astype(jnp.bfloat16)
            head[window, :, width:] = imag[:HALO].astype(jnp.bfloat16)
            tail[window, :, :width] = real[channels - HALO :].astype(jnp.bfloat16)
            tail[window, :, width:] = imag[channels - HALO :].astype(jnp.bfloat16)


def transform(traces, good, first_bin, width):
    windows, channels, length = traces.shape
    rows = windows * channels
    steps = QUARTER // STEP
    flat = traces.reshape(rows, length)
    coarse = unit_angles(np.arange(QUARTER // FINE) * FINE, 0, first_bin, width)
    angles = np.concatenate(coarse + unit_angles(np.arange(FINE), 0, first_bin, width), axis=0)
    whole = lambda *shape: pl.BlockSpec(shape, lambda k: (0,) * len(shape))
    return pl.pallas_call(
        functools.partial(transform_kernel, first_bin),
        grid=(steps,),
        in_specs=[pl.BlockSpec((rows, STEP), functools.partial(lambda q, k: (0, q * steps + k), q)) for q in range(4)]
        + [whole(*angles.shape), whole(1, channels)],
        out_specs=[whole(windows, channels, 2 * width), whole(windows, HALO, 2 * width), whole(windows, HALO, 2 * width)],
        out_shape=[
            jax.ShapeDtypeStruct((windows, channels, 2 * width), jnp.float32),
            jax.ShapeDtypeStruct((windows, HALO, 2 * width), jnp.bfloat16),
            jax.ShapeDtypeStruct((windows, HALO, 2 * width), jnp.bfloat16),
        ],
        scratch_shapes=[pltpu.VMEM((2, STEP, 2 * width), jnp.bfloat16), pltpu.VMEM((4 * rows, 2 * width), jnp.float32)],
        compiler_params=pltpu.CompilerParams(vmem_limit_bytes=60 * MIB),
        cost_estimate=pl.CostEstimate(flops=2 * rows * length * 2 * width, bytes_accessed=rows * length * 2, transcendentals=0),
    )(flat, flat, flat, flat, angles, good)


def pieces(value):
    high = value.astype(jnp.bfloat16)
    rest = value - high.astype(jnp.float32)
    middle = rest.astype(jnp.bfloat16)
    return high, middle, (rest - middle.astype(jnp.float32)).astype(jnp.bfloat16)


def whiten_kernel(halves, *refs):
    inputs, band, good, outs = refs[: 3 * halves], refs[3 * halves], refs[3 * halves + 1], refs[3 * halves + 2 :]
    windows, channels, both = inputs[0].shape
    keep = keep_column(good)
    real, imag = [], []
    for spec, left, right in zip(inputs[::3], inputs[1::3], inputs[2::3]):
        filtered = []
        for window in range(windows):
            stack = jnp.concatenate([left[window], *pieces(spec[window]), right[window]], axis=0)
            own = band[:, HALO : HALO + channels]
            taps = jnp.concatenate([band[:, :HALO], own, own, own, band[:, HALO + channels :]], axis=1)
            filtered.append(jnp.dot(taps, stack, preferred_element_type=jnp.float32) * keep)
        spectrum = jnp.concatenate(filtered, axis=0)
        real.append(spectrum[:, : both // 2])
        imag.append(spectrum[:, both // 2 :])
    real, imag = jnp.concatenate(real, axis=1), jnp.concatenate(imag, axis=1)
    magnitude = jnp.sqrt(real * real + imag * imag)
    bins = lax.broadcasted_iota(jnp.int32, (F, F), 0)
    others = lax.broadcasted_iota(jnp.int32, (F, F), 1)
    near = jnp.where(jnp.abs(bins - others) <= SMOOTH, 1.0, 0.0).astype(jnp.bfloat16)
    amplitude = sum(jnp.dot(piece, near, preferred_element_type=jnp.float32) for piece in pieces(magnitude))
    bin_row = lax.broadcasted_iota(jnp.int32, (1, F), 1)
    count = jnp.minimum(bin_row + SMOOTH, F - 1) - jnp.maximum(bin_row - SMOOTH, 0) + 1
    amplitude = amplitude * (1.0 / count.astype(jnp.float32))
    inverse = 1.0 / (amplitude + 1e-06)
    real = (real * inverse).astype(jnp.bfloat16)
    imag = (imag * inverse).astype(jnp.bfloat16)
    full, *parts = outs
    for window in range(windows):
        rows = slice(window * channels, (window + 1) * channels)
        full[window, :, :F] = real[rows]
        full[window, :, F:] = imag[rows]
        for part, (begin, end) in zip(parts, Z_GROUPS):
            for at, (start, width) in enumerate(CHUNKS[begin:end]):
                part[at, 0, window, :, :width] = real[rows, start : start + width]
                part[at, 0, window, :, width:] = imag[rows, start : start + width]


def whiten(halves, band, good):
    windows, channels, _ = halves[0][0].shape
    return pl.pallas_call(
        functools.partial(whiten_kernel, len(halves)),
        out_shape=[
            jax.ShapeDtypeStruct(shape, jnp.bfloat16)
            for shape in [(windows, channels, 2 * F)]
            + [(end - begin, 1, windows, channels, 2 * CHUNKS[0][1]) for begin, end in Z_GROUPS]
        ],
        compiler_params=pltpu.CompilerParams(vmem_limit_bytes=40 * MIB),
        cost_estimate=pl.CostEstimate(flops=2 * windows * channels * F * F * 3, bytes_accessed=5 * MIB // 2, transcendentals=windows * channels * F),
    )(*[array for half in halves for array in half], band, good)


def eye(size):
    rows = lax.broadcasted_iota(jnp.int32, (size, size), 0)
    cols = lax.broadcasted_iota(jnp.int32, (size, size), 1)
    return jnp.where(rows == cols, 1.0, 0.0).astype(jnp.bfloat16)


def turned(left_unit, rows):
    return lax.dot_general(left_unit, rows, NT, preferred_element_type=jnp.float32)


def swapper(outer, inner):
    size = outer * inner
    rows = lax.broadcasted_iota(jnp.int32, (size, size), 0)
    cols = lax.broadcasted_iota(jnp.int32, (size, size), 1)
    return jnp.where(cols == rows % outer * inner + rows // outer, 1.0, 0.0).astype(jnp.bfloat16)


def moved(swap, rows):
    return jnp.dot(swap, rows, preferred_element_type=jnp.float32).astype(jnp.bfloat16)


def own_kernel(here, near, far, out, by_window):
    own = [here, near.at[0], far, near.at[1]]
    each, channels, _ = here.shape
    windows, quads = each * len(own), channels // 4
    joined = GROUP // each
    swap = swapper(GROUP, GROUP)
    for start in range(0, windows, GROUP):
        for channel in range(0, channels, GROUP):
            block = [o[:, channel : channel + GROUP, :] for o in own[start // each : start // each + joined]]
            rows = moved(swap, jnp.concatenate(block, axis=0).reshape(GROUP * GROUP, 2 * F))
            by_window[channel : channel + GROUP, start : start + GROUP, :] = rows.reshape(GROUP, GROUP, 2 * F)
    unit = eye(F // 2)
    for quad in range(quads):
        for start in range(0, F, F // 2):
            rows = []
            for channel in range(quad, channels, quads):
                rows += [by_window[channel, :, side + start : side + start + F // 2] for side in (0, F)]
            out[quad, start : start + F // 2, :] = turned(unit, jnp.concatenate(rows, axis=0)).astype(jnp.bfloat16)


def turn_own(here, near, far):
    each, channels, _ = here.shape
    windows = each * 4
    return pl.pallas_call(
        own_kernel,
        out_shape=jax.ShapeDtypeStruct((channels // 4, F, 8 * windows), jnp.bfloat16),
        scratch_shapes=[pltpu.VMEM((channels, windows, 2 * F), jnp.bfloat16)],
        compiler_params=pltpu.CompilerParams(vmem_limit_bytes=40 * MIB),
        cost_estimate=pl.CostEstimate(flops=2 * 8192 * 65536, bytes_accessed=4 * MIB, transcendentals=0),
    )(here, near, far)


def cross_kernel(here, near, far, by_channel, out, by_window, sums):
    sources = [here, near.at[0], far.at[0], near.at[1]]
    each, count, both = here.shape
    quads, _, wide = by_channel.shape
    channels, half = 4 * quads, wide // 4
    windows, width = half // 2, both // 2
    unit = eye(width)
    swap = swapper(GROUP, GROUP)
    swap_quads = swapper(quads, GROUP)
    for window in range(0, windows, 2):
        rows = []
        for one in range(window, window + 2):
            source = sources[one // each]
            rows += [source[one % each, :, :width], source[one % each, :, width:]]
        both_turned = turned(unit, jnp.concatenate(rows, axis=0)).astype(jnp.bfloat16)
        by_window[window] = both_turned[:, : 2 * count]
        by_window[window + 1] = both_turned[:, 2 * count :]
    first = lax.broadcasted_iota(jnp.int32, (1, 2 * half), 1) < half
    sign = jnp.where(lax.broadcasted_iota(jnp.int32, (1, 2 * count), 1) < count, 1.0, -1.0)
    empty = jnp.zeros((2 * windows, 2 * count), jnp.bfloat16)

    def one_group(group, carry):
        bins = pl.ds(pl.multiple_of(group * GROUP, GROUP), GROUP)
        rows = [
            by_window[start : start + GROUP, bins, :].reshape(GROUP * GROUP, 2 * count)
            for start in range(0, windows, GROUP)
        ]
        rights = jnp.dot(swap, jnp.concatenate(rows, axis=1), preferred_element_type=jnp.float32)
        lefts = jnp.dot(
            swap_quads, by_channel[:, bins, :].reshape(quads * GROUP, 4 * half), preferred_element_type=jnp.float32
        )
        results = []
        for at in range(0, GROUP, 2):
            two = []
            for one in range(at, at + 2):
                here = rights[one * GROUP : (one + 1) * GROUP]
                src = jnp.concatenate(
                    [here[:, i * 2 * count : (i + 1) * 2 * count] for i in range(windows // GROUP)], axis=0
                )
                two.append(jnp.concatenate([src * sign, pltpu.roll(src, count, axis=1)], axis=0).astype(jnp.bfloat16))
            right = jnp.concatenate(
                [jnp.concatenate([two[0], empty], axis=1), jnp.concatenate([empty, two[1]], axis=1)], axis=0
            )
            left = []
            for tile in range(0, 4 * half, 2 * half):
                one, other = (lefts[i * quads : (i + 1) * quads, tile : tile + 2 * half] for i in (at, at + 1))
                left.append(jnp.where(first, one, pltpu.roll(other, half, axis=1)))
                left.append(jnp.where(first, pltpu.roll(one, half, axis=1), other))
            left = jnp.concatenate(left, axis=0).astype(jnp.bfloat16)
            result = jnp.dot(left, right, preferred_element_type=jnp.float32).astype(jnp.bfloat16)
            results += [result[:, : 2 * count], result[:, 2 * count :]]
        halves = [
            jnp.concatenate([r[start : start + GROUP] for r in results], axis=0) for start in range(0, channels, GROUP)
        ]
        done = moved(swap, jnp.concatenate(halves, axis=1))
        for channel in range(channels):
            row, side = channel % GROUP, channel // GROUP
            sums[channel, bins, :] = done[
                row * GROUP : (row + 1) * GROUP, side * 2 * count : (side + 1) * 2 * count
            ]
        return carry

    lax.fori_loop(0, width // GROUP, one_group, 0, unroll=8)
    unit = eye(2 * count)
    part = 256 // LAG_ROWS
    swap = swapper(LAG_ROWS, part)
    for group in range(channels // LAG_ROWS):
        by_bin = []
        for channel in range(group * LAG_ROWS, (group + 1) * LAG_ROWS, 2):
            rows = jnp.concatenate([sums[channel], sums[channel + 1]], axis=0)
            both_turned = turned(unit, rows).astype(jnp.bfloat16)
            by_bin += [both_turned[:, :width], both_turned[:, width:]]
        for start in range(0, count, part):
            rows = jnp.concatenate(
                [
                    jnp.concatenate([b[start : start + part], b[count + start : count + start + part]], axis=1)
                    for b in by_bin
                ],
                axis=0,
            )
            rows = moved(swap, rows)
            at = slice(start * LAG_ROWS, (start + part) * LAG_ROWS)
            out[group, 0, at, :] = rows[:, :width]
            out[group, 1, at, :] = rows[:, width:]


def cross(here, near, far, by_channel, first_bin):
    each, count, both = here.shape
    quads, _, wide = by_channel.shape
    channels, windows, width = 4 * quads, wide // 8, both // 2
    return pl.pallas_call(
        cross_kernel,
        grid=(1,),
        in_specs=[pl.BlockSpec(a.shape, functools.partial(lambda n, i: (0,) * n, a.ndim)) for a in (here, near, far)]
        + [pl.BlockSpec((quads, width, wide), lambda i: (0, first_bin // width, 0))],
        out_specs=pl.BlockSpec((channels // LAG_ROWS, 2, count * LAG_ROWS, width), lambda i: (0, 0, 0, 0)),
        out_shape=jax.ShapeDtypeStruct((channels // LAG_ROWS, 2, count * LAG_ROWS, width), jnp.bfloat16),
        scratch_shapes=[
            pltpu.VMEM((windows, width, 2 * count), jnp.bfloat16),
            pltpu.VMEM((channels, width, 2 * count), jnp.bfloat16),
        ],
        compiler_params=pltpu.CompilerParams(vmem_limit_bytes=40 * MIB),
        cost_estimate=pl.CostEstimate(flops=2 * width * 36 * 65536, bytes_accessed=4 * MIB, transcendentals=0),
    )(here, near, far, by_channel)


def lag_kernel(scaling, *refs):
    *stacked, table, edge, out = refs
    count, channels, _ = out.shape
    real, imag = (jnp.concatenate([chunk[0, side] for chunk in stacked], axis=1) for side in range(2))
    size = count * channels
    lane = lax.broadcasted_iota(jnp.int32, (size, LAG_FINE), 1)
    mirror = (LAG_FINE - lane) % LAG_FINE

    def parts(start, width):
        even = jnp.dot(real, table[:F, start : start + width], preferred_element_type=jnp.float32)
        odd = jnp.dot(imag, table[F:, start : start + width], preferred_element_type=jnp.float32)
        return even, odd

    half = LAGS // 2
    products = real.astype(jnp.float32) * edge[:1] + imag.astype(jnp.float32) * edge[1:]
    above = jnp.sum(products, axis=1, keepdims=True) * scaling
    for start in range(half - 2 * LAG_FINE, -1, -2 * LAG_FINE):
        even, odd = parts(start, 2 * LAG_FINE)
        after_zero = (even - odd) * scaling
        before_zero = (even + odd) * scaling
        out[:, :, half + start : half + start + 2 * LAG_FINE] = after_zero.reshape(count, channels, 2 * LAG_FINE)
        for tile in (1, 0):
            turned_round = jnp.take_along_axis(
                before_zero[:, tile * LAG_FINE : (tile + 1) * LAG_FINE], mirror, axis=1, mode="promise_in_bounds"
            )
            at = half - start - (tile + 1) * LAG_FINE
            out[:, :, at : at + LAG_FINE] = jnp.where(lane == 0, above, turned_round).reshape(count, channels, LAG_FINE)
            above = turned_round


def lagged(stacked, table, scaling):
    groups, _, size, _ = stacked[0].shape
    edge = np.concatenate(unit_angles(np.array([LAGS // 2]), 0), axis=0).astype(jnp.bfloat16).astype(np.float32)
    count = size // LAG_ROWS
    return pl.pallas_call(
        functools.partial(lag_kernel, scaling),
        grid=(groups,),
        in_specs=[pl.BlockSpec((1, 2, size, s.shape[3]), lambda i: (i, 0, 0, 0)) for s in stacked]
        + [pl.BlockSpec(a.shape, lambda i: (0, 0)) for a in (table, edge)],
        out_specs=pl.BlockSpec((count, LAG_ROWS, LAGS), lambda i: (0, i, 0)),
        out_shape=jax.ShapeDtypeStruct((count, groups * LAG_ROWS, LAGS), jnp.float32),
        compiler_params=pltpu.CompilerParams(vmem_limit_bytes=48 * MIB),
        cost_estimate=pl.CostEstimate(
            flops=2 * groups * size * F * LAGS, bytes_accessed=groups * size * LAGS * 4, transcendentals=0
        ),
    )(*stacked, table, edge)


def table_kernel(angles, out):
    fine_cos, fine_sin = angles[:, :LAG_FINE], angles[:, LAG_FINE : 2 * LAG_FINE]
    tiles = out.shape[1] // LAG_FINE
    for tile in range(tiles):
        big_cos = angles[:, 2 * LAG_FINE + tile : 2 * LAG_FINE + tile + 1]
        big_sin = angles[:, 2 * LAG_FINE + tiles + tile : 2 * LAG_FINE + tiles + tile + 1]
        cols = slice(tile * LAG_FINE, (tile + 1) * LAG_FINE)
        out[:F, cols] = (big_cos * fine_cos - big_sin * fine_sin).astype(jnp.bfloat16)
        out[F:, cols] = (big_sin * fine_cos + big_cos * fine_sin).astype(jnp.bfloat16)


def lag_table():
    tiles = LAGS // 2 // LAG_FINE
    coarse = unit_angles(np.arange(tiles) * LAG_FINE, 1)
    angles = np.concatenate(unit_angles(np.arange(LAG_FINE), 1) + coarse, axis=1)
    return pl.pallas_call(
        table_kernel,
        out_shape=jax.ShapeDtypeStruct((2 * F, tiles * LAG_FINE), jnp.bfloat16),
        compiler_params=pltpu.CompilerParams(vmem_limit_bytes=40 * MIB),
        cost_estimate=pl.CostEstimate(flops=8 * F * tiles * LAG_FINE, bytes_accessed=4 * MIB, transcendentals=0),
    )(angles)


def make_band(filter_taps, channel_count):
    kernel = jnp.concatenate(
        [
            -filter_taps[:HALO].astype(jnp.float32),
            jnp.ones((1,), jnp.float32),
            -filter_taps[HALO:].astype(jnp.float32),
        ]
    )
    row_ids = jnp.arange(channel_count, dtype=jnp.int32)[:, None]
    columns = jnp.arange(channel_count + 2 * HALO, dtype=jnp.int32)[None, :]
    offset = columns - row_ids
    choose = offset[:, :, None] == jnp.arange(2 * HALO + 1, dtype=jnp.int32)[None, None, :]
    return jnp.sum(jnp.where(choose, kernel[None, None, :], 0.0), axis=2).astype(jnp.bfloat16)


def pick_kernel(held, across, selector, here, near, far):
    count = here.shape[1]
    for window in range(held.shape[1]):
        rows = [blocks[i, window] for blocks in (held, across) for i in range(blocks.shape[0])]
        picked = jnp.dot(selector[...], jnp.concatenate(rows, axis=0), preferred_element_type=jnp.float32)
        picked = picked.astype(jnp.bfloat16)
        here[window] = picked[:count]
        near[window] = picked[count : 2 * count]
        for at in range(far.shape[0]):
            far[at, window] = picked[(2 + at) * count : (3 + at) * count]


def pick(held, across, selector, groups):
    _, windows, _, both = held.shape
    count = selector.shape[0] // groups
    one = (windows, count, both)
    return pl.pallas_call(
        pick_kernel,
        out_shape=[jax.ShapeDtypeStruct(shape, jnp.bfloat16) for shape in (one, one, (groups - 2, *one))],
        compiler_params=pltpu.CompilerParams(vmem_limit_bytes=40 * MIB),
        cost_estimate=pl.CostEstimate(
            flops=2 * windows * selector.size * both, bytes_accessed=2 * windows * both * sum(selector.shape), transcendentals=0
        ),
    )(held, across, selector)


def swapped(value, axis, step):
    return lax.ppermute(value, axis, [(i, i ^ step) for i in range(lax.axis_size(axis))])


def after(value, earlier):
    return lax.optimization_barrier((value, earlier))[0]


def per_device(traces, filter_taps, good_channels, source_index):
    window_count, channel_count, _ = traces.shape
    good = good_channels[None, :]
    blocks = lax.axis_size("chan")
    groups = lax.axis_size("win")
    halves = []
    for start in range(0, F, F // 2):
        spec, head, tail = transform(traces, good, start, F // 2)
        left = lax.ppermute(tail, "chan", [(i, i + 1) for i in range(blocks - 1)])
        right = lax.ppermute(head, "chan", [(i + 1, i) for i in range(blocks - 1)])
        halves.append((spec, left, right))
    table = lag_table()
    halves[-1] = (halves[-1][0], after(left, table), right)
    full, *parts = whiten(halves, make_band(filter_taps, channel_count), good)

    order = [0]
    step = blocks // 2
    while step:
        order += [place ^ step for place in order]
        step //= 2
    order = jnp.asarray(order, jnp.int32) ^ lax.axis_index("chan")
    own_ids = jnp.arange(channel_count, dtype=jnp.int32)
    channel_ids = (order[:, None] * channel_count + own_ids[None, :]).reshape(-1)
    by_group = source_index.reshape(groups, -1)
    here = lax.axis_index("win")
    wanted = jnp.concatenate([lax.dynamic_slice_in_dim(by_group, here ^ step, 1) for step in range(groups)], axis=0)
    selector = (wanted.reshape(-1)[:, None] == channel_ids[None, :]).astype(jnp.bfloat16)

    own_far = swapped(full, "win", 2)
    own_near = swapped(jnp.stack([full, own_far]), "win", 1)
    by_channel = turn_own(full, own_near, own_far)
    gathered, picked, stacked = [], [], []
    chunks = len(CHUNKS)

    def gather(part):
        held, step = part, blocks // 2
        while step > 1:
            received = swapped(held, "chan", step)
            if step > 2:
                held = jnp.concatenate([held, received], axis=1)
                if step == blocks // 2:
                    first_held.append(held)
                    if len(gathered) > 1:
                        held = after(held, picked[0][0])
            step //= 2
        gathered.extend(jnp.concatenate([held[i], received[i]], axis=0) for i in range(part.shape[0]))

    def exchange(at):
        held = after(gathered[at], picked[-1][0]) if at else gathered[at]
        across = swapped(held, "chan", 1)
        if at > 1:
            finish(at - 2)
        across = after(across, (stacked[-1] if stacked else by_channel) if at else gathered[1])
        here, near, far = pick(held, across, selector, groups)
        picked.append((here, near, swapped(far, "win", 2)))

    def finish(at):
        here, near, far = picked[at]
        if stacked:
            far = after(far, stacked[-1])
        near = swapped(jnp.stack([near, far[1]]), "win", 1)
        stacked.append(cross(here, near, far, by_channel, CHUNKS[at][0]))

    first_held = []
    for part in parts:
        gather(after(part, [first_held[-1]] + [own_far] * (len(first_held) > 1)) if first_held else part)
        if len(gathered) == 2:
            exchange(0)
    for at in range(1, chunks):
        exchange(at)
    for at in range(len(stacked), chunks):
        finish(at)
    return lagged(stacked, table, 1.0 / math.sqrt(F * window_count * groups))


def solution(mesh):
    placed = (P("win", "chan", None), P(), P("chan"), P())
    return jax.shard_map(
        per_device, mesh=mesh, in_specs=placed, out_specs=P("win", "chan", None), check_vma=False
    )
```

```python
import functools
import math

import jax
import jax.numpy as jnp
import numpy as np
from jax import lax
from jax.experimental import pallas as pl
from jax.experimental.pallas import tpu as pltpu
from jax.sharding import PartitionSpec as P

L = 7680
F = 512
LAGS = 2048
HALO = 16
SMOOTH = 64
K0 = 31
QUARTER = L // 4
STEP = 640
FINE = 32
CHUNKS = tuple((start, 128) for start in range(0, F, 128))
Z_GROUPS = ((0, 1), (1, 2), (2, 4))
GROUP = 16
LAG_FINE = 128
LAG_ROWS = 8
NT = (((1,), (1,)), ((), ()))
MIB = 1024 * 1024


def unit_angles(positions, axis):
    bins = K0 + np.arange(F, dtype=np.int64)
    phase = np.mod(np.expand_dims(positions, 1 - axis) * np.expand_dims(bins, axis), L)
    angles = phase * (2.0 * math.pi / L)
    return np.cos(angles).astype(np.float32), np.sin(angles).astype(np.float32)


def keep_column(good):
    count = good.shape[1]
    rows = lax.broadcasted_iota(jnp.int32, (count, count), 0)
    cols = lax.broadcasted_iota(jnp.int32, (count, count), 1)
    return jnp.sum(jnp.where(rows == cols, good[...].astype(jnp.float32), 0.0), axis=1, keepdims=True)


def transform_kernel(x0, x1, x2, x3, angles, good, spec, head, tail, table, total):
    step = pl.program_id(0)
    rows = x0.shape[0]
    coarse = QUARTER // FINE

    def fill(of_step):
        fine_cos = angles[2 * coarse : 2 * coarse + FINE, :]
        fine_sin = angles[2 * coarse + FINE :, :]
        for part in range(STEP // FINE):
            big_cos = angles[pl.ds(of_step * (STEP // FINE) + part, 1), :]
            big_sin = angles[pl.ds(coarse + of_step * (STEP // FINE) + part, 1), :]
            at = pl.ds(part * FINE, FINE)
            table[of_step % 2, at, :F] = (big_cos * fine_cos - big_sin * fine_sin).astype(jnp.bfloat16)
            table[of_step % 2, at, F:] = (-(big_sin * fine_cos + big_cos * fine_sin)).astype(jnp.bfloat16)

    @pl.when(step == 0)
    def _():
        total[...] = jnp.zeros_like(total)
        fill(step)

    for quarter, x in enumerate((x0, x1, x2, x3)):
        at = pl.ds(quarter * rows, rows)
        total[at, :] += jnp.dot(x[...], table[step % 2], preferred_element_type=jnp.float32)
    fill(jnp.minimum(step + 1, pl.num_programs(0) - 1))

    @pl.when(step == pl.num_programs(0) - 1)
    def _():
        turn = (K0 + lax.broadcasted_iota(jnp.int32, (1, F), 1)) % 4
        even = turn % 2 == 0
        sign = jnp.where(turn < 2, 1.0, -1.0)
        channels = good.shape[1]
        keep = keep_column(good)
        for window in range(rows // channels):
            re = [total[pl.ds(q * rows + window * channels, channels), :F] for q in range(4)]
            im = [total[pl.ds(q * rows + window * channels, channels), F:] for q in range(4)]
            real = jnp.where(even, re[0] + re[2] + sign * (re[1] + re[3]), re[0] - re[2] + sign * (im[1] - im[3])) * keep
            imag = jnp.where(even, im[0] + im[2] + sign * (im[1] + im[3]), im[0] - im[2] - sign * (re[1] - re[3])) * keep
            spec[window, :, :F] = real
            spec[window, :, F:] = imag
            head[window, :, :F] = real[:HALO].astype(jnp.bfloat16)
            head[window, :, F:] = imag[:HALO].astype(jnp.bfloat16)
            tail[window, :, :F] = real[channels - HALO :].astype(jnp.bfloat16)
            tail[window, :, F:] = imag[channels - HALO :].astype(jnp.bfloat16)


def transform(traces, good):
    windows, channels, length = traces.shape
    rows = windows * channels
    steps = QUARTER // STEP
    flat = traces.reshape(rows, length)
    coarse = unit_angles(np.arange(QUARTER // FINE) * FINE, 0)
    angles = np.concatenate(coarse + unit_angles(np.arange(FINE), 0), axis=0)
    whole = lambda *shape: pl.BlockSpec(shape, lambda k: (0,) * len(shape))
    return pl.pallas_call(
        transform_kernel,
        grid=(steps,),
        in_specs=[pl.BlockSpec((rows, STEP), functools.partial(lambda q, k: (0, q * steps + k), q)) for q in range(4)]
        + [whole(*angles.shape), whole(1, channels)],
        out_specs=[whole(windows, channels, 2 * F), whole(windows, HALO, 2 * F), whole(windows, HALO, 2 * F)],
        out_shape=[
            jax.ShapeDtypeStruct((windows, channels, 2 * F), jnp.float32),
            jax.ShapeDtypeStruct((windows, HALO, 2 * F), jnp.bfloat16),
            jax.ShapeDtypeStruct((windows, HALO, 2 * F), jnp.bfloat16),
        ],
        scratch_shapes=[pltpu.VMEM((2, STEP, 2 * F), jnp.bfloat16), pltpu.VMEM((4 * rows, 2 * F), jnp.float32)],
        compiler_params=pltpu.CompilerParams(vmem_limit_bytes=60 * MIB),
        cost_estimate=pl.CostEstimate(flops=2 * rows * length * 2 * F, bytes_accessed=rows * length * 2, transcendentals=0),
    )(flat, flat, flat, flat, angles, good)


def pieces(value):
    high = value.astype(jnp.bfloat16)
    rest = value - high.astype(jnp.float32)
    middle = rest.astype(jnp.bfloat16)
    return high, middle, (rest - middle.astype(jnp.float32)).astype(jnp.bfloat16)


def whiten_kernel(spec, left, right, band, good, *outs):
    windows, channels = spec.shape[:2]
    filtered = []
    keep = keep_column(good)
    for window in range(windows):
        stack = jnp.concatenate([left[window], *pieces(spec[window]), right[window]], axis=0)
        own = band[:, HALO : HALO + channels]
        taps = jnp.concatenate([band[:, :HALO], own, own, own, band[:, HALO + channels :]], axis=1)
        filtered.append(jnp.dot(taps, stack, preferred_element_type=jnp.float32) * keep)
    spectrum = jnp.concatenate(filtered, axis=0)
    real, imag = spectrum[:, :F], spectrum[:, F:]
    magnitude = jnp.sqrt(real * real + imag * imag)
    bins = lax.broadcasted_iota(jnp.int32, (F, F), 0)
    others = lax.broadcasted_iota(jnp.int32, (F, F), 1)
    near = jnp.where(jnp.abs(bins - others) <= SMOOTH, 1.0, 0.0).astype(jnp.bfloat16)
    amplitude = sum(jnp.dot(piece, near, preferred_element_type=jnp.float32) for piece in pieces(magnitude))
    bin_row = lax.broadcasted_iota(jnp.int32, (1, F), 1)
    count = jnp.minimum(bin_row + SMOOTH, F - 1) - jnp.maximum(bin_row - SMOOTH, 0) + 1
    amplitude = amplitude * (1.0 / count.astype(jnp.float32))
    inverse = 1.0 / (amplitude + 1e-06)
    real = (real * inverse).astype(jnp.bfloat16)
    imag = (imag * inverse).astype(jnp.bfloat16)
    full, *parts = outs
    for window in range(windows):
        rows = slice(window * channels, (window + 1) * channels)
        full[window, :, :F] = real[rows]
        full[window, :, F:] = imag[rows]
        for part, (begin, end) in zip(parts, Z_GROUPS):
            for at, (start, width) in enumerate(CHUNKS[begin:end]):
                part[at, 0, window, :, :width] = real[rows, start : start + width]
                part[at, 0, window, :, width:] = imag[rows, start : start + width]


def whiten(spec, left, right, band, good):
    windows, channels, _ = spec.shape
    return pl.pallas_call(
        whiten_kernel,
        out_shape=[
            jax.ShapeDtypeStruct(shape, jnp.bfloat16)
            for shape in [(windows, channels, 2 * F)]
            + [(end - begin, 1, windows, channels, 2 * CHUNKS[0][1]) for begin, end in Z_GROUPS]
        ],
        compiler_params=pltpu.CompilerParams(vmem_limit_bytes=40 * MIB),
        cost_estimate=pl.CostEstimate(flops=2 * windows * channels * F * F * 3, bytes_accessed=5 * MIB // 2, transcendentals=windows * channels * F),
    )(spec, left, right, band, good)


def eye(size):
    rows = lax.broadcasted_iota(jnp.int32, (size, size), 0)
    cols = lax.broadcasted_iota(jnp.int32, (size, size), 1)
    return jnp.where(rows == cols, 1.0, 0.0).astype(jnp.bfloat16)


def turned(left_unit, rows):
    return lax.dot_general(left_unit, rows, NT, preferred_element_type=jnp.float32)


def swapper(outer, inner):
    size = outer * inner
    rows = lax.broadcasted_iota(jnp.int32, (size, size), 0)
    cols = lax.broadcasted_iota(jnp.int32, (size, size), 1)
    return jnp.where(cols == rows % outer * inner + rows // outer, 1.0, 0.0).astype(jnp.bfloat16)


def moved(swap, rows):
    return jnp.dot(swap, rows, preferred_element_type=jnp.float32).astype(jnp.bfloat16)


def own_kernel(here, near, far, out, by_window):
    own = [here, near.at[0], far, near.at[1]]
    each, channels, _ = here.shape
    windows, quads = each * len(own), channels // 4
    joined = GROUP // each
    swap = swapper(GROUP, GROUP)
    for start in range(0, windows, GROUP):
        for channel in range(0, channels, GROUP):
            block = [o[:, channel : channel + GROUP, :] for o in own[start // each : start // each + joined]]
            rows = moved(swap, jnp.concatenate(block, axis=0).reshape(GROUP * GROUP, 2 * F))
            by_window[channel : channel + GROUP, start : start + GROUP, :] = rows.reshape(GROUP, GROUP, 2 * F)
    unit = eye(F // 2)
    for quad in range(quads):
        for start in range(0, F, F // 2):
            rows = []
            for channel in range(quad, channels, quads):
                rows += [by_window[channel, :, side + start : side + start + F // 2] for side in (0, F)]
            out[quad, start : start + F // 2, :] = turned(unit, jnp.concatenate(rows, axis=0)).astype(jnp.bfloat16)


def turn_own(here, near, far):
    each, channels, _ = here.shape
    windows = each * 4
    return pl.pallas_call(
        own_kernel,
        out_shape=jax.ShapeDtypeStruct((channels // 4, F, 8 * windows), jnp.bfloat16),
        scratch_shapes=[pltpu.VMEM((channels, windows, 2 * F), jnp.bfloat16)],
        compiler_params=pltpu.CompilerParams(vmem_limit_bytes=24 * MIB),
        cost_estimate=pl.CostEstimate(flops=2 * 8192 * 65536, bytes_accessed=4 * MIB, transcendentals=0),
    )(here, near, far)


def cross_kernel(here, near, far, by_channel, out, by_window, sums):
    sources = [here, near.at[0], far.at[0], near.at[1]]
    each, count, both = here.shape
    quads, _, wide = by_channel.shape
    channels, half = 4 * quads, wide // 4
    windows, width = half // 2, both // 2
    unit = eye(width)
    swap = swapper(GROUP, GROUP)
    swap_quads = swapper(quads, GROUP)
    for window in range(0, windows, 2):
        rows = []
        for one in range(window, window + 2):
            source = sources[one // each]
            rows += [source[one % each, :, :width], source[one % each, :, width:]]
        both_turned = turned(unit, jnp.concatenate(rows, axis=0)).astype(jnp.bfloat16)
        by_window[window] = both_turned[:, : 2 * count]
        by_window[window + 1] = both_turned[:, 2 * count :]
    first = lax.broadcasted_iota(jnp.int32, (1, 2 * half), 1) < half
    sign = jnp.where(lax.broadcasted_iota(jnp.int32, (1, 2 * count), 1) < count, 1.0, -1.0)
    empty = jnp.zeros((2 * windows, 2 * count), jnp.bfloat16)

    def one_group(group, carry):
        bins = pl.ds(pl.multiple_of(group * GROUP, GROUP), GROUP)
        rows = [
            by_window[start : start + GROUP, bins, :].reshape(GROUP * GROUP, 2 * count)
            for start in range(0, windows, GROUP)
        ]
        rights = jnp.dot(swap, jnp.concatenate(rows, axis=1), preferred_element_type=jnp.float32)
        lefts = jnp.dot(
            swap_quads, by_channel[:, bins, :].reshape(quads * GROUP, 4 * half), preferred_element_type=jnp.float32
        )
        results = []
        for at in range(0, GROUP, 2):
            two = []
            for one in range(at, at + 2):
                here = rights[one * GROUP : (one + 1) * GROUP]
                src = jnp.concatenate(
                    [here[:, i * 2 * count : (i + 1) * 2 * count] for i in range(windows // GROUP)], axis=0
                )
                two.append(jnp.concatenate([src * sign, pltpu.roll(src, count, axis=1)], axis=0).astype(jnp.bfloat16))
            right = jnp.concatenate(
                [jnp.concatenate([two[0], empty], axis=1), jnp.concatenate([empty, two[1]], axis=1)], axis=0
            )
            left = []
            for tile in range(0, 4 * half, 2 * half):
                one, other = (lefts[i * quads : (i + 1) * quads, tile : tile + 2 * half] for i in (at, at + 1))
                left.append(jnp.where(first, one, pltpu.roll(other, half, axis=1)))
                left.append(jnp.where(first, pltpu.roll(one, half, axis=1), other))
            left = jnp.concatenate(left, axis=0).astype(jnp.bfloat16)
            result = jnp.dot(left, right, preferred_element_type=jnp.float32).astype(jnp.bfloat16)
            results += [result[:, : 2 * count], result[:, 2 * count :]]
        halves = [
            jnp.concatenate([r[start : start + GROUP] for r in results], axis=0) for start in range(0, channels, GROUP)
        ]
        done = moved(swap, jnp.concatenate(halves, axis=1))
        for channel in range(channels):
            row, side = channel % GROUP, channel // GROUP
            sums[channel, bins, :] = done[
                row * GROUP : (row + 1) * GROUP, side * 2 * count : (side + 1) * 2 * count
            ]
        return carry

    lax.fori_loop(0, width // GROUP, one_group, 0, unroll=8)
    unit = eye(2 * count)
    part = 256 // LAG_ROWS
    swap = swapper(LAG_ROWS, part)
    for group in range(channels // LAG_ROWS):
        by_bin = []
        for channel in range(group * LAG_ROWS, (group + 1) * LAG_ROWS, 2):
            rows = jnp.concatenate([sums[channel], sums[channel + 1]], axis=0)
            both_turned = turned(unit, rows).astype(jnp.bfloat16)
            by_bin += [both_turned[:, :width], both_turned[:, width:]]
        for start in range(0, count, part):
            rows = jnp.concatenate(
                [
                    jnp.concatenate([b[start : start + part], b[count + start : count + start + part]], axis=1)
                    for b in by_bin
                ],
                axis=0,
            )
            rows = moved(swap, rows)
            at = slice(start * LAG_ROWS, (start + part) * LAG_ROWS)
            out[group, 0, at, :] = rows[:, :width]
            out[group, 1, at, :] = rows[:, width:]


def cross(here, near, far, by_channel, first_bin):
    each, count, both = here.shape
    quads, _, wide = by_channel.shape
    channels, windows, width = 4 * quads, wide // 8, both // 2
    return pl.pallas_call(
        cross_kernel,
        grid=(1,),
        in_specs=[pl.BlockSpec(a.shape, functools.partial(lambda n, i: (0,) * n, a.ndim)) for a in (here, near, far)]
        + [pl.BlockSpec((quads, width, wide), lambda i: (0, first_bin // width, 0))],
        out_specs=pl.BlockSpec((channels // LAG_ROWS, 2, count * LAG_ROWS, width), lambda i: (0, 0, 0, 0)),
        out_shape=jax.ShapeDtypeStruct((channels // LAG_ROWS, 2, count * LAG_ROWS, width), jnp.bfloat16),
        scratch_shapes=[
            pltpu.VMEM((windows, width, 2 * count), jnp.bfloat16),
            pltpu.VMEM((channels, width, 2 * count), jnp.bfloat16),
        ],
        compiler_params=pltpu.CompilerParams(vmem_limit_bytes=24 * MIB),
        cost_estimate=pl.CostEstimate(flops=2 * width * 36 * 65536, bytes_accessed=4 * MIB, transcendentals=0),
    )(here, near, far, by_channel)


def part_rows(table, side, chunk):
    first_bin, width = chunk
    return table[side * F + first_bin : side * F + first_bin + width]


def early_kernel(*refs):
    *stacked, table, even, odd = refs
    size, half = even.shape
    for side, out in enumerate((even, odd)):
        rows = jnp.concatenate([chunk[0, side] for chunk in stacked], axis=1)
        bins = rows.shape[1]
        for start in range(0, half, 2 * LAG_FINE):
            cols = slice(start, start + 2 * LAG_FINE)
            out[:, cols] = jnp.dot(rows, table[side * F : side * F + bins, cols], preferred_element_type=jnp.float32)


def lag_early(stacked, table):
    groups, _, size, _ = stacked[0].shape
    half = LAGS // 2
    return pl.pallas_call(
        early_kernel,
        grid=(groups,),
        in_specs=[pl.BlockSpec((1, 2, size, s.shape[3]), lambda i: (i, 0, 0, 0)) for s in stacked]
        + [pl.BlockSpec(table.shape, lambda i: (0, 0))],
        out_specs=[pl.BlockSpec((size, half), lambda i: (i, 0))] * 2,
        out_shape=[jax.ShapeDtypeStruct((groups * size, half), jnp.float32)] * 2,
        compiler_params=pltpu.CompilerParams(vmem_limit_bytes=28 * MIB),
        cost_estimate=pl.CostEstimate(
            flops=2 * groups * size * F * LAGS, bytes_accessed=groups * size * LAGS * 4, transcendentals=0
        ),
    )(*stacked, table)


def lag_kernel(scaling, *refs):
    *stacked, early_even, early_odd, table, edge, out = refs
    count, channels, _ = out.shape
    real, imag = (jnp.concatenate([chunk[0, side] for chunk in stacked], axis=1) for side in range(2))
    size = count * channels
    lane = lax.broadcasted_iota(jnp.int32, (size, LAG_FINE), 1)
    mirror = (LAG_FINE - lane) % LAG_FINE
    last = stacked[-1]

    def parts(cols):
        even = jnp.dot(last[0, 0], part_rows(table, 0, CHUNKS[-1])[:, cols], preferred_element_type=jnp.float32)
        odd = jnp.dot(last[0, 1], part_rows(table, 1, CHUNKS[-1])[:, cols], preferred_element_type=jnp.float32)
        return even + early_even[:, cols], odd + early_odd[:, cols]

    half = LAGS // 2
    products = real.astype(jnp.float32) * edge[:1] + imag.astype(jnp.float32) * edge[1:]
    above = jnp.sum(products, axis=1, keepdims=True) * scaling
    for start in range(half - 2 * LAG_FINE, -1, -2 * LAG_FINE):
        even, odd = parts(slice(start, start + 2 * LAG_FINE))
        after_zero = (even - odd) * scaling
        before_zero = (even + odd) * scaling
        out[:, :, half + start : half + start + 2 * LAG_FINE] = after_zero.reshape(count, channels, 2 * LAG_FINE)
        for tile in (1, 0):
            turned_round = jnp.take_along_axis(
                before_zero[:, tile * LAG_FINE : (tile + 1) * LAG_FINE], mirror, axis=1, mode="promise_in_bounds"
            )
            at = half - start - (tile + 1) * LAG_FINE
            out[:, :, at : at + LAG_FINE] = jnp.where(lane == 0, above, turned_round).reshape(count, channels, LAG_FINE)
            above = turned_round


def lagged(stacked, early, table, scaling):
    groups, _, size, _ = stacked[0].shape
    edge = np.concatenate(unit_angles(np.array([LAGS // 2]), 0), axis=0).astype(jnp.bfloat16).astype(np.float32)
    count = size // LAG_ROWS
    return pl.pallas_call(
        functools.partial(lag_kernel, scaling),
        grid=(groups,),
        in_specs=[pl.BlockSpec((1, 2, size, s.shape[3]), lambda i: (i, 0, 0, 0)) for s in stacked]
        + [pl.BlockSpec((size, LAGS // 2), lambda i: (i, 0))] * 2
        + [pl.BlockSpec(a.shape, lambda i: (0, 0)) for a in (table, edge)],
        out_specs=pl.BlockSpec((count, LAG_ROWS, LAGS), lambda i: (0, i, 0)),
        out_shape=jax.ShapeDtypeStruct((count, groups * LAG_ROWS, LAGS), jnp.float32),
        compiler_params=pltpu.CompilerParams(vmem_limit_bytes=32 * MIB),
        cost_estimate=pl.CostEstimate(
            flops=2 * groups * size * F * LAGS // 4, bytes_accessed=groups * size * LAGS * 4, transcendentals=0
        ),
    )(*stacked, *early, table, edge)


def table_kernel(angles, out):
    fine_cos, fine_sin = angles[:, :LAG_FINE], angles[:, LAG_FINE : 2 * LAG_FINE]
    tiles = out.shape[1] // LAG_FINE
    for tile in range(tiles):
        big_cos = angles[:, 2 * LAG_FINE + tile : 2 * LAG_FINE + tile + 1]
        big_sin = angles[:, 2 * LAG_FINE + tiles + tile : 2 * LAG_FINE + tiles + tile + 1]
        cols = slice(tile * LAG_FINE, (tile + 1) * LAG_FINE)
        out[:F, cols] = (big_cos * fine_cos - big_sin * fine_sin).astype(jnp.bfloat16)
        out[F:, cols] = (big_sin * fine_cos + big_cos * fine_sin).astype(jnp.bfloat16)


def lag_table():
    tiles = LAGS // 2 // LAG_FINE
    coarse = unit_angles(np.arange(tiles) * LAG_FINE, 1)
    angles = np.concatenate(unit_angles(np.arange(LAG_FINE), 1) + coarse, axis=1)
    return pl.pallas_call(
        table_kernel,
        out_shape=jax.ShapeDtypeStruct((2 * F, tiles * LAG_FINE), jnp.bfloat16),
        compiler_params=pltpu.CompilerParams(vmem_limit_bytes=40 * MIB),
        cost_estimate=pl.CostEstimate(flops=8 * F * tiles * LAG_FINE, bytes_accessed=4 * MIB, transcendentals=0),
    )(angles)


def make_band(filter_taps, channel_count):
    kernel = jnp.concatenate(
        [
            -filter_taps[:HALO].astype(jnp.float32),
            jnp.ones((1,), jnp.float32),
            -filter_taps[HALO:].astype(jnp.float32),
        ]
    )
    row_ids = jnp.arange(channel_count, dtype=jnp.int32)[:, None]
    columns = jnp.arange(channel_count + 2 * HALO, dtype=jnp.int32)[None, :]
    offset = columns - row_ids
    choose = offset[:, :, None] == jnp.arange(2 * HALO + 1, dtype=jnp.int32)[None, None, :]
    return jnp.sum(jnp.where(choose, kernel[None, None, :], 0.0), axis=2).astype(jnp.bfloat16)


def pick_kernel(held, across, selector, here, near, far):
    count = here.shape[1]
    for window in range(held.shape[1]):
        rows = [blocks[i, window] for blocks in (held, across) for i in range(blocks.shape[0])]
        picked = jnp.dot(selector[...], jnp.concatenate(rows, axis=0), preferred_element_type=jnp.float32)
        picked = picked.astype(jnp.bfloat16)
        here[window] = picked[:count]
        near[window] = picked[count : 2 * count]
        for at in range(far.shape[0]):
            far[at, window] = picked[(2 + at) * count : (3 + at) * count]


def pick(held, across, selector, groups):
    _, windows, _, both = held.shape
    count = selector.shape[0] // groups
    one = (windows, count, both)
    return pl.pallas_call(
        pick_kernel,
        out_shape=[jax.ShapeDtypeStruct(shape, jnp.bfloat16) for shape in (one, one, (groups - 2, *one))],
        compiler_params=pltpu.CompilerParams(vmem_limit_bytes=24 * MIB),
        cost_estimate=pl.CostEstimate(
            flops=2 * windows * selector.size * both, bytes_accessed=2 * windows * both * sum(selector.shape), transcendentals=0
        ),
    )(held, across, selector)


def swapped(value, axis, step):
    return lax.ppermute(value, axis, [(i, i ^ step) for i in range(lax.axis_size(axis))])


def after(value, earlier):
    return lax.optimization_barrier((value, earlier))[0]


def per_device(traces, filter_taps, good_channels, source_index):
    window_count, channel_count, _ = traces.shape
    good = good_channels[None, :]
    spec, head, tail = transform(traces, good)
    blocks = lax.axis_size("chan")
    groups = lax.axis_size("win")
    left = lax.ppermute(tail, "chan", [(i, i + 1) for i in range(blocks - 1)])
    right = lax.ppermute(head, "chan", [(i + 1, i) for i in range(blocks - 1)])
    table = lag_table()
    left = after(left, table)
    full, *parts = whiten(spec, left, right, make_band(filter_taps, channel_count), good)

    order = [0]
    step = blocks // 2
    while step:
        order += [place ^ step for place in order]
        step //= 2
    order = jnp.asarray(order, jnp.int32) ^ lax.axis_index("chan")
    own_ids = jnp.arange(channel_count, dtype=jnp.int32)
    channel_ids = (order[:, None] * channel_count + own_ids[None, :]).reshape(-1)
    by_group = source_index.reshape(groups, -1)
    here = lax.axis_index("win")
    wanted = jnp.concatenate([lax.dynamic_slice_in_dim(by_group, here ^ step, 1) for step in range(groups)], axis=0)
    selector = (wanted.reshape(-1)[:, None] == channel_ids[None, :]).astype(jnp.bfloat16)

    own_far = swapped(full, "win", 2)
    own_near = swapped(jnp.stack([full, own_far]), "win", 1)
    by_channel = turn_own(full, own_near, own_far)
    gathered, picked, stacked, early = [], [], [], []
    chunks = len(CHUNKS)

    def gather(part):
        held, step = part, blocks // 2
        while step > 1:
            received = swapped(held, "chan", step)
            if step > 2:
                held = jnp.concatenate([held, received], axis=1)
                if step == blocks // 2:
                    first_held.append(held)
                    if len(gathered) > 1:
                        held = after(held, picked[0][0])
            step //= 2
        gathered.extend(jnp.concatenate([held[i], received[i]], axis=0) for i in range(part.shape[0]))

    def exchange(at):
        held = after(gathered[at], picked[-1][0]) if at else gathered[at]
        across = swapped(held, "chan", 1)
        if at > 1:
            finish(at - 2)
        across = after(across, (stacked[-1] if stacked else by_channel) if at else gathered[1])
        here, near, far = pick(held, across, selector, groups)
        picked.append((here, near, swapped(far, "win", 2)))

    def finish(at):
        here, near, far = picked[at]
        if at == chunks - 1:
            early.extend(lag_early(stacked, table))
            far = after(far, early)
        elif stacked:
            far = after(far, stacked[-1])
        near = swapped(jnp.stack([near, far[1]]), "win", 1)
        stacked.append(cross(here, near, far, by_channel, CHUNKS[at][0]))

    first_held = []
    for part in parts:
        gather(after(part, [first_held[-1]] + [own_far] * (len(first_held) > 1)) if first_held else part)
        if len(gathered) == 2:
            exchange(0)
    for at in range(1, chunks):
        exchange(at)
    for at in range(len(stacked), chunks):
        finish(at)
    return lagged(stacked, early, table, 1.0 / math.sqrt(F * window_count * groups))


def solution(mesh):
    placed = (P("win", "chan", None), P(), P("chan"), P())
    return jax.shard_map(
        per_device, mesh=mesh, in_specs=placed, out_specs=P("win", "chan", None), check_vma=False
    )
```

```python
import functools
import math

import jax
import jax.numpy as jnp
import numpy as np
from jax import lax
from jax.experimental import pallas as pl
from jax.experimental.pallas import tpu as pltpu
from jax.sharding import PartitionSpec as P

L = 7680
F = 512
LAGS = 2048
HALO = 16
SMOOTH = 64
K0 = 31
QUARTER = L // 4
STEP = 640
FINE = 32
CHUNKS = tuple((start, 128) for start in range(0, F, 128))
Z_GROUPS = ((0, 1), (1, 2), (2, 4))
GROUP = 16
LAG_FINE = 128
LAG_ROWS = 8
NT = (((1,), (1,)), ((), ()))
MIB = 1024 * 1024


def unit_angles(positions, axis):
    bins = K0 + np.arange(F, dtype=np.int64)
    phase = np.mod(np.expand_dims(positions, 1 - axis) * np.expand_dims(bins, axis), L)
    angles = phase * (2.0 * math.pi / L)
    return np.cos(angles).astype(np.float32), np.sin(angles).astype(np.float32)


def keep_column(good):
    count = good.shape[1]
    rows = lax.broadcasted_iota(jnp.int32, (count, count), 0)
    cols = lax.broadcasted_iota(jnp.int32, (count, count), 1)
    return jnp.sum(jnp.where(rows == cols, good[...].astype(jnp.float32), 0.0), axis=1, keepdims=True)


def transform_kernel(x0, x1, x2, x3, angles, good, spec, head, tail, table, total):
    step = pl.program_id(0)
    rows = x0.shape[0]
    coarse = QUARTER // FINE

    def fill(of_step):
        fine_cos = angles[2 * coarse : 2 * coarse + FINE, :]
        fine_sin = angles[2 * coarse + FINE :, :]
        for part in range(STEP // FINE):
            big_cos = angles[pl.ds(of_step * (STEP // FINE) + part, 1), :]
            big_sin = angles[pl.ds(coarse + of_step * (STEP // FINE) + part, 1), :]
            at = pl.ds(part * FINE, FINE)
            table[of_step % 2, at, :F] = (big_cos * fine_cos - big_sin * fine_sin).astype(jnp.bfloat16)
            table[of_step % 2, at, F:] = (-(big_sin * fine_cos + big_cos * fine_sin)).astype(jnp.bfloat16)

    @pl.when(step == 0)
    def _():
        total[...] = jnp.zeros_like(total)
        fill(step)

    for quarter, x in enumerate((x0, x1, x2, x3)):
        at = pl.ds(quarter * rows, rows)
        total[at, :] += jnp.dot(x[...], table[step % 2], preferred_element_type=jnp.float32)
    fill(jnp.minimum(step + 1, pl.num_programs(0) - 1))

    @pl.when(step == pl.num_programs(0) - 1)
    def _():
        turn = (K0 + lax.broadcasted_iota(jnp.int32, (1, F), 1)) % 4
        even = turn % 2 == 0
        sign = jnp.where(turn < 2, 1.0, -1.0)
        channels = good.shape[1]
        keep = keep_column(good)
        for window in range(rows // channels):
            re = [total[pl.ds(q * rows + window * channels, channels), :F] for q in range(4)]
            im = [total[pl.ds(q * rows + window * channels, channels), F:] for q in range(4)]
            real = jnp.where(even, re[0] + re[2] + sign * (re[1] + re[3]), re[0] - re[2] + sign * (im[1] - im[3])) * keep
            imag = jnp.where(even, im[0] + im[2] + sign * (im[1] + im[3]), im[0] - im[2] - sign * (re[1] - re[3])) * keep
            spec[window, :, :F] = real
            spec[window, :, F:] = imag
            head[window, :, :F] = real[:HALO].astype(jnp.bfloat16)
            head[window, :, F:] = imag[:HALO].astype(jnp.bfloat16)
            tail[window, :, :F] = real[channels - HALO :].astype(jnp.bfloat16)
            tail[window, :, F:] = imag[channels - HALO :].astype(jnp.bfloat16)


def transform(traces, good):
    windows, channels, length = traces.shape
    rows = windows * channels
    steps = QUARTER // STEP
    flat = traces.reshape(rows, length)
    coarse = unit_angles(np.arange(QUARTER // FINE) * FINE, 0)
    angles = np.concatenate(coarse + unit_angles(np.arange(FINE), 0), axis=0)
    whole = lambda *shape: pl.BlockSpec(shape, lambda k: (0,) * len(shape))
    return pl.pallas_call(
        transform_kernel,
        grid=(steps,),
        in_specs=[pl.BlockSpec((rows, STEP), functools.partial(lambda q, k: (0, q * steps + k), q)) for q in range(4)]
        + [whole(*angles.shape), whole(1, channels)],
        out_specs=[whole(windows, channels, 2 * F), whole(windows, HALO, 2 * F), whole(windows, HALO, 2 * F)],
        out_shape=[
            jax.ShapeDtypeStruct((windows, channels, 2 * F), jnp.float32),
            jax.ShapeDtypeStruct((windows, HALO, 2 * F), jnp.bfloat16),
            jax.ShapeDtypeStruct((windows, HALO, 2 * F), jnp.bfloat16),
        ],
        scratch_shapes=[pltpu.VMEM((2, STEP, 2 * F), jnp.bfloat16), pltpu.VMEM((4 * rows, 2 * F), jnp.float32)],
        compiler_params=pltpu.CompilerParams(vmem_limit_bytes=60 * MIB),
        cost_estimate=pl.CostEstimate(flops=2 * rows * length * 2 * F, bytes_accessed=rows * length * 2, transcendentals=0),
    )(flat, flat, flat, flat, angles, good)


def pieces(value):
    high = value.astype(jnp.bfloat16)
    rest = value - high.astype(jnp.float32)
    middle = rest.astype(jnp.bfloat16)
    return high, middle, (rest - middle.astype(jnp.float32)).astype(jnp.bfloat16)


def whiten_kernel(spec, left, right, band, good, *outs):
    windows, channels = spec.shape[:2]
    filtered = []
    keep = keep_column(good)
    for window in range(windows):
        stack = jnp.concatenate([left[window], *pieces(spec[window]), right[window]], axis=0)
        own = band[:, HALO : HALO + channels]
        taps = jnp.concatenate([band[:, :HALO], own, own, own, band[:, HALO + channels :]], axis=1)
        filtered.append(jnp.dot(taps, stack, preferred_element_type=jnp.float32) * keep)
    spectrum = jnp.concatenate(filtered, axis=0)
    real, imag = spectrum[:, :F], spectrum[:, F:]
    magnitude = jnp.sqrt(real * real + imag * imag)
    bins = lax.broadcasted_iota(jnp.int32, (F, F), 0)
    others = lax.broadcasted_iota(jnp.int32, (F, F), 1)
    near = jnp.where(jnp.abs(bins - others) <= SMOOTH, 1.0, 0.0).astype(jnp.bfloat16)
    amplitude = sum(jnp.dot(piece, near, preferred_element_type=jnp.float32) for piece in pieces(magnitude))
    bin_row = lax.broadcasted_iota(jnp.int32, (1, F), 1)
    count = jnp.minimum(bin_row + SMOOTH, F - 1) - jnp.maximum(bin_row - SMOOTH, 0) + 1
    amplitude = amplitude * (1.0 / count.astype(jnp.float32))
    inverse = 1.0 / (amplitude + 1e-06)
    real = (real * inverse).astype(jnp.bfloat16)
    imag = (imag * inverse).astype(jnp.bfloat16)
    full, *parts = outs
    for window in range(windows):
        rows = slice(window * channels, (window + 1) * channels)
        full[window, :, :F] = real[rows]
        full[window, :, F:] = imag[rows]
        for part, (begin, end) in zip(parts, Z_GROUPS):
            for at, (start, width) in enumerate(CHUNKS[begin:end]):
                part[at, 0, window, :, :width] = real[rows, start : start + width]
                part[at, 0, window, :, width:] = imag[rows, start : start + width]


def whiten(spec, left, right, band, good):
    windows, channels, _ = spec.shape
    return pl.pallas_call(
        whiten_kernel,
        out_shape=[
            jax.ShapeDtypeStruct(shape, jnp.bfloat16)
            for shape in [(windows, channels, 2 * F)]
            + [(end - begin, 1, windows, channels, 2 * CHUNKS[0][1]) for begin, end in Z_GROUPS]
        ],
        compiler_params=pltpu.CompilerParams(vmem_limit_bytes=40 * MIB),
        cost_estimate=pl.CostEstimate(flops=2 * windows * channels * F * F * 3, bytes_accessed=5 * MIB // 2, transcendentals=windows * channels * F),
    )(spec, left, right, band, good)


def eye(size):
    rows = lax.broadcasted_iota(jnp.int32, (size, size), 0)
    cols = lax.broadcasted_iota(jnp.int32, (size, size), 1)
    return jnp.where(rows == cols, 1.0, 0.0).astype(jnp.bfloat16)


def turned(left_unit, rows):
    return lax.dot_general(left_unit, rows, NT, preferred_element_type=jnp.float32)


def swapper(outer, inner):
    size = outer * inner
    rows = lax.broadcasted_iota(jnp.int32, (size, size), 0)
    cols = lax.broadcasted_iota(jnp.int32, (size, size), 1)
    return jnp.where(cols == rows % outer * inner + rows // outer, 1.0, 0.0).astype(jnp.bfloat16)


def moved(swap, rows):
    return jnp.dot(swap, rows, preferred_element_type=jnp.float32).astype(jnp.bfloat16)


def own_kernel(here, near, far, out, by_window):
    own = [here, near.at[0], far, near.at[1]]
    each, channels, _ = here.shape
    windows, quads = each * len(own), channels // 4
    joined = GROUP // each
    swap = swapper(GROUP, GROUP)
    for start in range(0, windows, GROUP):
        for channel in range(0, channels, GROUP):
            block = [o[:, channel : channel + GROUP, :] for o in own[start // each : start // each + joined]]
            rows = moved(swap, jnp.concatenate(block, axis=0).reshape(GROUP * GROUP, 2 * F))
            by_window[channel : channel + GROUP, start : start + GROUP, :] = rows.reshape(GROUP, GROUP, 2 * F)
    unit = eye(F // 2)
    for quad in range(quads):
        for start in range(0, F, F // 2):
            rows = []
            for channel in range(quad, channels, quads):
                rows += [by_window[channel, :, side + start : side + start + F // 2] for side in (0, F)]
            out[quad, start : start + F // 2, :] = turned(unit, jnp.concatenate(rows, axis=0)).astype(jnp.bfloat16)


def turn_own(here, near, far):
    each, channels, _ = here.shape
    windows = each * 4
    return pl.pallas_call(
        own_kernel,
        out_shape=jax.ShapeDtypeStruct((channels // 4, F, 8 * windows), jnp.bfloat16),
        scratch_shapes=[pltpu.VMEM((channels, windows, 2 * F), jnp.bfloat16)],
        compiler_params=pltpu.CompilerParams(vmem_limit_bytes=40 * MIB),
        cost_estimate=pl.CostEstimate(flops=2 * 8192 * 65536, bytes_accessed=4 * MIB, transcendentals=0),
    )(here, near, far)


def cross_kernel(here, near, far, by_channel, out, by_window, sums):
    sources = [here, near.at[0], far.at[0], near.at[1]]
    each, count, both = here.shape
    quads, _, wide = by_channel.shape
    channels, half = 4 * quads, wide // 4
    windows, width = half // 2, both // 2
    unit = eye(width)
    swap = swapper(GROUP, GROUP)
    swap_quads = swapper(quads, GROUP)
    for window in range(0, windows, 2):
        rows = []
        for one in range(window, window + 2):
            source = sources[one // each]
            rows += [source[one % each, :, :width], source[one % each, :, width:]]
        both_turned = turned(unit, jnp.concatenate(rows, axis=0)).astype(jnp.bfloat16)
        by_window[window] = both_turned[:, : 2 * count]
        by_window[window + 1] = both_turned[:, 2 * count :]
    first = lax.broadcasted_iota(jnp.int32, (1, 2 * half), 1) < half
    sign = jnp.where(lax.broadcasted_iota(jnp.int32, (1, 2 * count), 1) < count, 1.0, -1.0)
    empty = jnp.zeros((2 * windows, 2 * count), jnp.bfloat16)

    def one_group(group, carry):
        bins = pl.ds(pl.multiple_of(group * GROUP, GROUP), GROUP)
        rows = [
            by_window[start : start + GROUP, bins, :].reshape(GROUP * GROUP, 2 * count)
            for start in range(0, windows, GROUP)
        ]
        rights = jnp.dot(swap, jnp.concatenate(rows, axis=1), preferred_element_type=jnp.float32)
        lefts = jnp.dot(
            swap_quads, by_channel[:, bins, :].reshape(quads * GROUP, 4 * half), preferred_element_type=jnp.float32
        )
        results = []
        for at in range(0, GROUP, 2):
            two = []
            for one in range(at, at + 2):
                here = rights[one * GROUP : (one + 1) * GROUP]
                src = jnp.concatenate(
                    [here[:, i * 2 * count : (i + 1) * 2 * count] for i in range(windows // GROUP)], axis=0
                )
                two.append(jnp.concatenate([src * sign, pltpu.roll(src, count, axis=1)], axis=0).astype(jnp.bfloat16))
            right = jnp.concatenate(
                [jnp.concatenate([two[0], empty], axis=1), jnp.concatenate([empty, two[1]], axis=1)], axis=0
            )
            left = []
            for tile in range(0, 4 * half, 2 * half):
                one, other = (lefts[i * quads : (i + 1) * quads, tile : tile + 2 * half] for i in (at, at + 1))
                left.append(jnp.where(first, one, pltpu.roll(other, half, axis=1)))
                left.append(jnp.where(first, pltpu.roll(one, half, axis=1), other))
            left = jnp.concatenate(left, axis=0).astype(jnp.bfloat16)
            result = jnp.dot(left, right, preferred_element_type=jnp.float32).astype(jnp.bfloat16)
            results += [result[:, : 2 * count], result[:, 2 * count :]]
        halves = [
            jnp.concatenate([r[start : start + GROUP] for r in results], axis=0) for start in range(0, channels, GROUP)
        ]
        done = moved(swap, jnp.concatenate(halves, axis=1))
        for channel in range(channels):
            row, side = channel % GROUP, channel // GROUP
            sums[channel, bins, :] = done[
                row * GROUP : (row + 1) * GROUP, side * 2 * count : (side + 1) * 2 * count
            ]
        return carry

    lax.fori_loop(0, width // GROUP, one_group, 0, unroll=8)
    unit = eye(2 * count)
    part = 256 // LAG_ROWS
    swap = swapper(LAG_ROWS, part)
    for group in range(channels // LAG_ROWS):
        by_bin = []
        for channel in range(group * LAG_ROWS, (group + 1) * LAG_ROWS, 2):
            rows = jnp.concatenate([sums[channel], sums[channel + 1]], axis=0)
            both_turned = turned(unit, rows).astype(jnp.bfloat16)
            by_bin += [both_turned[:, :width], both_turned[:, width:]]
        for start in range(0, count, part):
            rows = jnp.concatenate(
                [
                    jnp.concatenate([b[start : start + part], b[count + start : count + start + part]], axis=1)
                    for b in by_bin
                ],
                axis=0,
            )
            rows = moved(swap, rows)
            at = slice(start * LAG_ROWS, (start + part) * LAG_ROWS)
            out[group, 0, at, :] = rows[:, :width]
            out[group, 1, at, :] = rows[:, width:]


def cross(here, near, far, by_channel, first_bin):
    each, count, both = here.shape
    quads, _, wide = by_channel.shape
    channels, windows, width = 4 * quads, wide // 8, both // 2
    return pl.pallas_call(
        cross_kernel,
        grid=(1,),
        in_specs=[pl.BlockSpec(a.shape, functools.partial(lambda n, i: (0,) * n, a.ndim)) for a in (here, near, far)]
        + [pl.BlockSpec((quads, width, wide), lambda i: (0, first_bin // width, 0))],
        out_specs=pl.BlockSpec((channels // LAG_ROWS, 2, count * LAG_ROWS, width), lambda i: (0, 0, 0, 0)),
        out_shape=jax.ShapeDtypeStruct((channels // LAG_ROWS, 2, count * LAG_ROWS, width), jnp.bfloat16),
        scratch_shapes=[
            pltpu.VMEM((windows, width, 2 * count), jnp.bfloat16),
            pltpu.VMEM((channels, width, 2 * count), jnp.bfloat16),
        ],
        compiler_params=pltpu.CompilerParams(vmem_limit_bytes=40 * MIB),
        cost_estimate=pl.CostEstimate(flops=2 * width * 36 * 65536, bytes_accessed=4 * MIB, transcendentals=0),
    )(here, near, far, by_channel)


def lag_kernel(scaling, *refs):
    *stacked, table, edge, out = refs
    count, channels, _ = out.shape
    real, imag = (jnp.concatenate([chunk[0, side] for chunk in stacked], axis=1) for side in range(2))
    size = count * channels
    lane = lax.broadcasted_iota(jnp.int32, (size, LAG_FINE), 1)
    mirror = (LAG_FINE - lane) % LAG_FINE

    def parts(start, width):
        even = jnp.dot(real, table[:F, start : start + width], preferred_element_type=jnp.float32)
        odd = jnp.dot(imag, table[F:, start : start + width], preferred_element_type=jnp.float32)
        return even, odd

    half = LAGS // 2
    products = real.astype(jnp.float32) * edge[:1] + imag.astype(jnp.float32) * edge[1:]
    above = jnp.sum(products, axis=1, keepdims=True) * scaling
    for start in range(half - 2 * LAG_FINE, -1, -2 * LAG_FINE):
        even, odd = parts(start, 2 * LAG_FINE)
        after_zero = (even - odd) * scaling
        before_zero = (even + odd) * scaling
        out[:, :, half + start : half + start + 2 * LAG_FINE] = after_zero.reshape(count, channels, 2 * LAG_FINE)
        for tile in (1, 0):
            turned_round = jnp.take_along_axis(
                before_zero[:, tile * LAG_FINE : (tile + 1) * LAG_FINE], mirror, axis=1, mode="promise_in_bounds"
            )
            at = half - start - (tile + 1) * LAG_FINE
            out[:, :, at : at + LAG_FINE] = jnp.where(lane == 0, above, turned_round).reshape(count, channels, LAG_FINE)
            above = turned_round


def lagged(stacked, table, scaling):
    groups, _, size, _ = stacked[0].shape
    edge = np.concatenate(unit_angles(np.array([LAGS // 2]), 0), axis=0).astype(jnp.bfloat16).astype(np.float32)
    count = size // LAG_ROWS
    return pl.pallas_call(
        functools.partial(lag_kernel, scaling),
        grid=(groups,),
        in_specs=[pl.BlockSpec((1, 2, size, s.shape[3]), lambda i: (i, 0, 0, 0)) for s in stacked]
        + [pl.BlockSpec(a.shape, lambda i: (0, 0)) for a in (table, edge)],
        out_specs=pl.BlockSpec((count, LAG_ROWS, LAGS), lambda i: (0, i, 0)),
        out_shape=jax.ShapeDtypeStruct((count, groups * LAG_ROWS, LAGS), jnp.float32),
        compiler_params=pltpu.CompilerParams(vmem_limit_bytes=48 * MIB),
        cost_estimate=pl.CostEstimate(
            flops=2 * groups * size * F * LAGS, bytes_accessed=groups * size * LAGS * 4, transcendentals=0
        ),
    )(*stacked, table, edge)


def table_kernel(angles, out):
    fine_cos, fine_sin = angles[:, :LAG_FINE], angles[:, LAG_FINE : 2 * LAG_FINE]
    tiles = out.shape[1] // LAG_FINE
    for tile in range(tiles):
        big_cos = angles[:, 2 * LAG_FINE + tile : 2 * LAG_FINE + tile + 1]
        big_sin = angles[:, 2 * LAG_FINE + tiles + tile : 2 * LAG_FINE + tiles + tile + 1]
        cols = slice(tile * LAG_FINE, (tile + 1) * LAG_FINE)
        out[:F, cols] = (big_cos * fine_cos - big_sin * fine_sin).astype(jnp.bfloat16)
        out[F:, cols] = (big_sin * fine_cos + big_cos * fine_sin).astype(jnp.bfloat16)


def lag_table():
    tiles = LAGS // 2 // LAG_FINE
    coarse = unit_angles(np.arange(tiles) * LAG_FINE, 1)
    angles = np.concatenate(unit_angles(np.arange(LAG_FINE), 1) + coarse, axis=1)
    return pl.pallas_call(
        table_kernel,
        out_shape=jax.ShapeDtypeStruct((2 * F, tiles * LAG_FINE), jnp.bfloat16),
        compiler_params=pltpu.CompilerParams(vmem_limit_bytes=40 * MIB),
        cost_estimate=pl.CostEstimate(flops=8 * F * tiles * LAG_FINE, bytes_accessed=4 * MIB, transcendentals=0),
    )(angles)


def make_band(filter_taps, channel_count):
    kernel = jnp.concatenate(
        [
            -filter_taps[:HALO].astype(jnp.float32),
            jnp.ones((1,), jnp.float32),
            -filter_taps[HALO:].astype(jnp.float32),
        ]
    )
    row_ids = jnp.arange(channel_count, dtype=jnp.int32)[:, None]
    columns = jnp.arange(channel_count + 2 * HALO, dtype=jnp.int32)[None, :]
    offset = columns - row_ids
    choose = offset[:, :, None] == jnp.arange(2 * HALO + 1, dtype=jnp.int32)[None, None, :]
    return jnp.sum(jnp.where(choose, kernel[None, None, :], 0.0), axis=2).astype(jnp.bfloat16)


def pick_kernel(held, across, selector, here, near, far):
    count = here.shape[1]
    for window in range(held.shape[1]):
        rows = [blocks[i, window] for blocks in (held, across) for i in range(blocks.shape[0])]
        picked = jnp.dot(selector[...], jnp.concatenate(rows, axis=0), preferred_element_type=jnp.float32)
        picked = picked.astype(jnp.bfloat16)
        here[window] = picked[:count]
        near[window] = picked[count : 2 * count]
        for at in range(far.shape[0]):
            far[at, window] = picked[(2 + at) * count : (3 + at) * count]


def pick(held, across, selector, groups):
    _, windows, _, both = held.shape
    count = selector.shape[0] // groups
    one = (windows, count, both)
    return pl.pallas_call(
        pick_kernel,
        out_shape=[jax.ShapeDtypeStruct(shape, jnp.bfloat16) for shape in (one, one, (groups - 2, *one))],
        compiler_params=pltpu.CompilerParams(vmem_limit_bytes=40 * MIB),
        cost_estimate=pl.CostEstimate(
            flops=2 * windows * selector.size * both, bytes_accessed=2 * windows * both * sum(selector.shape), transcendentals=0
        ),
    )(held, across, selector)


def swapped(value, axis, step):
    return lax.ppermute(value, axis, [(i, i ^ step) for i in range(lax.axis_size(axis))])


def after(value, earlier):
    return lax.optimization_barrier((value, earlier))[0]


def per_device(traces, filter_taps, good_channels, source_index):
    window_count, channel_count, _ = traces.shape
    good = good_channels[None, :]
    spec, head, tail = transform(traces, good)
    blocks = lax.axis_size("chan")
    groups = lax.axis_size("win")
    left = lax.ppermute(tail, "chan", [(i, i + 1) for i in range(blocks - 1)])
    right = lax.ppermute(head, "chan", [(i + 1, i) for i in range(blocks - 1)])
    table = lag_table()
    left = after(left, table)
    full, *parts = whiten(spec, left, right, make_band(filter_taps, channel_count), good)

    order = [0]
    step = blocks // 2
    while step:
        order += [place ^ step for place in order]
        step //= 2
    order = jnp.asarray(order, jnp.int32) ^ lax.axis_index("chan")
    own_ids = jnp.arange(channel_count, dtype=jnp.int32)
    channel_ids = (order[:, None] * channel_count + own_ids[None, :]).reshape(-1)
    by_group = source_index.reshape(groups, -1)
    here = lax.axis_index("win")
    wanted = jnp.concatenate([lax.dynamic_slice_in_dim(by_group, here ^ step, 1) for step in range(groups)], axis=0)
    selector = (wanted.reshape(-1)[:, None] == channel_ids[None, :]).astype(jnp.bfloat16)

    own_far = swapped(full, "win", 2)
    own_near = swapped(jnp.stack([full, own_far]), "win", 1)
    by_channel = turn_own(full, own_near, own_far)
    gathered, picked, stacked = [], [], []
    chunks = len(CHUNKS)

    def gather(part):
        held, step = part, blocks // 2
        while step > 1:
            received = swapped(held, "chan", step)
            if step > 2:
                held = jnp.concatenate([held, received], axis=1)
                if step == blocks // 2:
                    first_held.append(held)
                    if len(gathered) > 1:
                        held = after(held, picked[0][0])
            step //= 2
        gathered.extend(jnp.concatenate([held[i], received[i]], axis=0) for i in range(part.shape[0]))

    def exchange(at):
        held = after(gathered[at], picked[-1][0]) if at else gathered[at]
        across = swapped(held, "chan", 1)
        if at > 1:
            finish(at - 2)
            across = after(across, stacked[-1])
        here, near, far = pick(held, across, selector, groups)
        picked.append((here, near, swapped(far, "win", 2)))

    def finish(at):
        here, near, far = picked[at]
        if at == chunks - 1:
            far = after(far, stacked[-1])
        near = swapped(jnp.stack([near, far[1]]), "win", 1)
        stacked.append(cross(here, near, far, by_channel, CHUNKS[at][0]))

    first_held = []
    for part in parts:
        gather(after(part, [first_held[-1]] + [own_far] * (len(first_held) > 1)) if first_held else part)
        if len(gathered) == 2:
            exchange(0)
    for at in range(1, chunks):
        exchange(at)
    for at in range(len(stacked), chunks):
        finish(at)
    return lagged(stacked, table, 1.0 / math.sqrt(F * window_count * groups))


def solution(mesh):
    placed = (P("win", "chan", None), P(), P("chan"), P())
    return jax.shard_map(
        per_device, mesh=mesh, in_specs=placed, out_specs=P("win", "chan", None), check_vma=False
    )
```

```python
import functools
import math

import jax
import jax.numpy as jnp
import numpy as np
from jax import lax
from jax.experimental import pallas as pl
from jax.experimental.pallas import tpu as pltpu
from jax.sharding import PartitionSpec as P

L = 7680
F = 512
LAGS = 2048
HALO = 16
SMOOTH = 64
K0 = 31
QUARTER = L // 4
STEP = 640
FINE = 32
CHUNKS = tuple((start, 128) for start in range(0, F, 128))
Z_GROUPS = ((0, 1), (1, 3), (3, 4))
GROUP = 16
LAG_FINE = 128
LAG_ROWS = 8
NT = (((1,), (1,)), ((), ()))
MIB = 1024 * 1024


def unit_angles(positions, axis):
    bins = K0 + np.arange(F, dtype=np.int64)
    phase = np.mod(np.expand_dims(positions, 1 - axis) * np.expand_dims(bins, axis), L)
    angles = phase * (2.0 * math.pi / L)
    return np.cos(angles).astype(np.float32), np.sin(angles).astype(np.float32)


def keep_column(good):
    count = good.shape[1]
    rows = lax.broadcasted_iota(jnp.int32, (count, count), 0)
    cols = lax.broadcasted_iota(jnp.int32, (count, count), 1)
    return jnp.sum(jnp.where(rows == cols, good[...].astype(jnp.float32), 0.0), axis=1, keepdims=True)


def transform_kernel(x0, x1, x2, x3, angles, good, spec, head, tail, table, total):
    step = pl.program_id(0)
    rows = x0.shape[0]
    coarse = QUARTER // FINE

    def fill(of_step):
        fine_cos = angles[2 * coarse : 2 * coarse + FINE, :]
        fine_sin = angles[2 * coarse + FINE :, :]
        for part in range(STEP // FINE):
            big_cos = angles[pl.ds(of_step * (STEP // FINE) + part, 1), :]
            big_sin = angles[pl.ds(coarse + of_step * (STEP // FINE) + part, 1), :]
            at = pl.ds(part * FINE, FINE)
            table[of_step % 2, at, :F] = (big_cos * fine_cos - big_sin * fine_sin).astype(jnp.bfloat16)
            table[of_step % 2, at, F:] = (-(big_sin * fine_cos + big_cos * fine_sin)).astype(jnp.bfloat16)

    @pl.when(step == 0)
    def _():
        total[...] = jnp.zeros_like(total)
        fill(step)

    for quarter, x in enumerate((x0, x1, x2, x3)):
        at = pl.ds(quarter * rows, rows)
        total[at, :] += jnp.dot(x[...], table[step % 2], preferred_element_type=jnp.float32)
    fill(jnp.minimum(step + 1, pl.num_programs(0) - 1))

    @pl.when(step == pl.num_programs(0) - 1)
    def _():
        turn = (K0 + lax.broadcasted_iota(jnp.int32, (1, F), 1)) % 4
        even = turn % 2 == 0
        sign = jnp.where(turn < 2, 1.0, -1.0)
        channels = good.shape[1]
        keep = keep_column(good)
        for window in range(rows // channels):
            re = [total[pl.ds(q * rows + window * channels, channels), :F] for q in range(4)]
            im = [total[pl.ds(q * rows + window * channels, channels), F:] for q in range(4)]
            real = jnp.where(even, re[0] + re[2] + sign * (re[1] + re[3]), re[0] - re[2] + sign * (im[1] - im[3])) * keep
            imag = jnp.where(even, im[0] + im[2] + sign * (im[1] + im[3]), im[0] - im[2] - sign * (re[1] - re[3])) * keep
            spec[window, :, :F] = real
            spec[window, :, F:] = imag
            head[window, :, :F] = real[:HALO].astype(jnp.bfloat16)
            head[window, :, F:] = imag[:HALO].astype(jnp.bfloat16)
            tail[window, :, :F] = real[channels - HALO :].astype(jnp.bfloat16)
            tail[window, :, F:] = imag[channels - HALO :].astype(jnp.bfloat16)


def transform(traces, good):
    windows, channels, length = traces.shape
    rows = windows * channels
    steps = QUARTER // STEP
    flat = traces.reshape(rows, length)
    coarse = unit_angles(np.arange(QUARTER // FINE) * FINE, 0)
    angles = np.concatenate(coarse + unit_angles(np.arange(FINE), 0), axis=0)
    whole = lambda *shape: pl.BlockSpec(shape, lambda k: (0,) * len(shape))
    return pl.pallas_call(
        transform_kernel,
        grid=(steps,),
        in_specs=[pl.BlockSpec((rows, STEP), functools.partial(lambda q, k: (0, q * steps + k), q)) for q in range(4)]
        + [whole(*angles.shape), whole(1, channels)],
        out_specs=[whole(windows, channels, 2 * F), whole(windows, HALO, 2 * F), whole(windows, HALO, 2 * F)],
        out_shape=[
            jax.ShapeDtypeStruct((windows, channels, 2 * F), jnp.float32),
            jax.ShapeDtypeStruct((windows, HALO, 2 * F), jnp.bfloat16),
            jax.ShapeDtypeStruct((windows, HALO, 2 * F), jnp.bfloat16),
        ],
        scratch_shapes=[pltpu.VMEM((2, STEP, 2 * F), jnp.bfloat16), pltpu.VMEM((4 * rows, 2 * F), jnp.float32)],
        compiler_params=pltpu.CompilerParams(vmem_limit_bytes=60 * MIB),
        cost_estimate=pl.CostEstimate(flops=2 * rows * length * 2 * F, bytes_accessed=rows * length * 2, transcendentals=0),
    )(flat, flat, flat, flat, angles, good)


def pieces(value):
    high = value.astype(jnp.bfloat16)
    rest = value - high.astype(jnp.float32)
    middle = rest.astype(jnp.bfloat16)
    return high, middle, (rest - middle.astype(jnp.float32)).astype(jnp.bfloat16)


def whiten_kernel(spec, left, right, band, good, *outs):
    windows, channels = spec.shape[:2]
    filtered = []
    keep = keep_column(good)
    for window in range(windows):
        stack = jnp.concatenate([left[window], *pieces(spec[window]), right[window]], axis=0)
        own = band[:, HALO : HALO + channels]
        taps = jnp.concatenate([band[:, :HALO], own, own, own, band[:, HALO + channels :]], axis=1)
        filtered.append(jnp.dot(taps, stack, preferred_element_type=jnp.float32) * keep)
    spectrum = jnp.concatenate(filtered, axis=0)
    real, imag = spectrum[:, :F], spectrum[:, F:]
    magnitude = jnp.sqrt(real * real + imag * imag)
    bins = lax.broadcasted_iota(jnp.int32, (F, F), 0)
    others = lax.broadcasted_iota(jnp.int32, (F, F), 1)
    near = jnp.where(jnp.abs(bins - others) <= SMOOTH, 1.0, 0.0).astype(jnp.bfloat16)
    amplitude = sum(jnp.dot(piece, near, preferred_element_type=jnp.float32) for piece in pieces(magnitude))
    bin_row = lax.broadcasted_iota(jnp.int32, (1, F), 1)
    count = jnp.minimum(bin_row + SMOOTH, F - 1) - jnp.maximum(bin_row - SMOOTH, 0) + 1
    amplitude = amplitude * (1.0 / count.astype(jnp.float32))
    inverse = 1.0 / (amplitude + 1e-06)
    real = (real * inverse).astype(jnp.bfloat16)
    imag = (imag * inverse).astype(jnp.bfloat16)
    full, *parts = outs
    for window in range(windows):
        rows = slice(window * channels, (window + 1) * channels)
        full[window, :, :F] = real[rows]
        full[window, :, F:] = imag[rows]
        for part, (begin, end) in zip(parts, Z_GROUPS):
            for at, (start, width) in enumerate(CHUNKS[begin:end]):
                part[at, 0, window, :, :width] = real[rows, start : start + width]
                part[at, 0, window, :, width:] = imag[rows, start : start + width]


def whiten(spec, left, right, band, good):
    windows, channels, _ = spec.shape
    return pl.pallas_call(
        whiten_kernel,
        out_shape=[
            jax.ShapeDtypeStruct(shape, jnp.bfloat16)
            for shape in [(windows, channels, 2 * F)]
            + [(end - begin, 1, windows, channels, 2 * CHUNKS[0][1]) for begin, end in Z_GROUPS]
        ],
        compiler_params=pltpu.CompilerParams(vmem_limit_bytes=40 * MIB),
        cost_estimate=pl.CostEstimate(flops=2 * windows * channels * F * F * 3, bytes_accessed=5 * MIB // 2, transcendentals=windows * channels * F),
    )(spec, left, right, band, good)


def eye(size):
    rows = lax.broadcasted_iota(jnp.int32, (size, size), 0)
    cols = lax.broadcasted_iota(jnp.int32, (size, size), 1)
    return jnp.where(rows == cols, 1.0, 0.0).astype(jnp.bfloat16)


def turned(left_unit, rows):
    return lax.dot_general(left_unit, rows, NT, preferred_element_type=jnp.float32)


def swapper(outer, inner):
    size = outer * inner
    rows = lax.broadcasted_iota(jnp.int32, (size, size), 0)
    cols = lax.broadcasted_iota(jnp.int32, (size, size), 1)
    return jnp.where(cols == rows % outer * inner + rows // outer, 1.0, 0.0).astype(jnp.bfloat16)


def moved(swap, rows):
    return jnp.dot(swap, rows, preferred_element_type=jnp.float32).astype(jnp.bfloat16)


def own_kernel(here, near, far, out, by_window):
    own = [here, near.at[0], far, near.at[1]]
    each, channels, _ = here.shape
    windows, quads = each * len(own), channels // 4
    joined = GROUP // each
    swap = swapper(GROUP, GROUP)
    for start in range(0, windows, GROUP):
        for channel in range(0, channels, GROUP):
            block = [o[:, channel : channel + GROUP, :] for o in own[start // each : start // each + joined]]
            rows = moved(swap, jnp.concatenate(block, axis=0).reshape(GROUP * GROUP, 2 * F))
            by_window[channel : channel + GROUP, start : start + GROUP, :] = rows.reshape(GROUP, GROUP, 2 * F)
    unit = eye(F // 2)
    for quad in range(quads):
        for start in range(0, F, F // 2):
            rows = []
            for channel in range(quad, channels, quads):
                rows += [by_window[channel, :, side + start : side + start + F // 2] for side in (0, F)]
            out[quad, start : start + F // 2, :] = turned(unit, jnp.concatenate(rows, axis=0)).astype(jnp.bfloat16)


def turn_own(here, near, far):
    each, channels, _ = here.shape
    windows = each * 4
    return pl.pallas_call(
        own_kernel,
        out_shape=jax.ShapeDtypeStruct((channels // 4, F, 8 * windows), jnp.bfloat16),
        scratch_shapes=[pltpu.VMEM((channels, windows, 2 * F), jnp.bfloat16)],
        compiler_params=pltpu.CompilerParams(vmem_limit_bytes=40 * MIB),
        cost_estimate=pl.CostEstimate(flops=2 * 8192 * 65536, bytes_accessed=4 * MIB, transcendentals=0),
    )(here, near, far)


def cross_kernel(here, near, far, by_channel, out, by_window, sums):
    sources = [here, near.at[0], far.at[0], near.at[1]]
    each, count, both = here.shape
    quads, _, wide = by_channel.shape
    channels, half = 4 * quads, wide // 4
    windows, width = half // 2, both // 2
    unit = eye(width)
    swap = swapper(GROUP, GROUP)
    swap_quads = swapper(quads, GROUP)
    for window in range(0, windows, 2):
        rows = []
        for one in range(window, window + 2):
            source = sources[one // each]
            rows += [source[one % each, :, :width], source[one % each, :, width:]]
        both_turned = turned(unit, jnp.concatenate(rows, axis=0)).astype(jnp.bfloat16)
        by_window[window] = both_turned[:, : 2 * count]
        by_window[window + 1] = both_turned[:, 2 * count :]
    first = lax.broadcasted_iota(jnp.int32, (1, 2 * half), 1) < half
    sign = jnp.where(lax.broadcasted_iota(jnp.int32, (1, 2 * count), 1) < count, 1.0, -1.0)
    empty = jnp.zeros((2 * windows, 2 * count), jnp.bfloat16)

    def one_group(group, carry):
        bins = pl.ds(pl.multiple_of(group * GROUP, GROUP), GROUP)
        rows = [
            by_window[start : start + GROUP, bins, :].reshape(GROUP * GROUP, 2 * count)
            for start in range(0, windows, GROUP)
        ]
        rights = jnp.dot(swap, jnp.concatenate(rows, axis=1), preferred_element_type=jnp.float32)
        lefts = jnp.dot(
            swap_quads, by_channel[:, bins, :].reshape(quads * GROUP, 4 * half), preferred_element_type=jnp.float32
        )
        results = []
        for at in range(0, GROUP, 2):
            two = []
            for one in range(at, at + 2):
                here = rights[one * GROUP : (one + 1) * GROUP]
                src = jnp.concatenate(
                    [here[:, i * 2 * count : (i + 1) * 2 * count] for i in range(windows // GROUP)], axis=0
                )
                two.append(jnp.concatenate([src * sign, pltpu.roll(src, count, axis=1)], axis=0).astype(jnp.bfloat16))
            right = jnp.concatenate(
                [jnp.concatenate([two[0], empty], axis=1), jnp.concatenate([empty, two[1]], axis=1)], axis=0
            )
            left = []
            for tile in range(0, 4 * half, 2 * half):
                one, other = (lefts[i * quads : (i + 1) * quads, tile : tile + 2 * half] for i in (at, at + 1))
                left.append(jnp.where(first, one, pltpu.roll(other, half, axis=1)))
                left.append(jnp.where(first, pltpu.roll(one, half, axis=1), other))
            left = jnp.concatenate(left, axis=0).astype(jnp.bfloat16)
            result = jnp.dot(left, right, preferred_element_type=jnp.float32).astype(jnp.bfloat16)
            results += [result[:, : 2 * count], result[:, 2 * count :]]
        halves = [
            jnp.concatenate([r[start : start + GROUP] for r in results], axis=0) for start in range(0, channels, GROUP)
        ]
        done = moved(swap, jnp.concatenate(halves, axis=1))
        for channel in range(channels):
            row, side = channel % GROUP, channel // GROUP
            sums[channel, bins, :] = done[
                row * GROUP : (row + 1) * GROUP, side * 2 * count : (side + 1) * 2 * count
            ]
        return carry

    lax.fori_loop(0, width // GROUP, one_group, 0, unroll=8)
    unit = eye(2 * count)
    part = 256 // LAG_ROWS
    swap = swapper(LAG_ROWS, part)
    for group in range(channels // LAG_ROWS):
        by_bin = []
        for channel in range(group * LAG_ROWS, (group + 1) * LAG_ROWS, 2):
            rows = jnp.concatenate([sums[channel], sums[channel + 1]], axis=0)
            both_turned = turned(unit, rows).astype(jnp.bfloat16)
            by_bin += [both_turned[:, :width], both_turned[:, width:]]
        for start in range(0, count, part):
            rows = jnp.concatenate(
                [
                    jnp.concatenate([b[start : start + part], b[count + start : count + start + part]], axis=1)
                    for b in by_bin
                ],
                axis=0,
            )
            rows = moved(swap, rows)
            at = slice(start * LAG_ROWS, (start + part) * LAG_ROWS)
            out[group, 0, at, :] = rows[:, :width]
            out[group, 1, at, :] = rows[:, width:]


def cross(here, near, far, by_channel, first_bin):
    each, count, both = here.shape
    quads, _, wide = by_channel.shape
    channels, windows, width = 4 * quads, wide // 8, both // 2
    return pl.pallas_call(
        cross_kernel,
        grid=(1,),
        in_specs=[pl.BlockSpec(a.shape, functools.partial(lambda n, i: (0,) * n, a.ndim)) for a in (here, near, far)]
        + [pl.BlockSpec((quads, width, wide), lambda i: (0, first_bin // width, 0))],
        out_specs=pl.BlockSpec((channels // LAG_ROWS, 2, count * LAG_ROWS, width), lambda i: (0, 0, 0, 0)),
        out_shape=jax.ShapeDtypeStruct((channels // LAG_ROWS, 2, count * LAG_ROWS, width), jnp.bfloat16),
        scratch_shapes=[
            pltpu.VMEM((windows, width, 2 * count), jnp.bfloat16),
            pltpu.VMEM((channels, width, 2 * count), jnp.bfloat16),
        ],
        compiler_params=pltpu.CompilerParams(vmem_limit_bytes=40 * MIB),
        cost_estimate=pl.CostEstimate(flops=2 * width * 36 * 65536, bytes_accessed=4 * MIB, transcendentals=0),
    )(here, near, far, by_channel)


def lag_kernel(scaling, *refs):
    *stacked, table, edge, out = refs
    count, channels, _ = out.shape
    real, imag = (jnp.concatenate([chunk[0, side] for chunk in stacked], axis=1) for side in range(2))
    size = count * channels
    lane = lax.broadcasted_iota(jnp.int32, (size, LAG_FINE), 1)
    mirror = (LAG_FINE - lane) % LAG_FINE

    def parts(start, width):
        even = jnp.dot(real, table[:F, start : start + width], preferred_element_type=jnp.float32)
        odd = jnp.dot(imag, table[F:, start : start + width], preferred_element_type=jnp.float32)
        return even, odd

    half = LAGS // 2
    products = real.astype(jnp.float32) * edge[:1] + imag.astype(jnp.float32) * edge[1:]
    above = jnp.sum(products, axis=1, keepdims=True) * scaling
    for start in range(half - 2 * LAG_FINE, -1, -2 * LAG_FINE):
        even, odd = parts(start, 2 * LAG_FINE)
        after_zero = (even - odd) * scaling
        before_zero = (even + odd) * scaling
        out[:, :, half + start : half + start + 2 * LAG_FINE] = after_zero.reshape(count, channels, 2 * LAG_FINE)
        for tile in (1, 0):
            turned_round = jnp.take_along_axis(
                before_zero[:, tile * LAG_FINE : (tile + 1) * LAG_FINE], mirror, axis=1, mode="promise_in_bounds"
            )
            at = half - start - (tile + 1) * LAG_FINE
            out[:, :, at : at + LAG_FINE] = jnp.where(lane == 0, above, turned_round).reshape(count, channels, LAG_FINE)
            above = turned_round


def lagged(stacked, table, scaling):
    groups, _, size, _ = stacked[0].shape
    edge = np.concatenate(unit_angles(np.array([LAGS // 2]), 0), axis=0).astype(jnp.bfloat16).astype(np.float32)
    count = size // LAG_ROWS
    return pl.pallas_call(
        functools.partial(lag_kernel, scaling),
        grid=(groups,),
        in_specs=[pl.BlockSpec((1, 2, size, s.shape[3]), lambda i: (i, 0, 0, 0)) for s in stacked]
        + [pl.BlockSpec(a.shape, lambda i: (0, 0)) for a in (table, edge)],
        out_specs=pl.BlockSpec((count, LAG_ROWS, LAGS), lambda i: (0, i, 0)),
        out_shape=jax.ShapeDtypeStruct((count, groups * LAG_ROWS, LAGS), jnp.float32),
        compiler_params=pltpu.CompilerParams(vmem_limit_bytes=48 * MIB),
        cost_estimate=pl.CostEstimate(
            flops=2 * groups * size * F * LAGS, bytes_accessed=groups * size * LAGS * 4, transcendentals=0
        ),
    )(*stacked, table, edge)


def table_kernel(angles, out):
    fine_cos, fine_sin = angles[:, :LAG_FINE], angles[:, LAG_FINE : 2 * LAG_FINE]
    tiles = out.shape[1] // LAG_FINE
    for tile in range(tiles):
        big_cos = angles[:, 2 * LAG_FINE + tile : 2 * LAG_FINE + tile + 1]
        big_sin = angles[:, 2 * LAG_FINE + tiles + tile : 2 * LAG_FINE + tiles + tile + 1]
        cols = slice(tile * LAG_FINE, (tile + 1) * LAG_FINE)
        out[:F, cols] = (big_cos * fine_cos - big_sin * fine_sin).astype(jnp.bfloat16)
        out[F:, cols] = (big_sin * fine_cos + big_cos * fine_sin).astype(jnp.bfloat16)


def lag_table():
    tiles = LAGS // 2 // LAG_FINE
    coarse = unit_angles(np.arange(tiles) * LAG_FINE, 1)
    angles = np.concatenate(unit_angles(np.arange(LAG_FINE), 1) + coarse, axis=1)
    return pl.pallas_call(
        table_kernel,
        out_shape=jax.ShapeDtypeStruct((2 * F, tiles * LAG_FINE), jnp.bfloat16),
        compiler_params=pltpu.CompilerParams(vmem_limit_bytes=40 * MIB),
        cost_estimate=pl.CostEstimate(flops=8 * F * tiles * LAG_FINE, bytes_accessed=4 * MIB, transcendentals=0),
    )(angles)


def make_band(filter_taps, channel_count):
    kernel = jnp.concatenate(
        [
            -filter_taps[:HALO].astype(jnp.float32),
            jnp.ones((1,), jnp.float32),
            -filter_taps[HALO:].astype(jnp.float32),
        ]
    )
    row_ids = jnp.arange(channel_count, dtype=jnp.int32)[:, None]
    columns = jnp.arange(channel_count + 2 * HALO, dtype=jnp.int32)[None, :]
    offset = columns - row_ids
    choose = offset[:, :, None] == jnp.arange(2 * HALO + 1, dtype=jnp.int32)[None, None, :]
    return jnp.sum(jnp.where(choose, kernel[None, None, :], 0.0), axis=2).astype(jnp.bfloat16)


def pick_kernel(held, across, selector, here, near, far):
    count = here.shape[1]
    for window in range(held.shape[1]):
        rows = [blocks[i, window] for blocks in (held, across) for i in range(blocks.shape[0])]
        picked = jnp.dot(selector[...], jnp.concatenate(rows, axis=0), preferred_element_type=jnp.float32)
        picked = picked.astype(jnp.bfloat16)
        here[window] = picked[:count]
        near[window] = picked[count : 2 * count]
        for at in range(far.shape[0]):
            far[at, window] = picked[(2 + at) * count : (3 + at) * count]


def pick(held, across, selector, groups):
    _, windows, _, both = held.shape
    count = selector.shape[0] // groups
    one = (windows, count, both)
    return pl.pallas_call(
        pick_kernel,
        out_shape=[jax.ShapeDtypeStruct(shape, jnp.bfloat16) for shape in (one, one, (groups - 2, *one))],
        compiler_params=pltpu.CompilerParams(vmem_limit_bytes=40 * MIB),
        cost_estimate=pl.CostEstimate(
            flops=2 * windows * selector.size * both, bytes_accessed=2 * windows * both * sum(selector.shape), transcendentals=0
        ),
    )(held, across, selector)


def swapped(value, axis, step):
    return lax.ppermute(value, axis, [(i, i ^ step) for i in range(lax.axis_size(axis))])


def after(value, earlier):
    return lax.optimization_barrier((value, earlier))[0]


def per_device(traces, filter_taps, good_channels, source_index):
    window_count, channel_count, _ = traces.shape
    good = good_channels[None, :]
    spec, head, tail = transform(traces, good)
    blocks = lax.axis_size("chan")
    groups = lax.axis_size("win")
    left = lax.ppermute(tail, "chan", [(i, i + 1) for i in range(blocks - 1)])
    right = lax.ppermute(head, "chan", [(i + 1, i) for i in range(blocks - 1)])
    table = lag_table()
    left = after(left, table)
    full, *parts = whiten(spec, left, right, make_band(filter_taps, channel_count), good)

    order = [0]
    step = blocks // 2
    while step:
        order += [place ^ step for place in order]
        step //= 2
    order = jnp.asarray(order, jnp.int32) ^ lax.axis_index("chan")
    own_ids = jnp.arange(channel_count, dtype=jnp.int32)
    channel_ids = (order[:, None] * channel_count + own_ids[None, :]).reshape(-1)
    by_group = source_index.reshape(groups, -1)
    here = lax.axis_index("win")
    wanted = jnp.concatenate([lax.dynamic_slice_in_dim(by_group, here ^ step, 1) for step in range(groups)], axis=0)
    selector = (wanted.reshape(-1)[:, None] == channel_ids[None, :]).astype(jnp.bfloat16)

    own_far = swapped(full, "win", 2)
    own_near = swapped(jnp.stack([full, own_far]), "win", 1)
    by_channel = turn_own(full, own_near, own_far)
    gathered, picked, stacked = [], [], []
    chunks = len(CHUNKS)

    def gather(part):
        held, step = part, blocks // 2
        while step > 1:
            received = swapped(held, "chan", step)
            if step > 2:
                held = jnp.concatenate([held, received], axis=1)
                if step == blocks // 2:
                    first_held.append(held)
                    if gathered:
                        held = after(held, picked[0][0] if picked else gathered[0])
            step //= 2
        gathered.extend(jnp.concatenate([held[i], received[i]], axis=0) for i in range(part.shape[0]))

    def exchange(at):
        held = after(gathered[at], picked[-1][0]) if at else gathered[at]
        across = swapped(held, "chan", 1)
        if at > 1:
            finish(at - 2)
        across = after(across, (stacked[-1] if stacked else by_channel) if at else gathered[1])
        here, near, far = pick(held, across, selector, groups)
        picked.append((here, near, swapped(far, "win", 2)))

    def finish(at):
        here, near, far = picked[at]
        if stacked:
            far = after(far, stacked[-1])
        near = swapped(jnp.stack([near, far[1]]), "win", 1)
        stacked.append(cross(here, near, far, by_channel, CHUNKS[at][0]))

    first_held = []
    for part in parts:
        gather(after(part, [first_held[-1]] + [own_far] * (len(first_held) > 1)) if first_held else part)
        if len(gathered) > 1 and not picked:
            exchange(0)
    for at in range(1, chunks):
        exchange(at)
    for at in range(len(stacked), chunks):
        finish(at)
    return lagged(stacked, table, 1.0 / math.sqrt(F * window_count * groups))


def solution(mesh):
    placed = (P("win", "chan", None), P(), P("chan"), P())
    return jax.shard_map(
        per_device, mesh=mesh, in_specs=placed, out_specs=P("win", "chan", None), check_vma=False
    )
```

```python
import functools
import math

import jax
import jax.numpy as jnp
import numpy as np
from jax import lax
from jax.experimental import pallas as pl
from jax.experimental.pallas import tpu as pltpu
from jax.sharding import PartitionSpec as P

L = 7680
F = 512
LAGS = 2048
HALO = 16
SMOOTH = 64
K0 = 31
QUARTER = L // 4
STEP = 640
FINE = 32
CHUNKS = tuple((start, 128) for start in range(0, F, 128))
Z_GROUPS = ((0, 1), (1, 2), (2, 4))
GROUP = 16
LAG_FINE = 128
LAG_ROWS = 8
NT = (((1,), (1,)), ((), ()))
MIB = 1024 * 1024


def unit_angles(positions, axis):
    bins = K0 + np.arange(F, dtype=np.int64)
    phase = np.mod(np.expand_dims(positions, 1 - axis) * np.expand_dims(bins, axis), L)
    angles = phase * (2.0 * math.pi / L)
    return np.cos(angles).astype(np.float32), np.sin(angles).astype(np.float32)


def keep_column(good):
    count = good.shape[1]
    rows = lax.broadcasted_iota(jnp.int32, (count, count), 0)
    cols = lax.broadcasted_iota(jnp.int32, (count, count), 1)
    return jnp.sum(jnp.where(rows == cols, good[...].astype(jnp.float32), 0.0), axis=1, keepdims=True)


def transform_kernel(x0, x1, x2, x3, angles, good, spec, head, tail, table, total):
    step = pl.program_id(0)
    rows = x0.shape[0]
    coarse = QUARTER // FINE

    def fill(of_step):
        fine_cos = angles[2 * coarse : 2 * coarse + FINE, :]
        fine_sin = angles[2 * coarse + FINE :, :]
        for part in range(STEP // FINE):
            big_cos = angles[pl.ds(of_step * (STEP // FINE) + part, 1), :]
            big_sin = angles[pl.ds(coarse + of_step * (STEP // FINE) + part, 1), :]
            at = pl.ds(part * FINE, FINE)
            table[of_step % 2, at, :F] = (big_cos * fine_cos - big_sin * fine_sin).astype(jnp.bfloat16)
            table[of_step % 2, at, F:] = (-(big_sin * fine_cos + big_cos * fine_sin)).astype(jnp.bfloat16)

    @pl.when(step == 0)
    def _():
        total[...] = jnp.zeros_like(total)
        fill(step)

    for quarter, x in enumerate((x0, x1, x2, x3)):
        at = pl.ds(quarter * rows, rows)
        total[at, :] += jnp.dot(x[...], table[step % 2], preferred_element_type=jnp.float32)
    fill(jnp.minimum(step + 1, pl.num_programs(0) - 1))

    @pl.when(step == pl.num_programs(0) - 1)
    def _():
        turn = (K0 + lax.broadcasted_iota(jnp.int32, (1, F), 1)) % 4
        even = turn % 2 == 0
        sign = jnp.where(turn < 2, 1.0, -1.0)
        channels = good.shape[1]
        keep = keep_column(good)
        for window in range(rows // channels):
            re = [total[pl.ds(q * rows + window * channels, channels), :F] for q in range(4)]
            im = [total[pl.ds(q * rows + window * channels, channels), F:] for q in range(4)]
            real = jnp.where(even, re[0] + re[2] + sign * (re[1] + re[3]), re[0] - re[2] + sign * (im[1] - im[3])) * keep
            imag = jnp.where(even, im[0] + im[2] + sign * (im[1] + im[3]), im[0] - im[2] - sign * (re[1] - re[3])) * keep
            spec[window, :, :F] = real
            spec[window, :, F:] = imag
            head[window, :, :F] = real[:HALO].astype(jnp.bfloat16)
            head[window, :, F:] = imag[:HALO].astype(jnp.bfloat16)
            tail[window, :, :F] = real[channels - HALO :].astype(jnp.bfloat16)
            tail[window, :, F:] = imag[channels - HALO :].astype(jnp.bfloat16)


def transform(traces, good):
    windows, channels, length = traces.shape
    rows = windows * channels
    steps = QUARTER // STEP
    flat = traces.reshape(rows, length)
    coarse = unit_angles(np.arange(QUARTER // FINE) * FINE, 0)
    angles = np.concatenate(coarse + unit_angles(np.arange(FINE), 0), axis=0)
    whole = lambda *shape: pl.BlockSpec(shape, lambda k: (0,) * len(shape))
    return pl.pallas_call(
        transform_kernel,
        grid=(steps,),
        in_specs=[pl.BlockSpec((rows, STEP), functools.partial(lambda q, k: (0, q * steps + k), q)) for q in range(4)]
        + [whole(*angles.shape), whole(1, channels)],
        out_specs=[whole(windows, channels, 2 * F), whole(windows, HALO, 2 * F), whole(windows, HALO, 2 * F)],
        out_shape=[
            jax.ShapeDtypeStruct((windows, channels, 2 * F), jnp.float32),
            jax.ShapeDtypeStruct((windows, HALO, 2 * F), jnp.bfloat16),
            jax.ShapeDtypeStruct((windows, HALO, 2 * F), jnp.bfloat16),
        ],
        scratch_shapes=[pltpu.VMEM((2, STEP, 2 * F), jnp.bfloat16), pltpu.VMEM((4 * rows, 2 * F), jnp.float32)],
        compiler_params=pltpu.CompilerParams(vmem_limit_bytes=60 * MIB),
        cost_estimate=pl.CostEstimate(flops=2 * rows * length * 2 * F, bytes_accessed=rows * length * 2, transcendentals=0),
    )(flat, flat, flat, flat, angles, good)


def pieces(value):
    high = value.astype(jnp.bfloat16)
    rest = value - high.astype(jnp.float32)
    middle = rest.astype(jnp.bfloat16)
    return high, middle, (rest - middle.astype(jnp.float32)).astype(jnp.bfloat16)


def whiten_kernel(spec, left, right, band, good, *outs):
    windows, channels = spec.shape[:2]
    filtered = []
    keep = keep_column(good)
    for window in range(windows):
        stack = jnp.concatenate([left[window], *pieces(spec[window]), right[window]], axis=0)
        own = band[:, HALO : HALO + channels]
        taps = jnp.concatenate([band[:, :HALO], own, own, own, band[:, HALO + channels :]], axis=1)
        filtered.append(jnp.dot(taps, stack, preferred_element_type=jnp.float32) * keep)
    spectrum = jnp.concatenate(filtered, axis=0)
    real, imag = spectrum[:, :F], spectrum[:, F:]
    magnitude = jnp.sqrt(real * real + imag * imag)
    bins = lax.broadcasted_iota(jnp.int32, (F, F), 0)
    others = lax.broadcasted_iota(jnp.int32, (F, F), 1)
    near = jnp.where(jnp.abs(bins - others) <= SMOOTH, 1.0, 0.0).astype(jnp.bfloat16)
    amplitude = sum(jnp.dot(piece, near, preferred_element_type=jnp.float32) for piece in pieces(magnitude))
    bin_row = lax.broadcasted_iota(jnp.int32, (1, F), 1)
    count = jnp.minimum(bin_row + SMOOTH, F - 1) - jnp.maximum(bin_row - SMOOTH, 0) + 1
    amplitude = amplitude * (1.0 / count.astype(jnp.float32))
    inverse = 1.0 / (amplitude + 1e-06)
    real = (real * inverse).astype(jnp.bfloat16)
    imag = (imag * inverse).astype(jnp.bfloat16)
    full, *parts = outs
    for window in range(windows):
        rows = slice(window * channels, (window + 1) * channels)
        full[window, :, :F] = real[rows]
        full[window, :, F:] = imag[rows]
        for part, (begin, end) in zip(parts, Z_GROUPS):
            for at, (start, width) in enumerate(CHUNKS[begin:end]):
                part[at, 0, window, :, :width] = real[rows, start : start + width]
                part[at, 0, window, :, width:] = imag[rows, start : start + width]


def whiten(spec, left, right, band, good):
    windows, channels, _ = spec.shape
    return pl.pallas_call(
        whiten_kernel,
        out_shape=[
            jax.ShapeDtypeStruct(shape, jnp.bfloat16)
            for shape in [(windows, channels, 2 * F)]
            + [(end - begin, 1, windows, channels, 2 * CHUNKS[0][1]) for begin, end in Z_GROUPS]
        ],
        compiler_params=pltpu.CompilerParams(vmem_limit_bytes=40 * MIB),
        cost_estimate=pl.CostEstimate(flops=2 * windows * channels * F * F * 3, bytes_accessed=5 * MIB // 2, transcendentals=windows * channels * F),
    )(spec, left, right, band, good)


def eye(size):
    rows = lax.broadcasted_iota(jnp.int32, (size, size), 0)
    cols = lax.broadcasted_iota(jnp.int32, (size, size), 1)
    return jnp.where(rows == cols, 1.0, 0.0).astype(jnp.bfloat16)


def turned(left_unit, rows):
    return lax.dot_general(left_unit, rows, NT, preferred_element_type=jnp.float32)


def swapper(outer, inner):
    size = outer * inner
    rows = lax.broadcasted_iota(jnp.int32, (size, size), 0)
    cols = lax.broadcasted_iota(jnp.int32, (size, size), 1)
    return jnp.where(cols == rows % outer * inner + rows // outer, 1.0, 0.0).astype(jnp.bfloat16)


def moved(swap, rows):
    return jnp.dot(swap, rows, preferred_element_type=jnp.float32).astype(jnp.bfloat16)


def own_kernel(here, near, far, out, by_window):
    own = [here, near.at[0], far, near.at[1]]
    each, channels, _ = here.shape
    windows, quads = each * len(own), channels // 4
    joined = GROUP // each
    swap = swapper(GROUP, GROUP)
    for start in range(0, windows, GROUP):
        for channel in range(0, channels, GROUP):
            block = [o[:, channel : channel + GROUP, :] for o in own[start // each : start // each + joined]]
            rows = moved(swap, jnp.concatenate(block, axis=0).reshape(GROUP * GROUP, 2 * F))
            by_window[channel : channel + GROUP, start : start + GROUP, :] = rows.reshape(GROUP, GROUP, 2 * F)
    unit = eye(F // 2)
    for quad in range(quads):
        for start in range(0, F, F // 2):
            rows = []
            for channel in range(quad, channels, quads):
                rows += [by_window[channel, :, side + start : side + start + F // 2] for side in (0, F)]
            out[quad, start : start + F // 2, :] = turned(unit, jnp.concatenate(rows, axis=0)).astype(jnp.bfloat16)


def turn_own(here, near, far):
    each, channels, _ = here.shape
    windows = each * 4
    return pl.pallas_call(
        own_kernel,
        out_shape=jax.ShapeDtypeStruct((channels // 4, F, 8 * windows), jnp.bfloat16),
        scratch_shapes=[pltpu.VMEM((channels, windows, 2 * F), jnp.bfloat16)],
        compiler_params=pltpu.CompilerParams(vmem_limit_bytes=40 * MIB),
        cost_estimate=pl.CostEstimate(flops=2 * 8192 * 65536, bytes_accessed=4 * MIB, transcendentals=0),
    )(here, near, far)


def cross_kernel(here, near, far, by_channel, out, by_window, sums):
    sources = [here, near.at[0], far.at[0], near.at[1]]
    each, count, both = here.shape
    quads, _, wide = by_channel.shape
    channels, half = 4 * quads, wide // 4
    windows, width = half // 2, both // 2
    unit = eye(width)
    swap = swapper(GROUP, GROUP)
    swap_quads = swapper(quads, GROUP)
    for window in range(0, windows, 2):
        rows = []
        for one in range(window, window + 2):
            source = sources[one // each]
            rows += [source[one % each, :, :width], source[one % each, :, width:]]
        both_turned = turned(unit, jnp.concatenate(rows, axis=0)).astype(jnp.bfloat16)
        by_window[window] = both_turned[:, : 2 * count]
        by_window[window + 1] = both_turned[:, 2 * count :]
    first = lax.broadcasted_iota(jnp.int32, (1, 2 * half), 1) < half
    sign = jnp.where(lax.broadcasted_iota(jnp.int32, (1, 2 * count), 1) < count, 1.0, -1.0)
    empty = jnp.zeros((2 * windows, 2 * count), jnp.bfloat16)

    def one_group(group, carry):
        bins = pl.ds(pl.multiple_of(group * GROUP, GROUP), GROUP)
        rows = [
            by_window[start : start + GROUP, bins, :].reshape(GROUP * GROUP, 2 * count)
            for start in range(0, windows, GROUP)
        ]
        rights = jnp.dot(swap, jnp.concatenate(rows, axis=1), preferred_element_type=jnp.float32)
        lefts = jnp.dot(
            swap_quads, by_channel[:, bins, :].reshape(quads * GROUP, 4 * half), preferred_element_type=jnp.float32
        )
        results = []
        for at in range(0, GROUP, 2):
            two = []
            for one in range(at, at + 2):
                here = rights[one * GROUP : (one + 1) * GROUP]
                src = jnp.concatenate(
                    [here[:, i * 2 * count : (i + 1) * 2 * count] for i in range(windows // GROUP)], axis=0
                )
                two.append(jnp.concatenate([src * sign, pltpu.roll(src, count, axis=1)], axis=0).astype(jnp.bfloat16))
            right = jnp.concatenate(
                [jnp.concatenate([two[0], empty], axis=1), jnp.concatenate([empty, two[1]], axis=1)], axis=0
            )
            left = []
            for tile in range(0, 4 * half, 2 * half):
                one, other = (lefts[i * quads : (i + 1) * quads, tile : tile + 2 * half] for i in (at, at + 1))
                left.append(jnp.where(first, one, pltpu.roll(other, half, axis=1)))
                left.append(jnp.where(first, pltpu.roll(one, half, axis=1), other))
            left = jnp.concatenate(left, axis=0).astype(jnp.bfloat16)
            result = jnp.dot(left, right, preferred_element_type=jnp.float32).astype(jnp.bfloat16)
            results += [result[:, : 2 * count], result[:, 2 * count :]]
        halves = [
            jnp.concatenate([r[start : start + GROUP] for r in results], axis=0) for start in range(0, channels, GROUP)
        ]
        done = moved(swap, jnp.concatenate(halves, axis=1))
        for channel in range(channels):
            row, side = channel % GROUP, channel // GROUP
            sums[channel, bins, :] = done[
                row * GROUP : (row + 1) * GROUP, side * 2 * count : (side + 1) * 2 * count
            ]
        return carry

    lax.fori_loop(0, width // GROUP, one_group, 0, unroll=8)
    unit = eye(2 * count)
    part = 256 // LAG_ROWS
    swap = swapper(LAG_ROWS, part)
    for group in range(channels // LAG_ROWS):
        by_bin = []
        for channel in range(group * LAG_ROWS, (group + 1) * LAG_ROWS, 2):
            rows = jnp.concatenate([sums[channel], sums[channel + 1]], axis=0)
            both_turned = turned(unit, rows).astype(jnp.bfloat16)
            by_bin += [both_turned[:, :width], both_turned[:, width:]]
        for start in range(0, count, part):
            rows = jnp.concatenate(
                [
                    jnp.concatenate([b[start : start + part], b[count + start : count + start + part]], axis=1)
                    for b in by_bin
                ],
                axis=0,
            )
            rows = moved(swap, rows)
            at = slice(start * LAG_ROWS, (start + part) * LAG_ROWS)
            out[group, 0, at, :] = rows[:, :width]
            out[group, 1, at, :] = rows[:, width:]


def cross(here, near, far, by_channel, first_bin):
    each, count, both = here.shape
    quads, _, wide = by_channel.shape
    channels, windows, width = 4 * quads, wide // 8, both // 2
    return pl.pallas_call(
        cross_kernel,
        grid=(1,),
        in_specs=[pl.BlockSpec(a.shape, functools.partial(lambda n, i: (0,) * n, a.ndim)) for a in (here, near, far)]
        + [pl.BlockSpec((quads, width, wide), lambda i: (0, first_bin // width, 0))],
        out_specs=pl.BlockSpec((channels // LAG_ROWS, 2, count * LAG_ROWS, width), lambda i: (0, 0, 0, 0)),
        out_shape=jax.ShapeDtypeStruct((channels // LAG_ROWS, 2, count * LAG_ROWS, width), jnp.bfloat16),
        scratch_shapes=[
            pltpu.VMEM((windows, width, 2 * count), jnp.bfloat16),
            pltpu.VMEM((channels, width, 2 * count), jnp.bfloat16),
        ],
        compiler_params=pltpu.CompilerParams(vmem_limit_bytes=40 * MIB),
        cost_estimate=pl.CostEstimate(flops=2 * width * 36 * 65536, bytes_accessed=4 * MIB, transcendentals=0),
    )(here, near, far, by_channel)


def lag_kernel(scaling, *refs):
    *stacked, table, edge, out = refs
    count, channels, _ = out.shape
    real, imag = (jnp.concatenate([chunk[0, side] for chunk in stacked], axis=1) for side in range(2))
    size = count * channels
    lane = lax.broadcasted_iota(jnp.int32, (size, LAG_FINE), 1)
    mirror = (LAG_FINE - lane) % LAG_FINE

    def parts(start, width):
        even = jnp.dot(real, table[:F, start : start + width], preferred_element_type=jnp.float32)
        odd = jnp.dot(imag, table[F:, start : start + width], preferred_element_type=jnp.float32)
        return even, odd

    half = LAGS // 2
    products = real.astype(jnp.float32) * edge[:1] + imag.astype(jnp.float32) * edge[1:]
    above = jnp.sum(products, axis=1, keepdims=True) * scaling
    for start in range(half - 2 * LAG_FINE, -1, -2 * LAG_FINE):
        even, odd = parts(start, 2 * LAG_FINE)
        after_zero = (even - odd) * scaling
        before_zero = (even + odd) * scaling
        out[:, :, half + start : half + start + 2 * LAG_FINE] = after_zero.reshape(count, channels, 2 * LAG_FINE)
        for tile in (1, 0):
            turned_round = jnp.take_along_axis(
                before_zero[:, tile * LAG_FINE : (tile + 1) * LAG_FINE], mirror, axis=1, mode="promise_in_bounds"
            )
            at = half - start - (tile + 1) * LAG_FINE
            out[:, :, at : at + LAG_FINE] = jnp.where(lane == 0, above, turned_round).reshape(count, channels, LAG_FINE)
            above = turned_round


def lagged(stacked, table, scaling):
    groups, _, size, _ = stacked[0].shape
    edge = np.concatenate(unit_angles(np.array([LAGS // 2]), 0), axis=0).astype(jnp.bfloat16).astype(np.float32)
    count = size // LAG_ROWS
    return pl.pallas_call(
        functools.partial(lag_kernel, scaling),
        grid=(groups,),
        in_specs=[pl.BlockSpec((1, 2, size, s.shape[3]), lambda i: (i, 0, 0, 0)) for s in stacked]
        + [pl.BlockSpec(a.shape, lambda i: (0, 0)) for a in (table, edge)],
        out_specs=pl.BlockSpec((count, LAG_ROWS, LAGS), lambda i: (0, i, 0)),
        out_shape=jax.ShapeDtypeStruct((count, groups * LAG_ROWS, LAGS), jnp.float32),
        compiler_params=pltpu.CompilerParams(vmem_limit_bytes=48 * MIB),
        cost_estimate=pl.CostEstimate(
            flops=2 * groups * size * F * LAGS, bytes_accessed=groups * size * LAGS * 4, transcendentals=0
        ),
    )(*stacked, table, edge)


def table_kernel(angles, out):
    fine_cos, fine_sin = angles[:, :LAG_FINE], angles[:, LAG_FINE : 2 * LAG_FINE]
    tiles = out.shape[1] // LAG_FINE
    for tile in range(tiles):
        big_cos = angles[:, 2 * LAG_FINE + tile : 2 * LAG_FINE + tile + 1]
        big_sin = angles[:, 2 * LAG_FINE + tiles + tile : 2 * LAG_FINE + tiles + tile + 1]
        cols = slice(tile * LAG_FINE, (tile + 1) * LAG_FINE)
        out[:F, cols] = (big_cos * fine_cos - big_sin * fine_sin).astype(jnp.bfloat16)
        out[F:, cols] = (big_sin * fine_cos + big_cos * fine_sin).astype(jnp.bfloat16)


def lag_table():
    tiles = LAGS // 2 // LAG_FINE
    coarse = unit_angles(np.arange(tiles) * LAG_FINE, 1)
    angles = np.concatenate(unit_angles(np.arange(LAG_FINE), 1) + coarse, axis=1)
    return pl.pallas_call(
        table_kernel,
        out_shape=jax.ShapeDtypeStruct((2 * F, tiles * LAG_FINE), jnp.bfloat16),
        compiler_params=pltpu.CompilerParams(vmem_limit_bytes=40 * MIB),
        cost_estimate=pl.CostEstimate(flops=8 * F * tiles * LAG_FINE, bytes_accessed=4 * MIB, transcendentals=0),
    )(angles)


def make_band(filter_taps, channel_count):
    kernel = jnp.concatenate(
        [
            -filter_taps[:HALO].astype(jnp.float32),
            jnp.ones((1,), jnp.float32),
            -filter_taps[HALO:].astype(jnp.float32),
        ]
    )
    row_ids = jnp.arange(channel_count, dtype=jnp.int32)[:, None]
    columns = jnp.arange(channel_count + 2 * HALO, dtype=jnp.int32)[None, :]
    offset = columns - row_ids
    choose = offset[:, :, None] == jnp.arange(2 * HALO + 1, dtype=jnp.int32)[None, None, :]
    return jnp.sum(jnp.where(choose, kernel[None, None, :], 0.0), axis=2).astype(jnp.bfloat16)


def pick_kernel(held, across, selector, here, near, far):
    count = here.shape[1]
    for window in range(held.shape[1]):
        rows = [blocks[i, window] for blocks in (held, across) for i in range(blocks.shape[0])]
        picked = jnp.dot(selector[...], jnp.concatenate(rows, axis=0), preferred_element_type=jnp.float32)
        picked = picked.astype(jnp.bfloat16)
        here[window] = picked[:count]
        near[window] = picked[count : 2 * count]
        for at in range(far.shape[0]):
            far[at, window] = picked[(2 + at) * count : (3 + at) * count]


def pick(held, across, selector, groups):
    _, windows, _, both = held.shape
    count = selector.shape[0] // groups
    one = (windows, count, both)
    return pl.pallas_call(
        pick_kernel,
        out_shape=[jax.ShapeDtypeStruct(shape, jnp.bfloat16) for shape in (one, one, (groups - 2, *one))],
        compiler_params=pltpu.CompilerParams(vmem_limit_bytes=40 * MIB),
        cost_estimate=pl.CostEstimate(
            flops=2 * windows * selector.size * both, bytes_accessed=2 * windows * both * sum(selector.shape), transcendentals=0
        ),
    )(held, across, selector)


def swapped(value, axis, step):
    return lax.ppermute(value, axis, [(i, i ^ step) for i in range(lax.axis_size(axis))])


def after(value, earlier):
    return lax.optimization_barrier((value, earlier))[0]


def per_device(traces, filter_taps, good_channels, source_index):
    window_count, channel_count, _ = traces.shape
    good = good_channels[None, :]
    spec, head, tail = transform(traces, good)
    blocks = lax.axis_size("chan")
    groups = lax.axis_size("win")
    left = lax.ppermute(tail, "chan", [(i, i + 1) for i in range(blocks - 1)])
    right = lax.ppermute(head, "chan", [(i + 1, i) for i in range(blocks - 1)])
    table = lag_table()
    left = after(left, table)
    full, *parts = whiten(spec, left, right, make_band(filter_taps, channel_count), good)

    order = [0]
    step = blocks // 2
    while step:
        order += [place ^ step for place in order]
        step //= 2
    order = jnp.asarray(order, jnp.int32) ^ lax.axis_index("chan")
    own_ids = jnp.arange(channel_count, dtype=jnp.int32)
    channel_ids = (order[:, None] * channel_count + own_ids[None, :]).reshape(-1)
    by_group = source_index.reshape(groups, -1)
    here = lax.axis_index("win")
    wanted = jnp.concatenate([lax.dynamic_slice_in_dim(by_group, here ^ step, 1) for step in range(groups)], axis=0)
    selector = (wanted.reshape(-1)[:, None] == channel_ids[None, :]).astype(jnp.bfloat16)

    own_far = swapped(full, "win", 2)
    own_near = swapped(jnp.stack([full, own_far]), "win", 1)
    by_channel = turn_own(full, own_near, own_far)
    gathered, picked, stacked = [], [], []
    chunks = len(CHUNKS)

    def gather(part):
        held, step = part, blocks // 2
        while step > 1:
            received = swapped(held, "chan", step)
            if step > 2:
                held = jnp.concatenate([held, received], axis=1)
                if step == blocks // 2:
                    first_held.append(held)
                    if len(gathered) > 1:
                        held = after(held, picked[0][0])
            step //= 2
        gathered.extend(jnp.concatenate([held[i], received[i]], axis=0) for i in range(part.shape[0]))

    def exchange(at):
        held = after(gathered[at], picked[-1][0]) if at else gathered[at]
        across = swapped(held, "chan", 1)
        if at > 1:
            finish(at - 2)
        across = after(across, (stacked[-1] if stacked else by_channel) if at else gathered[1])
        here, near, far = pick(held, across, selector, groups)
        picked.append((here, near, swapped(far, "win", 2)))

    def finish(at):
        here, near, far = picked[at]
        if stacked:
            far = after(far, stacked[-1])
        near = swapped(jnp.stack([near, far[1]]), "win", 1)
        stacked.append(cross(here, near, far, by_channel, CHUNKS[at][0]))

    first_held = []
    for part in parts:
        gather(after(part, [first_held[-1], own_far]) if len(first_held) > 1 else part)
        if len(gathered) == 2:
            exchange(0)
    for at in range(1, chunks):
        exchange(at)
    for at in range(len(stacked), chunks):
        finish(at)
    return lagged(stacked, table, 1.0 / math.sqrt(F * window_count * groups))


def solution(mesh):
    placed = (P("win", "chan", None), P(), P("chan"), P())
    return jax.shard_map(
        per_device, mesh=mesh, in_specs=placed, out_specs=P("win", "chan", None), check_vma=False
    )
```

```python
import functools
import math

import jax
import jax.numpy as jnp
import numpy as np
from jax import lax
from jax.experimental import pallas as pl
from jax.experimental.pallas import tpu as pltpu
from jax.sharding import PartitionSpec as P

L = 7680
F = 512
LAGS = 2048
HALO = 16
SMOOTH = 64
K0 = 31
QUARTER = L // 4
STEP = 640
FINE = 32
CHUNKS = tuple((start, 128) for start in range(0, F, 128))
Z_GROUPS = ((0, 1), (1, 2), (2, 4))
GROUP = 16
LAG_FINE = 128
LAG_ROWS = 8
NT = (((1,), (1,)), ((), ()))
MIB = 1024 * 1024


def unit_angles(positions, axis):
    bins = K0 + np.arange(F, dtype=np.int64)
    phase = np.mod(np.expand_dims(positions, 1 - axis) * np.expand_dims(bins, axis), L)
    angles = phase * (2.0 * math.pi / L)
    return np.cos(angles).astype(np.float32), np.sin(angles).astype(np.float32)


def keep_column(good):
    count = good.shape[1]
    rows = lax.broadcasted_iota(jnp.int32, (count, count), 0)
    cols = lax.broadcasted_iota(jnp.int32, (count, count), 1)
    return jnp.sum(jnp.where(rows == cols, good[...].astype(jnp.float32), 0.0), axis=1, keepdims=True)


def transform_kernel(x0, x1, x2, x3, angles, good, spec, head, tail, table, total):
    step = pl.program_id(0)
    rows = x0.shape[0]
    coarse = QUARTER // FINE

    def fill(of_step):
        fine_cos = angles[2 * coarse : 2 * coarse + FINE, :]
        fine_sin = angles[2 * coarse + FINE :, :]
        for part in range(STEP // FINE):
            big_cos = angles[pl.ds(of_step * (STEP // FINE) + part, 1), :]
            big_sin = angles[pl.ds(coarse + of_step * (STEP // FINE) + part, 1), :]
            at = pl.ds(part * FINE, FINE)
            table[of_step % 2, at, :F] = (big_cos * fine_cos - big_sin * fine_sin).astype(jnp.bfloat16)
            table[of_step % 2, at, F:] = (-(big_sin * fine_cos + big_cos * fine_sin)).astype(jnp.bfloat16)

    @pl.when(step == 0)
    def _():
        total[...] = jnp.zeros_like(total)
        fill(step)

    for quarter, x in enumerate((x0, x1, x2, x3)):
        at = pl.ds(quarter * rows, rows)
        total[at, :] += jnp.dot(x[...], table[step % 2], preferred_element_type=jnp.float32)
    fill(jnp.minimum(step + 1, pl.num_programs(0) - 1))

    @pl.when(step == pl.num_programs(0) - 1)
    def _():
        turn = (K0 + lax.broadcasted_iota(jnp.int32, (1, F), 1)) % 4
        even = turn % 2 == 0
        sign = jnp.where(turn < 2, 1.0, -1.0)
        channels = good.shape[1]
        keep = keep_column(good)
        for window in range(rows // channels):
            re = [total[pl.ds(q * rows + window * channels, channels), :F] for q in range(4)]
            im = [total[pl.ds(q * rows + window * channels, channels), F:] for q in range(4)]
            real = jnp.where(even, re[0] + re[2] + sign * (re[1] + re[3]), re[0] - re[2] + sign * (im[1] - im[3])) * keep
            imag = jnp.where(even, im[0] + im[2] + sign * (im[1] + im[3]), im[0] - im[2] - sign * (re[1] - re[3])) * keep
            spec[window, :, :F] = real
            spec[window, :, F:] = imag
            head[window, :, :F] = real[:HALO].astype(jnp.bfloat16)
            head[window, :, F:] = imag[:HALO].astype(jnp.bfloat16)
            tail[window, :, :F] = real[channels - HALO :].astype(jnp.bfloat16)
            tail[window, :, F:] = imag[channels - HALO :].astype(jnp.bfloat16)


def transform(traces, good):
    windows, channels, length = traces.shape
    rows = windows * channels
    steps = QUARTER // STEP
    flat = traces.reshape(rows, length)
    coarse = unit_angles(np.arange(QUARTER // FINE) * FINE, 0)
    angles = np.concatenate(coarse + unit_angles(np.arange(FINE), 0), axis=0)
    whole = lambda *shape: pl.BlockSpec(shape, lambda k: (0,) * len(shape))
    return pl.pallas_call(
        transform_kernel,
        grid=(steps,),
        in_specs=[pl.BlockSpec((rows, STEP), functools.partial(lambda q, k: (0, q * steps + k), q)) for q in range(4)]
        + [whole(*angles.shape), whole(1, channels)],
        out_specs=[whole(windows, channels, 2 * F), whole(windows, HALO, 2 * F), whole(windows, HALO, 2 * F)],
        out_shape=[
            jax.ShapeDtypeStruct((windows, channels, 2 * F), jnp.float32),
            jax.ShapeDtypeStruct((windows, HALO, 2 * F), jnp.bfloat16),
            jax.ShapeDtypeStruct((windows, HALO, 2 * F), jnp.bfloat16),
        ],
        scratch_shapes=[pltpu.VMEM((2, STEP, 2 * F), jnp.bfloat16), pltpu.VMEM((4 * rows, 2 * F), jnp.float32)],
        compiler_params=pltpu.CompilerParams(vmem_limit_bytes=60 * MIB),
        cost_estimate=pl.CostEstimate(flops=2 * rows * length * 2 * F, bytes_accessed=rows * length * 2, transcendentals=0),
    )(flat, flat, flat, flat, angles, good)


def pieces(value):
    high = value.astype(jnp.bfloat16)
    rest = value - high.astype(jnp.float32)
    middle = rest.astype(jnp.bfloat16)
    return high, middle, (rest - middle.astype(jnp.float32)).astype(jnp.bfloat16)


def whiten_kernel(spec, left, right, band, good, *outs):
    windows, channels = spec.shape[:2]
    filtered = []
    keep = keep_column(good)
    for window in range(windows):
        stack = jnp.concatenate([left[window], *pieces(spec[window]), right[window]], axis=0)
        own = band[:, HALO : HALO + channels]
        taps = jnp.concatenate([band[:, :HALO], own, own, own, band[:, HALO + channels :]], axis=1)
        filtered.append(jnp.dot(taps, stack, preferred_element_type=jnp.float32) * keep)
    spectrum = jnp.concatenate(filtered, axis=0)
    real, imag = spectrum[:, :F], spectrum[:, F:]
    magnitude = jnp.sqrt(real * real + imag * imag)
    bins = lax.broadcasted_iota(jnp.int32, (F, F), 0)
    others = lax.broadcasted_iota(jnp.int32, (F, F), 1)
    near = jnp.where(jnp.abs(bins - others) <= SMOOTH, 1.0, 0.0).astype(jnp.bfloat16)
    amplitude = sum(jnp.dot(piece, near, preferred_element_type=jnp.float32) for piece in pieces(magnitude))
    bin_row = lax.broadcasted_iota(jnp.int32, (1, F), 1)
    count = jnp.minimum(bin_row + SMOOTH, F - 1) - jnp.maximum(bin_row - SMOOTH, 0) + 1
    amplitude = amplitude * (1.0 / count.astype(jnp.float32))
    inverse = 1.0 / (amplitude + 1e-06)
    real = (real * inverse).astype(jnp.bfloat16)
    imag = (imag * inverse).astype(jnp.bfloat16)
    full, *parts = outs
    for window in range(windows):
        rows = slice(window * channels, (window + 1) * channels)
        full[window, :, :F] = real[rows]
        full[window, :, F:] = imag[rows]
        for part, (begin, end) in zip(parts, Z_GROUPS):
            for at, (start, width) in enumerate(CHUNKS[begin:end]):
                part[at, 0, window, :, :width] = real[rows, start : start + width]
                part[at, 0, window, :, width:] = imag[rows, start : start + width]


def whiten(spec, left, right, band, good):
    windows, channels, _ = spec.shape
    return pl.pallas_call(
        whiten_kernel,
        out_shape=[
            jax.ShapeDtypeStruct(shape, jnp.bfloat16)
            for shape in [(windows, channels, 2 * F)]
            + [(end - begin, 1, windows, channels, 2 * CHUNKS[0][1]) for begin, end in Z_GROUPS]
        ],
        compiler_params=pltpu.CompilerParams(vmem_limit_bytes=40 * MIB),
        cost_estimate=pl.CostEstimate(flops=2 * windows * channels * F * F * 3, bytes_accessed=5 * MIB // 2, transcendentals=windows * channels * F),
    )(spec, left, right, band, good)


def eye(size):
    rows = lax.broadcasted_iota(jnp.int32, (size, size), 0)
    cols = lax.broadcasted_iota(jnp.int32, (size, size), 1)
    return jnp.where(rows == cols, 1.0, 0.0).astype(jnp.bfloat16)


def turned(left_unit, rows):
    return lax.dot_general(left_unit, rows, NT, preferred_element_type=jnp.float32)


def swapper(outer, inner):
    size = outer * inner
    rows = lax.broadcasted_iota(jnp.int32, (size, size), 0)
    cols = lax.broadcasted_iota(jnp.int32, (size, size), 1)
    return jnp.where(cols == rows % outer * inner + rows // outer, 1.0, 0.0).astype(jnp.bfloat16)


def moved(swap, rows):
    return jnp.dot(swap, rows, preferred_element_type=jnp.float32).astype(jnp.bfloat16)


def own_kernel(here, near, far, out, by_window):
    own = [here, near.at[0], far, near.at[1]]
    each, channels, _ = here.shape
    windows, quads = each * len(own), channels // 4
    joined = GROUP // each
    swap = swapper(GROUP, GROUP)
    for start in range(0, windows, GROUP):
        for channel in range(0, channels, GROUP):
            block = [o[:, channel : channel + GROUP, :] for o in own[start // each : start // each + joined]]
            rows = moved(swap, jnp.concatenate(block, axis=0).reshape(GROUP * GROUP, 2 * F))
            by_window[channel : channel + GROUP, start : start + GROUP, :] = rows.reshape(GROUP, GROUP, 2 * F)
    unit = eye(F // 2)
    for quad in range(quads):
        for start in range(0, F, F // 2):
            rows = []
            for channel in range(quad, channels, quads):
                rows += [by_window[channel, :, side + start : side + start + F // 2] for side in (0, F)]
            out[quad, start : start + F // 2, :] = turned(unit, jnp.concatenate(rows, axis=0)).astype(jnp.bfloat16)


def turn_own(here, near, far):
    each, channels, _ = here.shape
    windows = each * 4
    return pl.pallas_call(
        own_kernel,
        out_shape=jax.ShapeDtypeStruct((channels // 4, F, 8 * windows), jnp.bfloat16),
        scratch_shapes=[pltpu.VMEM((channels, windows, 2 * F), jnp.bfloat16)],
        compiler_params=pltpu.CompilerParams(vmem_limit_bytes=40 * MIB),
        cost_estimate=pl.CostEstimate(flops=2 * 8192 * 65536, bytes_accessed=4 * MIB, transcendentals=0),
    )(here, near, far)


def cross_kernel(here, near, far, by_channel, out, by_window, sums):
    sources = [here, near.at[0], far.at[0], near.at[1]]
    each, count, both = here.shape
    quads, _, wide = by_channel.shape
    channels, half = 4 * quads, wide // 4
    windows, width = half // 2, both // 2
    unit = eye(width)
    swap = swapper(GROUP, GROUP)
    swap_quads = swapper(quads, GROUP)
    for window in range(0, windows, 2):
        rows = []
        for one in range(window, window + 2):
            source = sources[one // each]
            rows += [source[one % each, :, :width], source[one % each, :, width:]]
        both_turned = turned(unit, jnp.concatenate(rows, axis=0)).astype(jnp.bfloat16)
        by_window[window] = both_turned[:, : 2 * count]
        by_window[window + 1] = both_turned[:, 2 * count :]
    first = lax.broadcasted_iota(jnp.int32, (1, 2 * half), 1) < half
    sign = jnp.where(lax.broadcasted_iota(jnp.int32, (1, 2 * count), 1) < count, 1.0, -1.0)
    empty = jnp.zeros((2 * windows, 2 * count), jnp.bfloat16)

    def one_group(group, carry):
        bins = pl.ds(pl.multiple_of(group * GROUP, GROUP), GROUP)
        rows = [
            by_window[start : start + GROUP, bins, :].reshape(GROUP * GROUP, 2 * count)
            for start in range(0, windows, GROUP)
        ]
        rights = jnp.dot(swap, jnp.concatenate(rows, axis=1), preferred_element_type=jnp.float32)
        lefts = jnp.dot(
            swap_quads, by_channel[:, bins, :].reshape(quads * GROUP, 4 * half), preferred_element_type=jnp.float32
        )
        results = []
        for at in range(0, GROUP, 2):
            two = []
            for one in range(at, at + 2):
                here = rights[one * GROUP : (one + 1) * GROUP]
                src = jnp.concatenate(
                    [here[:, i * 2 * count : (i + 1) * 2 * count] for i in range(windows // GROUP)], axis=0
                )
                two.append(jnp.concatenate([src * sign, pltpu.roll(src, count, axis=1)], axis=0).astype(jnp.bfloat16))
            right = jnp.concatenate(
                [jnp.concatenate([two[0], empty], axis=1), jnp.concatenate([empty, two[1]], axis=1)], axis=0
            )
            left = []
            for tile in range(0, 4 * half, 2 * half):
                one, other = (lefts[i * quads : (i + 1) * quads, tile : tile + 2 * half] for i in (at, at + 1))
                left.append(jnp.where(first, one, pltpu.roll(other, half, axis=1)))
                left.append(jnp.where(first, pltpu.roll(one, half, axis=1), other))
            left = jnp.concatenate(left, axis=0).astype(jnp.bfloat16)
            result = jnp.dot(left, right, preferred_element_type=jnp.float32).astype(jnp.bfloat16)
            results += [result[:, : 2 * count], result[:, 2 * count :]]
        halves = [
            jnp.concatenate([r[start : start + GROUP] for r in results], axis=0) for start in range(0, channels, GROUP)
        ]
        done = moved(swap, jnp.concatenate(halves, axis=1))
        for channel in range(channels):
            row, side = channel % GROUP, channel // GROUP
            sums[channel, bins, :] = done[
                row * GROUP : (row + 1) * GROUP, side * 2 * count : (side + 1) * 2 * count
            ]
        return carry

    lax.fori_loop(0, width // GROUP, one_group, 0, unroll=8)
    unit = eye(2 * count)
    part = 256 // LAG_ROWS
    swap = swapper(LAG_ROWS, part)
    for group in range(channels // LAG_ROWS):
        by_bin = []
        for channel in range(group * LAG_ROWS, (group + 1) * LAG_ROWS, 2):
            rows = jnp.concatenate([sums[channel], sums[channel + 1]], axis=0)
            both_turned = turned(unit, rows).astype(jnp.bfloat16)
            by_bin += [both_turned[:, :width], both_turned[:, width:]]
        for start in range(0, count, part):
            rows = jnp.concatenate(
                [
                    jnp.concatenate([b[start : start + part], b[count + start : count + start + part]], axis=1)
                    for b in by_bin
                ],
                axis=0,
            )
            rows = moved(swap, rows)
            at = slice(start * LAG_ROWS, (start + part) * LAG_ROWS)
            out[group, 0, at, :] = rows[:, :width]
            out[group, 1, at, :] = rows[:, width:]


def cross(here, near, far, by_channel, first_bin):
    each, count, both = here.shape
    quads, _, wide = by_channel.shape
    channels, windows, width = 4 * quads, wide // 8, both // 2
    return pl.pallas_call(
        cross_kernel,
        grid=(1,),
        in_specs=[pl.BlockSpec(a.shape, functools.partial(lambda n, i: (0,) * n, a.ndim)) for a in (here, near, far)]
        + [pl.BlockSpec((quads, width, wide), lambda i: (0, first_bin // width, 0))],
        out_specs=pl.BlockSpec((channels // LAG_ROWS, 2, count * LAG_ROWS, width), lambda i: (0, 0, 0, 0)),
        out_shape=jax.ShapeDtypeStruct((channels // LAG_ROWS, 2, count * LAG_ROWS, width), jnp.bfloat16),
        scratch_shapes=[
            pltpu.VMEM((windows, width, 2 * count), jnp.bfloat16),
            pltpu.VMEM((channels, width, 2 * count), jnp.bfloat16),
        ],
        compiler_params=pltpu.CompilerParams(vmem_limit_bytes=40 * MIB),
        cost_estimate=pl.CostEstimate(flops=2 * width * 36 * 65536, bytes_accessed=4 * MIB, transcendentals=0),
    )(here, near, far, by_channel)


def lag_kernel(scaling, *refs):
    *stacked, table, edge, out = refs
    count, channels, _ = out.shape
    real, imag = (jnp.concatenate([chunk[0, side] for chunk in stacked], axis=1) for side in range(2))
    size = count * channels
    lane = lax.broadcasted_iota(jnp.int32, (size, LAG_FINE), 1)
    mirror = (LAG_FINE - lane) % LAG_FINE

    def parts(start, width):
        even = jnp.dot(real, table[:F, start : start + width], preferred_element_type=jnp.float32)
        odd = jnp.dot(imag, table[F:, start : start + width], preferred_element_type=jnp.float32)
        return even, odd

    half = LAGS // 2
    products = real.astype(jnp.float32) * edge[:1] + imag.astype(jnp.float32) * edge[1:]
    above = jnp.sum(products, axis=1, keepdims=True) * scaling
    for start in range(half - 2 * LAG_FINE, -1, -2 * LAG_FINE):
        even, odd = parts(start, 2 * LAG_FINE)
        after_zero = (even - odd) * scaling
        before_zero = (even + odd) * scaling
        out[:, :, half + start : half + start + 2 * LAG_FINE] = after_zero.reshape(count, channels, 2 * LAG_FINE)
        for tile in (1, 0):
            turned_round = jnp.take_along_axis(
                before_zero[:, tile * LAG_FINE : (tile + 1) * LAG_FINE], mirror, axis=1, mode="promise_in_bounds"
            )
            at = half - start - (tile + 1) * LAG_FINE
            out[:, :, at : at + LAG_FINE] = jnp.where(lane == 0, above, turned_round).reshape(count, channels, LAG_FINE)
            above = turned_round


def lagged(stacked, table, scaling):
    groups, _, size, _ = stacked[0].shape
    edge = np.concatenate(unit_angles(np.array([LAGS // 2]), 0), axis=0).astype(jnp.bfloat16).astype(np.float32)
    count = size // LAG_ROWS
    return pl.pallas_call(
        functools.partial(lag_kernel, scaling),
        grid=(groups,),
        in_specs=[pl.BlockSpec((1, 2, size, s.shape[3]), lambda i: (i, 0, 0, 0)) for s in stacked]
        + [pl.BlockSpec(a.shape, lambda i: (0, 0)) for a in (table, edge)],
        out_specs=pl.BlockSpec((count, LAG_ROWS, LAGS), lambda i: (0, i, 0)),
        out_shape=jax.ShapeDtypeStruct((count, groups * LAG_ROWS, LAGS), jnp.float32),
        compiler_params=pltpu.CompilerParams(vmem_limit_bytes=48 * MIB),
        cost_estimate=pl.CostEstimate(
            flops=2 * groups * size * F * LAGS, bytes_accessed=groups * size * LAGS * 4, transcendentals=0
        ),
    )(*stacked, table, edge)


def table_kernel(angles, out):
    fine_cos, fine_sin = angles[:, :LAG_FINE], angles[:, LAG_FINE : 2 * LAG_FINE]
    tiles = out.shape[1] // LAG_FINE
    for tile in range(tiles):
        big_cos = angles[:, 2 * LAG_FINE + tile : 2 * LAG_FINE + tile + 1]
        big_sin = angles[:, 2 * LAG_FINE + tiles + tile : 2 * LAG_FINE + tiles + tile + 1]
        cols = slice(tile * LAG_FINE, (tile + 1) * LAG_FINE)
        out[:F, cols] = (big_cos * fine_cos - big_sin * fine_sin).astype(jnp.bfloat16)
        out[F:, cols] = (big_sin * fine_cos + big_cos * fine_sin).astype(jnp.bfloat16)


def lag_table():
    tiles = LAGS // 2 // LAG_FINE
    coarse = unit_angles(np.arange(tiles) * LAG_FINE, 1)
    angles = np.concatenate(unit_angles(np.arange(LAG_FINE), 1) + coarse, axis=1)
    return pl.pallas_call(
        table_kernel,
        out_shape=jax.ShapeDtypeStruct((2 * F, tiles * LAG_FINE), jnp.bfloat16),
        compiler_params=pltpu.CompilerParams(vmem_limit_bytes=40 * MIB),
        cost_estimate=pl.CostEstimate(flops=8 * F * tiles * LAG_FINE, bytes_accessed=4 * MIB, transcendentals=0),
    )(angles)


def make_band(filter_taps, channel_count):
    kernel = jnp.concatenate(
        [
            -filter_taps[:HALO].astype(jnp.float32),
            jnp.ones((1,), jnp.float32),
            -filter_taps[HALO:].astype(jnp.float32),
        ]
    )
    row_ids = jnp.arange(channel_count, dtype=jnp.int32)[:, None]
    columns = jnp.arange(channel_count + 2 * HALO, dtype=jnp.int32)[None, :]
    offset = columns - row_ids
    choose = offset[:, :, None] == jnp.arange(2 * HALO + 1, dtype=jnp.int32)[None, None, :]
    return jnp.sum(jnp.where(choose, kernel[None, None, :], 0.0), axis=2).astype(jnp.bfloat16)


def pick_kernel(held, across, selector, here, near, far):
    count = here.shape[1]
    for window in range(held.shape[1]):
        rows = [blocks[i, window] for blocks in (held, across) for i in range(blocks.shape[0])]
        picked = jnp.dot(selector[...], jnp.concatenate(rows, axis=0), preferred_element_type=jnp.float32)
        picked = picked.astype(jnp.bfloat16)
        here[window] = picked[:count]
        near[window] = picked[count : 2 * count]
        for at in range(far.shape[0]):
            far[at, window] = picked[(2 + at) * count : (3 + at) * count]


def pick(held, across, selector, groups):
    _, windows, _, both = held.shape
    count = selector.shape[0] // groups
    one = (windows, count, both)
    return pl.pallas_call(
        pick_kernel,
        out_shape=[jax.ShapeDtypeStruct(shape, jnp.bfloat16) for shape in (one, one, (groups - 2, *one))],
        compiler_params=pltpu.CompilerParams(vmem_limit_bytes=40 * MIB),
        cost_estimate=pl.CostEstimate(
            flops=2 * windows * selector.size * both, bytes_accessed=2 * windows * both * sum(selector.shape), transcendentals=0
        ),
    )(held, across, selector)


def swapped(value, axis, step):
    return lax.ppermute(value, axis, [(i, i ^ step) for i in range(lax.axis_size(axis))])


def after(value, earlier):
    return lax.optimization_barrier((value, earlier))[0]


def per_device(traces, filter_taps, good_channels, source_index):
    window_count, channel_count, _ = traces.shape
    good = good_channels[None, :]
    spec, head, tail = transform(traces, good)
    blocks = lax.axis_size("chan")
    groups = lax.axis_size("win")
    left = lax.ppermute(tail, "chan", [(i, i + 1) for i in range(blocks - 1)])
    right = lax.ppermute(head, "chan", [(i + 1, i) for i in range(blocks - 1)])
    table = lag_table()
    left = after(left, table)
    full, *parts = whiten(spec, left, right, make_band(filter_taps, channel_count), good)

    order = [0]
    step = blocks // 2
    while step:
        order += [place ^ step for place in order]
        step //= 2
    order = jnp.asarray(order, jnp.int32) ^ lax.axis_index("chan")
    own_ids = jnp.arange(channel_count, dtype=jnp.int32)
    channel_ids = (order[:, None] * channel_count + own_ids[None, :]).reshape(-1)
    by_group = source_index.reshape(groups, -1)
    here = lax.axis_index("win")
    wanted = jnp.concatenate([lax.dynamic_slice_in_dim(by_group, here ^ step, 1) for step in range(groups)], axis=0)
    selector = (wanted.reshape(-1)[:, None] == channel_ids[None, :]).astype(jnp.bfloat16)

    own_far = swapped(full, "win", 2)
    own_near = swapped(jnp.stack([full, own_far]), "win", 1)
    by_channel = turn_own(full, own_near, own_far)
    gathered, picked, stacked = [], [], []
    chunks = len(CHUNKS)

    def gather(part):
        held, step = part, blocks // 2
        while step > 1:
            received = swapped(held, "chan", step)
            if step > 2:
                held = jnp.concatenate([held, received], axis=1)
                if step == blocks // 2:
                    first_held.append(held)
                    if gathered:
                        held = after(held, picked[0][0] if picked else own_far)
            step //= 2
        gathered.extend(jnp.concatenate([held[i], received[i]], axis=0) for i in range(part.shape[0]))

    def exchange(at):
        held = after(gathered[at], picked[-1][0]) if at else gathered[at]
        across = swapped(held, "chan", 1)
        if at > 1:
            finish(at - 2)
        across = after(across, (stacked[-1] if stacked else by_channel) if at else gathered[1])
        here, near, far = pick(held, across, selector, groups)
        picked.append((here, near, swapped(far, "win", 2)))

    def finish(at):
        here, near, far = picked[at]
        if stacked:
            far = after(far, stacked[-1])
        near = swapped(jnp.stack([near, far[1]]), "win", 1)
        stacked.append(cross(here, near, far, by_channel, CHUNKS[at][0]))

    first_held = []
    for part in parts:
        gather(after(part, first_held[-1]) if len(first_held) > 1 else part)
        if len(gathered) == 2:
            exchange(0)
    for at in range(1, chunks):
        exchange(at)
    for at in range(len(stacked), chunks):
        finish(at)
    return lagged(stacked, table, 1.0 / math.sqrt(F * window_count * groups))


def solution(mesh):
    placed = (P("win", "chan", None), P(), P("chan"), P())
    return jax.shard_map(
        per_device, mesh=mesh, in_specs=placed, out_specs=P("win", "chan", None), check_vma=False
    )
```

```python
import functools
import math

import jax
import jax.numpy as jnp
import numpy as np
from jax import lax
from jax.experimental import pallas as pl
from jax.experimental.pallas import tpu as pltpu
from jax.sharding import PartitionSpec as P

L = 7680
F = 512
LAGS = 2048
HALO = 16
SMOOTH = 64
K0 = 31
QUARTER = L // 4
STEP = 640
FINE = 32
CHUNKS = tuple((start, 128) for start in range(0, F, 128))
Z_GROUPS = ((0, 1), (1, 2), (2, 3), (3, 4))
GROUP = 16
LAG_FINE = 128
LAG_ROWS = 8
NT = (((1,), (1,)), ((), ()))
MIB = 1024 * 1024


def unit_angles(positions, axis):
    bins = K0 + np.arange(F, dtype=np.int64)
    phase = np.mod(np.expand_dims(positions, 1 - axis) * np.expand_dims(bins, axis), L)
    angles = phase * (2.0 * math.pi / L)
    return np.cos(angles).astype(np.float32), np.sin(angles).astype(np.float32)


def keep_column(good):
    count = good.shape[1]
    rows = lax.broadcasted_iota(jnp.int32, (count, count), 0)
    cols = lax.broadcasted_iota(jnp.int32, (count, count), 1)
    return jnp.sum(jnp.where(rows == cols, good[...].astype(jnp.float32), 0.0), axis=1, keepdims=True)


def transform_kernel(x0, x1, x2, x3, angles, good, spec, head, tail, table, total):
    step = pl.program_id(0)
    rows = x0.shape[0]
    coarse = QUARTER // FINE

    def fill(of_step):
        fine_cos = angles[2 * coarse : 2 * coarse + FINE, :]
        fine_sin = angles[2 * coarse + FINE :, :]
        for part in range(STEP // FINE):
            big_cos = angles[pl.ds(of_step * (STEP // FINE) + part, 1), :]
            big_sin = angles[pl.ds(coarse + of_step * (STEP // FINE) + part, 1), :]
            at = pl.ds(part * FINE, FINE)
            table[of_step % 2, at, :F] = (big_cos * fine_cos - big_sin * fine_sin).astype(jnp.bfloat16)
            table[of_step % 2, at, F:] = (-(big_sin * fine_cos + big_cos * fine_sin)).astype(jnp.bfloat16)

    @pl.when(step == 0)
    def _():
        total[...] = jnp.zeros_like(total)
        fill(step)

    for quarter, x in enumerate((x0, x1, x2, x3)):
        at = pl.ds(quarter * rows, rows)
        total[at, :] += jnp.dot(x[...], table[step % 2], preferred_element_type=jnp.float32)
    fill(jnp.minimum(step + 1, pl.num_programs(0) - 1))

    @pl.when(step == pl.num_programs(0) - 1)
    def _():
        turn = (K0 + lax.broadcasted_iota(jnp.int32, (1, F), 1)) % 4
        even = turn % 2 == 0
        sign = jnp.where(turn < 2, 1.0, -1.0)
        channels = good.shape[1]
        keep = keep_column(good)
        for window in range(rows // channels):
            re = [total[pl.ds(q * rows + window * channels, channels), :F] for q in range(4)]
            im = [total[pl.ds(q * rows + window * channels, channels), F:] for q in range(4)]
            real = jnp.where(even, re[0] + re[2] + sign * (re[1] + re[3]), re[0] - re[2] + sign * (im[1] - im[3])) * keep
            imag = jnp.where(even, im[0] + im[2] + sign * (im[1] + im[3]), im[0] - im[2] - sign * (re[1] - re[3])) * keep
            spec[window, :, :F] = real
            spec[window, :, F:] = imag
            head[window, :, :F] = real[:HALO].astype(jnp.bfloat16)
            head[window, :, F:] = imag[:HALO].astype(jnp.bfloat16)
            tail[window, :, :F] = real[channels - HALO :].astype(jnp.bfloat16)
            tail[window, :, F:] = imag[channels - HALO :].astype(jnp.bfloat16)


def transform(traces, good):
    windows, channels, length = traces.shape
    rows = windows * channels
    steps = QUARTER // STEP
    flat = traces.reshape(rows, length)
    coarse = unit_angles(np.arange(QUARTER // FINE) * FINE, 0)
    angles = np.concatenate(coarse + unit_angles(np.arange(FINE), 0), axis=0)
    whole = lambda *shape: pl.BlockSpec(shape, lambda k: (0,) * len(shape))
    return pl.pallas_call(
        transform_kernel,
        grid=(steps,),
        in_specs=[pl.BlockSpec((rows, STEP), functools.partial(lambda q, k: (0, q * steps + k), q)) for q in range(4)]
        + [whole(*angles.shape), whole(1, channels)],
        out_specs=[whole(windows, channels, 2 * F), whole(windows, HALO, 2 * F), whole(windows, HALO, 2 * F)],
        out_shape=[
            jax.ShapeDtypeStruct((windows, channels, 2 * F), jnp.float32),
            jax.ShapeDtypeStruct((windows, HALO, 2 * F), jnp.bfloat16),
            jax.ShapeDtypeStruct((windows, HALO, 2 * F), jnp.bfloat16),
        ],
        scratch_shapes=[pltpu.VMEM((2, STEP, 2 * F), jnp.bfloat16), pltpu.VMEM((4 * rows, 2 * F), jnp.float32)],
        compiler_params=pltpu.CompilerParams(vmem_limit_bytes=60 * MIB),
        cost_estimate=pl.CostEstimate(flops=2 * rows * length * 2 * F, bytes_accessed=rows * length * 2, transcendentals=0),
    )(flat, flat, flat, flat, angles, good)


def pieces(value):
    high = value.astype(jnp.bfloat16)
    rest = value - high.astype(jnp.float32)
    middle = rest.astype(jnp.bfloat16)
    return high, middle, (rest - middle.astype(jnp.float32)).astype(jnp.bfloat16)


def whiten_kernel(spec, left, right, band, good, *outs):
    windows, channels = spec.shape[:2]
    filtered = []
    keep = keep_column(good)
    for window in range(windows):
        stack = jnp.concatenate([left[window], *pieces(spec[window]), right[window]], axis=0)
        own = band[:, HALO : HALO + channels]
        taps = jnp.concatenate([band[:, :HALO], own, own, own, band[:, HALO + channels :]], axis=1)
        filtered.append(jnp.dot(taps, stack, preferred_element_type=jnp.float32) * keep)
    spectrum = jnp.concatenate(filtered, axis=0)
    real, imag = spectrum[:, :F], spectrum[:, F:]
    magnitude = jnp.sqrt(real * real + imag * imag)
    bins = lax.broadcasted_iota(jnp.int32, (F, F), 0)
    others = lax.broadcasted_iota(jnp.int32, (F, F), 1)
    near = jnp.where(jnp.abs(bins - others) <= SMOOTH, 1.0, 0.0).astype(jnp.bfloat16)
    amplitude = sum(jnp.dot(piece, near, preferred_element_type=jnp.float32) for piece in pieces(magnitude))
    bin_row = lax.broadcasted_iota(jnp.int32, (1, F), 1)
    count = jnp.minimum(bin_row + SMOOTH, F - 1) - jnp.maximum(bin_row - SMOOTH, 0) + 1
    amplitude = amplitude * (1.0 / count.astype(jnp.float32))
    inverse = 1.0 / (amplitude + 1e-06)
    real = (real * inverse).astype(jnp.bfloat16)
    imag = (imag * inverse).astype(jnp.bfloat16)
    full, *parts = outs
    for window in range(windows):
        rows = slice(window * channels, (window + 1) * channels)
        full[window, :, :F] = real[rows]
        full[window, :, F:] = imag[rows]
        for part, (begin, end) in zip(parts, Z_GROUPS):
            for at, (start, width) in enumerate(CHUNKS[begin:end]):
                part[at, 0, window, :, :width] = real[rows, start : start + width]
                part[at, 0, window, :, width:] = imag[rows, start : start + width]


def whiten(spec, left, right, band, good):
    windows, channels, _ = spec.shape
    return pl.pallas_call(
        whiten_kernel,
        out_shape=[
            jax.ShapeDtypeStruct(shape, jnp.bfloat16)
            for shape in [(windows, channels, 2 * F)]
            + [(end - begin, 1, windows, channels, 2 * CHUNKS[0][1]) for begin, end in Z_GROUPS]
        ],
        compiler_params=pltpu.CompilerParams(vmem_limit_bytes=40 * MIB),
        cost_estimate=pl.CostEstimate(flops=2 * windows * channels * F * F * 3, bytes_accessed=5 * MIB // 2, transcendentals=windows * channels * F),
    )(spec, left, right, band, good)


def eye(size):
    rows = lax.broadcasted_iota(jnp.int32, (size, size), 0)
    cols = lax.broadcasted_iota(jnp.int32, (size, size), 1)
    return jnp.where(rows == cols, 1.0, 0.0).astype(jnp.bfloat16)


def turned(left_unit, rows):
    return lax.dot_general(left_unit, rows, NT, preferred_element_type=jnp.float32)


def swapper(outer, inner):
    size = outer * inner
    rows = lax.broadcasted_iota(jnp.int32, (size, size), 0)
    cols = lax.broadcasted_iota(jnp.int32, (size, size), 1)
    return jnp.where(cols == rows % outer * inner + rows // outer, 1.0, 0.0).astype(jnp.bfloat16)


def moved(swap, rows):
    return jnp.dot(swap, rows, preferred_element_type=jnp.float32).astype(jnp.bfloat16)


def own_kernel(here, near, far, out, by_window):
    own = [here, near.at[0], far, near.at[1]]
    each, channels, _ = here.shape
    windows, quads = each * len(own), channels // 4
    joined = GROUP // each
    swap = swapper(GROUP, GROUP)
    for start in range(0, windows, GROUP):
        for channel in range(0, channels, GROUP):
            block = [o[:, channel : channel + GROUP, :] for o in own[start // each : start // each + joined]]
            rows = moved(swap, jnp.concatenate(block, axis=0).reshape(GROUP * GROUP, 2 * F))
            by_window[channel : channel + GROUP, start : start + GROUP, :] = rows.reshape(GROUP, GROUP, 2 * F)
    unit = eye(F // 2)
    for quad in range(quads):
        for start in range(0, F, F // 2):
            rows = []
            for channel in range(quad, channels, quads):
                rows += [by_window[channel, :, side + start : side + start + F // 2] for side in (0, F)]
            out[quad, start : start + F // 2, :] = turned(unit, jnp.concatenate(rows, axis=0)).astype(jnp.bfloat16)


def turn_own(here, near, far):
    each, channels, _ = here.shape
    windows = each * 4
    return pl.pallas_call(
        own_kernel,
        out_shape=jax.ShapeDtypeStruct((channels // 4, F, 8 * windows), jnp.bfloat16),
        scratch_shapes=[pltpu.VMEM((channels, windows, 2 * F), jnp.bfloat16)],
        compiler_params=pltpu.CompilerParams(vmem_limit_bytes=40 * MIB),
        cost_estimate=pl.CostEstimate(flops=2 * 8192 * 65536, bytes_accessed=4 * MIB, transcendentals=0),
    )(here, near, far)


def cross_kernel(here, near, far, by_channel, out, by_window, sums):
    sources = [here, near.at[0], far.at[0], near.at[1]]
    each, count, both = here.shape
    quads, _, wide = by_channel.shape
    channels, half = 4 * quads, wide // 4
    windows, width = half // 2, both // 2
    unit = eye(width)
    swap = swapper(GROUP, GROUP)
    swap_quads = swapper(quads, GROUP)
    for window in range(0, windows, 2):
        rows = []
        for one in range(window, window + 2):
            source = sources[one // each]
            rows += [source[one % each, :, :width], source[one % each, :, width:]]
        both_turned = turned(unit, jnp.concatenate(rows, axis=0)).astype(jnp.bfloat16)
        by_window[window] = both_turned[:, : 2 * count]
        by_window[window + 1] = both_turned[:, 2 * count :]
    first = lax.broadcasted_iota(jnp.int32, (1, 2 * half), 1) < half
    sign = jnp.where(lax.broadcasted_iota(jnp.int32, (1, 2 * count), 1) < count, 1.0, -1.0)
    empty = jnp.zeros((2 * windows, 2 * count), jnp.bfloat16)

    def one_group(group, carry):
        bins = pl.ds(pl.multiple_of(group * GROUP, GROUP), GROUP)
        rows = [
            by_window[start : start + GROUP, bins, :].reshape(GROUP * GROUP, 2 * count)
            for start in range(0, windows, GROUP)
        ]
        rights = jnp.dot(swap, jnp.concatenate(rows, axis=1), preferred_element_type=jnp.float32)
        lefts = jnp.dot(
            swap_quads, by_channel[:, bins, :].reshape(quads * GROUP, 4 * half), preferred_element_type=jnp.float32
        )
        results = []
        for at in range(0, GROUP, 2):
            two = []
            for one in range(at, at + 2):
                here = rights[one * GROUP : (one + 1) * GROUP]
                src = jnp.concatenate(
                    [here[:, i * 2 * count : (i + 1) * 2 * count] for i in range(windows // GROUP)], axis=0
                )
                two.append(jnp.concatenate([src * sign, pltpu.roll(src, count, axis=1)], axis=0).astype(jnp.bfloat16))
            right = jnp.concatenate(
                [jnp.concatenate([two[0], empty], axis=1), jnp.concatenate([empty, two[1]], axis=1)], axis=0
            )
            left = []
            for tile in range(0, 4 * half, 2 * half):
                one, other = (lefts[i * quads : (i + 1) * quads, tile : tile + 2 * half] for i in (at, at + 1))
                left.append(jnp.where(first, one, pltpu.roll(other, half, axis=1)))
                left.append(jnp.where(first, pltpu.roll(one, half, axis=1), other))
            left = jnp.concatenate(left, axis=0).astype(jnp.bfloat16)
            result = jnp.dot(left, right, preferred_element_type=jnp.float32).astype(jnp.bfloat16)
            results += [result[:, : 2 * count], result[:, 2 * count :]]
        halves = [
            jnp.concatenate([r[start : start + GROUP] for r in results], axis=0) for start in range(0, channels, GROUP)
        ]
        done = moved(swap, jnp.concatenate(halves, axis=1))
        for channel in range(channels):
            row, side = channel % GROUP, channel // GROUP
            sums[channel, bins, :] = done[
                row * GROUP : (row + 1) * GROUP, side * 2 * count : (side + 1) * 2 * count
            ]
        return carry

    lax.fori_loop(0, width // GROUP, one_group, 0, unroll=8)
    unit = eye(2 * count)
    part = 256 // LAG_ROWS
    swap = swapper(LAG_ROWS, part)
    for group in range(channels // LAG_ROWS):
        by_bin = []
        for channel in range(group * LAG_ROWS, (group + 1) * LAG_ROWS, 2):
            rows = jnp.concatenate([sums[channel], sums[channel + 1]], axis=0)
            both_turned = turned(unit, rows).astype(jnp.bfloat16)
            by_bin += [both_turned[:, :width], both_turned[:, width:]]
        for start in range(0, count, part):
            rows = jnp.concatenate(
                [
                    jnp.concatenate([b[start : start + part], b[count + start : count + start + part]], axis=1)
                    for b in by_bin
                ],
                axis=0,
            )
            rows = moved(swap, rows)
            at = slice(start * LAG_ROWS, (start + part) * LAG_ROWS)
            out[group, 0, at, :] = rows[:, :width]
            out[group, 1, at, :] = rows[:, width:]


def cross(here, near, far, by_channel, first_bin):
    each, count, both = here.shape
    quads, _, wide = by_channel.shape
    channels, windows, width = 4 * quads, wide // 8, both // 2
    return pl.pallas_call(
        cross_kernel,
        grid=(1,),
        in_specs=[pl.BlockSpec(a.shape, functools.partial(lambda n, i: (0,) * n, a.ndim)) for a in (here, near, far)]
        + [pl.BlockSpec((quads, width, wide), lambda i: (0, first_bin // width, 0))],
        out_specs=pl.BlockSpec((channels // LAG_ROWS, 2, count * LAG_ROWS, width), lambda i: (0, 0, 0, 0)),
        out_shape=jax.ShapeDtypeStruct((channels // LAG_ROWS, 2, count * LAG_ROWS, width), jnp.bfloat16),
        scratch_shapes=[
            pltpu.VMEM((windows, width, 2 * count), jnp.bfloat16),
            pltpu.VMEM((channels, width, 2 * count), jnp.bfloat16),
        ],
        compiler_params=pltpu.CompilerParams(vmem_limit_bytes=40 * MIB),
        cost_estimate=pl.CostEstimate(flops=2 * width * 36 * 65536, bytes_accessed=4 * MIB, transcendentals=0),
    )(here, near, far, by_channel)


def lag_kernel(scaling, *refs):
    *stacked, table, edge, out = refs
    count, channels, _ = out.shape
    real, imag = (jnp.concatenate([chunk[0, side] for chunk in stacked], axis=1) for side in range(2))
    size = count * channels
    lane = lax.broadcasted_iota(jnp.int32, (size, LAG_FINE), 1)
    mirror = (LAG_FINE - lane) % LAG_FINE

    def parts(start, width):
        even = jnp.dot(real, table[:F, start : start + width], preferred_element_type=jnp.float32)
        odd = jnp.dot(imag, table[F:, start : start + width], preferred_element_type=jnp.float32)
        return even, odd

    half = LAGS // 2
    products = real.astype(jnp.float32) * edge[:1] + imag.astype(jnp.float32) * edge[1:]
    above = jnp.sum(products, axis=1, keepdims=True) * scaling
    for start in range(half - 2 * LAG_FINE, -1, -2 * LAG_FINE):
        even, odd = parts(start, 2 * LAG_FINE)
        after_zero = (even - odd) * scaling
        before_zero = (even + odd) * scaling
        out[:, :, half + start : half + start + 2 * LAG_FINE] = after_zero.reshape(count, channels, 2 * LAG_FINE)
        for tile in (1, 0):
            turned_round = jnp.take_along_axis(
                before_zero[:, tile * LAG_FINE : (tile + 1) * LAG_FINE], mirror, axis=1, mode="promise_in_bounds"
            )
            at = half - start - (tile + 1) * LAG_FINE
            out[:, :, at : at + LAG_FINE] = jnp.where(lane == 0, above, turned_round).reshape(count, channels, LAG_FINE)
            above = turned_round


def lagged(stacked, table, scaling):
    groups, _, size, _ = stacked[0].shape
    edge = np.concatenate(unit_angles(np.array([LAGS // 2]), 0), axis=0).astype(jnp.bfloat16).astype(np.float32)
    count = size // LAG_ROWS
    return pl.pallas_call(
        functools.partial(lag_kernel, scaling),
        grid=(groups,),
        in_specs=[pl.BlockSpec((1, 2, size, s.shape[3]), lambda i: (i, 0, 0, 0)) for s in stacked]
        + [pl.BlockSpec(a.shape, lambda i: (0, 0)) for a in (table, edge)],
        out_specs=pl.BlockSpec((count, LAG_ROWS, LAGS), lambda i: (0, i, 0)),
        out_shape=jax.ShapeDtypeStruct((count, groups * LAG_ROWS, LAGS), jnp.float32),
        compiler_params=pltpu.CompilerParams(vmem_limit_bytes=48 * MIB),
        cost_estimate=pl.CostEstimate(
            flops=2 * groups * size * F * LAGS, bytes_accessed=groups * size * LAGS * 4, transcendentals=0
        ),
    )(*stacked, table, edge)


def table_kernel(angles, out):
    fine_cos, fine_sin = angles[:, :LAG_FINE], angles[:, LAG_FINE : 2 * LAG_FINE]
    tiles = out.shape[1] // LAG_FINE
    for tile in range(tiles):
        big_cos = angles[:, 2 * LAG_FINE + tile : 2 * LAG_FINE + tile + 1]
        big_sin = angles[:, 2 * LAG_FINE + tiles + tile : 2 * LAG_FINE + tiles + tile + 1]
        cols = slice(tile * LAG_FINE, (tile + 1) * LAG_FINE)
        out[:F, cols] = (big_cos * fine_cos - big_sin * fine_sin).astype(jnp.bfloat16)
        out[F:, cols] = (big_sin * fine_cos + big_cos * fine_sin).astype(jnp.bfloat16)


def lag_table():
    tiles = LAGS // 2 // LAG_FINE
    coarse = unit_angles(np.arange(tiles) * LAG_FINE, 1)
    angles = np.concatenate(unit_angles(np.arange(LAG_FINE), 1) + coarse, axis=1)
    return pl.pallas_call(
        table_kernel,
        out_shape=jax.ShapeDtypeStruct((2 * F, tiles * LAG_FINE), jnp.bfloat16),
        compiler_params=pltpu.CompilerParams(vmem_limit_bytes=40 * MIB),
        cost_estimate=pl.CostEstimate(flops=8 * F * tiles * LAG_FINE, bytes_accessed=4 * MIB, transcendentals=0),
    )(angles)


def make_band(filter_taps, channel_count):
    kernel = jnp.concatenate(
        [
            -filter_taps[:HALO].astype(jnp.float32),
            jnp.ones((1,), jnp.float32),
            -filter_taps[HALO:].astype(jnp.float32),
        ]
    )
    row_ids = jnp.arange(channel_count, dtype=jnp.int32)[:, None]
    columns = jnp.arange(channel_count + 2 * HALO, dtype=jnp.int32)[None, :]
    offset = columns - row_ids
    choose = offset[:, :, None] == jnp.arange(2 * HALO + 1, dtype=jnp.int32)[None, None, :]
    return jnp.sum(jnp.where(choose, kernel[None, None, :], 0.0), axis=2).astype(jnp.bfloat16)


def pick_kernel(held, across, selector, here, near, far):
    count = here.shape[1]
    for window in range(held.shape[1]):
        rows = [blocks[i, window] for blocks in (held, across) for i in range(blocks.shape[0])]
        picked = jnp.dot(selector[...], jnp.concatenate(rows, axis=0), preferred_element_type=jnp.float32)
        picked = picked.astype(jnp.bfloat16)
        here[window] = picked[:count]
        near[window] = picked[count : 2 * count]
        for at in range(far.shape[0]):
            far[at, window] = picked[(2 + at) * count : (3 + at) * count]


def pick(held, across, selector, groups):
    _, windows, _, both = held.shape
    count = selector.shape[0] // groups
    one = (windows, count, both)
    return pl.pallas_call(
        pick_kernel,
        out_shape=[jax.ShapeDtypeStruct(shape, jnp.bfloat16) for shape in (one, one, (groups - 2, *one))],
        compiler_params=pltpu.CompilerParams(vmem_limit_bytes=40 * MIB),
        cost_estimate=pl.CostEstimate(
            flops=2 * windows * selector.size * both, bytes_accessed=2 * windows * both * sum(selector.shape), transcendentals=0
        ),
    )(held, across, selector)


def swapped(value, axis, step):
    return lax.ppermute(value, axis, [(i, i ^ step) for i in range(lax.axis_size(axis))])


def after(value, earlier):
    return lax.optimization_barrier((value, earlier))[0]


def per_device(traces, filter_taps, good_channels, source_index):
    window_count, channel_count, _ = traces.shape
    good = good_channels[None, :]
    spec, head, tail = transform(traces, good)
    blocks = lax.axis_size("chan")
    groups = lax.axis_size("win")
    left = lax.ppermute(tail, "chan", [(i, i + 1) for i in range(blocks - 1)])
    right = lax.ppermute(head, "chan", [(i + 1, i) for i in range(blocks - 1)])
    table = lag_table()
    left = after(left, table)
    full, *parts = whiten(spec, left, right, make_band(filter_taps, channel_count), good)

    order = [0]
    step = blocks // 2
    while step:
        order += [place ^ step for place in order]
        step //= 2
    order = jnp.asarray(order, jnp.int32) ^ lax.axis_index("chan")
    own_ids = jnp.arange(channel_count, dtype=jnp.int32)
    channel_ids = (order[:, None] * channel_count + own_ids[None, :]).reshape(-1)
    by_group = source_index.reshape(groups, -1)
    here = lax.axis_index("win")
    wanted = jnp.concatenate([lax.dynamic_slice_in_dim(by_group, here ^ step, 1) for step in range(groups)], axis=0)
    selector = (wanted.reshape(-1)[:, None] == channel_ids[None, :]).astype(jnp.bfloat16)

    own_far = swapped(full, "win", 2)
    own_near = swapped(jnp.stack([full, own_far]), "win", 1)
    by_channel = turn_own(full, own_near, own_far)
    gathered, picked, stacked = [], [], []
    chunks = len(CHUNKS)

    def gather(part):
        held, step = part, blocks // 2
        while step > 1:
            received = swapped(held, "chan", step)
            if step > 2:
                held = jnp.concatenate([held, received], axis=1)
                if step == blocks // 2:
                    first_held.append(held)
                    if gathered:
                        held = after(held, gathered[-1] if picked else own_far)
            step //= 2
        gathered.extend(jnp.concatenate([held[i], received[i]], axis=0) for i in range(part.shape[0]))

    def exchange(at):
        held = after(gathered[at], picked[-1][0]) if at else gathered[at]
        across = swapped(held, "chan", 1)
        if at > 1:
            finish(at - 2)
        across = after(across, (stacked[-1] if stacked else by_channel) if at else gathered[1])
        here, near, far = pick(held, across, selector, groups)
        picked.append((here, near, swapped(far, "win", 2)))

    def finish(at):
        here, near, far = picked[at]
        if stacked:
            far = after(far, stacked[-1])
        near = swapped(jnp.stack([near, far[1]]), "win", 1)
        stacked.append(cross(here, near, far, by_channel, CHUNKS[at][0]))

    first_held = []
    for part in parts:
        gather(after(part, first_held[-1]) if len(first_held) > 1 else part)
        if len(gathered) == 2:
            exchange(0)
    for at in range(1, chunks):
        exchange(at)
    for at in range(len(stacked), chunks):
        finish(at)
    return lagged(stacked, table, 1.0 / math.sqrt(F * window_count * groups))


def solution(mesh):
    placed = (P("win", "chan", None), P(), P("chan"), P())
    return jax.shard_map(
        per_device, mesh=mesh, in_specs=placed, out_specs=P("win", "chan", None), check_vma=False
    )
```

```python
import functools
import math

import jax
import jax.numpy as jnp
import numpy as np
from jax import lax
from jax.experimental import pallas as pl
from jax.experimental.pallas import tpu as pltpu
from jax.sharding import PartitionSpec as P

L = 7680
F = 512
LAGS = 2048
HALO = 16
SMOOTH = 64
K0 = 31
QUARTER = L // 4
STEP = 640
FINE = 32
CHUNKS = tuple((start, 128) for start in range(0, F, 128))
Z_GROUPS = ((0, 1), (1, 2), (2, 4))
GROUP = 16
LAG_FINE = 128
LAG_ROWS = 8
NT = (((1,), (1,)), ((), ()))
MIB = 1024 * 1024


def unit_angles(positions, axis):
    bins = K0 + np.arange(F, dtype=np.int64)
    phase = np.mod(np.expand_dims(positions, 1 - axis) * np.expand_dims(bins, axis), L)
    angles = phase * (2.0 * math.pi / L)
    return np.cos(angles).astype(np.float32), np.sin(angles).astype(np.float32)


def keep_column(good):
    count = good.shape[1]
    rows = lax.broadcasted_iota(jnp.int32, (count, count), 0)
    cols = lax.broadcasted_iota(jnp.int32, (count, count), 1)
    return jnp.sum(jnp.where(rows == cols, good[...].astype(jnp.float32), 0.0), axis=1, keepdims=True)


def transform_kernel(x0, x1, x2, x3, angles, good, spec, head, tail, table, total):
    step = pl.program_id(0)
    rows = x0.shape[0]
    coarse = QUARTER // FINE

    def fill(of_step):
        fine_cos = angles[2 * coarse : 2 * coarse + FINE, :]
        fine_sin = angles[2 * coarse + FINE :, :]
        for part in range(STEP // FINE):
            big_cos = angles[pl.ds(of_step * (STEP // FINE) + part, 1), :]
            big_sin = angles[pl.ds(coarse + of_step * (STEP // FINE) + part, 1), :]
            at = pl.ds(part * FINE, FINE)
            table[of_step % 2, at, :F] = (big_cos * fine_cos - big_sin * fine_sin).astype(jnp.bfloat16)
            table[of_step % 2, at, F:] = (-(big_sin * fine_cos + big_cos * fine_sin)).astype(jnp.bfloat16)

    @pl.when(step == 0)
    def _():
        total[...] = jnp.zeros_like(total)
        fill(step)

    for quarter, x in enumerate((x0, x1, x2, x3)):
        at = pl.ds(quarter * rows, rows)
        total[at, :] += jnp.dot(x[...], table[step % 2], preferred_element_type=jnp.float32)
    fill(jnp.minimum(step + 1, pl.num_programs(0) - 1))

    @pl.when(step == pl.num_programs(0) - 1)
    def _():
        turn = (K0 + lax.broadcasted_iota(jnp.int32, (1, F), 1)) % 4
        even = turn % 2 == 0
        sign = jnp.where(turn < 2, 1.0, -1.0)
        channels = good.shape[1]
        keep = keep_column(good)
        for window in range(rows // channels):
            re = [total[pl.ds(q * rows + window * channels, channels), :F] for q in range(4)]
            im = [total[pl.ds(q * rows + window * channels, channels), F:] for q in range(4)]
            real = jnp.where(even, re[0] + re[2] + sign * (re[1] + re[3]), re[0] - re[2] + sign * (im[1] - im[3])) * keep
            imag = jnp.where(even, im[0] + im[2] + sign * (im[1] + im[3]), im[0] - im[2] - sign * (re[1] - re[3])) * keep
            spec[window, :, :F] = real
            spec[window, :, F:] = imag
            head[window, :, :F] = real[:HALO].astype(jnp.bfloat16)
            head[window, :, F:] = imag[:HALO].astype(jnp.bfloat16)
            tail[window, :, :F] = real[channels - HALO :].astype(jnp.bfloat16)
            tail[window, :, F:] = imag[channels - HALO :].astype(jnp.bfloat16)


def transform(traces, good):
    windows, channels, length = traces.shape
    rows = windows * channels
    steps = QUARTER // STEP
    flat = traces.reshape(rows, length)
    coarse = unit_angles(np.arange(QUARTER // FINE) * FINE, 0)
    angles = np.concatenate(coarse + unit_angles(np.arange(FINE), 0), axis=0)
    whole = lambda *shape: pl.BlockSpec(shape, lambda k: (0,) * len(shape))
    return pl.pallas_call(
        transform_kernel,
        grid=(steps,),
        in_specs=[pl.BlockSpec((rows, STEP), functools.partial(lambda q, k: (0, q * steps + k), q)) for q in range(4)]
        + [whole(*angles.shape), whole(1, channels)],
        out_specs=[whole(windows, channels, 2 * F), whole(windows, HALO, 2 * F), whole(windows, HALO, 2 * F)],
        out_shape=[
            jax.ShapeDtypeStruct((windows, channels, 2 * F), jnp.float32),
            jax.ShapeDtypeStruct((windows, HALO, 2 * F), jnp.bfloat16),
            jax.ShapeDtypeStruct((windows, HALO, 2 * F), jnp.bfloat16),
        ],
        scratch_shapes=[pltpu.VMEM((2, STEP, 2 * F), jnp.bfloat16), pltpu.VMEM((4 * rows, 2 * F), jnp.float32)],
        compiler_params=pltpu.CompilerParams(vmem_limit_bytes=60 * MIB),
        cost_estimate=pl.CostEstimate(flops=2 * rows * length * 2 * F, bytes_accessed=rows * length * 2, transcendentals=0),
    )(flat, flat, flat, flat, angles, good)


def pieces(value):
    high = value.astype(jnp.bfloat16)
    rest = value - high.astype(jnp.float32)
    middle = rest.astype(jnp.bfloat16)
    return high, middle, (rest - middle.astype(jnp.float32)).astype(jnp.bfloat16)


def whiten_kernel(spec, left, right, band, good, *outs):
    windows, channels = spec.shape[:2]
    filtered = []
    keep = keep_column(good)
    for window in range(windows):
        stack = jnp.concatenate([left[window], *pieces(spec[window]), right[window]], axis=0)
        own = band[:, HALO : HALO + channels]
        taps = jnp.concatenate([band[:, :HALO], own, own, own, band[:, HALO + channels :]], axis=1)
        filtered.append(jnp.dot(taps, stack, preferred_element_type=jnp.float32) * keep)
    spectrum = jnp.concatenate(filtered, axis=0)
    real, imag = spectrum[:, :F], spectrum[:, F:]
    magnitude = jnp.sqrt(real * real + imag * imag)
    bins = lax.broadcasted_iota(jnp.int32, (F, F), 0)
    others = lax.broadcasted_iota(jnp.int32, (F, F), 1)
    near = jnp.where(jnp.abs(bins - others) <= SMOOTH, 1.0, 0.0).astype(jnp.bfloat16)
    amplitude = sum(jnp.dot(piece, near, preferred_element_type=jnp.float32) for piece in pieces(magnitude))
    bin_row = lax.broadcasted_iota(jnp.int32, (1, F), 1)
    count = jnp.minimum(bin_row + SMOOTH, F - 1) - jnp.maximum(bin_row - SMOOTH, 0) + 1
    amplitude = amplitude * (1.0 / count.astype(jnp.float32))
    inverse = 1.0 / (amplitude + 1e-06)
    real = (real * inverse).astype(jnp.bfloat16)
    imag = (imag * inverse).astype(jnp.bfloat16)
    full, *parts = outs
    for window in range(windows):
        rows = slice(window * channels, (window + 1) * channels)
        full[window, :, :F] = real[rows]
        full[window, :, F:] = imag[rows]
        for part, (begin, end) in zip(parts, Z_GROUPS):
            for at, (start, width) in enumerate(CHUNKS[begin:end]):
                part[at, 0, window, :, :width] = real[rows, start : start + width]
                part[at, 0, window, :, width:] = imag[rows, start : start + width]


def whiten(spec, left, right, band, good):
    windows, channels, _ = spec.shape
    return pl.pallas_call(
        whiten_kernel,
        out_shape=[
            jax.ShapeDtypeStruct(shape, jnp.bfloat16)
            for shape in [(windows, channels, 2 * F)]
            + [(end - begin, 1, windows, channels, 2 * CHUNKS[0][1]) for begin, end in Z_GROUPS]
        ],
        compiler_params=pltpu.CompilerParams(vmem_limit_bytes=40 * MIB),
        cost_estimate=pl.CostEstimate(flops=2 * windows * channels * F * F * 3, bytes_accessed=5 * MIB // 2, transcendentals=windows * channels * F),
    )(spec, left, right, band, good)


def eye(size):
    rows = lax.broadcasted_iota(jnp.int32, (size, size), 0)
    cols = lax.broadcasted_iota(jnp.int32, (size, size), 1)
    return jnp.where(rows == cols, 1.0, 0.0).astype(jnp.bfloat16)


def turned(left_unit, rows):
    return lax.dot_general(left_unit, rows, NT, preferred_element_type=jnp.float32)


def swapper(outer, inner):
    size = outer * inner
    rows = lax.broadcasted_iota(jnp.int32, (size, size), 0)
    cols = lax.broadcasted_iota(jnp.int32, (size, size), 1)
    return jnp.where(cols == rows % outer * inner + rows // outer, 1.0, 0.0).astype(jnp.bfloat16)


def moved(swap, rows):
    return jnp.dot(swap, rows, preferred_element_type=jnp.float32).astype(jnp.bfloat16)


def own_kernel(here, near, far, out, by_window):
    own = [here, near.at[0], far, near.at[1]]
    each, channels, _ = here.shape
    windows, quads = each * len(own), channels // 4
    joined = GROUP // each
    swap = swapper(GROUP, GROUP)
    for start in range(0, windows, GROUP):
        for channel in range(0, channels, GROUP):
            block = [o[:, channel : channel + GROUP, :] for o in own[start // each : start // each + joined]]
            rows = moved(swap, jnp.concatenate(block, axis=0).reshape(GROUP * GROUP, 2 * F))
            by_window[channel : channel + GROUP, start : start + GROUP, :] = rows.reshape(GROUP, GROUP, 2 * F)
    unit = eye(F // 2)
    for quad in range(quads):
        for start in range(0, F, F // 2):
            rows = []
            for channel in range(quad, channels, quads):
                rows += [by_window[channel, :, side + start : side + start + F // 2] for side in (0, F)]
            out[quad, start : start + F // 2, :] = turned(unit, jnp.concatenate(rows, axis=0)).astype(jnp.bfloat16)


def turn_own(here, near, far):
    each, channels, _ = here.shape
    windows = each * 4
    return pl.pallas_call(
        own_kernel,
        out_shape=jax.ShapeDtypeStruct((channels // 4, F, 8 * windows), jnp.bfloat16),
        scratch_shapes=[pltpu.VMEM((channels, windows, 2 * F), jnp.bfloat16)],
        compiler_params=pltpu.CompilerParams(vmem_limit_bytes=40 * MIB),
        cost_estimate=pl.CostEstimate(flops=2 * 8192 * 65536, bytes_accessed=4 * MIB, transcendentals=0),
    )(here, near, far)


def cross_kernel(*refs):
    *sources, by_channel, out, by_window, sums = refs
    if len(sources) == 3:
        here, near, far = sources
        sources = [here, near.at[0], far.at[0], near.at[1]]
    here = sources[0]
    each, count, both = here.shape
    quads, _, wide = by_channel.shape
    channels, half = 4 * quads, wide // 4
    windows, width = half // 2, both // 2
    unit = eye(width)
    swap = swapper(GROUP, GROUP)
    swap_quads = swapper(quads, GROUP)
    for window in range(0, windows, 2):
        rows = []
        for one in range(window, window + 2):
            source = sources[one // each]
            rows += [source[one % each, :, :width], source[one % each, :, width:]]
        both_turned = turned(unit, jnp.concatenate(rows, axis=0)).astype(jnp.bfloat16)
        by_window[window] = both_turned[:, : 2 * count]
        by_window[window + 1] = both_turned[:, 2 * count :]
    first = lax.broadcasted_iota(jnp.int32, (1, 2 * half), 1) < half
    sign = jnp.where(lax.broadcasted_iota(jnp.int32, (1, 2 * count), 1) < count, 1.0, -1.0)
    empty = jnp.zeros((2 * windows, 2 * count), jnp.bfloat16)

    def one_group(group, carry):
        bins = pl.ds(pl.multiple_of(group * GROUP, GROUP), GROUP)
        rows = [
            by_window[start : start + GROUP, bins, :].reshape(GROUP * GROUP, 2 * count)
            for start in range(0, windows, GROUP)
        ]
        rights = jnp.dot(swap, jnp.concatenate(rows, axis=1), preferred_element_type=jnp.float32)
        lefts = jnp.dot(
            swap_quads, by_channel[:, bins, :].reshape(quads * GROUP, 4 * half), preferred_element_type=jnp.float32
        )
        results = []
        for at in range(0, GROUP, 2):
            two = []
            for one in range(at, at + 2):
                here = rights[one * GROUP : (one + 1) * GROUP]
                src = jnp.concatenate(
                    [here[:, i * 2 * count : (i + 1) * 2 * count] for i in range(windows // GROUP)], axis=0
                )
                two.append(jnp.concatenate([src * sign, pltpu.roll(src, count, axis=1)], axis=0).astype(jnp.bfloat16))
            right = jnp.concatenate(
                [jnp.concatenate([two[0], empty], axis=1), jnp.concatenate([empty, two[1]], axis=1)], axis=0
            )
            left = []
            for tile in range(0, 4 * half, 2 * half):
                one, other = (lefts[i * quads : (i + 1) * quads, tile : tile + 2 * half] for i in (at, at + 1))
                left.append(jnp.where(first, one, pltpu.roll(other, half, axis=1)))
                left.append(jnp.where(first, pltpu.roll(one, half, axis=1), other))
            left = jnp.concatenate(left, axis=0).astype(jnp.bfloat16)
            result = jnp.dot(left, right, preferred_element_type=jnp.float32).astype(jnp.bfloat16)
            results += [result[:, : 2 * count], result[:, 2 * count :]]
        halves = [
            jnp.concatenate([r[start : start + GROUP] for r in results], axis=0) for start in range(0, channels, GROUP)
        ]
        done = moved(swap, jnp.concatenate(halves, axis=1))
        for channel in range(channels):
            row, side = channel % GROUP, channel // GROUP
            sums[channel, bins, :] = done[
                row * GROUP : (row + 1) * GROUP, side * 2 * count : (side + 1) * 2 * count
            ]
        return carry

    lax.fori_loop(0, width // GROUP, one_group, 0, unroll=8)
    unit = eye(2 * count)
    part = 256 // LAG_ROWS
    swap = swapper(LAG_ROWS, part)
    for group in range(channels // LAG_ROWS):
        by_bin = []
        for channel in range(group * LAG_ROWS, (group + 1) * LAG_ROWS, 2):
            rows = jnp.concatenate([sums[channel], sums[channel + 1]], axis=0)
            both_turned = turned(unit, rows).astype(jnp.bfloat16)
            by_bin += [both_turned[:, :width], both_turned[:, width:]]
        for start in range(0, count, part):
            rows = jnp.concatenate(
                [
                    jnp.concatenate([b[start : start + part], b[count + start : count + start + part]], axis=1)
                    for b in by_bin
                ],
                axis=0,
            )
            rows = moved(swap, rows)
            at = slice(start * LAG_ROWS, (start + part) * LAG_ROWS)
            out[group, 0, at, :] = rows[:, :width]
            out[group, 1, at, :] = rows[:, width:]


def cross(sources, by_channel, first_bin):
    each, count, both = sources[0].shape
    quads, _, wide = by_channel.shape
    channels, windows, width = 4 * quads, wide // 8, both // 2
    return pl.pallas_call(
        cross_kernel,
        grid=(1,),
        in_specs=[pl.BlockSpec(a.shape, functools.partial(lambda n, i: (0,) * n, a.ndim)) for a in sources]
        + [pl.BlockSpec((quads, width, wide), lambda i: (0, first_bin // width, 0))],
        out_specs=pl.BlockSpec((channels // LAG_ROWS, 2, count * LAG_ROWS, width), lambda i: (0, 0, 0, 0)),
        out_shape=jax.ShapeDtypeStruct((channels // LAG_ROWS, 2, count * LAG_ROWS, width), jnp.bfloat16),
        scratch_shapes=[
            pltpu.VMEM((windows, width, 2 * count), jnp.bfloat16),
            pltpu.VMEM((channels, width, 2 * count), jnp.bfloat16),
        ],
        compiler_params=pltpu.CompilerParams(vmem_limit_bytes=40 * MIB),
        cost_estimate=pl.CostEstimate(flops=2 * width * 36 * 65536, bytes_accessed=4 * MIB, transcendentals=0),
    )(*sources, by_channel)


def lag_kernel(scaling, *refs):
    *stacked, table, edge, out = refs
    count, channels, _ = out.shape
    real, imag = (jnp.concatenate([chunk[0, side] for chunk in stacked], axis=1) for side in range(2))
    size = count * channels
    lane = lax.broadcasted_iota(jnp.int32, (size, LAG_FINE), 1)
    mirror = (LAG_FINE - lane) % LAG_FINE

    def parts(start, width):
        even = jnp.dot(real, table[:F, start : start + width], preferred_element_type=jnp.float32)
        odd = jnp.dot(imag, table[F:, start : start + width], preferred_element_type=jnp.float32)
        return even, odd

    half = LAGS // 2
    products = real.astype(jnp.float32) * edge[:1] + imag.astype(jnp.float32) * edge[1:]
    above = jnp.sum(products, axis=1, keepdims=True) * scaling
    for start in range(half - 2 * LAG_FINE, -1, -2 * LAG_FINE):
        even, odd = parts(start, 2 * LAG_FINE)
        after_zero = (even - odd) * scaling
        before_zero = (even + odd) * scaling
        out[:, :, half + start : half + start + 2 * LAG_FINE] = after_zero.reshape(count, channels, 2 * LAG_FINE)
        for tile in (1, 0):
            turned_round = jnp.take_along_axis(
                before_zero[:, tile * LAG_FINE : (tile + 1) * LAG_FINE], mirror, axis=1, mode="promise_in_bounds"
            )
            at = half - start - (tile + 1) * LAG_FINE
            out[:, :, at : at + LAG_FINE] = jnp.where(lane == 0, above, turned_round).reshape(count, channels, LAG_FINE)
            above = turned_round


def lagged(stacked, table, scaling):
    groups, _, rows, _ = stacked[0].shape
    size = rows // 2
    edge = np.concatenate(unit_angles(np.array([LAGS // 2]), 0), axis=0).astype(jnp.bfloat16).astype(np.float32)
    count = size // LAG_ROWS
    return pl.pallas_call(
        functools.partial(lag_kernel, scaling),
        grid=(groups, 2),
        in_specs=[pl.BlockSpec((1, 2, size, s.shape[3]), lambda i, j: (i, 0, j, 0)) for s in stacked]
        + [pl.BlockSpec(a.shape, lambda i, j: (0, 0)) for a in (table, edge)],
        out_specs=pl.BlockSpec((count, LAG_ROWS, LAGS), lambda i, j: (j, i, 0)),
        out_shape=jax.ShapeDtypeStruct((2 * count, groups * LAG_ROWS, LAGS), jnp.float32),
        compiler_params=pltpu.CompilerParams(vmem_limit_bytes=48 * MIB),
        cost_estimate=pl.CostEstimate(
            flops=2 * groups * rows * F * LAGS, bytes_accessed=groups * rows * LAGS * 4, transcendentals=0
        ),
    )(*stacked, table, edge)


def table_kernel(angles, out):
    fine_cos, fine_sin = angles[:, :LAG_FINE], angles[:, LAG_FINE : 2 * LAG_FINE]
    tiles = out.shape[1] // LAG_FINE
    for tile in range(tiles):
        big_cos = angles[:, 2 * LAG_FINE + tile : 2 * LAG_FINE + tile + 1]
        big_sin = angles[:, 2 * LAG_FINE + tiles + tile : 2 * LAG_FINE + tiles + tile + 1]
        cols = slice(tile * LAG_FINE, (tile + 1) * LAG_FINE)
        out[:F, cols] = (big_cos * fine_cos - big_sin * fine_sin).astype(jnp.bfloat16)
        out[F:, cols] = (big_sin * fine_cos + big_cos * fine_sin).astype(jnp.bfloat16)


def lag_table():
    tiles = LAGS // 2 // LAG_FINE
    coarse = unit_angles(np.arange(tiles) * LAG_FINE, 1)
    angles = np.concatenate(unit_angles(np.arange(LAG_FINE), 1) + coarse, axis=1)
    return pl.pallas_call(
        table_kernel,
        out_shape=jax.ShapeDtypeStruct((2 * F, tiles * LAG_FINE), jnp.bfloat16),
        compiler_params=pltpu.CompilerParams(vmem_limit_bytes=40 * MIB),
        cost_estimate=pl.CostEstimate(flops=8 * F * tiles * LAG_FINE, bytes_accessed=4 * MIB, transcendentals=0),
    )(angles)


def make_band(filter_taps, channel_count):
    kernel = jnp.concatenate(
        [
            -filter_taps[:HALO].astype(jnp.float32),
            jnp.ones((1,), jnp.float32),
            -filter_taps[HALO:].astype(jnp.float32),
        ]
    )
    row_ids = jnp.arange(channel_count, dtype=jnp.int32)[:, None]
    columns = jnp.arange(channel_count + 2 * HALO, dtype=jnp.int32)[None, :]
    offset = columns - row_ids
    choose = offset[:, :, None] == jnp.arange(2 * HALO + 1, dtype=jnp.int32)[None, None, :]
    return jnp.sum(jnp.where(choose, kernel[None, None, :], 0.0), axis=2).astype(jnp.bfloat16)


def pick_kernel(held, across, selector, here, near, *far):
    count = here.shape[1]
    for window in range(held.shape[1]):
        rows = [blocks[i, window] for blocks in (held, across) for i in range(blocks.shape[0])]
        picked = jnp.dot(selector[...], jnp.concatenate(rows, axis=0), preferred_element_type=jnp.float32)
        picked = picked.astype(jnp.bfloat16)
        here[window] = picked[:count]
        near[window] = picked[count : 2 * count]
        for at, out in enumerate([far[0].at[i] for i in range(far[0].shape[0])] if len(far) == 1 else far):
            out[window] = picked[(2 + at) * count : (3 + at) * count]


def pick(held, across, selector, groups, apart=False):
    _, windows, _, both = held.shape
    count = selector.shape[0] // groups
    one = (windows, count, both)
    return pl.pallas_call(
        pick_kernel,
        out_shape=[jax.ShapeDtypeStruct(shape, jnp.bfloat16) for shape in [one, one] + ([one] * (groups - 2) if apart else [(groups - 2, *one)])],
        compiler_params=pltpu.CompilerParams(vmem_limit_bytes=40 * MIB),
        cost_estimate=pl.CostEstimate(
            flops=2 * windows * selector.size * both, bytes_accessed=2 * windows * both * sum(selector.shape), transcendentals=0
        ),
    )(held, across, selector)


def swapped(value, axis, step):
    return lax.ppermute(value, axis, [(i, i ^ step) for i in range(lax.axis_size(axis))])


def after(value, earlier):
    return lax.optimization_barrier((value, earlier))[0]


def per_device(traces, filter_taps, good_channels, source_index):
    window_count, channel_count, _ = traces.shape
    good = good_channels[None, :]
    spec, head, tail = transform(traces, good)
    blocks = lax.axis_size("chan")
    groups = lax.axis_size("win")
    left = lax.ppermute(tail, "chan", [(i, i + 1) for i in range(blocks - 1)])
    right = lax.ppermute(head, "chan", [(i + 1, i) for i in range(blocks - 1)])
    table = lag_table()
    left = after(left, table)
    full, *parts = whiten(spec, left, right, make_band(filter_taps, channel_count), good)

    order = [0]
    step = blocks // 2
    while step:
        order += [place ^ step for place in order]
        step //= 2
    order = jnp.asarray(order, jnp.int32) ^ lax.axis_index("chan")
    own_ids = jnp.arange(channel_count, dtype=jnp.int32)
    channel_ids = (order[:, None] * channel_count + own_ids[None, :]).reshape(-1)
    by_group = source_index.reshape(groups, -1)
    here = lax.axis_index("win")
    wanted = jnp.concatenate([lax.dynamic_slice_in_dim(by_group, here ^ step, 1) for step in range(groups)], axis=0)
    selector = (wanted.reshape(-1)[:, None] == channel_ids[None, :]).astype(jnp.bfloat16)

    own_far = swapped(full, "win", 2)
    own_near = swapped(jnp.stack([full, own_far]), "win", 1)
    by_channel = turn_own(full, own_near, own_far)
    gathered, picked, stacked = [], [], []
    chunks = len(CHUNKS)

    def gather(part):
        held, step = part, blocks // 2
        while step > 1:
            received = swapped(held, "chan", step)
            if step > 2:
                held = jnp.concatenate([held, received], axis=1)
                if step == blocks // 2:
                    first_held.append(held)
                    if len(gathered) > 1:
                        held = after(held, picked[0][0])
            step //= 2
        gathered.extend(jnp.concatenate([held[i], received[i]], axis=0) for i in range(part.shape[0]))

    def exchange(at):
        held = after(gathered[at], picked[-1][0]) if at else gathered[at]
        across = swapped(held, "chan", 1)
        if at > 1:
            finish(at - 2)
        across = after(across, (stacked[-1] if stacked else by_channel) if at else gathered[1])
        if at < chunks - 1:
            here, near, far = pick(held, across, selector, groups)
            picked.append((here, near, swapped(far, "win", 2)))
        else:
            here, *others = pick(held, across, selector, groups, True)
            picked.append((here, *(swapped(other, "win", step + 1) for step, other in enumerate(others))))

    def finish(at):
        if at == chunks - 1:
            here, *others = picked[at]
            stacked.append(cross(after([here, *others], stacked[-1]), by_channel, CHUNKS[at][0]))
            return
        here, near, far = picked[at]
        if stacked:
            far = after(far, stacked[-1])
        near = swapped(jnp.stack([near, far[1]]), "win", 1)
        stacked.append(cross([here, near, far], by_channel, CHUNKS[at][0]))

    first_held = []
    for part in parts:
        gather(after(part, [first_held[-1], own_far]) if len(first_held) > 1 else part)
        if len(gathered) == 2:
            exchange(0)
    for at in range(1, chunks):
        exchange(at)
    for at in range(len(stacked), chunks):
        finish(at)
    return lagged(stacked, table, 1.0 / math.sqrt(F * window_count * groups))


def solution(mesh):
    placed = (P("win", "chan", None), P(), P("chan"), P())
    return jax.shard_map(
        per_device, mesh=mesh, in_specs=placed, out_specs=P("win", "chan", None), check_vma=False
    )
```
